32 devices in a mesh: dp: 4 (over y, x), mp: 8 (over z, core).
Axes of the slice: x: 2, y: 2, z: 4, core: 2. Of those that a mesh axis runs over, the one named last changes fastest.
Arguments:
- incoming_signal: bfloat16 [4, 4, 1024, 1024], P(None, 'dp', 'mp'), may hold values from -6 to 6
- series_number_table: int32 [4, 4, 1024], P(None, 'dp', 'mp'), may hold values from 0 to 2, as said below
- upstream_adjoint: bfloat16 [4, 4, 1024, 1024], P(None, 'dp', 'mp'), may hold values from -6 to 6
- first_scaling_factor: bfloat16 [1024], replicated, may hold values from 0.5 to 1.5
- first_scaling_offset: bfloat16 [1024], replicated, may hold values from -3 to 3
- logarithmic_fading_speeds: bfloat16 [1024], replicated, as said below
- present_step_extra: bfloat16 [1024], replicated, may hold values from -1 to 1
- lookup_shift_mixture: bfloat16 [1024], replicated, may hold values from 0.049804688 to 0.94921875
- content_shift_mixture: bfloat16 [1024], replicated, may hold values from 0.049804688 to 0.94921875
- admit_lookup_shift_mixture: bfloat16 [1024], replicated, may hold values from 0.049804688 to 0.94921875
- attention_lookup_matrix: bfloat16 [1024, 1024], replicated, may hold values from -0.1875 to 0.1875
- attention_content_matrix: bfloat16 [1024, 1024], replicated, may hold values from -0.1875 to 0.1875
- attention_admit_matrix: bfloat16 [1024, 1024], replicated, may hold values from -0.1875 to 0.1875
- attention_result_matrix: bfloat16 [1024, 1024], replicated, may hold values from -0.5 to 0.5
- second_scaling_factor: bfloat16 [1024], replicated, may hold values from 0.5 to 1.5
- second_scaling_offset: bfloat16 [1024], replicated, may hold values from -3 to 3
- inner_shift_mixture: bfloat16 [1024], replicated, may hold values from 0.049804688 to 0.94921875
- admit_shift_mixture: bfloat16 [1024], replicated, may hold values from 0.049804688 to 0.94921875
- feedforward_lookup_matrix: bfloat16 [1024, 4096], P(None, 'mp'), may hold values from -0.1875 to 0.1875
- feedforward_content_matrix: bfloat16 [4096, 1024], P('mp'), may hold values from -0.09375 to 0.09375
- feedforward_admit_matrix: bfloat16 [1024, 1024], replicated, may hold values from -0.1875 to 0.1875
Outputs:
- output: float32 [4, 4, 1024, 1024], P(None, 'dp', 'mp')
- input_grad: float32 [4, 4, 1024, 1024], P(None, 'dp', 'mp')
- grad_first_gain: float32 [1024], P(('dp', 'mp'))
- grad_first_bias: float32 [1024], P(('dp', 'mp'))
- grad_decay_log: float32 [1024], P(('dp', 'mp'))
- grad_first_bonus: float32 [1024], P(('dp', 'mp'))
- grad_key_shift: float32 [1024], P(('dp', 'mp'))
- grad_value_shift: float32 [1024], P(('dp', 'mp'))
- grad_recept_shift: float32 [1024], P(('dp', 'mp'))
- grad_key_weight: float32 [1024, 1024], P(('dp', 'mp'))
- grad_value_weight: float32 [1024, 1024], P(('dp', 'mp'))
- grad_recept_weight: float32 [1024, 1024], P(('dp', 'mp'))
- grad_output_weight: float32 [1024, 1024], P(('dp', 'mp'))
- grad_second_gain: float32 [1024], P(('dp', 'mp'))
- grad_second_bias: float32 [1024], P(('dp', 'mp'))
- grad_hidden_shift: float32 [1024], P(('dp', 'mp'))
- grad_gate_shift: float32 [1024], P(('dp', 'mp'))
- grad_hidden_weight: float32 [1024, 4096], P('dp', 'mp')
- grad_return_weight: float32 [4096, 1024], P('mp', 'dp')
- grad_gate_weight: float32 [1024, 1024], P(('dp', 'mp'))
The draws below stay inside these ranges and needn't reach their ends.
Inputs may be any that keep to these rules, and one draw needn't show every extreme that they name: `series_number_table`: within a row the numbers never fall; each row is cut at two positions into at most three sequences numbered 0, 1, 2. For every index of the second dimension, one row chosen by the seed holds a sequence that starts within positions 1 to 64 and ends within the 64 positions that come just before the row's last position. Every rate exp(logarithmic_fading_speeds) lies below 0.101.
All inputs are finite; a program needn't handle non-finite values.
Results may differ from the reference program's by a relative error of at most 0.018.
Values may be sent and summed in bfloat16 or wider, within the bound.
A program may use at most 320 MiB of HBM per device.

```python
import math
import jax
import jax.numpy as jnp
from jax import lax

NETWORK_BREADTH = 1024
FF = 4096
TOK_MB = 128
MICRO = 4
GROUPS = 4
LEN = 1024


def draw_series_number_table(key, part):
    key = jax.random.fold_in(key, 3)
    pick_key, free_key, head_key, tail_key = jax.random.split(key, 4)
    span_row = jax.random.randint(pick_key, (GROUPS,), 0, MICRO)
    free_cuts = jax.random.randint(free_key, (MICRO, GROUPS, 2), 1, LEN)
    head_cut = jax.random.randint(head_key, (MICRO, GROUPS, 1), 1, TOK_MB // 2 + 1)
    tail_cut = LEN - jax.random.randint(tail_key, (MICRO, GROUPS, 1), 1, TOK_MB // 2 + 1)
    span_cuts = jnp.concatenate([head_cut, tail_cut], axis=2)
    chosen = (jnp.arange(MICRO)[:, None] == span_row[None, :])[:, :, None]
    cut_points = jnp.where(chosen, span_cuts, free_cuts)
    places = jnp.arange(LEN)
    numbers = jnp.sum((cut_points[:, :, None, :] <= places[None, None, :, None]).astype(jnp.int32), axis=3)
    return numbers.astype(jnp.int32)


def draw_logarithmic_fading_speeds(key, part):
    key = jax.random.fold_in(key, 5)
    pick_key, slow_key, fast_key = jax.random.split(key, 3)
    slow_share = 0.5
    slow_flag = jax.random.uniform(pick_key, (NETWORK_BREADTH,)) < slow_share
    slow_rate = jnp.exp(jax.random.uniform(slow_key, (NETWORK_BREADTH,), minval=math.log(0.2 / LEN), maxval=math.log(2.0 / LEN)))
    fast_rate = jnp.exp(jax.random.uniform(fast_key, (NETWORK_BREADTH,), minval=math.log(0.02), maxval=math.log(0.1)))
    return jnp.log(jnp.where(slow_flag, slow_rate, fast_rate)).astype(jnp.bfloat16)


def level_of(own_key, extent, cuts, low, top_value):
    def one(dim, blocks):
        heights = jax.random.uniform(jax.random.fold_in(jax.random.fold_in(own_key, 6), dim), (blocks,), jnp.float32, low / len(cuts), top_value / len(cuts))
        return jnp.repeat(jnp.exp(heights), extent[dim] // blocks).reshape((-1,) + (1,) * (len(extent) - dim - 1))

    factor_of = one(*cuts[0])
    for cut in cuts[1:]:
        factor_of = factor_of * one(*cut)
    return factor_of


def scatter_about(stream_key, dims, scale, bound, cuts=(), kind=jnp.bfloat16):
    level = level_of(stream_key, dims, cuts, -0.22, 0.18) if cuts else 1.0
    drawn = jax.random.normal(stream_key, dims, jnp.float32) * scale * level
    return jnp.minimum(jnp.maximum(drawn, -bound), bound).astype(kind)


def setup_inputs(seed: int = 0) -> dict:
    seeds = jax.random.split(jax.random.key(seed), 22)
    incoming_signal = scatter_about(seeds[0], (MICRO, GROUPS, LEN, NETWORK_BREADTH), 1.0, 6.0, ((1, 4), (2, 8)))
    series_number_table = draw_series_number_table(jax.random.fold_in(seeds[21], 71), 0)
    upstream_adjoint = scatter_about(seeds[2], (MICRO, GROUPS, LEN, NETWORK_BREADTH), 1.0, 6.0, ((1, 4), (2, 8)))
    first_scaling_factor = jnp.clip(1.0 + 0.1 * jax.random.normal(seeds[3], (NETWORK_BREADTH,), jnp.float32), 0.5, 1.5).astype(jnp.bfloat16)
    first_scaling_offset = scatter_about(seeds[4], (NETWORK_BREADTH,), 0.5, 3.0)
    logarithmic_fading_speeds = draw_logarithmic_fading_speeds(jax.random.fold_in(seeds[21], 71), 0)
    present_step_extra = jnp.clip(jax.random.uniform(seeds[6], (NETWORK_BREADTH,), jnp.float32, -1.0, 1.0), -1.0, 1.0).astype(jnp.bfloat16)
    lookup_shift_mixture = jnp.clip(jax.random.uniform(seeds[7], (NETWORK_BREADTH,), jnp.float32, 0.049804688, 0.94921875), 0.049804688, 0.94921875).astype(jnp.bfloat16)
    content_shift_mixture = jnp.clip(jax.random.uniform(seeds[8], (NETWORK_BREADTH,), jnp.float32, 0.049804688, 0.94921875), 0.049804688, 0.94921875).astype(jnp.bfloat16)
    admit_lookup_shift_mixture = jnp.clip(jax.random.uniform(seeds[9], (NETWORK_BREADTH,), jnp.float32, 0.049804688, 0.94921875), 0.049804688, 0.94921875).astype(jnp.bfloat16)
    attention_lookup_matrix = scatter_about(seeds[10], (NETWORK_BREADTH, NETWORK_BREADTH), NETWORK_BREADTH ** -0.5, 0.1875)
    attention_content_matrix = scatter_about(seeds[11], (NETWORK_BREADTH, NETWORK_BREADTH), NETWORK_BREADTH ** -0.5, 0.1875)
    attention_admit_matrix = scatter_about(seeds[12], (NETWORK_BREADTH, NETWORK_BREADTH), NETWORK_BREADTH ** -0.5, 0.1875)
    attention_result_matrix = scatter_about(seeds[13], (NETWORK_BREADTH, NETWORK_BREADTH), (NETWORK_BREADTH // 8) ** -0.5, 0.5)
    second_scaling_factor = jnp.clip(1.0 + 0.1 * jax.random.normal(seeds[14], (NETWORK_BREADTH,), jnp.float32), 0.5, 1.5).astype(jnp.bfloat16)
    second_scaling_offset = scatter_about(seeds[15], (NETWORK_BREADTH,), 0.5, 3.0)
    inner_shift_mixture = jnp.clip(jax.random.uniform(seeds[16], (NETWORK_BREADTH,), jnp.float32, 0.049804688, 0.94921875), 0.049804688, 0.94921875).astype(jnp.bfloat16)
    admit_shift_mixture = jnp.clip(jax.random.uniform(seeds[17], (NETWORK_BREADTH,), jnp.float32, 0.049804688, 0.94921875), 0.049804688, 0.94921875).astype(jnp.bfloat16)
    feedforward_lookup_matrix = scatter_about(seeds[18], (NETWORK_BREADTH, FF), NETWORK_BREADTH ** -0.5, 0.1875, ((1, 8),))
    feedforward_content_matrix = scatter_about(seeds[19], (FF, NETWORK_BREADTH), FF ** -0.5, 0.09375, ((0, 8),))
    feedforward_admit_matrix = scatter_about(seeds[20], (NETWORK_BREADTH, NETWORK_BREADTH), NETWORK_BREADTH ** -0.5, 0.1875)
    return dict(incoming_signal=incoming_signal, series_number_table=series_number_table, upstream_adjoint=upstream_adjoint, first_scaling_factor=first_scaling_factor, first_scaling_offset=first_scaling_offset, logarithmic_fading_speeds=logarithmic_fading_speeds, present_step_extra=present_step_extra, lookup_shift_mixture=lookup_shift_mixture, content_shift_mixture=content_shift_mixture, admit_lookup_shift_mixture=admit_lookup_shift_mixture, attention_lookup_matrix=attention_lookup_matrix, attention_content_matrix=attention_content_matrix, attention_admit_matrix=attention_admit_matrix, attention_result_matrix=attention_result_matrix, second_scaling_factor=second_scaling_factor, second_scaling_offset=second_scaling_offset, inner_shift_mixture=inner_shift_mixture, admit_shift_mixture=admit_shift_mixture, feedforward_lookup_matrix=feedforward_lookup_matrix, feedforward_content_matrix=feedforward_content_matrix, feedforward_admit_matrix=feedforward_admit_matrix)


EPS = 1e-05
HIGH = lax.Precision.HIGHEST

@jax.custom_vjp
def low(v):
    return lax.optimization_barrier(v.astype(jnp.bfloat16)).astype(jnp.float32)

@jax.custom_vjp
def low_back(v):
    return v

def low_keep(v):
    return (low(v), None)

def low_pass(kept, grad):
    return (grad,)

def back_keep(v):
    return (v, None)

def back_low(kept, grad):
    return (low(grad),)
low.defvjp(low_keep, low_pass)
low_back.defvjp(back_keep, back_low)

def layer_norm(values, gain, bias):
    average = lax.optimization_barrier(jnp.mean(values, axis=-1, keepdims=True))
    centre = values - average
    spread = lax.optimization_barrier(jnp.mean(centre * centre, axis=-1, keepdims=True))
    return centre * lax.rsqrt(spread + EPS) * gain + bias

def state_advance(lookup_series, content_series, same_series_mask, feature_fading, extra_array):
    decay_step = jnp.exp(-feature_fading)

    def advance(carried, element):
        dividend, divisor = carried
        lookup_present, content_present, keep_now = element
        dividend = dividend * keep_now
        divisor = divisor * keep_now
        extra_summand = jnp.exp(extra_array + lookup_present)
        ultimate_result = (dividend + extra_summand * content_present) / (divisor + extra_summand)
        raised_lookup = jnp.exp(lookup_present)
        return ((decay_step * dividend + raised_lookup * content_present, decay_step * divisor + raised_lookup), ultimate_result)
    elements = (jnp.moveaxis(lookup_series, 2, 0), jnp.moveaxis(content_series, 2, 0), jnp.moveaxis(same_series_mask, 2, 0))
    zero_state = jnp.zeros(lookup_series.shape[:2] + lookup_series.shape[3:], jnp.float32)
    _, results = lax.scan(jax.checkpoint(advance), (zero_state, zero_state), elements)
    return jnp.moveaxis(results, 0, 2)

def block_forward(block_in, same_series_mask, block_settings):
    first_scaling_factor, first_scaling_offset, logarithmic_fading_speeds, present_step_extra, lookup_shift_mixture, content_shift_mixture, admit_lookup_shift_mixture, attention_lookup_matrix, attention_content_matrix, attention_admit_matrix, attention_result_matrix, second_scaling_factor, second_scaling_offset, inner_shift_mixture, admit_shift_mixture, feedforward_lookup_matrix, feedforward_content_matrix, feedforward_admit_matrix = block_settings

    def shifted(values):
        return jnp.concatenate([jnp.zeros_like(values[:, :, :1]), values[:, :, :-1]], axis=2) * same_series_mask

    def multiply(left, right):
        return jnp.einsum('mgtd,de->mgte', left, right, precision=HIGH)
    normed_a = layer_norm(block_in, first_scaling_factor, first_scaling_offset)
    shift_a = shifted(normed_a)
    delta_a = normed_a - shift_a
    lookup_series = low_back(multiply(low(shift_a + delta_a * lookup_shift_mixture), attention_lookup_matrix))
    content_series = low_back(multiply(low(shift_a + delta_a * content_shift_mixture), attention_content_matrix))
    recept = jax.nn.sigmoid(low_back(multiply(low(shift_a + delta_a * admit_lookup_shift_mixture), attention_admit_matrix)))
    mixture_result = state_advance(lookup_series, content_series, same_series_mask, jnp.exp(logarithmic_fading_speeds), present_step_extra)
    block_mid = block_in + low_back(multiply(low(recept * mixture_result), attention_result_matrix))
    normed_b = layer_norm(block_mid, second_scaling_factor, second_scaling_offset)
    shift_b = shifted(normed_b)
    delta_b = normed_b - shift_b
    pre_act = low_back(multiply(low(shift_b + delta_b * inner_shift_mixture), feedforward_lookup_matrix))
    rectified = jnp.maximum(pre_act, 0.0)
    returned = low_back(multiply(low(rectified * rectified), feedforward_content_matrix))
    gate_two = jax.nn.sigmoid(low_back(multiply(low(shift_b + delta_b * admit_shift_mixture), feedforward_admit_matrix)))
    return block_mid + gate_two * returned

def reference(incoming_signal, series_number_table, upstream_adjoint, first_scaling_factor, first_scaling_offset, logarithmic_fading_speeds, present_step_extra, lookup_shift_mixture, content_shift_mixture, admit_lookup_shift_mixture, attention_lookup_matrix, attention_content_matrix, attention_admit_matrix, attention_result_matrix, second_scaling_factor, second_scaling_offset, inner_shift_mixture, admit_shift_mixture, feedforward_lookup_matrix, feedforward_content_matrix, feedforward_admit_matrix):
    equal_next = (series_number_table[:, :, 1:] == series_number_table[:, :, :-1]).astype(jnp.float32)
    same_series_mask = jnp.concatenate([jnp.zeros(series_number_table.shape[:2] + (1,), jnp.float32), equal_next], axis=2)[..., None]
    block_settings = tuple((start_item.astype(jnp.float32) for start_item in (first_scaling_factor, first_scaling_offset, logarithmic_fading_speeds, present_step_extra, lookup_shift_mixture, content_shift_mixture, admit_lookup_shift_mixture, attention_lookup_matrix, attention_content_matrix, attention_admit_matrix, attention_result_matrix, second_scaling_factor, second_scaling_offset, inner_shift_mixture, admit_shift_mixture, feedforward_lookup_matrix, feedforward_content_matrix, feedforward_admit_matrix)))
    block_in = incoming_signal.astype(jnp.float32)

    def forward(values, weights):
        return block_forward(values, same_series_mask, weights)
    output, pullback = jax.vjp(forward, block_in, block_settings)
    input_grad, grads = pullback(upstream_adjoint.astype(jnp.float32))
    return (output, input_grad, grads[0], grads[1], grads[2], grads[3], grads[4], grads[5], grads[6], grads[7], grads[8], grads[9], grads[10], grads[11], grads[12], grads[13], grads[14], grads[15], grads[16], grads[17])
```

```python
import jax
import jax.numpy as jnp
from jax import lax
from jax.sharding import PartitionSpec as P

EPS = 1e-05
HIGH = lax.Precision.HIGHEST


def from_behind(block, axis, distance):
    devices = range(lax.axis_size(axis))
    route = [(i - distance, i) for i in devices if i - distance in devices]
    return lax.ppermute(block, axis, route)


def carried_in(shard, axis, combine, identity, reverse):
    length, mine = (lax.axis_size(axis), lax.axis_index(axis))
    everything = jax.tree.map(lambda part: lax.all_gather(part, axis), shard)
    start = jax.tree.map(
        lambda part, zero: jnp.broadcast_to(jnp.asarray(zero, part.dtype), part.shape),
        shard,
        identity,
    )

    def step(k, before):
        at = length - 1 - k if reverse else k
        reached = at > mine if reverse else at < mine
        new = combine(before, jax.tree.map(lambda part: part[at], everything))
        return jax.tree.map(lambda a, b: jnp.where(reached, a, b), new, before)

    return lax.fori_loop(0, length, step, start)


def reduced_precision(values):
    return values.astype(jnp.bfloat16)


def product(left, right):
    return jnp.dot(left, right, preferred_element_type=jnp.float32)


def product_tn(left, right):
    return lax.dot_general(
        left, right, (((0,), (0,)), ((), ())), preferred_element_type=jnp.float32
    )


def product_nt(left, right):
    return lax.dot_general(
        left, right, (((1,), (1,)), ((), ())), preferred_element_type=jnp.float32
    )


def layer_norm(values, gain, bias):
    average = jnp.mean(values, axis=-1, keepdims=True)
    centre = values - average
    inverse = lax.rsqrt(jnp.mean(centre * centre, axis=-1, keepdims=True) + EPS)
    unit = centre * inverse
    return (unit * gain + bias, unit, inverse)


def norm_back(grad_in, unit, inverse, gain):
    scaled = grad_in * gain
    grad_values = inverse * (
        scaled
        - jnp.mean(scaled, axis=-1, keepdims=True)
        - unit * jnp.mean(scaled * unit, axis=-1, keepdims=True)
    )
    return (grad_values, jnp.sum(grad_in * unit, axis=0), jnp.sum(grad_in, axis=0))


def state_join(earlier, latter):
    return (
        latter[4] * earlier[0] + latter[0],
        latter[4] * earlier[1] + latter[1],
        latter[4] * earlier[2] + latter[5] * earlier[0] + latter[2],
        latter[4] * earlier[3] + latter[5] * earlier[1] + latter[3],
        earlier[4] * latter[4],
        earlier[5] * latter[4] + earlier[4] * latter[5],
    )


def suffix_join(earlier, latter):
    return (
        latter[0] + latter[2] * earlier[0],
        latter[1] + latter[2] * earlier[1],
        latter[2] * earlier[2],
    )


def one_micro(block_in, seg_ids, grad_out, vectors, matrices, hidden_w, return_w):
    (
        gain_one,
        bias_one,
        decay_vec,
        extra_array,
        mix_key,
        mix_value,
        mix_recept,
        gain_two,
        bias_two,
        mix_hidden,
        mix_gate,
    ) = vectors
    key_w, value_w, recept_w, output_w, gate_w = matrices
    row_count = block_in.shape[0]
    model_width = block_in.shape[1]
    seg_float = seg_ids.astype(jnp.float32)
    normed_a, unit_a, inv_a = layer_norm(block_in, gain_one, bias_one)
    prev_row, prev_seg = from_behind((normed_a[-1:], seg_float[-1:]), "mp", 1)
    same_row = jnp.concatenate(
        [
            (seg_float[:1] == prev_seg).astype(jnp.float32),
            (seg_ids[1:] == seg_ids[:-1]).astype(jnp.float32),
        ]
    )
    same_col = same_row[:, None]
    shifted_a = jnp.concatenate([prev_row, normed_a[:-1]], axis=0) * same_col
    delta_a = normed_a - shifted_a
    low_key = reduced_precision(shifted_a + delta_a * mix_key)
    low_value = reduced_precision(shifted_a + delta_a * mix_value)
    low_recept = reduced_precision(shifted_a + delta_a * mix_recept)
    lookup_start = product(low_key, key_w)
    content_start = product(low_value, value_w)
    recept = jax.nn.sigmoid(product(low_recept, recept_w))
    feature_fading = jnp.exp(decay_vec)
    positions = jnp.arange(row_count, dtype=jnp.float32)[:, None]
    rising = jnp.exp(positions * feature_fading)
    falling = jnp.exp(-(positions - 1.0) * feature_fading)
    falling_zero = jnp.exp(-positions * feature_fading)
    raised_lookup = jnp.exp(lookup_start)
    weighted_average = raised_lookup * content_start
    order_rows = jnp.arange(row_count)
    lower_tri = jnp.logical_and(
        seg_ids[:, None] == seg_ids[None, :], order_rows[None, :] < order_rows[:, None]
    ).astype(jnp.float32)
    last_mask = (seg_ids == seg_ids[-1]).astype(jnp.float32)
    first_mask = (seg_ids == seg_ids[0]).astype(jnp.float32) * same_row[0]
    forward_mat = jnp.concatenate([lower_tri, last_mask[None]], axis=0)
    stacked = jnp.concatenate(
        [
            rising * weighted_average,
            rising * raised_lookup,
            positions * rising * weighted_average,
            positions * rising * raised_lookup,
        ],
        axis=1,
    )
    summed = jnp.dot(forward_mat, stacked, precision=HIGH)
    inner_sums = summed[:row_count]
    closing = summed[row_count]
    num_loc = falling * inner_sums[:, :model_width]
    den_loc = falling * inner_sums[:, model_width : 2 * model_width]
    num_der = (
        -(positions - 1.0) * num_loc + falling * inner_sums[:, 2 * model_width : 3 * model_width]
    )
    den_der = -(positions - 1.0) * den_loc + falling * inner_sums[:, 3 * model_width :]
    end_fall = jnp.exp(-(row_count - 1.0) * feature_fading)
    state_num = end_fall * closing[:model_width]
    state_den = end_fall * closing[model_width : 2 * model_width]
    state_num_der = (
        -(row_count - 1.0) * state_num + end_fall * closing[2 * model_width : 3 * model_width]
    )
    state_den_der = -(row_count - 1.0) * state_den + end_fall * closing[3 * model_width :]
    uniform_flag = (seg_ids[-1] == seg_ids[0]).astype(jnp.float32) * same_row[0]
    carry_pass = uniform_flag * jnp.exp(-row_count * feature_fading)
    carry_der = -row_count * carry_pass
    zero_vec = jnp.zeros_like(feature_fading)
    one_vec = jnp.ones_like(feature_fading)
    in_num, in_den, in_num_der, in_den_der, pass_total, pass_der = carried_in(
        (state_num, state_den, state_num_der, state_den_der, carry_pass, carry_der),
        "mp",
        state_join,
        (zero_vec, zero_vec, zero_vec, zero_vec, one_vec, zero_vec),
        False,
    )
    carried = first_mask[:, None] * falling_zero
    dividend = num_loc + carried * in_num
    divisor_portion = den_loc + carried * in_den
    numer_der = num_der + carried * (in_num_der - positions * in_num)
    denom_der = den_der + carried * (in_den_der - positions * in_den)
    extra_summand = jnp.exp(extra_array + lookup_start)
    divisor_complete = divisor_portion + extra_summand
    mixture_result = (dividend + extra_summand * content_start) / divisor_complete
    gated = reduced_precision(recept * mixture_result)
    block_mid = block_in + product(gated, output_w)
    normed_b, unit_b, inv_b = layer_norm(block_mid, gain_two, bias_two)
    prev_mid = from_behind(normed_b[-1:], "mp", 1)
    shifted_b = jnp.concatenate([prev_mid, normed_b[:-1]], axis=0) * same_col
    delta_b = normed_b - shifted_b
    low_hidden = reduced_precision(shifted_b + delta_b * mix_hidden)
    low_gate = reduced_precision(shifted_b + delta_b * mix_gate)
    gate_two = jax.nn.sigmoid(product(low_gate, gate_w))
    hidden_rows = lax.all_gather(low_hidden, "mp", axis=0, tiled=True)
    pre_act = product(hidden_rows, hidden_w)
    rectified = jnp.maximum(pre_act, 0.0)
    squared = reduced_precision(rectified * rectified)
    returned = lax.psum_scatter(
        product(squared, return_w).astype(jnp.bfloat16), "mp", scatter_dimension=0, tiled=True
    ).astype(jnp.float32)
    output = block_mid + gate_two * returned
    grad_ret = reduced_precision(grad_out * gate_two)
    grad_gate_pre = reduced_precision(grad_out * returned * gate_two * (1.0 - gate_two))
    d_gate_w = (low_gate, grad_gate_pre)
    grad_low_gate = product_nt(grad_gate_pre, gate_w)
    grad_rows = lax.all_gather(grad_ret, "mp", axis=0, tiled=True)
    grad_squared = product_nt(grad_rows, return_w)
    d_return = (squared, grad_rows)
    grad_pre = reduced_precision(grad_squared * 2.0 * rectified)
    d_hidden = (hidden_rows, grad_pre)
    grad_low_hidden = lax.psum_scatter(
        product_nt(grad_pre, hidden_w).astype(jnp.bfloat16), "mp", scatter_dimension=0, tiled=True
    ).astype(jnp.float32)
    d_mix_hidden = jnp.sum(grad_low_hidden * delta_b, axis=0)
    d_mix_gate = jnp.sum(grad_low_gate * delta_b, axis=0)
    grad_shift_b = (
        grad_low_hidden * (1.0 - mix_hidden) + grad_low_gate * (1.0 - mix_gate)
    ) * same_col
    from_next_b = from_behind(grad_shift_b[:1], "mp", -1)
    grad_norm_b = (
        grad_low_hidden * mix_hidden
        + grad_low_gate * mix_gate
        + jnp.concatenate([grad_shift_b[1:], from_next_b], axis=0)
    )
    grad_mid_norm, d_gain_two, d_bias_two = norm_back(grad_norm_b, unit_b, inv_b, gain_two)
    grad_mid = grad_out + grad_mid_norm
    grad_att = reduced_precision(grad_mid)
    d_output_w = (gated, grad_att)
    grad_gated = product_nt(grad_att, output_w)
    grad_recept_pre = reduced_precision(grad_gated * mixture_result * recept * (1.0 - recept))
    grad_mixed = grad_gated * recept
    d_recept_w = (low_recept, grad_recept_pre)
    grad_low_recept = product_nt(grad_recept_pre, recept_w)
    dividend_adjoint = grad_mixed / divisor_complete
    divisor_adjoint = -dividend_adjoint * mixture_result
    extra_derivative_part = dividend_adjoint * content_start + divisor_adjoint
    extra_derivative = jnp.sum(extra_derivative_part * extra_summand, axis=0)
    d_rate = jnp.sum(dividend_adjoint * numer_der + divisor_adjoint * denom_der, axis=0)
    backward_mat = jnp.concatenate([lower_tri.T, first_mask[None]], axis=0)
    back_sum = jnp.dot(
        backward_mat,
        jnp.concatenate([falling * dividend_adjoint, falling * divisor_adjoint], axis=1),
        precision=HIGH,
    )
    step_back = jnp.exp(-feature_fading)
    from_num = step_back * back_sum[row_count, :model_width]
    from_den = step_back * back_sum[row_count, model_width:]
    out_num, out_den, out_pass = carried_in(
        (from_num, from_den, carry_pass), "mp", suffix_join, (zero_vec, zero_vec, one_vec), True
    )
    tail_fall = last_mask[:, None] * jnp.exp(-(row_count - 1.0 - positions) * feature_fading)
    cumulative_dividend = rising * back_sum[:row_count, :model_width] + tail_fall * out_num
    running_denominator = rising * back_sum[:row_count, model_width:] + tail_fall * out_den
    value_gradient = reduced_precision(
        dividend_adjoint * extra_summand + cumulative_dividend * raised_lookup
    )
    key_gradient = reduced_precision(
        extra_derivative_part * extra_summand
        + cumulative_dividend * weighted_average
        + running_denominator * raised_lookup
    )
    d_key_w = (low_key, key_gradient)
    d_value_w = (low_value, value_gradient)
    grad_low_key = product_nt(key_gradient, key_w)
    grad_low_value = product_nt(value_gradient, value_w)
    d_mix_key = jnp.sum(grad_low_key * delta_a, axis=0)
    d_mix_value = jnp.sum(grad_low_value * delta_a, axis=0)
    d_mix_recept = jnp.sum(grad_low_recept * delta_a, axis=0)
    grad_shift_a = (
        grad_low_key * (1.0 - mix_key)
        + grad_low_value * (1.0 - mix_value)
        + grad_low_recept * (1.0 - mix_recept)
    ) * same_col
    from_next_a = from_behind(grad_shift_a[:1], "mp", -1)
    grad_norm_a = (
        grad_low_key * mix_key
        + grad_low_value * mix_value
        + grad_low_recept * mix_recept
        + jnp.concatenate([grad_shift_a[1:], from_next_a], axis=0)
    )
    grad_in_norm, d_gain_one, d_bias_one = norm_back(grad_norm_a, unit_a, inv_a, gain_one)
    input_grad = grad_mid + grad_in_norm
    grads = (
        d_gain_one,
        d_bias_one,
        d_rate * feature_fading,
        extra_derivative,
        d_mix_key,
        d_mix_value,
        d_mix_recept,
        d_key_w,
        d_value_w,
        d_recept_w,
        d_output_w,
        d_gain_two,
        d_bias_two,
        d_mix_hidden,
        d_mix_gate,
        d_hidden,
        d_return,
        d_gate_w,
    )
    return (output, input_grad, grads)


def body(
    incoming_signal,
    series_number_table,
    upstream_adjoint,
    first_scaling_factor,
    first_scaling_offset,
    logarithmic_fading_speeds,
    present_step_extra,
    lookup_shift_mixture,
    content_shift_mixture,
    admit_lookup_shift_mixture,
    attention_lookup_matrix,
    attention_content_matrix,
    attention_admit_matrix,
    attention_result_matrix,
    second_scaling_factor,
    second_scaling_offset,
    inner_shift_mixture,
    admit_shift_mixture,
    feedforward_lookup_matrix,
    feedforward_content_matrix,
    feedforward_admit_matrix,
):
    hidden_full, return_full = (feedforward_lookup_matrix, feedforward_content_matrix)
    vectors = tuple(
        (
            start_item.astype(jnp.float32)
            for start_item in (
                first_scaling_factor,
                first_scaling_offset,
                logarithmic_fading_speeds,
                present_step_extra,
                lookup_shift_mixture,
                content_shift_mixture,
                admit_lookup_shift_mixture,
                second_scaling_factor,
                second_scaling_offset,
                inner_shift_mixture,
                admit_shift_mixture,
            )
        )
    )
    matrices = (
        attention_lookup_matrix,
        attention_content_matrix,
        attention_admit_matrix,
        attention_result_matrix,
        feedforward_admit_matrix,
    )
    output, input_grad, grads = jax.vmap(
        lambda rows, ids, adjoint: one_micro(
            rows, ids, adjoint, vectors, matrices, hidden_full, return_full
        )
    )(
        incoming_signal[:, 0].astype(jnp.float32),
        series_number_table[:, 0],
        upstream_adjoint[:, 0].astype(jnp.float32),
    )
    totals = tuple(
        product_tn(*(side.reshape(-1, side.shape[-1]) for side in grad))
        if isinstance(grad, tuple)
        else jnp.sum(grad, axis=0)
        for grad in grads
    )
    square = [index for index in range(18) if totals[index].shape == totals[7].shape]
    lines = [index for index in range(18) if totals[index].ndim == 1]
    wide = lax.psum_scatter(
        jnp.concatenate([reduced_precision(totals[index]) for index in square], axis=1),
        ("dp", "mp"),
        scatter_dimension=0,
        tiled=True,
    ).astype(jnp.float32)
    thin = lax.psum_scatter(
        jnp.stack([totals[index] for index in lines], axis=1),
        ("dp", "mp"),
        scatter_dimension=0,
        tiled=True,
    )
    held = dict(zip(square, jnp.split(wide, len(square), axis=1)))
    held.update({index: thin[:, place] for place, index in enumerate(lines)})
    output, input_grad = (output[:, None], input_grad[:, None])
    owned = tuple(held[index] for index in sorted(held))
    hidden_own, return_own = (
        lax.psum_scatter(
            totals[15].astype(jnp.bfloat16), "dp", scatter_dimension=0, tiled=True
        ).astype(jnp.float32),
        lax.psum_scatter(
            totals[16].astype(jnp.bfloat16), "dp", scatter_dimension=1, tiled=True
        ).astype(jnp.float32),
    )
    return (
        output,
        input_grad,
        owned[0],
        owned[1],
        owned[2],
        owned[3],
        owned[4],
        owned[5],
        owned[6],
        owned[7],
        owned[8],
        owned[9],
        owned[10],
        owned[11],
        owned[12],
        owned[13],
        owned[14],
        hidden_own,
        return_own,
        owned[15],
    )


def solution(mesh):
    placed = (
        P(None, "dp", "mp", None),
        P(None, "dp", "mp"),
        P(None, "dp", "mp", None),
        P(),
        P(),
        P(),
        P(),
        P(),
        P(),
        P(),
        P(),
        P(),
        P(),
        P(),
        P(),
        P(),
        P(),
        P(),
        P(None, "mp"),
        P("mp", None),
        P(),
    )
    return jax.shard_map(
        body,
        mesh=mesh,
        in_specs=placed,
        out_specs=(
            P(None, "dp", "mp", None),
            P(None, "dp", "mp", None),
            P(("dp", "mp")),
            P(("dp", "mp")),
            P(("dp", "mp")),
            P(("dp", "mp")),
            P(("dp", "mp")),
            P(("dp", "mp")),
            P(("dp", "mp")),
            P(("dp", "mp"), None),
            P(("dp", "mp"), None),
            P(("dp", "mp"), None),
            P(("dp", "mp"), None),
            P(("dp", "mp")),
            P(("dp", "mp")),
            P(("dp", "mp")),
            P(("dp", "mp")),
            P("dp", "mp"),
            P("mp", "dp"),
            P(("dp", "mp"), None),
        ),
        check_vma=False,
    )
```

```python
import functools

import jax
import jax.numpy as jnp
from jax import lax
from jax.experimental import pallas as pl
from jax.experimental.pallas import tpu as pltpu
from jax.sharding import PartitionSpec as P

EPS = 1e-05
HIGH = lax.Precision.HIGHEST


def from_behind(block, axis, distance):
    devices = range(lax.axis_size(axis))
    route = [(i - distance, i) for i in devices if i - distance in devices]
    return lax.ppermute(block, axis, route)


def carried_in(shard, axis, combine, identity, reverse):
    length, mine = (lax.axis_size(axis), lax.axis_index(axis))
    everything = jax.tree.map(lambda part: lax.all_gather(part, axis), shard)
    start = jax.tree.map(
        lambda part, zero: jnp.broadcast_to(jnp.asarray(zero, part.dtype), part.shape),
        shard,
        identity,
    )

    def step(k, before):
        at = length - 1 - k if reverse else k
        reached = at > mine if reverse else at < mine
        new = combine(before, jax.tree.map(lambda part: part[at], everything))
        return jax.tree.map(lambda a, b: jnp.where(reached, a, b), new, before)

    return lax.fori_loop(0, length, step, start)


def reduced_precision(values):
    return values.astype(jnp.bfloat16)


def product(left, right):
    return jnp.dot(left, right, preferred_element_type=jnp.float32)


def product_tn(left, right):
    return lax.dot_general(
        left, right, (((0,), (0,)), ((), ())), preferred_element_type=jnp.float32
    )


def product_nt(left, right):
    return lax.dot_general(
        left, right, (((1,), (1,)), ((), ())), preferred_element_type=jnp.float32
    )


def layer_norm(values, gain, bias):
    average = jnp.mean(values, axis=-1, keepdims=True)
    centre = values - average
    inverse = lax.rsqrt(jnp.mean(centre * centre, axis=-1, keepdims=True) + EPS)
    unit = centre * inverse
    return (unit * gain + bias, unit, inverse)


def norm_back(grad_in, unit, inverse, gain):
    scaled = grad_in * gain
    grad_values = inverse * (
        scaled
        - jnp.mean(scaled, axis=-1, keepdims=True)
        - unit * jnp.mean(scaled * unit, axis=-1, keepdims=True)
    )
    return (grad_values, jnp.sum(grad_in * unit, axis=0), jnp.sum(grad_in, axis=0))


def state_join(earlier, latter):
    return (
        latter[4] * earlier[0] + latter[0],
        latter[4] * earlier[1] + latter[1],
        latter[4] * earlier[2] + latter[5] * earlier[0] + latter[2],
        latter[4] * earlier[3] + latter[5] * earlier[1] + latter[3],
        earlier[4] * latter[4],
        earlier[5] * latter[4] + earlier[4] * latter[5],
    )


def suffix_join(earlier, latter):
    return (
        latter[0] + latter[2] * earlier[0],
        latter[1] + latter[2] * earlier[1],
        latter[2] * earlier[2],
    )


BF = jnp.bfloat16
F32 = jnp.float32
MESH = pl.DeviceIdType.MESH
NN = (((1,), (0,)), ((), ()))
NT = (((1,), (1,)), ((), ()))
TN = (((0,), (0,)), ((), ()))


def dot(left, right, form=NN):
    return lax.dot_general(left, right, form, preferred_element_type=F32)


def dot_exact_left(left, right):
    high = right.astype(BF)
    rest = (right - high.astype(F32)).astype(BF)
    return dot(left, high) + dot(left, rest)


def wide(lanes, width):
    return jnp.concatenate([lanes] * (width // 128), axis=1)


def tile(index, size):
    return pl.ds(pl.multiple_of(index * size, size), size)


def unit_of(values):
    average = jnp.mean(values, axis=-1, keepdims=True)
    centre = values - average
    inverse = lax.rsqrt(jnp.mean(centre * centre, axis=-1, keepdims=True) + EPS)
    return (centre * inverse, inverse)


def remote(source, target, send, receive, device):
    return pltpu.make_async_remote_copy(
        src_ref=source,
        dst_ref=target,
        send_sem=send,
        recv_sem=receive,
        device_id=device,
        device_id_type=MESH,
    )


class Place:
    def __init__(self, planes):
        self.planes = planes
        self.dp, self.mp = (lax.axis_index("dp"), lax.axis_index("mp"))
        self.z = lax.div(self.mp, 2)
        self.core = lax.rem(self.mp, 2)
        self.count = 2 * planes
        self.other = (self.dp, self.mp + 1 - 2 * self.core)
        self.side_x = (self.dp + 1 - 2 * lax.rem(self.dp, 2), self.mp)
        self.side_y = (lax.rem(self.dp + 2, 4), self.mp)

    def ahead(self, steps):
        return (self.dp, lax.rem(self.mp + steps + self.count, self.count))

    def plane(self, steps):
        return (self.dp, lax.rem(self.z + steps + self.planes, self.planes) * 2 + self.core)


def greet(devices):
    barrier = pltpu.get_barrier_semaphore()
    for device in devices:
        pl.semaphore_signal(barrier, inc=1, device_id=device, device_id_type=MESH)
    pl.semaphore_wait(barrier, len(devices))


def forward_kernel(
    planes,
    micros,
    rows,
    x_ref,
    last_ref,
    segcol_ref,
    segrow_ref,
    segpay_ref,
    vec_ref,
    adj_ref,
    key_w,
    value_w,
    recept_w,
    output_w,
    gate_w,
    w1_ref,
    w2_ref,
    k_out,
    v_out,
    r_out,
    num_out,
    den_out,
    mid_out,
    gate_out,
    mk_out,
    mv_out,
    mr_out,
    gated_out,
    mg_out,
    small_out,
    mh_all,
    ret_all,
    w1_all,
    w2_all,
    wk,
    wv,
    wr,
    wo,
    wg,
    k_s,
    v_s,
    r_s,
    num_s,
    den_s,
    mid_s,
    gate_s,
    xb_s,
    mk_s,
    mv_s,
    mr_s,
    gated_s,
    mg_s,
    mh_s,
    ret_s,
    keep_s,
    mask_s,
    halo_a,
    near_a,
    pay_b,
    halo_b,
    segs_s,
    state_own,
    state_other,
    state_chip,
    state_in,
    carry_s,
    w_sem,
    out_sem,
    small_sem,
    z_sem,
    s_sem,
):
    at = Place(planes)
    dp, mp, z, core = (at.dp, at.mp, at.z, at.core)
    tokens = micros * rows
    peers = [at.ahead(step) for step in range(1, at.count)]
    greet(peers + [at.side_x, at.side_y])

    quarter1, quarter2 = (w1_ref.shape[0] // 4, w2_ref.shape[0] // 4)
    q1, q2 = (tile(dp, quarter1), tile(dp, quarter2))
    z_copies = []
    for step in range(1, planes):
        to = at.plane(-step)
        z_copies.append(
            (
                remote(w1_ref.at[q1], w1_all.at[step - 1, q1], z_sem.at[step - 1, 0, 0], z_sem.at[step - 1, 0, 1], to),
                remote(w2_ref.at[q2], w2_all.at[step - 1, q2], z_sem.at[step - 1, 1, 0], z_sem.at[step - 1, 1, 1], to),
            )
        )

    halo_copy = remote(last_ref, halo_a, small_sem.at[0, 0], small_sem.at[0, 1], at.ahead(1))
    halo_copy.start()
    seg_copies = [
        remote(segpay_ref, segs_s.at[mp], small_sem.at[1 + step, 0], small_sem.at[1 + step, 1], device)
        for step, device in enumerate(peers)
    ]
    for copy in seg_copies:
        copy.start()
    segs_s[mp] = segpay_ref[...]
    loads = []
    for index, (source, target) in enumerate(
        ((key_w, wk), (value_w, wv), (recept_w, wr), (output_w, wo), (gate_w, wg))
    ):
        loads.append(pltpu.make_async_copy(source, target, w_sem.at[index]))
        loads[-1].start()
    for copy in z_copies[0]:
        copy.start()
    halo_copy.wait()
    for copy in seg_copies:
        copy.wait()

    before = lax.rem(mp + at.count - 1, at.count)
    has_before = mp > 0
    first_row = lax.broadcasted_iota(jnp.int32, (rows, 128), 0) == 0
    row_at = lax.broadcasted_iota(jnp.int32, (rows, rows), 0)
    col_at = lax.broadcasted_iota(jnp.int32, (rows, rows), 1)
    for m in range(micros):
        here = segcol_ref[m * rows : (m + 1) * rows, :]
        behind = jnp.where(
            first_row, segs_s[before, m : m + 1, :], pltpu.roll(here, 1, 0)
        )
        same = jnp.logical_and(
            here == behind, jnp.logical_or(jnp.logical_not(first_row), has_before)
        )
        keep_s[m * rows : (m + 1) * rows, :] = same.astype(F32)
        mask_s[m] = jnp.logical_and(
            here == segrow_ref[m : m + 1, :], col_at < row_at
        ).astype(F32).astype(BF)

    block = 16
    at_first = lax.broadcasted_iota(jnp.int32, (block, 1024), 0) == 0
    gain, bias = (vec_ref[0:1, :], vec_ref[1:2, :])
    near_a[...] = unit_of(halo_a[...])[0] * gain + bias
    for m in range(micros):

        def mix_a(b, prev, m=m):
            span = tile(m * (rows // block) + b, block)
            normed = unit_of(x_ref[span, :].astype(F32))[0] * gain + bias
            shifted = jnp.where(at_first, prev, pltpu.roll(normed, 1, 0)) * wide(
                keep_s[span, :], 1024
            )
            delta = normed - shifted
            mk_s[span, :] = (shifted + delta * vec_ref[4:5, :]).astype(BF)
            mv_s[span, :] = (shifted + delta * vec_ref[5:6, :]).astype(BF)
            mr_s[span, :] = (shifted + delta * vec_ref[6:7, :]).astype(BF)
            return normed[block - 1 : block, :]

        lax.fori_loop(0, rows // block, mix_a, near_a[m : m + 1, :])

    outs = []

    def put(source, target):
        copy = pltpu.make_async_copy(source, target, out_sem.at[len(outs)])
        copy.start()
        outs.append(copy)

    put(mk_s, mk_out)
    put(mv_s, mv_out)
    put(mr_s, mr_out)

    loads[0].wait()
    loads[1].wait()
    width = 256
    place = lax.broadcasted_iota(jnp.int32, (rows, width), 0).astype(F32)

    @pl.loop(0, 1024 // width)
    def _(i):
        cols = tile(i, width)
        rate = jnp.exp(vec_ref[2:3, cols])
        rising = jnp.exp(place * rate)
        falling = jnp.exp((1.0 - place) * rate)
        step_back = jnp.exp(-rate)
        keys = dot(mk_s[...], wk[:, cols])
        values = dot(mv_s[...], wv[:, cols])
        for m in range(micros):
            span = slice(m * rows, (m + 1) * rows)
            key, value = (keys[span], values[span])
            raised = jnp.exp(key)
            weighted = raised * value
            num = falling * dot_exact_left(mask_s[m], rising * weighted)
            den = falling * dot_exact_left(mask_s[m], rising * raised)
            k_s[span, cols] = key
            v_s[span, cols] = value
            num_s[span, cols] = num
            den_s[span, cols] = den
            state_own[m : m + 1, cols] = step_back * num[rows - 1 :] + weighted[rows - 1 :]
            state_own[micros + m : micros + m + 1, cols] = (
                step_back * den[rows - 1 :] + raised[rows - 1 :]
            )

    put(k_s, k_out)
    put(v_s, v_out)
    core_copy = remote(state_own, state_other, s_sem.at[0, 0], s_sem.at[0, 1], at.other)
    core_copy.start()
    for copy in z_copies[0]:
        copy.wait()
    xy_copies = []

    def along(step):
        group = []
        own1, own2 = (w1_all.at[step, q1], w2_all.at[step, q2])
        return (
            remote(own1, own1, z_sem.at[step, 2, 0], z_sem.at[step, 2, 1], at.side_x),
            remote(own2, own2, z_sem.at[step, 3, 0], z_sem.at[step, 3, 1], at.side_y),
        )

    def across(step):
        both1 = w1_all.at[step, tile(lax.div(dp, 2), 2 * quarter1)]
        own2 = w2_all.at[step, q2]
        far2 = w2_all.at[step, tile(lax.rem(dp + 2, 4), quarter2)]
        return (
            remote(both1, both1, z_sem.at[step, 4, 0], z_sem.at[step, 4, 1], at.side_y),
            remote(own2, own2, z_sem.at[step, 5, 0], z_sem.at[step, 5, 1], at.side_x),
            remote(far2, far2, z_sem.at[step, 6, 0], z_sem.at[step, 6, 1], at.side_x),
        )

    def start(group):
        for copy in group:
            copy.start()

    def finish(group):
        for copy in group:
            copy.wait()

    along_0, along_1, along_2 = (along(0), along(1), along(2))
    across_0, across_1, across_2 = (across(0), across(1), across(2))
    start(along_0)
    start(z_copies[2])
    loads[2].wait()

    @pl.loop(0, 2)
    def _(i):
        span = tile(i, tokens // 2)
        r_s[span, :] = jax.nn.sigmoid(dot(mr_s[span, :], wr[...]))

    put(r_s, r_out)

    pair = lax.div(mp, 2) * 2
    decay_all = jnp.exp(-float(rows) * jnp.exp(vec_ref[2:3, :]))
    core_copy.wait()

    def last_of(device):
        return wide(segs_s[lax.rem(device + at.count, at.count), 0 : 2 * micros, :], 1024)

    even = jnp.where(core == 0, state_own[...], state_other[...])
    odd = jnp.where(core == 0, state_other[...], state_own[...])
    state_chip[...] = odd + jnp.where(last_of(pair) == last_of(pair + 1), decay_all * even, 0.0)
    chip_copies = [
        remote(state_chip, state_in.at[step - 1], s_sem.at[step, 0], s_sem.at[step, 1], at.plane(step))
        for step in range(1, planes)
    ]
    start(chip_copies)
    finish(along_0)
    start(across_0)
    finish(chip_copies)
    total = jnp.zeros_like(state_chip[...])
    power = jnp.ones_like(decay_all)
    for step in range(1, planes):
        fits = jnp.logical_and(
            last_of(pair - 2 * step + 1) == last_of(pair - 1), z >= step
        )
        total = total + jnp.where(fits, power * state_in[step - 1], 0.0)
        power = power * decay_all * decay_all
    joined = state_other[...] + jnp.where(last_of(pair) == last_of(pair - 1), decay_all * total, 0.0)
    carry_s[...] = jnp.where(core == 0, total, joined)

    @pl.loop(0, 1024 // width)
    def _(i):
        cols = tile(i, width)
        rate = jnp.exp(vec_ref[2:3, cols])
        falling = jnp.exp(-place * rate)
        extra = vec_ref[3:4, cols]
        for m in range(micros):
            span = slice(m * rows, (m + 1) * rows)
            fits = jnp.logical_and(
                segcol_ref[span, :] == segs_s[before, m : m + 1, :], has_before
            ).astype(F32)
            carried = wide(fits, width) * falling
            num = num_s[span, cols] + carried * carry_s[m : m + 1, cols]
            den = den_s[span, cols] + carried * carry_s[micros + m : micros + m + 1, cols]
            bonus = jnp.exp(extra + k_s[span, cols])
            mixed = (num + bonus * v_s[span, cols]) / (den + bonus)
            num_s[span, cols] = num
            den_s[span, cols] = den
            gated_s[span, cols] = (r_s[span, cols] * mixed).astype(BF)

    put(num_s, num_out)
    put(den_s, den_out)
    put(gated_s, gated_out)
    loads[3].wait()

    @pl.loop(0, 2)
    def _(i):
        span = tile(i, tokens // 2)
        mid_s[span, :] = x_ref[span, :].astype(F32) + dot(gated_s[span, :], wo[...])

    put(mid_s, mid_out)
    gain_b, bias_b = (vec_ref[7:8, :], vec_ref[8:9, :])

    def norm_b(b):
        span = tile(b, block)
        xb_s[span, :] = unit_of(mid_s[span, :])[0] * gain_b + bias_b

    for m in range(micros):
        norm_b((m + 1) * (rows // block) - 1)
        pay_b[m : m + 1, :] = xb_s[(m + 1) * rows - 1 : (m + 1) * rows, :]
    pay_b[micros:, :] = jnp.zeros((8 - micros, 1024), F32)
    halo_b_copy = remote(pay_b, halo_b, s_sem.at[planes, 0], s_sem.at[planes, 1], at.ahead(1))
    halo_b_copy.start()
    for m in range(micros):

        @pl.loop(m * (rows // block), (m + 1) * (rows // block) - 1)
        def _(b):
            norm_b(b)

    finish(z_copies[2])
    start(along_2)
    start(z_copies[1])
    halo_b_copy.wait()
    for m in range(micros):

        def mix_b(b, prev, m=m):
            span = tile(m * (rows // block) + b, block)
            normed = xb_s[span, :]
            shifted = jnp.where(at_first, prev, pltpu.roll(normed, 1, 0)) * wide(
                keep_s[span, :], 1024
            )
            delta = normed - shifted
            mh_s[span, :] = (shifted + delta * vec_ref[9:10, :]).astype(BF)
            mg_s[span, :] = (shifted + delta * vec_ref[10:11, :]).astype(BF)
            return normed[block - 1 : block, :]

        lax.fori_loop(0, rows // block, mix_b, halo_b[m : m + 1, :])

    mh_copy = remote(
        mh_s, mh_all.at[1], s_sem.at[planes + 1, 0], s_sem.at[planes + 1, 1], at.other
    )
    mh_copy.start()
    put(mh_s, mh_all.at[0])
    put(mg_s, mg_out)
    loads[4].wait()

    @pl.loop(0, 2)
    def _(i):
        span = tile(i, tokens // 2)
        gate = jax.nn.sigmoid(dot(mg_s[span, :], wg[...]))
        gate_s[span, :] = gate
        ret_s[span, :] = (adj_ref[span, :].astype(F32) * gate).astype(BF)

    ret_copy = remote(
        ret_s, ret_all.at[1], s_sem.at[planes + 2, 0], s_sem.at[planes + 2, 1], at.other
    )
    ret_copy.start()
    put(ret_s, ret_all.at[0])
    put(gate_s, gate_out)
    finish(across_0)
    finish(along_2)
    start(across_2)
    finish(z_copies[1])
    start(along_1)
    finish(across_2)
    finish(along_1)
    start(across_1)
    put(near_a, small_out.at[0])
    put(halo_b, small_out.at[1])
    finish(across_1)
    mh_copy.wait()
    ret_copy.wait()
    for copy in outs:
        copy.wait()


ANY = pl.BlockSpec(memory_space=pl.ANY)
VM = pl.BlockSpec(memory_space=pltpu.VMEM)


def forward_call(planes, micros, rows, operands):
    tokens = micros * rows
    hidden = operands[-1].shape[0]

    def big(kind):
        return jax.ShapeDtypeStruct((tokens, 1024), kind)

    def hold(kind):
        return pltpu.VMEM((tokens, 1024), kind)

    square = pltpu.VMEM((1024, 1024), BF)
    few = pltpu.VMEM((8, 1024), F32)
    pair = pltpu.SemaphoreType.DMA
    return pl.pallas_call(
        functools.partial(forward_kernel, planes, micros, rows),
        out_shape=[big(F32)] * 7
        + [big(BF)] * 5
        + [jax.ShapeDtypeStruct((2, 8, 1024), F32)]
        + [jax.ShapeDtypeStruct((2, tokens, 1024), BF)] * 2
        + [
            jax.ShapeDtypeStruct((planes - 1, 1024, hidden), BF),
            jax.ShapeDtypeStruct((planes - 1, hidden, 1024), BF),
        ],
        in_specs=[VM] * 7 + [ANY] * 7,
        out_specs=[ANY] * 17,
        scratch_shapes=[square] * 5
        + [hold(F32)] * 8
        + [hold(BF)] * 7
        + [
            pltpu.VMEM((tokens, 128), F32),
            pltpu.VMEM((micros, rows, rows), BF),
            few,
            few,
            few,
            few,
            pltpu.VMEM((2 * planes, 16, 128), F32),
            few,
            few,
            few,
            pltpu.VMEM((planes - 1, 8, 1024), F32),
            few,
            pair((5,)),
            pair((18,)),
            pair((2 * planes + 1, 2)),
            pair((planes - 1, 7, 2)),
            pair((planes + 3, 2)),
        ],
        compiler_params=pltpu.CompilerParams(
            collective_id=0, has_side_effects=True, vmem_limit_bytes=58 << 20
        ),
        cost_estimate=pl.CostEstimate(
            flops=10 * tokens * 1024 * 1024, bytes_accessed=40 << 20, transcendentals=6 * tokens * 1024
        ),
        name="time_mix_forward",
    )(*operands)


def one_micro_back(block_in, seg_ids, grad_out, kept, vectors, matrices, hidden_w, return_w):
    lookup_start, content_start, recept, dividend, divisor_portion, block_mid, gate_two, low_key, low_value, low_recept, gated, low_gate, low_hidden, grad_ret = kept
    (
        gain_one,
        bias_one,
        decay_vec,
        extra_array,
        mix_key,
        mix_value,
        mix_recept,
        gain_two,
        bias_two,
        mix_hidden,
        mix_gate,
    ) = vectors
    key_w, value_w, recept_w, output_w, gate_w = matrices
    row_count = block_in.shape[0]
    model_width = block_in.shape[1]
    seg_float = seg_ids.astype(jnp.float32)
    normed_a, unit_a, inv_a = layer_norm(block_in, gain_one, bias_one)
    prev_row, prev_seg = from_behind((normed_a[-1:], seg_float[-1:]), "mp", 1)
    same_row = jnp.concatenate(
        [
            (seg_float[:1] == prev_seg).astype(jnp.float32),
            (seg_ids[1:] == seg_ids[:-1]).astype(jnp.float32),
        ]
    )
    same_col = same_row[:, None]
    shifted_a = jnp.concatenate([prev_row, normed_a[:-1]], axis=0) * same_col
    delta_a = normed_a - shifted_a
    feature_fading = jnp.exp(decay_vec)
    positions = jnp.arange(row_count, dtype=jnp.float32)[:, None]
    rising = jnp.exp(positions * feature_fading)
    falling = jnp.exp(-(positions - 1.0) * feature_fading)
    falling_zero = jnp.exp(-positions * feature_fading)
    raised_lookup = jnp.exp(lookup_start)
    weighted_average = raised_lookup * content_start
    order_rows = jnp.arange(row_count)
    lower_tri = jnp.logical_and(
        seg_ids[:, None] == seg_ids[None, :], order_rows[None, :] < order_rows[:, None]
    ).astype(jnp.float32)
    last_mask = (seg_ids == seg_ids[-1]).astype(jnp.float32)
    first_mask = (seg_ids == seg_ids[0]).astype(jnp.float32) * same_row[0]
    uniform_flag = (seg_ids[-1] == seg_ids[0]).astype(jnp.float32) * same_row[0]
    carry_pass = uniform_flag * jnp.exp(-row_count * feature_fading)
    zero_vec = jnp.zeros_like(feature_fading)
    one_vec = jnp.ones_like(feature_fading)
    extra_summand = jnp.exp(extra_array + lookup_start)
    divisor_complete = divisor_portion + extra_summand
    mixture_result = (dividend + extra_summand * content_start) / divisor_complete
    normed_b, unit_b, inv_b = layer_norm(block_mid, gain_two, bias_two)
    prev_mid = from_behind(normed_b[-1:], "mp", 1)
    shifted_b = jnp.concatenate([prev_mid, normed_b[:-1]], axis=0) * same_col
    delta_b = normed_b - shifted_b
    hidden_rows = lax.all_gather(low_hidden, "mp", axis=0, tiled=True)
    pre_act = product(hidden_rows, hidden_w)
    rectified = jnp.maximum(pre_act, 0.0)
    squared = reduced_precision(rectified * rectified)
    returned = lax.psum_scatter(
        product(squared, return_w).astype(jnp.bfloat16), "mp", scatter_dimension=0, tiled=True
    ).astype(jnp.float32)
    output = block_mid + gate_two * returned
    grad_gate_pre = reduced_precision(grad_out * returned * gate_two * (1.0 - gate_two))
    d_gate_w = (low_gate, grad_gate_pre)
    grad_low_gate = product_nt(grad_gate_pre, gate_w)
    grad_rows = lax.all_gather(grad_ret, "mp", axis=0, tiled=True)
    grad_squared = product_nt(grad_rows, return_w)
    d_return = (squared, grad_rows)
    grad_pre = reduced_precision(grad_squared * 2.0 * rectified)
    d_hidden = (hidden_rows, grad_pre)
    grad_low_hidden = lax.psum_scatter(
        product_nt(grad_pre, hidden_w).astype(jnp.bfloat16), "mp", scatter_dimension=0, tiled=True
    ).astype(jnp.float32)
    d_mix_hidden = jnp.sum(grad_low_hidden * delta_b, axis=0)
    d_mix_gate = jnp.sum(grad_low_gate * delta_b, axis=0)
    grad_shift_b = (
        grad_low_hidden * (1.0 - mix_hidden) + grad_low_gate * (1.0 - mix_gate)
    ) * same_col
    from_next_b = from_behind(grad_shift_b[:1], "mp", -1)
    grad_norm_b = (
        grad_low_hidden * mix_hidden
        + grad_low_gate * mix_gate
        + jnp.concatenate([grad_shift_b[1:], from_next_b], axis=0)
    )
    grad_mid_norm, d_gain_two, d_bias_two = norm_back(grad_norm_b, unit_b, inv_b, gain_two)
    grad_mid = grad_out + grad_mid_norm
    grad_att = reduced_precision(grad_mid)
    d_output_w = (gated, grad_att)
    grad_gated = product_nt(grad_att, output_w)
    grad_recept_pre = reduced_precision(grad_gated * mixture_result * recept * (1.0 - recept))
    grad_mixed = grad_gated * recept
    d_recept_w = (low_recept, grad_recept_pre)
    grad_low_recept = product_nt(grad_recept_pre, recept_w)
    dividend_adjoint = grad_mixed / divisor_complete
    divisor_adjoint = -dividend_adjoint * mixture_result
    extra_derivative_part = dividend_adjoint * content_start + divisor_adjoint
    extra_derivative = jnp.sum(extra_derivative_part * extra_summand, axis=0)
    backward_mat = jnp.concatenate([lower_tri.T, first_mask[None]], axis=0)
    back_sum = jnp.dot(
        backward_mat,
        jnp.concatenate([falling * dividend_adjoint, falling * divisor_adjoint], axis=1),
        precision=HIGH,
    )
    step_back = jnp.exp(-feature_fading)
    from_num = step_back * back_sum[row_count, :model_width]
    from_den = step_back * back_sum[row_count, model_width:]
    out_num, out_den, out_pass = carried_in(
        (from_num, from_den, carry_pass), "mp", suffix_join, (zero_vec, zero_vec, one_vec), True
    )
    tail_fall = last_mask[:, None] * jnp.exp(-(row_count - 1.0 - positions) * feature_fading)
    cumulative_dividend = rising * back_sum[:row_count, :model_width] + tail_fall * out_num
    running_denominator = rising * back_sum[:row_count, model_width:] + tail_fall * out_den
    d_rate = -step_back * jnp.sum(
        cumulative_dividend * dividend + running_denominator * divisor_portion, axis=0
    )
    value_gradient = reduced_precision(
        dividend_adjoint * extra_summand + cumulative_dividend * raised_lookup
    )
    key_gradient = reduced_precision(
        extra_derivative_part * extra_summand
        + cumulative_dividend * weighted_average
        + running_denominator * raised_lookup
    )
    d_key_w = (low_key, key_gradient)
    d_value_w = (low_value, value_gradient)
    grad_low_key = product_nt(key_gradient, key_w)
    grad_low_value = product_nt(value_gradient, value_w)
    d_mix_key = jnp.sum(grad_low_key * delta_a, axis=0)
    d_mix_value = jnp.sum(grad_low_value * delta_a, axis=0)
    d_mix_recept = jnp.sum(grad_low_recept * delta_a, axis=0)
    grad_shift_a = (
        grad_low_key * (1.0 - mix_key)
        + grad_low_value * (1.0 - mix_value)
        + grad_low_recept * (1.0 - mix_recept)
    ) * same_col
    from_next_a = from_behind(grad_shift_a[:1], "mp", -1)
    grad_norm_a = (
        grad_low_key * mix_key
        + grad_low_value * mix_value
        + grad_low_recept * mix_recept
        + jnp.concatenate([grad_shift_a[1:], from_next_a], axis=0)
    )
    grad_in_norm, d_gain_one, d_bias_one = norm_back(grad_norm_a, unit_a, inv_a, gain_one)
    input_grad = grad_mid + grad_in_norm
    grads = (
        d_gain_one,
        d_bias_one,
        d_rate * feature_fading,
        extra_derivative,
        d_mix_key,
        d_mix_value,
        d_mix_recept,
        d_key_w,
        d_value_w,
        d_recept_w,
        d_output_w,
        d_gain_two,
        d_bias_two,
        d_mix_hidden,
        d_mix_gate,
        d_hidden,
        d_return,
        d_gate_w,
    )
    return (output, input_grad, grads)


def one_micro(block_in, seg_ids, grad_out, vectors, matrices, hidden_w, return_w):
    (
        gain_one,
        bias_one,
        decay_vec,
        extra_array,
        mix_key,
        mix_value,
        mix_recept,
        gain_two,
        bias_two,
        mix_hidden,
        mix_gate,
    ) = vectors
    key_w, value_w, recept_w, output_w, gate_w = matrices
    row_count = block_in.shape[0]
    model_width = block_in.shape[1]
    seg_float = seg_ids.astype(jnp.float32)
    normed_a, unit_a, inv_a = layer_norm(block_in, gain_one, bias_one)
    prev_row, prev_seg = from_behind((normed_a[-1:], seg_float[-1:]), "mp", 1)
    same_row = jnp.concatenate(
        [
            (seg_float[:1] == prev_seg).astype(jnp.float32),
            (seg_ids[1:] == seg_ids[:-1]).astype(jnp.float32),
        ]
    )
    same_col = same_row[:, None]
    shifted_a = jnp.concatenate([prev_row, normed_a[:-1]], axis=0) * same_col
    delta_a = normed_a - shifted_a
    low_key = reduced_precision(shifted_a + delta_a * mix_key)
    low_value = reduced_precision(shifted_a + delta_a * mix_value)
    low_recept = reduced_precision(shifted_a + delta_a * mix_recept)
    lookup_start = product(low_key, key_w)
    content_start = product(low_value, value_w)
    recept = jax.nn.sigmoid(product(low_recept, recept_w))
    feature_fading = jnp.exp(decay_vec)
    positions = jnp.arange(row_count, dtype=jnp.float32)[:, None]
    rising = jnp.exp(positions * feature_fading)
    falling = jnp.exp(-(positions - 1.0) * feature_fading)
    falling_zero = jnp.exp(-positions * feature_fading)
    raised_lookup = jnp.exp(lookup_start)
    weighted_average = raised_lookup * content_start
    order_rows = jnp.arange(row_count)
    lower_tri = jnp.logical_and(
        seg_ids[:, None] == seg_ids[None, :], order_rows[None, :] < order_rows[:, None]
    ).astype(jnp.float32)
    last_mask = (seg_ids == seg_ids[-1]).astype(jnp.float32)
    first_mask = (seg_ids == seg_ids[0]).astype(jnp.float32) * same_row[0]
    forward_mat = jnp.concatenate([lower_tri, last_mask[None]], axis=0)
    stacked = jnp.concatenate(
        [
            rising * weighted_average,
            rising * raised_lookup,
            positions * rising * weighted_average,
            positions * rising * raised_lookup,
        ],
        axis=1,
    )
    summed = jnp.dot(forward_mat, stacked, precision=HIGH)
    inner_sums = summed[:row_count]
    closing = summed[row_count]
    num_loc = falling * inner_sums[:, :model_width]
    den_loc = falling * inner_sums[:, model_width : 2 * model_width]
    num_der = (
        -(positions - 1.0) * num_loc + falling * inner_sums[:, 2 * model_width : 3 * model_width]
    )
    den_der = -(positions - 1.0) * den_loc + falling * inner_sums[:, 3 * model_width :]
    end_fall = jnp.exp(-(row_count - 1.0) * feature_fading)
    state_num = end_fall * closing[:model_width]
    state_den = end_fall * closing[model_width : 2 * model_width]
    state_num_der = (
        -(row_count - 1.0) * state_num + end_fall * closing[2 * model_width : 3 * model_width]
    )
    state_den_der = -(row_count - 1.0) * state_den + end_fall * closing[3 * model_width :]
    uniform_flag = (seg_ids[-1] == seg_ids[0]).astype(jnp.float32) * same_row[0]
    carry_pass = uniform_flag * jnp.exp(-row_count * feature_fading)
    carry_der = -row_count * carry_pass
    zero_vec = jnp.zeros_like(feature_fading)
    one_vec = jnp.ones_like(feature_fading)
    in_num, in_den, in_num_der, in_den_der, pass_total, pass_der = carried_in(
        (state_num, state_den, state_num_der, state_den_der, carry_pass, carry_der),
        "mp",
        state_join,
        (zero_vec, zero_vec, zero_vec, zero_vec, one_vec, zero_vec),
        False,
    )
    carried = first_mask[:, None] * falling_zero
    dividend = num_loc + carried * in_num
    divisor_portion = den_loc + carried * in_den
    numer_der = num_der + carried * (in_num_der - positions * in_num)
    denom_der = den_der + carried * (in_den_der - positions * in_den)
    extra_summand = jnp.exp(extra_array + lookup_start)
    divisor_complete = divisor_portion + extra_summand
    mixture_result = (dividend + extra_summand * content_start) / divisor_complete
    gated = reduced_precision(recept * mixture_result)
    block_mid = block_in + product(gated, output_w)
    normed_b, unit_b, inv_b = layer_norm(block_mid, gain_two, bias_two)
    prev_mid = from_behind(normed_b[-1:], "mp", 1)
    shifted_b = jnp.concatenate([prev_mid, normed_b[:-1]], axis=0) * same_col
    delta_b = normed_b - shifted_b
    low_hidden = reduced_precision(shifted_b + delta_b * mix_hidden)
    low_gate = reduced_precision(shifted_b + delta_b * mix_gate)
    gate_two = jax.nn.sigmoid(product(low_gate, gate_w))
    hidden_rows = lax.all_gather(low_hidden, "mp", axis=0, tiled=True)
    pre_act = product(hidden_rows, hidden_w)
    rectified = jnp.maximum(pre_act, 0.0)
    squared = reduced_precision(rectified * rectified)
    returned = lax.psum_scatter(
        product(squared, return_w).astype(jnp.bfloat16), "mp", scatter_dimension=0, tiled=True
    ).astype(jnp.float32)
    output = block_mid + gate_two * returned
    grad_ret = reduced_precision(grad_out * gate_two)
    grad_gate_pre = reduced_precision(grad_out * returned * gate_two * (1.0 - gate_two))
    d_gate_w = (low_gate, grad_gate_pre)
    grad_low_gate = product_nt(grad_gate_pre, gate_w)
    grad_rows = lax.all_gather(grad_ret, "mp", axis=0, tiled=True)
    grad_squared = product_nt(grad_rows, return_w)
    d_return = (squared, grad_rows)
    grad_pre = reduced_precision(grad_squared * 2.0 * rectified)
    d_hidden = (hidden_rows, grad_pre)
    grad_low_hidden = lax.psum_scatter(
        product_nt(grad_pre, hidden_w).astype(jnp.bfloat16), "mp", scatter_dimension=0, tiled=True
    ).astype(jnp.float32)
    d_mix_hidden = jnp.sum(grad_low_hidden * delta_b, axis=0)
    d_mix_gate = jnp.sum(grad_low_gate * delta_b, axis=0)
    grad_shift_b = (
        grad_low_hidden * (1.0 - mix_hidden) + grad_low_gate * (1.0 - mix_gate)
    ) * same_col
    from_next_b = from_behind(grad_shift_b[:1], "mp", -1)
    grad_norm_b = (
        grad_low_hidden * mix_hidden
        + grad_low_gate * mix_gate
        + jnp.concatenate([grad_shift_b[1:], from_next_b], axis=0)
    )
    grad_mid_norm, d_gain_two, d_bias_two = norm_back(grad_norm_b, unit_b, inv_b, gain_two)
    grad_mid = grad_out + grad_mid_norm
    grad_att = reduced_precision(grad_mid)
    d_output_w = (gated, grad_att)
    grad_gated = product_nt(grad_att, output_w)
    grad_recept_pre = reduced_precision(grad_gated * mixture_result * recept * (1.0 - recept))
    grad_mixed = grad_gated * recept
    d_recept_w = (low_recept, grad_recept_pre)
    grad_low_recept = product_nt(grad_recept_pre, recept_w)
    dividend_adjoint = grad_mixed / divisor_complete
    divisor_adjoint = -dividend_adjoint * mixture_result
    extra_derivative_part = dividend_adjoint * content_start + divisor_adjoint
    extra_derivative = jnp.sum(extra_derivative_part * extra_summand, axis=0)
    d_rate = jnp.sum(dividend_adjoint * numer_der + divisor_adjoint * denom_der, axis=0)
    backward_mat = jnp.concatenate([lower_tri.T, first_mask[None]], axis=0)
    back_sum = jnp.dot(
        backward_mat,
        jnp.concatenate([falling * dividend_adjoint, falling * divisor_adjoint], axis=1),
        precision=HIGH,
    )
    step_back = jnp.exp(-feature_fading)
    from_num = step_back * back_sum[row_count, :model_width]
    from_den = step_back * back_sum[row_count, model_width:]
    out_num, out_den, out_pass = carried_in(
        (from_num, from_den, carry_pass), "mp", suffix_join, (zero_vec, zero_vec, one_vec), True
    )
    tail_fall = last_mask[:, None] * jnp.exp(-(row_count - 1.0 - positions) * feature_fading)
    cumulative_dividend = rising * back_sum[:row_count, :model_width] + tail_fall * out_num
    running_denominator = rising * back_sum[:row_count, model_width:] + tail_fall * out_den
    value_gradient = reduced_precision(
        dividend_adjoint * extra_summand + cumulative_dividend * raised_lookup
    )
    key_gradient = reduced_precision(
        extra_derivative_part * extra_summand
        + cumulative_dividend * weighted_average
        + running_denominator * raised_lookup
    )
    d_key_w = (low_key, key_gradient)
    d_value_w = (low_value, value_gradient)
    grad_low_key = product_nt(key_gradient, key_w)
    grad_low_value = product_nt(value_gradient, value_w)
    d_mix_key = jnp.sum(grad_low_key * delta_a, axis=0)
    d_mix_value = jnp.sum(grad_low_value * delta_a, axis=0)
    d_mix_recept = jnp.sum(grad_low_recept * delta_a, axis=0)
    grad_shift_a = (
        grad_low_key * (1.0 - mix_key)
        + grad_low_value * (1.0 - mix_value)
        + grad_low_recept * (1.0 - mix_recept)
    ) * same_col
    from_next_a = from_behind(grad_shift_a[:1], "mp", -1)
    grad_norm_a = (
        grad_low_key * mix_key
        + grad_low_value * mix_value
        + grad_low_recept * mix_recept
        + jnp.concatenate([grad_shift_a[1:], from_next_a], axis=0)
    )
    grad_in_norm, d_gain_one, d_bias_one = norm_back(grad_norm_a, unit_a, inv_a, gain_one)
    input_grad = grad_mid + grad_in_norm
    grads = (
        d_gain_one,
        d_bias_one,
        d_rate * feature_fading,
        extra_derivative,
        d_mix_key,
        d_mix_value,
        d_mix_recept,
        d_key_w,
        d_value_w,
        d_recept_w,
        d_output_w,
        d_gain_two,
        d_bias_two,
        d_mix_hidden,
        d_mix_gate,
        d_hidden,
        d_return,
        d_gate_w,
    )
    return (output, input_grad, grads)


def generic_body(
    incoming_signal,
    series_number_table,
    upstream_adjoint,
    first_scaling_factor,
    first_scaling_offset,
    logarithmic_fading_speeds,
    present_step_extra,
    lookup_shift_mixture,
    content_shift_mixture,
    admit_lookup_shift_mixture,
    attention_lookup_matrix,
    attention_content_matrix,
    attention_admit_matrix,
    attention_result_matrix,
    second_scaling_factor,
    second_scaling_offset,
    inner_shift_mixture,
    admit_shift_mixture,
    feedforward_lookup_matrix,
    feedforward_content_matrix,
    feedforward_admit_matrix,
):
    hidden_full, return_full = (feedforward_lookup_matrix, feedforward_content_matrix)
    vectors = tuple(
        (
            start_item.astype(jnp.float32)
            for start_item in (
                first_scaling_factor,
                first_scaling_offset,
                logarithmic_fading_speeds,
                present_step_extra,
                lookup_shift_mixture,
                content_shift_mixture,
                admit_lookup_shift_mixture,
                second_scaling_factor,
                second_scaling_offset,
                inner_shift_mixture,
                admit_shift_mixture,
            )
        )
    )
    matrices = (
        attention_lookup_matrix,
        attention_content_matrix,
        attention_admit_matrix,
        attention_result_matrix,
        feedforward_admit_matrix,
    )
    output, input_grad, grads = jax.vmap(
        lambda rows, ids, adjoint: one_micro(
            rows, ids, adjoint, vectors, matrices, hidden_full, return_full
        )
    )(
        incoming_signal[:, 0].astype(jnp.float32),
        series_number_table[:, 0],
        upstream_adjoint[:, 0].astype(jnp.float32),
    )
    totals = tuple(
        product_tn(*(side.reshape(-1, side.shape[-1]) for side in grad))
        if isinstance(grad, tuple)
        else jnp.sum(grad, axis=0)
        for grad in grads
    )
    square = [index for index in range(18) if totals[index].shape == totals[7].shape]
    lines = [index for index in range(18) if totals[index].ndim == 1]
    wide = lax.psum_scatter(
        jnp.concatenate([reduced_precision(totals[index]) for index in square], axis=1),
        ("dp", "mp"),
        scatter_dimension=0,
        tiled=True,
    ).astype(jnp.float32)
    thin = lax.psum_scatter(
        jnp.stack([totals[index] for index in lines], axis=1),
        ("dp", "mp"),
        scatter_dimension=0,
        tiled=True,
    )
    held = dict(zip(square, jnp.split(wide, len(square), axis=1)))
    held.update({index: thin[:, place] for place, index in enumerate(lines)})
    output, input_grad = (output[:, None], input_grad[:, None])
    owned = tuple(held[index] for index in sorted(held))
    hidden_own, return_own = (
        lax.psum_scatter(
            totals[15].astype(jnp.bfloat16), "dp", scatter_dimension=0, tiled=True
        ).astype(jnp.float32),
        lax.psum_scatter(
            totals[16].astype(jnp.bfloat16), "dp", scatter_dimension=1, tiled=True
        ).astype(jnp.float32),
    )
    return (
        output,
        input_grad,
        owned[0],
        owned[1],
        owned[2],
        owned[3],
        owned[4],
        owned[5],
        owned[6],
        owned[7],
        owned[8],
        owned[9],
        owned[10],
        owned[11],
        owned[12],
        owned[13],
        owned[14],
        hidden_own,
        return_own,
        owned[15],
    )


def kernel_body(
    incoming_signal,
    series_number_table,
    upstream_adjoint,
    first_scaling_factor,
    first_scaling_offset,
    logarithmic_fading_speeds,
    present_step_extra,
    lookup_shift_mixture,
    content_shift_mixture,
    admit_lookup_shift_mixture,
    attention_lookup_matrix,
    attention_content_matrix,
    attention_admit_matrix,
    attention_result_matrix,
    second_scaling_factor,
    second_scaling_offset,
    inner_shift_mixture,
    admit_shift_mixture,
    feedforward_lookup_matrix,
    feedforward_content_matrix,
    feedforward_admit_matrix,
):
    hidden_full, return_full = (feedforward_lookup_matrix, feedforward_content_matrix)
    vectors = tuple(
        (
            start_item.astype(jnp.float32)
            for start_item in (
                first_scaling_factor,
                first_scaling_offset,
                logarithmic_fading_speeds,
                present_step_extra,
                lookup_shift_mixture,
                content_shift_mixture,
                admit_lookup_shift_mixture,
                second_scaling_factor,
                second_scaling_offset,
                inner_shift_mixture,
                admit_shift_mixture,
            )
        )
    )
    matrices = (
        attention_lookup_matrix,
        attention_content_matrix,
        attention_admit_matrix,
        attention_result_matrix,
        feedforward_admit_matrix,
    )
    micros, _, rows, depth = incoming_signal.shape
    planes = lax.axis_size("mp") // 2
    numbers = series_number_table[:, 0].astype(jnp.float32)
    firsts, lasts = (numbers[:, :1], numbers[:, -1:])
    operands = (
        incoming_signal.reshape(micros * rows, depth),
        jnp.pad(incoming_signal[:, 0, -1].astype(jnp.float32), ((0, 8 - micros), (0, 0))),
        jnp.broadcast_to(numbers.reshape(-1, 1), (micros * rows, 128)),
        jnp.pad(numbers, ((0, 8 - micros), (0, 0))),
        jnp.broadcast_to(
            jnp.concatenate([lasts, lasts, firsts, firsts], axis=0), (4 * micros, 128)
        ),
        jnp.pad(jnp.stack(vectors), ((0, 5), (0, 0))),
        upstream_adjoint.reshape(micros * rows, depth),
        *matrices,
        hidden_full,
        return_full,
    )
    made = forward_call(planes, micros, rows, operands)
    kept = [part.reshape(micros, rows, depth) for part in made[:12]]
    kept += [made[13][0].reshape(micros, rows, depth), made[14][0].reshape(micros, rows, depth)]
    output, input_grad, grads = jax.vmap(
        lambda rows, ids, adjoint, kept: one_micro_back(
            rows, ids, adjoint, kept, vectors, matrices, hidden_full, return_full
        )
    )(
        incoming_signal[:, 0].astype(jnp.float32),
        series_number_table[:, 0],
        upstream_adjoint[:, 0].astype(jnp.float32),
        kept,
    )
    totals = tuple(
        product_tn(*(side.reshape(-1, side.shape[-1]) for side in grad))
        if isinstance(grad, tuple)
        else jnp.sum(grad, axis=0)
        for grad in grads
    )
    square = [index for index in range(18) if totals[index].shape == totals[7].shape]
    lines = [index for index in range(18) if totals[index].ndim == 1]
    wide = lax.psum_scatter(
        jnp.concatenate([reduced_precision(totals[index]) for index in square], axis=1),
        ("dp", "mp"),
        scatter_dimension=0,
        tiled=True,
    ).astype(jnp.float32)
    thin = lax.psum_scatter(
        jnp.stack([totals[index] for index in lines], axis=1),
        ("dp", "mp"),
        scatter_dimension=0,
        tiled=True,
    )
    held = dict(zip(square, jnp.split(wide, len(square), axis=1)))
    held.update({index: thin[:, place] for place, index in enumerate(lines)})
    output, input_grad = (output[:, None], input_grad[:, None])
    owned = tuple(held[index] for index in sorted(held))
    hidden_own, return_own = (
        lax.psum_scatter(
            totals[15].astype(jnp.bfloat16), "dp", scatter_dimension=0, tiled=True
        ).astype(jnp.float32),
        lax.psum_scatter(
            totals[16].astype(jnp.bfloat16), "dp", scatter_dimension=1, tiled=True
        ).astype(jnp.float32),
    )
    return (
        output,
        input_grad,
        owned[0],
        owned[1],
        owned[2],
        owned[3],
        owned[4],
        owned[5],
        owned[6],
        owned[7],
        owned[8],
        owned[9],
        owned[10],
        owned[11],
        owned[12],
        owned[13],
        owned[14],
        hidden_own,
        return_own,
        owned[15],
    )


def solution(mesh):
    placed = (
        P(None, "dp", "mp", None),
        P(None, "dp", "mp"),
        P(None, "dp", "mp", None),
        P(),
        P(),
        P(),
        P(),
        P(),
        P(),
        P(),
        P(),
        P(),
        P(),
        P(),
        P(),
        P(),
        P(),
        P(),
        P(None, "mp"),
        P("mp", None),
        P(),
    )
    fits = mesh.shape["dp"] == 4 and mesh.shape["mp"] == 8
    return jax.shard_map(
        kernel_body if fits else generic_body,
        mesh=mesh,
        in_specs=placed,
        out_specs=(
            P(None, "dp", "mp", None),
            P(None, "dp", "mp", None),
            P(("dp", "mp")),
            P(("dp", "mp")),
            P(("dp", "mp")),
            P(("dp", "mp")),
            P(("dp", "mp")),
            P(("dp", "mp")),
            P(("dp", "mp")),
            P(("dp", "mp"), None),
            P(("dp", "mp"), None),
            P(("dp", "mp"), None),
            P(("dp", "mp"), None),
            P(("dp", "mp")),
            P(("dp", "mp")),
            P(("dp", "mp")),
            P(("dp", "mp")),
            P("dp", "mp"),
            P("mp", "dp"),
            P(("dp", "mp"), None),
        ),
        check_vma=False,
    )
```

```python
import functools

import jax
import jax.numpy as jnp
from jax import lax
from jax.experimental import pallas as pl
from jax.experimental.pallas import tpu as pltpu
from jax.sharding import PartitionSpec as P

EPS = 1e-05
HIGH = lax.Precision.HIGHEST


def from_behind(block, axis, distance):
    devices = range(lax.axis_size(axis))
    route = [(i - distance, i) for i in devices if i - distance in devices]
    return lax.ppermute(block, axis, route)


def carried_in(shard, axis, combine, identity, reverse):
    length, mine = (lax.axis_size(axis), lax.axis_index(axis))
    everything = jax.tree.map(lambda part: lax.all_gather(part, axis), shard)
    start = jax.tree.map(
        lambda part, zero: jnp.broadcast_to(jnp.asarray(zero, part.dtype), part.shape),
        shard,
        identity,
    )

    def step(k, before):
        at = length - 1 - k if reverse else k
        reached = at > mine if reverse else at < mine
        new = combine(before, jax.tree.map(lambda part: part[at], everything))
        return jax.tree.map(lambda a, b: jnp.where(reached, a, b), new, before)

    return lax.fori_loop(0, length, step, start)


def reduced_precision(values):
    return values.astype(jnp.bfloat16)


def product(left, right):
    return jnp.dot(left, right, preferred_element_type=jnp.float32)


def product_tn(left, right):
    return lax.dot_general(
        left, right, (((0,), (0,)), ((), ())), preferred_element_type=jnp.float32
    )


def product_nt(left, right):
    return lax.dot_general(
        left, right, (((1,), (1,)), ((), ())), preferred_element_type=jnp.float32
    )


def layer_norm(values, gain, bias):
    average = jnp.mean(values, axis=-1, keepdims=True)
    centre = values - average
    inverse = lax.rsqrt(jnp.mean(centre * centre, axis=-1, keepdims=True) + EPS)
    unit = centre * inverse
    return (unit * gain + bias, unit, inverse)


def norm_back(grad_in, unit, inverse, gain):
    scaled = grad_in * gain
    grad_values = inverse * (
        scaled
        - jnp.mean(scaled, axis=-1, keepdims=True)
        - unit * jnp.mean(scaled * unit, axis=-1, keepdims=True)
    )
    return (grad_values, jnp.sum(grad_in * unit, axis=0), jnp.sum(grad_in, axis=0))


def state_join(earlier, latter):
    return (
        latter[4] * earlier[0] + latter[0],
        latter[4] * earlier[1] + latter[1],
        latter[4] * earlier[2] + latter[5] * earlier[0] + latter[2],
        latter[4] * earlier[3] + latter[5] * earlier[1] + latter[3],
        earlier[4] * latter[4],
        earlier[5] * latter[4] + earlier[4] * latter[5],
    )


def suffix_join(earlier, latter):
    return (
        latter[0] + latter[2] * earlier[0],
        latter[1] + latter[2] * earlier[1],
        latter[2] * earlier[2],
    )


BF = jnp.bfloat16
F32 = jnp.float32
MESH = pl.DeviceIdType.MESH
NN = (((1,), (0,)), ((), ()))
NT = (((1,), (1,)), ((), ()))
TN = (((0,), (0,)), ((), ()))


def dot(left, right, form=NN):
    return lax.dot_general(left, right, form, preferred_element_type=F32)


def dot_exact_left(left, right):
    high = right.astype(BF)
    rest = (right - high.astype(F32)).astype(BF)
    return dot(left, high) + dot(left, rest)


def wide(lanes, width):
    return jnp.concatenate([lanes] * (width // 128), axis=1)


def tile(index, size):
    return pl.ds(pl.multiple_of(index * size, size), size)


def unit_of(values):
    average = jnp.mean(values, axis=-1, keepdims=True)
    centre = values - average
    inverse = lax.rsqrt(jnp.mean(centre * centre, axis=-1, keepdims=True) + EPS)
    return (centre * inverse, inverse)


def remote(source, target, send, receive, device):
    return pltpu.make_async_remote_copy(
        src_ref=source,
        dst_ref=target,
        send_sem=send,
        recv_sem=receive,
        device_id=device,
        device_id_type=MESH,
    )


class Place:
    def __init__(self, planes):
        self.planes = planes
        self.dp, self.mp = (lax.axis_index("dp"), lax.axis_index("mp"))
        self.z = lax.div(self.mp, 2)
        self.core = lax.rem(self.mp, 2)
        self.count = 2 * planes
        self.other = (self.dp, self.mp + 1 - 2 * self.core)
        self.side_x = (self.dp + 1 - 2 * lax.rem(self.dp, 2), self.mp)
        self.side_y = (lax.rem(self.dp + 2, 4), self.mp)

    def ahead(self, steps):
        return (self.dp, lax.rem(self.mp + steps + self.count, self.count))

    def plane(self, steps):
        return (self.dp, lax.rem(self.z + steps + self.planes, self.planes) * 2 + self.core)


def greet(devices):
    barrier = pltpu.get_barrier_semaphore()
    for device in devices:
        pl.semaphore_signal(barrier, inc=1, device_id=device, device_id_type=MESH)
    pl.semaphore_wait(barrier, len(devices))


def forward_kernel(
    planes,
    micros,
    rows,
    x_ref,
    last_ref,
    segcol_ref,
    segrow_ref,
    segpay_ref,
    vec_ref,
    adj_ref,
    key_w,
    value_w,
    recept_w,
    output_w,
    gate_w,
    w1_ref,
    w2_ref,
    k_out,
    v_out,
    r_out,
    num_out,
    den_out,
    mid_out,
    gate_out,
    mk_out,
    mv_out,
    mr_out,
    gated_out,
    mg_out,
    da_out,
    db_out,
    keep_out,
    segs_out,
    mh_all,
    ret_all,
    w1_all,
    w2_all,
    wk,
    wv,
    wr,
    wo,
    wg,
    k_s,
    v_s,
    r_s,
    num_s,
    den_s,
    mid_s,
    gate_s,
    xb_s,
    da_s,
    mk_s,
    mv_s,
    mr_s,
    gated_s,
    mg_s,
    mh_s,
    ret_s,
    keep_s,
    mask_s,
    halo_a,
    near_a,
    pay_b,
    halo_b,
    segs_s,
    state_own,
    state_other,
    state_chip,
    state_in,
    carry_s,
    w_sem,
    out_sem,
    small_sem,
    z_sem,
    s_sem,
):
    at = Place(planes)
    dp, mp, z, core = (at.dp, at.mp, at.z, at.core)
    tokens = micros * rows
    peers = [at.ahead(step) for step in range(1, at.count)]
    greet(peers + [at.side_x, at.side_y])

    quarter1, quarter2 = (w1_ref.shape[0] // 4, w2_ref.shape[0] // 4)
    q1, q2 = (tile(dp, quarter1), tile(dp, quarter2))
    z_copies = []
    for step in range(1, planes):
        to = at.plane(-step)
        z_copies.append(
            (
                remote(w1_ref.at[q1], w1_all.at[step - 1, q1], z_sem.at[step - 1, 0, 0], z_sem.at[step - 1, 0, 1], to),
                remote(w2_ref.at[q2], w2_all.at[step - 1, q2], z_sem.at[step - 1, 1, 0], z_sem.at[step - 1, 1, 1], to),
            )
        )

    halo_copy = remote(last_ref, halo_a, small_sem.at[0, 0], small_sem.at[0, 1], at.ahead(1))
    halo_copy.start()
    seg_copies = [
        remote(segpay_ref, segs_s.at[mp], small_sem.at[1 + step, 0], small_sem.at[1 + step, 1], device)
        for step, device in enumerate(peers)
    ]
    for copy in seg_copies:
        copy.start()
    segs_s[mp] = segpay_ref[...]
    loads = []
    for index, (source, target) in enumerate(
        ((key_w, wk), (value_w, wv), (recept_w, wr), (output_w, wo), (gate_w, wg))
    ):
        loads.append(pltpu.make_async_copy(source, target, w_sem.at[index]))
        loads[-1].start()
    for copy in z_copies[0]:
        copy.start()
    halo_copy.wait()
    for copy in seg_copies:
        copy.wait()

    before = lax.rem(mp + at.count - 1, at.count)
    has_before = mp > 0
    first_row = lax.broadcasted_iota(jnp.int32, (rows, 128), 0) == 0
    row_at = lax.broadcasted_iota(jnp.int32, (rows, rows), 0)
    col_at = lax.broadcasted_iota(jnp.int32, (rows, rows), 1)
    for m in range(micros):
        here = segcol_ref[m * rows : (m + 1) * rows, :]
        behind = jnp.where(
            first_row, segs_s[before, m : m + 1, :], pltpu.roll(here, 1, 0)
        )
        same = jnp.logical_and(
            here == behind, jnp.logical_or(jnp.logical_not(first_row), has_before)
        )
        keep_s[m * rows : (m + 1) * rows, :] = same.astype(F32)
        mask_s[m] = jnp.logical_and(
            here == segrow_ref[m : m + 1, :], col_at < row_at
        ).astype(F32).astype(BF)

    block = 16
    at_first = lax.broadcasted_iota(jnp.int32, (block, 1024), 0) == 0
    gain, bias = (vec_ref[0:1, :], vec_ref[1:2, :])
    near_a[...] = unit_of(halo_a[...])[0] * gain + bias
    for m in range(micros):

        def mix_a(b, prev, m=m):
            span = tile(m * (rows // block) + b, block)
            normed = unit_of(x_ref[span, :].astype(F32))[0] * gain + bias
            shifted = jnp.where(at_first, prev, pltpu.roll(normed, 1, 0)) * wide(
                keep_s[span, :], 1024
            )
            delta = normed - shifted
            da_s[span, :] = delta
            mk_s[span, :] = (shifted + delta * vec_ref[4:5, :]).astype(BF)
            mv_s[span, :] = (shifted + delta * vec_ref[5:6, :]).astype(BF)
            mr_s[span, :] = (shifted + delta * vec_ref[6:7, :]).astype(BF)
            return normed[block - 1 : block, :]

        lax.fori_loop(0, rows // block, mix_a, near_a[m : m + 1, :])

    outs = []

    def put(source, target):
        copy = pltpu.make_async_copy(source, target, out_sem.at[len(outs)])
        copy.start()
        outs.append(copy)

    put(da_s, da_out)
    put(keep_s, keep_out)
    put(segs_s, segs_out)
    put(mk_s, mk_out)
    put(mv_s, mv_out)
    put(mr_s, mr_out)

    loads[0].wait()
    loads[1].wait()
    width = 256
    place = lax.broadcasted_iota(jnp.int32, (rows, width), 0).astype(F32)

    @pl.loop(0, 1024 // width)
    def _(i):
        cols = tile(i, width)
        rate = jnp.exp(vec_ref[2:3, cols])
        rising = jnp.exp(place * rate)
        falling = jnp.exp((1.0 - place) * rate)
        step_back = jnp.exp(-rate)
        keys = dot(mk_s[...], wk[:, cols])
        values = dot(mv_s[...], wv[:, cols])
        for m in range(micros):
            span = slice(m * rows, (m + 1) * rows)
            key, value = (keys[span], values[span])
            raised = jnp.exp(key)
            weighted = raised * value
            num = falling * dot_exact_left(mask_s[m], rising * weighted)
            den = falling * dot_exact_left(mask_s[m], rising * raised)
            k_s[span, cols] = key
            v_s[span, cols] = value
            num_s[span, cols] = num
            den_s[span, cols] = den
            state_own[m : m + 1, cols] = step_back * num[rows - 1 :] + weighted[rows - 1 :]
            state_own[micros + m : micros + m + 1, cols] = (
                step_back * den[rows - 1 :] + raised[rows - 1 :]
            )

    put(k_s, k_out)
    put(v_s, v_out)
    core_copy = remote(state_own, state_other, s_sem.at[0, 0], s_sem.at[0, 1], at.other)
    core_copy.start()
    for copy in z_copies[0]:
        copy.wait()
    xy_copies = []

    def along(step):
        group = []
        own1, own2 = (w1_all.at[step, q1], w2_all.at[step, q2])
        return (
            remote(own1, own1, z_sem.at[step, 2, 0], z_sem.at[step, 2, 1], at.side_x),
            remote(own2, own2, z_sem.at[step, 3, 0], z_sem.at[step, 3, 1], at.side_y),
        )

    def across(step):
        both1 = w1_all.at[step, tile(lax.div(dp, 2), 2 * quarter1)]
        own2 = w2_all.at[step, q2]
        far2 = w2_all.at[step, tile(lax.rem(dp + 2, 4), quarter2)]
        return (
            remote(both1, both1, z_sem.at[step, 4, 0], z_sem.at[step, 4, 1], at.side_y),
            remote(own2, own2, z_sem.at[step, 5, 0], z_sem.at[step, 5, 1], at.side_x),
            remote(far2, far2, z_sem.at[step, 6, 0], z_sem.at[step, 6, 1], at.side_x),
        )

    def start(group):
        for copy in group:
            copy.start()

    def finish(group):
        for copy in group:
            copy.wait()

    along_0, along_1, along_2 = (along(0), along(1), along(2))
    across_0, across_1, across_2 = (across(0), across(1), across(2))
    start(along_0)
    start(z_copies[2])
    loads[2].wait()

    @pl.loop(0, 2)
    def _(i):
        span = tile(i, tokens // 2)
        r_s[span, :] = jax.nn.sigmoid(dot(mr_s[span, :], wr[...]))

    put(r_s, r_out)

    pair = lax.div(mp, 2) * 2
    decay_all = jnp.exp(-float(rows) * jnp.exp(vec_ref[2:3, :]))
    core_copy.wait()

    def last_of(device):
        return wide(segs_s[lax.rem(device + at.count, at.count), 0 : 2 * micros, :], 1024)

    even = jnp.where(core == 0, state_own[...], state_other[...])
    odd = jnp.where(core == 0, state_other[...], state_own[...])
    state_chip[...] = odd + jnp.where(last_of(pair) == last_of(pair + 1), decay_all * even, 0.0)
    chip_copies = [
        remote(state_chip, state_in.at[step - 1], s_sem.at[step, 0], s_sem.at[step, 1], at.plane(step))
        for step in range(1, planes)
    ]
    start(chip_copies)
    finish(along_0)
    start(across_0)
    finish(chip_copies)
    total = jnp.zeros_like(state_chip[...])
    power = jnp.ones_like(decay_all)
    for step in range(1, planes):
        fits = jnp.logical_and(
            last_of(pair - 2 * step + 1) == last_of(pair - 1), z >= step
        )
        total = total + jnp.where(fits, power * state_in[step - 1], 0.0)
        power = power * decay_all * decay_all
    joined = state_other[...] + jnp.where(last_of(pair) == last_of(pair - 1), decay_all * total, 0.0)
    carry_s[...] = jnp.where(core == 0, total, joined)

    @pl.loop(0, 1024 // width)
    def _(i):
        cols = tile(i, width)
        rate = jnp.exp(vec_ref[2:3, cols])
        falling = jnp.exp(-place * rate)
        extra = vec_ref[3:4, cols]
        for m in range(micros):
            span = slice(m * rows, (m + 1) * rows)
            fits = jnp.logical_and(
                segcol_ref[span, :] == segs_s[before, m : m + 1, :], has_before
            ).astype(F32)
            carried = wide(fits, width) * falling
            num = num_s[span, cols] + carried * carry_s[m : m + 1, cols]
            den = den_s[span, cols] + carried * carry_s[micros + m : micros + m + 1, cols]
            bonus = jnp.exp(extra + k_s[span, cols])
            mixed = (num + bonus * v_s[span, cols]) / (den + bonus)
            num_s[span, cols] = num
            den_s[span, cols] = den
            gated_s[span, cols] = (r_s[span, cols] * mixed).astype(BF)

    put(num_s, num_out)
    put(den_s, den_out)
    put(gated_s, gated_out)
    loads[3].wait()

    @pl.loop(0, 2)
    def _(i):
        span = tile(i, tokens // 2)
        mid_s[span, :] = x_ref[span, :].astype(F32) + dot(gated_s[span, :], wo[...])

    put(mid_s, mid_out)
    gain_b, bias_b = (vec_ref[7:8, :], vec_ref[8:9, :])

    def norm_b(b):
        span = tile(b, block)
        xb_s[span, :] = unit_of(mid_s[span, :])[0] * gain_b + bias_b

    for m in range(micros):
        norm_b((m + 1) * (rows // block) - 1)
        pay_b[m : m + 1, :] = xb_s[(m + 1) * rows - 1 : (m + 1) * rows, :]
    pay_b[micros:, :] = jnp.zeros((8 - micros, 1024), F32)
    halo_b_copy = remote(pay_b, halo_b, s_sem.at[planes, 0], s_sem.at[planes, 1], at.ahead(1))
    halo_b_copy.start()
    for m in range(micros):

        @pl.loop(m * (rows // block), (m + 1) * (rows // block) - 1)
        def _(b):
            norm_b(b)

    finish(z_copies[2])
    start(along_2)
    start(z_copies[1])
    halo_b_copy.wait()
    for m in range(micros):

        def mix_b(b, prev, m=m):
            span = tile(m * (rows // block) + b, block)
            normed = xb_s[span, :]
            shifted = jnp.where(at_first, prev, pltpu.roll(normed, 1, 0)) * wide(
                keep_s[span, :], 1024
            )
            delta = normed - shifted
            xb_s[span, :] = delta
            mh_s[span, :] = (shifted + delta * vec_ref[9:10, :]).astype(BF)
            mg_s[span, :] = (shifted + delta * vec_ref[10:11, :]).astype(BF)
            return normed[block - 1 : block, :]

        lax.fori_loop(0, rows // block, mix_b, halo_b[m : m + 1, :])

    mh_copy = remote(
        mh_s, mh_all.at[1], s_sem.at[planes + 1, 0], s_sem.at[planes + 1, 1], at.other
    )
    mh_copy.start()
    put(mh_s, mh_all.at[0])
    put(mg_s, mg_out)
    put(xb_s, db_out)
    loads[4].wait()

    @pl.loop(0, 2)
    def _(i):
        span = tile(i, tokens // 2)
        gate = jax.nn.sigmoid(dot(mg_s[span, :], wg[...]))
        gate_s[span, :] = gate
        ret_s[span, :] = (adj_ref[span, :].astype(F32) * gate).astype(BF)

    ret_copy = remote(
        ret_s, ret_all.at[1], s_sem.at[planes + 2, 0], s_sem.at[planes + 2, 1], at.other
    )
    ret_copy.start()
    put(ret_s, ret_all.at[0])
    put(gate_s, gate_out)
    finish(across_0)
    finish(along_2)
    start(across_2)
    finish(z_copies[1])
    start(along_1)
    finish(across_2)
    finish(along_1)
    start(across_1)
    finish(across_1)
    mh_copy.wait()
    ret_copy.wait()
    for copy in outs:
        copy.wait()


ANY = pl.BlockSpec(memory_space=pl.ANY)
VM = pl.BlockSpec(memory_space=pltpu.VMEM)


def forward_call(planes, micros, rows, operands):
    tokens = micros * rows
    hidden = operands[-1].shape[0]

    def big(kind):
        return jax.ShapeDtypeStruct((tokens, 1024), kind)

    def hold(kind):
        return pltpu.VMEM((tokens, 1024), kind)

    square = pltpu.VMEM((1024, 1024), BF)
    few = pltpu.VMEM((8, 1024), F32)
    pair = pltpu.SemaphoreType.DMA
    return pl.pallas_call(
        functools.partial(forward_kernel, planes, micros, rows),
        out_shape=[big(F32)] * 7
        + [big(BF)] * 5
        + [big(F32)] * 2
        + [
            jax.ShapeDtypeStruct((tokens, 128), F32),
            jax.ShapeDtypeStruct((2 * planes, 16, 128), F32),
        ]
        + [jax.ShapeDtypeStruct((2, tokens, 1024), BF)] * 2
        + [
            jax.ShapeDtypeStruct((planes - 1, 1024, hidden), BF),
            jax.ShapeDtypeStruct((planes - 1, hidden, 1024), BF),
        ],
        in_specs=[VM] * 7 + [ANY] * 7,
        out_specs=[ANY] * 20,
        scratch_shapes=[square] * 5
        + [hold(F32)] * 9
        + [hold(BF)] * 7
        + [
            pltpu.VMEM((tokens, 128), F32),
            pltpu.VMEM((micros, rows, rows), BF),
            few,
            few,
            few,
            few,
            pltpu.VMEM((2 * planes, 16, 128), F32),
            few,
            few,
            few,
            pltpu.VMEM((planes - 1, 8, 1024), F32),
            few,
            pair((5,)),
            pair((20,)),
            pair((2 * planes + 1, 2)),
            pair((planes - 1, 7, 2)),
            pair((planes + 3, 2)),
        ],
        compiler_params=pltpu.CompilerParams(
            collective_id=0, has_side_effects=True, vmem_limit_bytes=58 << 20
        ),
        cost_estimate=pl.CostEstimate(
            flops=10 * tokens * 1024 * 1024, bytes_accessed=40 << 20, transcendentals=6 * tokens * 1024
        ),
        name="time_mix_forward",
    )(*operands)


class Reduce:
    def __init__(self, at, parts, first, second, far, sems, slot, x_first):
        self.at, self.parts, self.slot = (at, parts, slot)
        side = lax.rem(at.dp, 2)
        line = lax.div(at.dp, 2)
        self.one, self.two = (side, line) if x_first else (line, side)
        near, next_to = (at.side_x, at.side_y) if x_first else (at.side_y, at.side_x)
        self.first, self.second, self.far = (first, second, far)
        self.copy_1 = remote(parts.at[1 - self.one], first, sems.at[0, 0], sems.at[0, 1], near)
        self.copy_2 = remote(
            parts.at[self.one, 1 - self.two], second, sems.at[1, 0], sems.at[1, 1], next_to
        )
        if slot:
            self.copy_3 = remote(
                parts.at[self.one, self.two], far, sems.at[2, 0], sems.at[2, 1], at.plane(slot)
            )

    def start(self):
        self.copy_1.start()

    def add(self, half, other):
        mine = self.parts.at[self.one, half]

        @pl.loop(0, mine.shape[0] // 64)
        def _(i):
            span = tile(i, 64)
            mine[span, :] = (mine[span, :].astype(F32) + other[span, :].astype(F32)).astype(BF)

    def middle(self):
        self.copy_1.wait()
        self.add(1 - self.two, self.first.at[1 - self.two])
        self.copy_2.start()
        self.add(self.two, self.first.at[self.two])

    def last(self):
        self.copy_2.wait()
        self.add(self.two, self.second)
        if self.slot:
            self.copy_3.start()

    def close(self):
        if self.slot:
            self.copy_3.wait()


def sum_rows(into, index, values):
    total = values[0:8]
    for start in range(8, values.shape[0], 8):
        total = total + values[start : start + 8]
    into[index] = into[index] + total


def norm_back_rows(grad, unit, inverse, gain):
    scaled = grad * gain
    return inverse * (
        scaled
        - jnp.mean(scaled, axis=-1, keepdims=True)
        - unit * jnp.mean(scaled * unit, axis=-1, keepdims=True)
    )


def middle_kernel(
    planes,
    micros,
    rows,
    vec_ref,
    keep_ref,
    segs_ref,
    segcol_ref,
    segrow_ref,
    w1_ref,
    w2_ref,
    w1_all,
    w2_all,
    mh_all,
    ret_all,
    mid_ref,
    gate_ref,
    adj_ref,
    db_ref,
    k_ref,
    v_ref,
    r_ref,
    num_ref,
    den_ref,
    gate_w,
    output_w,
    out_ref,
    gmid_out,
    ggp_out,
    gatt_out,
    grp_out,
    gk_out,
    gv_out,
    sums_out,
    own1_out,
    own2_out,
    parts1,
    parts2,
    first1,
    first2,
    second1,
    second2,
    far1,
    far2,
    ret_acc,
    gmh_acc,
    ret_send,
    gmh_send,
    ret_recv,
    gmh_recv,
    mid_s,
    gate_s,
    adj_s,
    db_s,
    sums_s,
    sums_flat,
    mask_s,
    pay_b,
    halo_b,
    state_own,
    state_other,
    state_chip,
    state_in,
    carry_s,
    own1_s,
    own2_s,
    load_sem,
    out_sem,
    rs_sem,
    s_sem,
):
    at = Place(planes)
    dp, mp, z, core = (at.dp, at.mp, at.z, at.core)
    tokens = micros * rows
    hidden = w1_ref.shape[1]
    outs = []

    def put(source, target):
        copy = pltpu.make_async_copy(source, target, out_sem.at[len(outs)])
        copy.start()
        outs.append(copy)

    loaded = []

    def load(source, target):
        copy = pltpu.make_async_copy(source, target, load_sem.at[len(loaded)])
        copy.start()
        loaded.append(copy)
        return copy

    greet(
        [at.other, at.side_x, at.side_y]
        + [at.plane(step) for step in range(1, planes)]
        + [at.ahead(1), at.ahead(-1)]
    )
    reduces = []
    for slot in range(planes):
        reduces.append(
            (
                Reduce(at, parts1.at[slot], first1.at[slot], second1.at[slot],
                       far1.at[max(slot - 1, 0)], rs_sem.at[slot, 0], slot, True),
                Reduce(at, parts2.at[slot], first2.at[slot], second2.at[slot],
                       far2.at[max(slot - 1, 0)], rs_sem.at[slot, 1], slot, False),
            )
        )
    ret_copy = remote(ret_send, ret_recv, s_sem.at[0, 0], s_sem.at[0, 1], at.other)
    gmh_copy = remote(gmh_send, gmh_recv, s_sem.at[1, 0], s_sem.at[1, 1], at.other)

    def feed_forward(w1, w2, mh2, gr2, sq_s, gp_s):
        slots = []
        mh_load = [load(mh_all.at[0], mh2.at[0:tokens]), load(ret_all.at[0], gr2.at[0:tokens])]
        slots.append((load(w1_ref, w1.at[0]), load(w2_ref, w2.at[0])))
        mh_load += [
            load(mh_all.at[1], mh2.at[tokens : 2 * tokens]),
            load(ret_all.at[1], gr2.at[tokens : 2 * tokens]),
        ]
        for slot in range(1, planes):
            slots.append(
                (load(w1_all.at[slot - 1], w1.at[slot]), load(w2_all.at[slot - 1], w2.at[slot]))
            )
        late = [load(mid_ref, mid_s), load(gate_ref, gate_s), load(adj_ref, adj_s), load(db_ref, db_s)]
        for copy in mh_load:
            copy.wait()
        for slot in range(planes):
            for copy in slots[slot]:
                copy.wait()

            def rows_of(i, slot=slot):
                span = tile(i, 256)
                pre = dot(mh2[span, :], w1[slot])
                rectified = jnp.maximum(pre, 0.0)
                squared = (rectified * rectified).astype(BF)
                sq_s[span, :] = squared
                grad_squared = dot(gr2[span, :], w2[slot], NT)
                grad_pre = (grad_squared * 2.0 * rectified).astype(BF)
                gp_s[span, :] = grad_pre
                if slot == 0:
                    ret_acc[span, :] = dot(squared, w2[slot])
                    gmh_acc[span, :] = dot(grad_pre, w1[slot], NT)
                else:
                    ret_acc[span, :] += dot(squared, w2[slot])
                    gmh_acc[span, :] += dot(grad_pre, w1[slot], NT)

            half = tokens // 256
            pl.loop(half, 2 * half)(rows_of)
            if slot == planes - 1:

                @pl.loop(0, tokens // 64)
                def _(i):
                    span = tile(i, 64)
                    far_span = tile(tokens // 64 + i, 64)
                    ret_send[span, :] = ret_acc[far_span, :].astype(BF)
                    gmh_send[span, :] = gmh_acc[far_span, :].astype(BF)

                ret_copy.start()
                gmh_copy.start()
            pl.loop(0, half)(rows_of)

            @pl.loop(0, 4)
            def _(q, slot=slot):
                line, side = (lax.div(q, 2), lax.rem(q, 2))
                cols = tile(q, 256)
                parts1[slot, side, line] = dot(mh2[:, cols], gp_s[...], TN).astype(BF)
                parts2[slot, line, side] = dot(gr2[:, cols], sq_s[...], TN).astype(BF)

            for reduce in reduces[slot]:
                reduce.start()
            if slot >= 2:
                for reduce in reduces[slot - 2]:
                    reduce.middle()
        for copy in late:
            copy.wait()

    wide_w = pltpu.VMEM((planes, 1024, hidden), BF)
    pl.run_scoped(
        feed_forward,
        wide_w,
        pltpu.VMEM((planes, hidden, 1024), BF),
        pltpu.VMEM((2 * tokens, 1024), BF),
        pltpu.VMEM((2 * tokens, 1024), BF),
        pltpu.VMEM((2 * tokens, hidden), BF),
        pltpu.VMEM((2 * tokens, hidden), BF),
    )
    own = slice(0, tokens)
    far = slice(tokens, 2 * tokens)
    block = 16

    def attention(k_s, v_s, r_s, num_s, den_s, wg, wo, ggp_s, gatt_s, grp_s, gk_s, gv_s):
        need_wg = load(gate_w, wg)
        need_wo = load(output_w, wo)
        need = [
            load(k_ref, k_s),
            load(v_ref, v_s),
            load(r_ref, r_s),
            load(num_ref, num_s),
            load(den_ref, den_s),
        ]
        sums_s[...] = jnp.zeros_like(sums_s)
        row_at = lax.broadcasted_iota(jnp.int32, (rows, rows), 0)
        col_at = lax.broadcasted_iota(jnp.int32, (rows, rows), 1)
        for m in range(micros):
            mask_s[m] = jnp.logical_and(
                segcol_ref[m * rows : (m + 1) * rows, :] == segrow_ref[m : m + 1, :],
                col_at > row_at,
            ).astype(F32).astype(BF)
        ret_copy.wait()

        @pl.loop(0, tokens // block)
        def _(b):
            span = tile(b, block)
            returned = ret_acc[span, :] + ret_recv[span, :].astype(F32)
            gate = gate_s[span, :]
            product_in = gate * returned
            ret_acc[span, :] = mid_s[span, :] + product_in
            ggp_s[span, :] = (adj_s[span, :].astype(F32) * product_in * (1.0 - gate)).astype(BF)

        put(ret_acc.at[own], out_ref)
        put(ggp_s, ggp_out)
        need_wg.wait()

        @pl.loop(0, 2)
        def _(i):
            span = tile(i, tokens // 2)
            ret_acc[tile(2 + i, tokens // 2), :] = dot(ggp_s[span, :], wg[...], NT)

        for reduce in reduces[planes - 2]:
            reduce.middle()
        for reduce in reduces[0]:
            reduce.last()
        gmg = ret_acc.at[far]
        gmh_copy.wait()
        mix_h, mix_g = (vec_ref[9:10, :], vec_ref[10:11, :])
        gain = vec_ref[7:8, :]

        def combine(b):
            span = tile(b, block)
            grad_h = gmh_acc[span, :] + gmh_recv[span, :].astype(F32)
            grad_g = gmg[span, :]
            shift = (grad_h * (1.0 - mix_h) + grad_g * (1.0 - mix_g)) * wide(keep_ref[span, :], 1024)
            return (span, grad_h, grad_g, shift)

        for m in range(micros):
            pay_b[m : m + 1, :] = combine(m * (rows // block))[3][0:1, :]
        pay_b[micros:, :] = jnp.zeros((8 - micros, 1024), F32)
        halo_copy = remote(pay_b, halo_b, s_sem.at[2, 0], s_sem.at[2, 1], at.ahead(-1))
        halo_copy.start()
        at_last = lax.broadcasted_iota(jnp.int32, (block, 1024), 0) == block - 1
        halo_copy.wait()
        for m in range(micros):

            def back_b(i, after, m=m):
                span, grad_h, grad_g, shift = combine((m + 1) * (rows // block) - 1 - i)
                delta = db_s[span, :]
                sum_rows(sums_s, 9, grad_h * delta)
                sum_rows(sums_s, 10, grad_g * delta)
                moved = jnp.where(at_last, after, pltpu.roll(shift, block - 1, 0))
                grad = grad_h * mix_h + grad_g * mix_g + moved
                unit, inverse = unit_of(mid_s[span, :])
                sum_rows(sums_s, 7, grad * unit)
                sum_rows(sums_s, 8, grad)
                total = adj_s[span, :].astype(F32) + norm_back_rows(grad, unit, inverse, gain)
                gmh_acc[span, :] = total
                gatt_s[span, :] = total.astype(BF)
                return shift[0:1, :]

            lax.fori_loop(0, rows // block, back_b, halo_b[m : m + 1, :])

        put(gmh_acc.at[own], gmid_out)
        put(gatt_s, gatt_out)
        need_wo.wait()

        @pl.loop(0, 2)
        def _(i):
            span = tile(i, tokens // 2)
            gmh_acc[tile(2 + i, tokens // 2), :] = dot(gatt_s[span, :], wo[...], NT)

        for reduce in reduces[planes - 1]:
            reduce.middle()
        for reduce in reduces[1]:
            reduce.last()
        for copy in need:
            copy.wait()
        width = 256
        place = lax.broadcasted_iota(jnp.int32, (rows, width), 0).astype(F32)

        @pl.loop(0, 1024 // width)
        def _(i):
            cols = tile(i, width)
            rate = jnp.exp(vec_ref[2:3, cols])
            rising = jnp.exp(place * rate)
            falling = jnp.exp((1.0 - place) * rate)
            step_back = jnp.exp(-rate)
            extra = vec_ref[3:4, cols]
            for m in range(micros):
                span = slice(m * rows, (m + 1) * rows)
                far_span = slice(tokens + m * rows, tokens + (m + 1) * rows)
                bonus = jnp.exp(extra + k_s[span, cols])
                recept = r_s[span, cols]
                inverse = 1.0 / (den_s[span, cols] + bonus)
                mixed = (num_s[span, cols] + bonus * v_s[span, cols]) * inverse
                grad_gated = gmh_acc[far_span, cols]
                grad_mixed = grad_gated * recept
                grp_s[span, cols] = (grad_mixed * mixed * (1.0 - recept)).astype(BF)
                up = grad_mixed * inverse
                down = -up * mixed
                up_sum = rising * dot_exact_left(mask_s[m], falling * up)
                down_sum = rising * dot_exact_left(mask_s[m], falling * down)
                gmh_acc[far_span, cols] = up
                db_s[span, cols] = down
                mid_s[span, cols] = up_sum
                gate_s[span, cols] = down_sum
                state_own[m : m + 1, cols] = up[0:1] + step_back * up_sum[0:1]
                state_own[micros + m : micros + m + 1, cols] = down[0:1] + step_back * down_sum[0:1]

        put(grp_s, grp_out)
        core_copy = remote(state_own, state_other, s_sem.at[3, 0], s_sem.at[3, 1], at.other)
        core_copy.start()
        pair = lax.div(mp, 2) * 2
        decay_all = jnp.exp(-float(rows) * jnp.exp(vec_ref[2:3, :]))

        def seen(device, last):
            index = lax.rem(device + at.count, at.count)
            start = 0 if last else 2 * micros
            return wide(segs_ref[index, start : start + 2 * micros, :], 1024)

        core_copy.wait()
        even = jnp.where(core == 0, state_own[...], state_other[...])
        odd = jnp.where(core == 0, state_other[...], state_own[...])
        state_chip[...] = even + jnp.where(
            seen(pair, False) == seen(pair + 1, False), decay_all * odd, 0.0
        )
        chip_copies = [
            remote(state_chip, state_in.at[step - 1], s_sem.at[3 + step, 0], s_sem.at[3 + step, 1], at.plane(-step))
            for step in range(1, planes)
        ]
        for copy in chip_copies:
            copy.start()
        for copy in chip_copies:
            copy.wait()
        total = jnp.zeros_like(state_chip[...])
        power = jnp.ones_like(decay_all)
        for step in range(1, planes):
            fits = jnp.logical_and(
                seen(pair + 2 * step, False) == seen(mp, True), z + step < planes
            )
            total = total + jnp.where(fits, power * state_in[step - 1], 0.0)
            power = power * decay_all * decay_all
        joined = decay_all * total + jnp.where(
            seen(pair + 1, False) == seen(pair, True), state_other[...], 0.0
        )
        carry_s[...] = jnp.where(core == 0, joined, total)
        for reduce in reduces[2]:
            reduce.last()

        @pl.loop(0, 1024 // width)
        def _(i):
            cols = tile(i, width)
            rate = jnp.exp(vec_ref[2:3, cols])
            tail = jnp.exp((place - (rows - 1.0)) * rate)
            extra = vec_ref[3:4, cols]
            step_back = jnp.exp(-rate)
            for m in range(micros):
                span = slice(m * rows, (m + 1) * rows)
                far_span = slice(tokens + m * rows, tokens + (m + 1) * rows)
                fits = (segcol_ref[span, :] == segs_ref[mp, m : m + 1, :]).astype(F32)
                carried = wide(fits, width) * tail
                up_sum = mid_s[span, cols] + carried * carry_s[m : m + 1, cols]
                down_sum = gate_s[span, cols] + carried * carry_s[micros + m : micros + m + 1, cols]
                up, down = (gmh_acc[far_span, cols], db_s[span, cols])
                key, value = (k_s[span, cols], v_s[span, cols])
                bonus = jnp.exp(extra + key)
                raised = jnp.exp(key)
                direct = (up * value + down) * bonus
                gk_s[span, cols] = (direct + raised * (value * up_sum + down_sum)).astype(BF)
                gv_s[span, cols] = (up * bonus + raised * up_sum).astype(BF)
                rate_part = -rate * step_back * (up_sum * num_s[span, cols] + down_sum * den_s[span, cols])
                for index, part in ((2, rate_part), (3, direct)):
                    summed = part[0:8]
                    for start in range(8, rows, 8):
                        summed = summed + part[start : start + 8]
                    sums_s[index, :, cols] = sums_s[index, :, cols] + summed

        put(gk_s, gk_out)
        put(gv_s, gv_out)
        for index in range(16):
            sums_flat[index : index + 1, :] = jnp.sum(sums_s[index], axis=0, keepdims=True)
        put(sums_flat, sums_out)
        for reduce in reduces[3]:
            reduce.last()
        for slot in range(planes):
            for reduce in reduces[slot]:
                reduce.close()
        for parts, far_parts, own_s, own_out, one, two, turned in (
            (parts1, far1, own1_s, own1_out, lax.rem(dp, 2), lax.div(dp, 2), False),
            (parts2, far2, own2_s, own2_out, lax.div(dp, 2), lax.rem(dp, 2), True),
        ):
            total = parts[0, one, two].astype(F32)
            for slot in range(planes - 1):
                total = total + far_parts[slot].astype(F32)
            own_s[...] = total.T if turned else total
            put(own_s, own_out)
        for copy in outs:
            copy.wait()

    def hold(kind):
        return pltpu.VMEM((tokens, 1024), kind)

    square = pltpu.VMEM((1024, 1024), BF)
    pl.run_scoped(attention, *([hold(F32)] * 5), square, square, *([hold(BF)] * 5))


def middle_call(planes, micros, rows, operands):
    tokens = micros * rows
    hidden = operands[5].shape[1]

    def big(kind):
        return jax.ShapeDtypeStruct((tokens, 1024), kind)

    def hold(count, kind):
        return pltpu.VMEM((count, 1024), kind)

    few = hold(8, F32)
    quarter = (256, hidden)
    sems = pltpu.SemaphoreType.DMA
    return pl.pallas_call(
        functools.partial(middle_kernel, planes, micros, rows),
        out_shape=[big(F32)] * 2
        + [big(BF)] * 5
        + [jax.ShapeDtypeStruct((16, 1024), F32)]
        + [jax.ShapeDtypeStruct(quarter, F32), jax.ShapeDtypeStruct(quarter[::-1], F32)],
        in_specs=[VM] * 5 + [ANY] * 17,
        out_specs=[ANY] * 10,
        scratch_shapes=[pltpu.VMEM((planes, 2, 2) + quarter, BF)] * 2
        + [pltpu.VMEM((planes, 2) + quarter, BF)] * 2
        + [pltpu.VMEM((planes,) + quarter, BF)] * 2
        + [pltpu.VMEM((planes - 1,) + quarter, BF)] * 2
        + [hold(2 * tokens, F32)] * 2
        + [hold(tokens, BF)] * 4
        + [hold(tokens, F32), hold(tokens, F32), hold(tokens, BF), hold(tokens, F32)]
        + [
            pltpu.VMEM((16, 8, 1024), F32),
            pltpu.VMEM((16, 1024), F32),
            pltpu.VMEM((micros, rows, rows), BF),
            few,
            few,
            few,
            few,
            few,
            pltpu.VMEM((planes - 1, 8, 1024), F32),
            few,
            pltpu.VMEM(quarter, F32),
            pltpu.VMEM(quarter[::-1], F32),
            sems((24,)),
            sems((10,)),
            sems((planes, 2, 3, 2)),
            sems((3 + planes, 2)),
        ],
        compiler_params=pltpu.CompilerParams(
            collective_id=1, has_side_effects=True, vmem_limit_bytes=62 << 20
        ),
        cost_estimate=pl.CostEstimate(
            flops=52 * tokens * 1024 * 1024, bytes_accessed=60 << 20, transcendentals=6 * tokens * 1024
        ),
        name="channel_mix_and_adjoint",
    )(*operands)


class ReduceSquare:
    def __init__(self, at, parts, across, first, second, far, sems, x_first):
        self.at, self.across, self.first, self.second, self.far = (at, across, first, second, far)
        self.x_first = x_first
        side = lax.rem(at.dp, 2)
        line = lax.div(at.dp, 2)
        self.one, self.two = (side, line) if x_first else (line, side)
        near, next_to = (at.side_x, at.side_y) if x_first else (at.side_y, at.side_x)
        self.parts = parts
        self.mine = parts.at[at.core]
        self.copy_0 = remote(parts.at[1 - at.core], across, sems.at[0, 0], sems.at[0, 1], at.other)
        self.copy_1 = remote(self.mine.at[1 - self.one], first, sems.at[1, 0], sems.at[1, 1], near)
        self.copy_2 = remote(
            self.mine.at[self.one, 1 - self.two], second, sems.at[2, 0], sems.at[2, 1], next_to
        )
        self.copies_3 = [
            remote(
                self.mine.at[self.one, self.two, lax.rem(at.z + step, at.planes)],
                far.at[step - 1],
                sems.at[2 + step, 0],
                sems.at[2 + step, 1],
                at.plane(step),
            )
            for step in range(1, at.planes)
        ]

    def fill(self, left, right):
        planes = self.at.planes

        @pl.loop(0, 4)
        def _(q):
            line, side = (lax.div(q, 2), lax.rem(q, 2))
            one, two = (side, line) if self.x_first else (line, side)
            made = dot(left[:, tile(q, 256)], right[...], TN).astype(BF)
            split = made.reshape(planes, 2, 256 // (2 * planes), 1024)
            self.parts[0, one, two] = split[:, 0]
            self.parts[1, one, two] = split[:, 1]

        self.copy_0.start()

    def add(self, one, two, other):
        @pl.loop(0, self.at.planes)
        def _(i):
            self.mine[one, two, i] = (
                self.mine[one, two, i].astype(F32) + other[i].astype(F32)
            ).astype(BF)

    def begin(self):
        self.copy_0.wait()
        for two in range(2):
            self.add(1 - self.one, two, self.across.at[1 - self.one, two])
        self.copy_1.start()
        for two in range(2):
            self.add(self.one, two, self.across.at[self.one, two])

    def middle(self):
        self.copy_1.wait()
        self.add(self.one, 1 - self.two, self.first.at[1 - self.two])
        self.copy_2.start()
        self.add(self.one, self.two, self.first.at[self.two])

    def last(self):
        self.copy_2.wait()
        self.add(self.one, self.two, self.second)
        for copy in self.copies_3:
            copy.start()

    def close(self):
        for copy in self.copies_3:
            copy.wait()
        total = self.mine[self.one, self.two, self.at.z].astype(F32)
        for step in range(self.at.planes - 1):
            total = total + self.far[step].astype(F32)
        return total


def last_kernel(
    planes,
    micros,
    rows,
    vec_ref,
    keep_ref,
    sums_ref,
    gated_ref,
    gatt_ref,
    mg_ref,
    ggp_ref,
    mr_ref,
    grp_ref,
    mv_ref,
    gv_ref,
    mk_ref,
    gk_ref,
    recept_w,
    value_w,
    key_w,
    x_ref,
    da_ref,
    gmid_ref,
    grad_out,
    sums_out,
    own_output,
    own_gate,
    own_recept,
    own_value,
    own_key,
    left_s,
    right_s,
    w_s,
    x_s,
    da_s,
    total_s,
    g_s,
    sums_s,
    parts,
    across,
    first,
    second,
    far,
    own_s,
    pay_a,
    halo_a,
    flat_s,
    flat_recv,
    load_sem,
    out_sem,
    rs_sem,
    s_sem,
):
    at = Place(planes)
    tokens = micros * rows
    outs = []

    def put(source, target):
        copy = pltpu.make_async_copy(source, target, out_sem.at[len(outs)])
        copy.start()
        outs.append(copy)

    loaded = []

    def load(source, target):
        copy = pltpu.make_async_copy(source, target, load_sem.at[len(loaded)])
        copy.start()
        loaded.append(copy)
        return copy

    sides = (
        (gated_ref, gatt_ref),
        (mg_ref, ggp_ref),
        (mr_ref, grp_ref),
        (mv_ref, gv_ref),
        (mk_ref, gk_ref),
    )
    side_loads = [
        (load(left, left_s.at[index]), load(right, right_s.at[index]))
        for index, (left, right) in enumerate(sides)
    ]
    w_loads = [
        load(source, w_s.at[index]) for index, source in enumerate((recept_w, value_w, key_w))
    ]
    row_loads = [load(x_ref, x_s), load(da_ref, da_s), load(gmid_ref, total_s)]
    greet(
        [at.other, at.side_x, at.side_y]
        + [at.plane(step) for step in range(1, planes)]
        + [at.ahead(1), at.ahead(-1)]
    )
    reduces = [
        ReduceSquare(
            at, parts.at[index], across.at[index], first.at[index], second.at[index],
            far.at[index], rs_sem.at[index], index % 2 == 0,
        )
        for index in range(5)
    ]
    sums_s[...] = jnp.zeros_like(sums_s)
    for index, reduce in enumerate(reduces):
        for copy in side_loads[index]:
            copy.wait()
        reduce.fill(left_s.at[index], right_s.at[index])
        if index:
            reduces[index - 1].begin()
    for index, copy in enumerate(w_loads):
        copy.wait()

        @pl.loop(0, 2)
        def _(i, index=index):
            span = tile(i, tokens // 2)
            g_s[index, span, :] = dot(right_s[2 + index, span, :], w_s[index], NT)

        if index == 0:
            reduces[4].begin()
    for copy in row_loads:
        copy.wait()
    block = 16
    mixes = (vec_ref[6:7, :], vec_ref[5:6, :], vec_ref[4:5, :])
    gain = vec_ref[0:1, :]

    def combine(b):
        span = tile(b, block)
        grads = [g_s[index, span, :] for index in range(3)]
        shift = sum(grad * (1.0 - mix) for grad, mix in zip(grads, mixes))
        return (span, grads, shift * wide(keep_ref[span, :], 1024))

    for m in range(micros):
        pay_a[m : m + 1, :] = combine(m * (rows // block))[2][0:1, :]
    pay_a[micros:, :] = jnp.zeros((8 - micros, 1024), F32)
    halo_copy = remote(pay_a, halo_a, s_sem.at[0, 0], s_sem.at[0, 1], at.ahead(-1))
    halo_copy.start()
    at_last = lax.broadcasted_iota(jnp.int32, (block, 1024), 0) == block - 1
    halo_copy.wait()
    for m in range(micros):

        def back_a(i, after, m=m):
            span, grads, shift = combine((m + 1) * (rows // block) - 1 - i)
            delta = da_s[span, :]
            for index, grad in enumerate(grads):
                sum_rows(sums_s, 2 - index, grad * delta)
            moved = jnp.where(at_last, after, pltpu.roll(shift, block - 1, 0))
            grad = sum(part * mix for part, mix in zip(grads, mixes)) + moved
            unit, inverse = unit_of(x_s[span, :].astype(F32))
            sum_rows(sums_s, 3, grad * unit)
            sum_rows(sums_s, 4, grad)
            total_s[span, :] = total_s[span, :] + norm_back_rows(grad, unit, inverse, gain)
            return shift[0:1, :]

        lax.fori_loop(0, rows // block, back_a, halo_a[m : m + 1, :])
    put(total_s, grad_out)
    flat_s[0] = sums_ref[...]
    for index, row in enumerate((4, 5, 6, 0, 1)):
        flat_s[0, row : row + 1, :] = jnp.sum(sums_s[index], axis=0, keepdims=True)
    for step, device in enumerate((at.other, at.side_x, at.side_y)):
        copy = remote(flat_s.at[step], flat_recv.at[step], s_sem.at[1 + step, 0], s_sem.at[1 + step, 1], device)
        copy.start()
        if step == 0:
            reduces[0].middle()
            reduces[1].middle()
        copy.wait()
        flat_s[step + 1] = flat_s[step] + flat_recv[step]
    flat_copies = [
        remote(
            flat_s.at[3],
            flat_recv.at[2 + step],
            s_sem.at[3 + step, 0],
            s_sem.at[3 + step, 1],
            at.plane(step),
        )
        for step in range(1, planes)
    ]
    for copy in flat_copies:
        copy.start()
    reduces[2].middle()
    reduces[3].middle()
    reduces[0].last()
    reduces[1].last()
    reduces[4].middle()
    reduces[2].last()
    reduces[3].last()
    for copy in flat_copies:
        copy.wait()
    flat_s[0] = flat_s[3] + sum(flat_recv[2 + step] for step in range(1, planes))
    put(flat_s.at[0], sums_out)
    reduces[4].last()
    for index, target in enumerate((own_output, own_gate, own_recept, own_value, own_key)):
        own_s[index] = reduces[index].close()
        put(own_s.at[index], target)
    for copy in outs:
        copy.wait()


def last_call(planes, micros, rows, operands):
    tokens = micros * rows

    def hold(count, kind):
        return pltpu.VMEM((count, tokens, 1024), kind)

    piece = (1024 // (8 * planes), 1024)
    sems = pltpu.SemaphoreType.DMA
    few = pltpu.VMEM((8, 1024), F32)
    return pl.pallas_call(
        functools.partial(last_kernel, planes, micros, rows),
        out_shape=[
            jax.ShapeDtypeStruct((tokens, 1024), F32),
            jax.ShapeDtypeStruct((16, 1024), F32),
        ]
        + [jax.ShapeDtypeStruct(piece, F32)] * 5,
        in_specs=[VM] * 3 + [ANY] * 16,
        out_specs=[ANY] * 7,
        scratch_shapes=[
            hold(5, BF),
            hold(5, BF),
            pltpu.VMEM((3, 1024, 1024), BF),
            pltpu.VMEM((tokens, 1024), BF),
            pltpu.VMEM((tokens, 1024), F32),
            pltpu.VMEM((tokens, 1024), F32),
            hold(3, F32),
            pltpu.VMEM((5, 8, 1024), F32),
            pltpu.VMEM((5, 2, 2, 2, planes) + piece, BF),
            pltpu.VMEM((5, 2, 2, planes) + piece, BF),
            pltpu.VMEM((5, 2, planes) + piece, BF),
            pltpu.VMEM((5, planes) + piece, BF),
            pltpu.VMEM((5, planes - 1) + piece, BF),
            pltpu.VMEM((5,) + piece, F32),
            few,
            few,
            pltpu.VMEM((4, 16, 1024), F32),
            pltpu.VMEM((2 + planes, 16, 1024), F32),
            sems((16,)),
            sems((7,)),
            sems((5, 2 + planes, 2)),
            sems((3 + planes, 2)),
        ],
        compiler_params=pltpu.CompilerParams(
            collective_id=2, has_side_effects=True, vmem_limit_bytes=62 << 20
        ),
        cost_estimate=pl.CostEstimate(
            flops=16 * tokens * 1024 * 1024, bytes_accessed=30 << 20, transcendentals=0
        ),
        name="time_mix_weights",
    )(*operands)


def one_micro(block_in, seg_ids, grad_out, vectors, matrices, hidden_w, return_w):
    (
        gain_one,
        bias_one,
        decay_vec,
        extra_array,
        mix_key,
        mix_value,
        mix_recept,
        gain_two,
        bias_two,
        mix_hidden,
        mix_gate,
    ) = vectors
    key_w, value_w, recept_w, output_w, gate_w = matrices
    row_count = block_in.shape[0]
    model_width = block_in.shape[1]
    seg_float = seg_ids.astype(jnp.float32)
    normed_a, unit_a, inv_a = layer_norm(block_in, gain_one, bias_one)
    prev_row, prev_seg = from_behind((normed_a[-1:], seg_float[-1:]), "mp", 1)
    same_row = jnp.concatenate(
        [
            (seg_float[:1] == prev_seg).astype(jnp.float32),
            (seg_ids[1:] == seg_ids[:-1]).astype(jnp.float32),
        ]
    )
    same_col = same_row[:, None]
    shifted_a = jnp.concatenate([prev_row, normed_a[:-1]], axis=0) * same_col
    delta_a = normed_a - shifted_a
    low_key = reduced_precision(shifted_a + delta_a * mix_key)
    low_value = reduced_precision(shifted_a + delta_a * mix_value)
    low_recept = reduced_precision(shifted_a + delta_a * mix_recept)
    lookup_start = product(low_key, key_w)
    content_start = product(low_value, value_w)
    recept = jax.nn.sigmoid(product(low_recept, recept_w))
    feature_fading = jnp.exp(decay_vec)
    positions = jnp.arange(row_count, dtype=jnp.float32)[:, None]
    rising = jnp.exp(positions * feature_fading)
    falling = jnp.exp(-(positions - 1.0) * feature_fading)
    falling_zero = jnp.exp(-positions * feature_fading)
    raised_lookup = jnp.exp(lookup_start)
    weighted_average = raised_lookup * content_start
    order_rows = jnp.arange(row_count)
    lower_tri = jnp.logical_and(
        seg_ids[:, None] == seg_ids[None, :], order_rows[None, :] < order_rows[:, None]
    ).astype(jnp.float32)
    last_mask = (seg_ids == seg_ids[-1]).astype(jnp.float32)
    first_mask = (seg_ids == seg_ids[0]).astype(jnp.float32) * same_row[0]
    forward_mat = jnp.concatenate([lower_tri, last_mask[None]], axis=0)
    stacked = jnp.concatenate(
        [
            rising * weighted_average,
            rising * raised_lookup,
            positions * rising * weighted_average,
            positions * rising * raised_lookup,
        ],
        axis=1,
    )
    summed = jnp.dot(forward_mat, stacked, precision=HIGH)
    inner_sums = summed[:row_count]
    closing = summed[row_count]
    num_loc = falling * inner_sums[:, :model_width]
    den_loc = falling * inner_sums[:, model_width : 2 * model_width]
    num_der = (
        -(positions - 1.0) * num_loc + falling * inner_sums[:, 2 * model_width : 3 * model_width]
    )
    den_der = -(positions - 1.0) * den_loc + falling * inner_sums[:, 3 * model_width :]
    end_fall = jnp.exp(-(row_count - 1.0) * feature_fading)
    state_num = end_fall * closing[:model_width]
    state_den = end_fall * closing[model_width : 2 * model_width]
    state_num_der = (
        -(row_count - 1.0) * state_num + end_fall * closing[2 * model_width : 3 * model_width]
    )
    state_den_der = -(row_count - 1.0) * state_den + end_fall * closing[3 * model_width :]
    uniform_flag = (seg_ids[-1] == seg_ids[0]).astype(jnp.float32) * same_row[0]
    carry_pass = uniform_flag * jnp.exp(-row_count * feature_fading)
    carry_der = -row_count * carry_pass
    zero_vec = jnp.zeros_like(feature_fading)
    one_vec = jnp.ones_like(feature_fading)
    in_num, in_den, in_num_der, in_den_der, pass_total, pass_der = carried_in(
        (state_num, state_den, state_num_der, state_den_der, carry_pass, carry_der),
        "mp",
        state_join,
        (zero_vec, zero_vec, zero_vec, zero_vec, one_vec, zero_vec),
        False,
    )
    carried = first_mask[:, None] * falling_zero
    dividend = num_loc + carried * in_num
    divisor_portion = den_loc + carried * in_den
    numer_der = num_der + carried * (in_num_der - positions * in_num)
    denom_der = den_der + carried * (in_den_der - positions * in_den)
    extra_summand = jnp.exp(extra_array + lookup_start)
    divisor_complete = divisor_portion + extra_summand
    mixture_result = (dividend + extra_summand * content_start) / divisor_complete
    gated = reduced_precision(recept * mixture_result)
    block_mid = block_in + product(gated, output_w)
    normed_b, unit_b, inv_b = layer_norm(block_mid, gain_two, bias_two)
    prev_mid = from_behind(normed_b[-1:], "mp", 1)
    shifted_b = jnp.concatenate([prev_mid, normed_b[:-1]], axis=0) * same_col
    delta_b = normed_b - shifted_b
    low_hidden = reduced_precision(shifted_b + delta_b * mix_hidden)
    low_gate = reduced_precision(shifted_b + delta_b * mix_gate)
    gate_two = jax.nn.sigmoid(product(low_gate, gate_w))
    hidden_rows = lax.all_gather(low_hidden, "mp", axis=0, tiled=True)
    pre_act = product(hidden_rows, hidden_w)
    rectified = jnp.maximum(pre_act, 0.0)
    squared = reduced_precision(rectified * rectified)
    returned = lax.psum_scatter(
        product(squared, return_w).astype(jnp.bfloat16), "mp", scatter_dimension=0, tiled=True
    ).astype(jnp.float32)
    output = block_mid + gate_two * returned
    grad_ret = reduced_precision(grad_out * gate_two)
    grad_gate_pre = reduced_precision(grad_out * returned * gate_two * (1.0 - gate_two))
    d_gate_w = (low_gate, grad_gate_pre)
    grad_low_gate = product_nt(grad_gate_pre, gate_w)
    grad_rows = lax.all_gather(grad_ret, "mp", axis=0, tiled=True)
    grad_squared = product_nt(grad_rows, return_w)
    d_return = (squared, grad_rows)
    grad_pre = reduced_precision(grad_squared * 2.0 * rectified)
    d_hidden = (hidden_rows, grad_pre)
    grad_low_hidden = lax.psum_scatter(
        product_nt(grad_pre, hidden_w).astype(jnp.bfloat16), "mp", scatter_dimension=0, tiled=True
    ).astype(jnp.float32)
    d_mix_hidden = jnp.sum(grad_low_hidden * delta_b, axis=0)
    d_mix_gate = jnp.sum(grad_low_gate * delta_b, axis=0)
    grad_shift_b = (
        grad_low_hidden * (1.0 - mix_hidden) + grad_low_gate * (1.0 - mix_gate)
    ) * same_col
    from_next_b = from_behind(grad_shift_b[:1], "mp", -1)
    grad_norm_b = (
        grad_low_hidden * mix_hidden
        + grad_low_gate * mix_gate
        + jnp.concatenate([grad_shift_b[1:], from_next_b], axis=0)
    )
    grad_mid_norm, d_gain_two, d_bias_two = norm_back(grad_norm_b, unit_b, inv_b, gain_two)
    grad_mid = grad_out + grad_mid_norm
    grad_att = reduced_precision(grad_mid)
    d_output_w = (gated, grad_att)
    grad_gated = product_nt(grad_att, output_w)
    grad_recept_pre = reduced_precision(grad_gated * mixture_result * recept * (1.0 - recept))
    grad_mixed = grad_gated * recept
    d_recept_w = (low_recept, grad_recept_pre)
    grad_low_recept = product_nt(grad_recept_pre, recept_w)
    dividend_adjoint = grad_mixed / divisor_complete
    divisor_adjoint = -dividend_adjoint * mixture_result
    extra_derivative_part = dividend_adjoint * content_start + divisor_adjoint
    extra_derivative = jnp.sum(extra_derivative_part * extra_summand, axis=0)
    d_rate = jnp.sum(dividend_adjoint * numer_der + divisor_adjoint * denom_der, axis=0)
    backward_mat = jnp.concatenate([lower_tri.T, first_mask[None]], axis=0)
    back_sum = jnp.dot(
        backward_mat,
        jnp.concatenate([falling * dividend_adjoint, falling * divisor_adjoint], axis=1),
        precision=HIGH,
    )
    step_back = jnp.exp(-feature_fading)
    from_num = step_back * back_sum[row_count, :model_width]
    from_den = step_back * back_sum[row_count, model_width:]
    out_num, out_den, out_pass = carried_in(
        (from_num, from_den, carry_pass), "mp", suffix_join, (zero_vec, zero_vec, one_vec), True
    )
    tail_fall = last_mask[:, None] * jnp.exp(-(row_count - 1.0 - positions) * feature_fading)
    cumulative_dividend = rising * back_sum[:row_count, :model_width] + tail_fall * out_num
    running_denominator = rising * back_sum[:row_count, model_width:] + tail_fall * out_den
    value_gradient = reduced_precision(
        dividend_adjoint * extra_summand + cumulative_dividend * raised_lookup
    )
    key_gradient = reduced_precision(
        extra_derivative_part * extra_summand
        + cumulative_dividend * weighted_average
        + running_denominator * raised_lookup
    )
    d_key_w = (low_key, key_gradient)
    d_value_w = (low_value, value_gradient)
    grad_low_key = product_nt(key_gradient, key_w)
    grad_low_value = product_nt(value_gradient, value_w)
    d_mix_key = jnp.sum(grad_low_key * delta_a, axis=0)
    d_mix_value = jnp.sum(grad_low_value * delta_a, axis=0)
    d_mix_recept = jnp.sum(grad_low_recept * delta_a, axis=0)
    grad_shift_a = (
        grad_low_key * (1.0 - mix_key)
        + grad_low_value * (1.0 - mix_value)
        + grad_low_recept * (1.0 - mix_recept)
    ) * same_col
    from_next_a = from_behind(grad_shift_a[:1], "mp", -1)
    grad_norm_a = (
        grad_low_key * mix_key
        + grad_low_value * mix_value
        + grad_low_recept * mix_recept
        + jnp.concatenate([grad_shift_a[1:], from_next_a], axis=0)
    )
    grad_in_norm, d_gain_one, d_bias_one = norm_back(grad_norm_a, unit_a, inv_a, gain_one)
    input_grad = grad_mid + grad_in_norm
    grads = (
        d_gain_one,
        d_bias_one,
        d_rate * feature_fading,
        extra_derivative,
        d_mix_key,
        d_mix_value,
        d_mix_recept,
        d_key_w,
        d_value_w,
        d_recept_w,
        d_output_w,
        d_gain_two,
        d_bias_two,
        d_mix_hidden,
        d_mix_gate,
        d_hidden,
        d_return,
        d_gate_w,
    )
    return (output, input_grad, grads)


def generic_body(
    incoming_signal,
    series_number_table,
    upstream_adjoint,
    first_scaling_factor,
    first_scaling_offset,
    logarithmic_fading_speeds,
    present_step_extra,
    lookup_shift_mixture,
    content_shift_mixture,
    admit_lookup_shift_mixture,
    attention_lookup_matrix,
    attention_content_matrix,
    attention_admit_matrix,
    attention_result_matrix,
    second_scaling_factor,
    second_scaling_offset,
    inner_shift_mixture,
    admit_shift_mixture,
    feedforward_lookup_matrix,
    feedforward_content_matrix,
    feedforward_admit_matrix,
):
    hidden_full, return_full = (feedforward_lookup_matrix, feedforward_content_matrix)
    vectors = tuple(
        (
            start_item.astype(jnp.float32)
            for start_item in (
                first_scaling_factor,
                first_scaling_offset,
                logarithmic_fading_speeds,
                present_step_extra,
                lookup_shift_mixture,
                content_shift_mixture,
                admit_lookup_shift_mixture,
                second_scaling_factor,
                second_scaling_offset,
                inner_shift_mixture,
                admit_shift_mixture,
            )
        )
    )
    matrices = (
        attention_lookup_matrix,
        attention_content_matrix,
        attention_admit_matrix,
        attention_result_matrix,
        feedforward_admit_matrix,
    )
    output, input_grad, grads = jax.vmap(
        lambda rows, ids, adjoint: one_micro(
            rows, ids, adjoint, vectors, matrices, hidden_full, return_full
        )
    )(
        incoming_signal[:, 0].astype(jnp.float32),
        series_number_table[:, 0],
        upstream_adjoint[:, 0].astype(jnp.float32),
    )
    totals = tuple(
        product_tn(*(side.reshape(-1, side.shape[-1]) for side in grad))
        if isinstance(grad, tuple)
        else jnp.sum(grad, axis=0)
        for grad in grads
    )
    square = [index for index in range(18) if totals[index].shape == totals[7].shape]
    lines = [index for index in range(18) if totals[index].ndim == 1]
    wide = lax.psum_scatter(
        jnp.concatenate([reduced_precision(totals[index]) for index in square], axis=1),
        ("dp", "mp"),
        scatter_dimension=0,
        tiled=True,
    ).astype(jnp.float32)
    thin = lax.psum_scatter(
        jnp.stack([totals[index] for index in lines], axis=1),
        ("dp", "mp"),
        scatter_dimension=0,
        tiled=True,
    )
    held = dict(zip(square, jnp.split(wide, len(square), axis=1)))
    held.update({index: thin[:, place] for place, index in enumerate(lines)})
    output, input_grad = (output[:, None], input_grad[:, None])
    owned = tuple(held[index] for index in sorted(held))
    hidden_own, return_own = (
        lax.psum_scatter(
            totals[15].astype(jnp.bfloat16), "dp", scatter_dimension=0, tiled=True
        ).astype(jnp.float32),
        lax.psum_scatter(
            totals[16].astype(jnp.bfloat16), "dp", scatter_dimension=1, tiled=True
        ).astype(jnp.float32),
    )
    return (
        output,
        input_grad,
        owned[0],
        owned[1],
        owned[2],
        owned[3],
        owned[4],
        owned[5],
        owned[6],
        owned[7],
        owned[8],
        owned[9],
        owned[10],
        owned[11],
        owned[12],
        owned[13],
        owned[14],
        hidden_own,
        return_own,
        owned[15],
    )


def kernel_body(
    incoming_signal,
    series_number_table,
    upstream_adjoint,
    first_scaling_factor,
    first_scaling_offset,
    logarithmic_fading_speeds,
    present_step_extra,
    lookup_shift_mixture,
    content_shift_mixture,
    admit_lookup_shift_mixture,
    attention_lookup_matrix,
    attention_content_matrix,
    attention_admit_matrix,
    attention_result_matrix,
    second_scaling_factor,
    second_scaling_offset,
    inner_shift_mixture,
    admit_shift_mixture,
    feedforward_lookup_matrix,
    feedforward_content_matrix,
    feedforward_admit_matrix,
):
    hidden_full, return_full = (feedforward_lookup_matrix, feedforward_content_matrix)
    vectors = tuple(
        (
            start_item.astype(jnp.float32)
            for start_item in (
                first_scaling_factor,
                first_scaling_offset,
                logarithmic_fading_speeds,
                present_step_extra,
                lookup_shift_mixture,
                content_shift_mixture,
                admit_lookup_shift_mixture,
                second_scaling_factor,
                second_scaling_offset,
                inner_shift_mixture,
                admit_shift_mixture,
            )
        )
    )
    matrices = (
        attention_lookup_matrix,
        attention_content_matrix,
        attention_admit_matrix,
        attention_result_matrix,
        feedforward_admit_matrix,
    )
    micros, _, rows, depth = incoming_signal.shape
    planes = lax.axis_size("mp") // 2
    numbers = series_number_table[:, 0].astype(jnp.float32)
    firsts, lasts = (numbers[:, :1], numbers[:, -1:])
    operands = (
        incoming_signal.reshape(micros * rows, depth),
        jnp.pad(incoming_signal[:, 0, -1].astype(jnp.float32), ((0, 8 - micros), (0, 0))),
        jnp.broadcast_to(numbers.reshape(-1, 1), (micros * rows, 128)),
        jnp.pad(numbers, ((0, 8 - micros), (0, 0))),
        jnp.broadcast_to(
            jnp.concatenate([lasts, lasts, firsts, firsts], axis=0), (4 * micros, 128)
        ),
        jnp.pad(jnp.stack(vectors), ((0, 5), (0, 0))),
        upstream_adjoint.reshape(micros * rows, depth),
        *matrices,
        hidden_full,
        return_full,
    )
    (
        keys, values, recept, num, den, mid, gate, mk, mv, mr, gated, mg, delta_a, delta_b,
        keep, segs, mh_all, ret_all, w1_all, w2_all,
    ) = forward_call(planes, micros, rows, operands)
    x, _, segcol, segrow, _, table, adjoint = operands[:7]
    key_w, value_w, recept_w, output_w, gate_w = matrices
    (
        output, grad_mid, grad_gate, grad_att, grad_recept, grad_key, grad_value, sums,
        own_hidden, own_return,
    ) = middle_call(
        planes,
        micros,
        rows,
        (
            table, keep, segs, segcol, segrow, hidden_full, return_full, w1_all, w2_all,
            mh_all, ret_all, mid, gate, adjoint, delta_b, keys, values, recept, num, den,
            gate_w, output_w,
        ),
    )
    input_grad, sums, own_output, own_gate, own_recept, own_value, own_key = last_call(
        planes,
        micros,
        rows,
        (
            table, keep, sums, gated, grad_att, mg, grad_gate, mr, grad_recept, mv, grad_value,
            mk, grad_key, recept_w, value_w, key_w, x, delta_a, grad_mid,
        ),
    )
    span = depth // (lax.axis_size("dp") * lax.axis_size("mp"))
    mine = lax.dynamic_slice_in_dim(
        sums, lax.axis_index(("dp", "mp")) * span, span, axis=1
    )
    line = [mine[index] for index in range(11)]
    shape = incoming_signal.shape
    return (
        output.reshape(shape),
        input_grad.reshape(shape),
        *line[:7],
        own_key,
        own_value,
        own_recept,
        own_output,
        *line[7:],
        own_hidden,
        own_return,
        own_gate,
    )


def solution(mesh):
    placed = (
        P(None, "dp", "mp", None),
        P(None, "dp", "mp"),
        P(None, "dp", "mp", None),
        P(),
        P(),
        P(),
        P(),
        P(),
        P(),
        P(),
        P(),
        P(),
        P(),
        P(),
        P(),
        P(),
        P(),
        P(),
        P(None, "mp"),
        P("mp", None),
        P(),
    )
    fits = mesh.shape["dp"] == 4 and mesh.shape["mp"] == 8
    return jax.shard_map(
        kernel_body if fits else generic_body,
        mesh=mesh,
        in_specs=placed,
        out_specs=(
            P(None, "dp", "mp", None),
            P(None, "dp", "mp", None),
            P(("dp", "mp")),
            P(("dp", "mp")),
            P(("dp", "mp")),
            P(("dp", "mp")),
            P(("dp", "mp")),
            P(("dp", "mp")),
            P(("dp", "mp")),
            P(("dp", "mp"), None),
            P(("dp", "mp"), None),
            P(("dp", "mp"), None),
            P(("dp", "mp"), None),
            P(("dp", "mp")),
            P(("dp", "mp")),
            P(("dp", "mp")),
            P(("dp", "mp")),
            P("dp", "mp"),
            P("mp", "dp"),
            P(("dp", "mp"), None),
        ),
        check_vma=False,
    )
```

```python
import functools

import jax
import jax.numpy as jnp
from jax import lax
from jax.experimental import pallas as pl
from jax.experimental.pallas import tpu as pltpu
from jax.sharding import PartitionSpec as P

EPS = 1e-05
HIGH = lax.Precision.HIGHEST


def from_behind(block, axis, distance):
    devices = range(lax.axis_size(axis))
    route = [(i - distance, i) for i in devices if i - distance in devices]
    return lax.ppermute(block, axis, route)


def carried_in(shard, axis, combine, identity, reverse):
    length, mine = (lax.axis_size(axis), lax.axis_index(axis))
    everything = jax.tree.map(lambda part: lax.all_gather(part, axis), shard)
    start = jax.tree.map(
        lambda part, zero: jnp.broadcast_to(jnp.asarray(zero, part.dtype), part.shape),
        shard,
        identity,
    )

    def step(k, before):
        at = length - 1 - k if reverse else k
        reached = at > mine if reverse else at < mine
        new = combine(before, jax.tree.map(lambda part: part[at], everything))
        return jax.tree.map(lambda a, b: jnp.where(reached, a, b), new, before)

    return lax.fori_loop(0, length, step, start)


def reduced_precision(values):
    return values.astype(jnp.bfloat16)


def product(left, right):
    return jnp.dot(left, right, preferred_element_type=jnp.float32)


def product_tn(left, right):
    return lax.dot_general(
        left, right, (((0,), (0,)), ((), ())), preferred_element_type=jnp.float32
    )


def product_nt(left, right):
    return lax.dot_general(
        left, right, (((1,), (1,)), ((), ())), preferred_element_type=jnp.float32
    )


def layer_norm(values, gain, bias):
    average = jnp.mean(values, axis=-1, keepdims=True)
    centre = values - average
    inverse = lax.rsqrt(jnp.mean(centre * centre, axis=-1, keepdims=True) + EPS)
    unit = centre * inverse
    return (unit * gain + bias, unit, inverse)


def norm_back(grad_in, unit, inverse, gain):
    scaled = grad_in * gain
    grad_values = inverse * (
        scaled
        - jnp.mean(scaled, axis=-1, keepdims=True)
        - unit * jnp.mean(scaled * unit, axis=-1, keepdims=True)
    )
    return (grad_values, jnp.sum(grad_in * unit, axis=0), jnp.sum(grad_in, axis=0))


def state_join(earlier, latter):
    return (
        latter[4] * earlier[0] + latter[0],
        latter[4] * earlier[1] + latter[1],
        latter[4] * earlier[2] + latter[5] * earlier[0] + latter[2],
        latter[4] * earlier[3] + latter[5] * earlier[1] + latter[3],
        earlier[4] * latter[4],
        earlier[5] * latter[4] + earlier[4] * latter[5],
    )


def suffix_join(earlier, latter):
    return (
        latter[0] + latter[2] * earlier[0],
        latter[1] + latter[2] * earlier[1],
        latter[2] * earlier[2],
    )


BF = jnp.bfloat16
F32 = jnp.float32
MESH = pl.DeviceIdType.MESH
NN = (((1,), (0,)), ((), ()))
NT = (((1,), (1,)), ((), ()))
TN = (((0,), (0,)), ((), ()))


def dot(left, right, form=NN):
    return lax.dot_general(left, right, form, preferred_element_type=F32)


def dot_exact_left(left, right):
    high = right.astype(BF)
    rest = (right - high.astype(F32)).astype(BF)
    return dot(left, high) + dot(left, rest)


def wide(lanes, width):
    return jnp.concatenate([lanes] * (width // 128), axis=1)


def tile(index, size):
    return pl.ds(pl.multiple_of(index * size, size), size)


def unit_of(values):
    average = jnp.mean(values, axis=-1, keepdims=True)
    centre = values - average
    inverse = lax.rsqrt(jnp.mean(centre * centre, axis=-1, keepdims=True) + EPS)
    return (centre * inverse, inverse)


def remote(source, target, send, receive, device):
    return pltpu.make_async_remote_copy(
        src_ref=source,
        dst_ref=target,
        send_sem=send,
        recv_sem=receive,
        device_id=device,
        device_id_type=MESH,
    )


class Place:
    def __init__(self, planes):
        self.planes = planes
        self.dp, self.mp = (lax.axis_index("dp"), lax.axis_index("mp"))
        self.z = lax.div(self.mp, 2)
        self.core = lax.rem(self.mp, 2)
        self.count = 2 * planes
        self.other = (self.dp, self.mp + 1 - 2 * self.core)
        self.side_x = (self.dp + 1 - 2 * lax.rem(self.dp, 2), self.mp)
        self.side_y = (lax.rem(self.dp + 2, 4), self.mp)

    def ahead(self, steps):
        return (self.dp, lax.rem(self.mp + steps + self.count, self.count))

    def plane(self, steps):
        return (self.dp, lax.rem(self.z + steps + self.planes, self.planes) * 2 + self.core)


def greet(devices):
    barrier = pltpu.get_barrier_semaphore()
    for device in devices:
        pl.semaphore_signal(barrier, inc=1, device_id=device, device_id_type=MESH)
    pl.semaphore_wait(barrier, len(devices))


def feed_rows(w1, w2, mh2, gr2, sq_s, gp_s, ret_acc, gmh_acc, fresh):
    def rows_of(i):
        span = tile(i, 256)
        pre = dot(mh2[span, :], w1[...])
        rectified = jnp.maximum(pre, 0.0)
        squared = (rectified * rectified).astype(BF)
        sq_s[span, :] = squared
        grad_squared = dot(gr2[span, :], w2[...], NT)
        grad_pre = (grad_squared * 2.0 * rectified).astype(BF)
        gp_s[span, :] = grad_pre
        if fresh:
            ret_acc[span, :] = dot(squared, w2[...])
            gmh_acc[span, :] = dot(grad_pre, w1[...], NT)
        else:
            ret_acc[span, :] += dot(squared, w2[...])
            gmh_acc[span, :] += dot(grad_pre, w1[...], NT)

    return rows_of


def feed_grads(mh2, gr2, sq_s, gp_s, parts1, parts2):
    @pl.loop(0, 4)
    def _(q):
        line, side = (lax.div(q, 2), lax.rem(q, 2))
        cols = tile(q, 256)
        parts1[side, line] = dot(mh2[:, cols], gp_s[...], TN).astype(BF)
        parts2[line, side] = dot(gr2[:, cols], sq_s[...], TN).astype(BF)


def forward_kernel(
    planes,
    micros,
    rows,
    x_ref,
    table_ref,
    adj_ref,
    *refs,
):
    (
    lines, refs) = (refs[:11], refs[11:])
    (
    key_w,
    value_w,
    recept_w,
    output_w,
    gate_w,
    w1_ref,
    w2_ref,
    k_out,
    v_out,
    r_out,
    num_out,
    den_out,
    mid_out,
    gate_out,
    mk_out,
    mv_out,
    mr_out,
    gated_out,
    mg_out,
    da_out,
    db_out,
    keep_out,
    segs_out,
    vec_out,
    segcol_out,
    segrow_out,
    mh_all,
    ret_all,
    w1_all,
    w2_all,
    ret_acc_out,
    gmh_acc_out,
    parts1_out,
    parts2_out,
    wk,
    wv,
    wr,
    wo,
    wg,
    k_s,
    v_s,
    r_s,
    num_s,
    den_s,
    mid_s,
    gate_s,
    xb_s,
    da_s,
    mk_s,
    mv_s,
    mr_s,
    gated_s,
    mg_s,
    keep_s,
    segcol_ref,
    segrow_ref,
    segpay_ref,
    last_ref,
    mask_s,
    halo_a,
    near_a,
    pay_b,
    halo_b,
    segs_s,
    state_own,
    state_other,
    state_chip,
    state_in,
    carry_s,
    w_sem,
    out_sem,
    small_sem,
    z_sem,
    s_sem,
    vec_ref,
    mh2,
    gr2,
    sq_s,
    gp_s,
    ret_acc,
    gmh_acc,
    parts1,
    parts2,
    ff_sem,
    ) = refs
    at = Place(planes)
    dp, mp, z, core = (at.dp, at.mp, at.z, at.core)
    tokens = micros * rows
    peers = [at.ahead(step) for step in range(1, at.count)]
    greet(peers + [at.side_x, at.side_y])

    for index, line in enumerate(lines):
        vec_ref[index : index + 1, :] = line[...].astype(F32).reshape(1, 1024)
    vec_ref[11:16, :] = jnp.zeros((5, 1024), F32)

    numbers = table_ref[...].astype(F32)
    rest = jnp.zeros((8 - micros, rows), F32)
    segrow_ref[...] = jnp.concatenate([numbers, rest], axis=0)
    columns = segrow_ref[...].T
    ends = [jnp.broadcast_to(numbers[:, at_end], (micros, 128)) for at_end in (slice(rows - 1, rows), slice(0, 1))]
    segpay_ref[...] = jnp.concatenate([ends[0], ends[0], ends[1], ends[1]], axis=0)
    last_ref[...] = jnp.zeros((8, 1024), F32)
    for m in range(micros):
        segcol_ref[m * rows : (m + 1) * rows, :] = jnp.broadcast_to(columns[:, m : m + 1], (rows, 128))
        last_ref[m : m + 1, :] = x_ref[(m + 1) * rows - 16 : (m + 1) * rows, :].astype(F32)[15:16]

    quarter1, quarter2 = (w1_ref.shape[0] // 4, w2_ref.shape[0] // 4)
    q1, q2 = (tile(dp, quarter1), tile(dp, quarter2))
    z_copies = {}
    for step in (1, planes - 1):
        to = at.plane(-step)
        z_copies[step - 1] = (
            remote(w1_ref.at[q1], w1_all.at[step - 1, q1], z_sem.at[step - 1, 0, 0], z_sem.at[step - 1, 0, 1], to),
            remote(w2_ref.at[q2], w2_all.at[step - 1, q2], z_sem.at[step - 1, 1, 0], z_sem.at[step - 1, 1, 1], to),
        )
    half1 = tile(lax.div(dp, 2), 2 * quarter1)
    far2 = tile(lax.rem(dp + 2, 4), quarter2)
    back = at.plane(-1)
    onward_1 = remote(w1_all.at[0, half1], w1_all.at[1, half1], z_sem.at[1, 0, 0], z_sem.at[1, 0, 1], back)
    onward_2 = (
        remote(w2_all.at[0, q2], w2_all.at[1, q2], z_sem.at[1, 1, 0], z_sem.at[1, 1, 1], back),
        remote(w2_all.at[0, far2], w2_all.at[1, far2], z_sem.at[1, 2, 0], z_sem.at[1, 2, 1], back),
    )

    halo_copy = remote(last_ref, halo_a, small_sem.at[0, 0], small_sem.at[0, 1], at.ahead(1))
    halo_copy.start()
    seg_copies = [
        remote(segpay_ref, segs_s.at[mp], small_sem.at[1 + step, 0], small_sem.at[1 + step, 1], device)
        for step, device in enumerate(peers)
    ]
    for copy in seg_copies:
        copy.start()
    segs_s[mp] = segpay_ref[...]
    loads = []
    for index, (source, target) in enumerate(
        ((key_w, wk), (value_w, wv), (recept_w, wr), (output_w, wo), (gate_w, wg))
    ):
        loads.append(pltpu.make_async_copy(source, target, w_sem.at[index]))
        loads[-1].start()
    for copy in z_copies[0] + z_copies[2]:
        copy.start()
    halo_copy.wait()
    for copy in seg_copies:
        copy.wait()

    before = lax.rem(mp + at.count - 1, at.count)
    has_before = mp > 0
    first_row = lax.broadcasted_iota(jnp.int32, (rows, 128), 0) == 0
    row_at = lax.broadcasted_iota(jnp.int32, (rows, rows), 0)
    col_at = lax.broadcasted_iota(jnp.int32, (rows, rows), 1)
    for m in range(micros):
        here = segcol_ref[m * rows : (m + 1) * rows, :]
        behind = jnp.where(
            first_row, segs_s[before, m : m + 1, :], pltpu.roll(here, 1, 0)
        )
        same = jnp.logical_and(
            here == behind, jnp.logical_or(jnp.logical_not(first_row), has_before)
        )
        keep_s[m * rows : (m + 1) * rows, :] = same.astype(F32)
        mask_s[m] = jnp.logical_and(
            here == segrow_ref[m : m + 1, :], col_at < row_at
        ).astype(F32).astype(BF)

    block = 16
    at_first = lax.broadcasted_iota(jnp.int32, (block, 1024), 0) == 0
    gain, bias = (vec_ref[0:1, :], vec_ref[1:2, :])
    near_a[...] = unit_of(halo_a[...])[0] * gain + bias
    for m in range(micros):

        def mix_a(b, prev, m=m):
            span = tile(m * (rows // block) + b, block)
            normed = unit_of(x_ref[span, :].astype(F32))[0] * gain + bias
            shifted = jnp.where(at_first, prev, pltpu.roll(normed, 1, 0)) * wide(
                keep_s[span, :], 1024
            )
            delta = normed - shifted
            da_s[span, :] = delta
            mk_s[span, :] = (shifted + delta * vec_ref[4:5, :]).astype(BF)
            mv_s[span, :] = (shifted + delta * vec_ref[5:6, :]).astype(BF)
            mr_s[span, :] = (shifted + delta * vec_ref[6:7, :]).astype(BF)
            return normed[block - 1 : block, :]

        lax.fori_loop(0, rows // block, mix_a, near_a[m : m + 1, :])

    outs = []

    def put(source, target):
        copy = pltpu.make_async_copy(source, target, out_sem.at[len(outs)])
        copy.start()
        outs.append(copy)

    put(da_s, da_out)
    put(keep_s, keep_out)
    put(segs_s, segs_out)
    put(segcol_ref, segcol_out)
    put(vec_ref, vec_out)
    put(segrow_ref, segrow_out)
    put(mk_s, mk_out)
    put(mv_s, mv_out)
    put(mr_s, mr_out)

    loads[0].wait()
    loads[1].wait()
    width = 256
    place = lax.broadcasted_iota(jnp.int32, (rows, width), 0).astype(F32)

    @pl.loop(0, 1024 // width)
    def _(i):
        cols = tile(i, width)
        rate = jnp.exp(vec_ref[2:3, cols])
        rising = jnp.exp(place * rate)
        falling = jnp.exp((1.0 - place) * rate)
        step_back = jnp.exp(-rate)
        keys = dot(mk_s[...], wk[:, cols])
        values = dot(mv_s[...], wv[:, cols])
        for m in range(micros):
            span = slice(m * rows, (m + 1) * rows)
            key, value = (keys[span], values[span])
            raised = jnp.exp(key)
            weighted = raised * value
            num = falling * dot_exact_left(mask_s[m], rising * weighted)
            den = falling * dot_exact_left(mask_s[m], rising * raised)
            k_s[span, cols] = key
            v_s[span, cols] = value
            num_s[span, cols] = num
            den_s[span, cols] = den
            state_own[m : m + 1, cols] = step_back * num[rows - 1 :] + weighted[rows - 1 :]
            state_own[micros + m : micros + m + 1, cols] = (
                step_back * den[rows - 1 :] + raised[rows - 1 :]
            )

    put(k_s, k_out)
    put(v_s, v_out)
    core_copy = remote(state_own, state_other, s_sem.at[0, 0], s_sem.at[0, 1], at.other)
    core_copy.start()
    for copy in z_copies[0]:
        copy.wait()
    xy_copies = []

    def along(step):
        group = []
        own1, own2 = (w1_all.at[step, q1], w2_all.at[step, q2])
        return (
            remote(own1, own1, z_sem.at[step, 2, 0], z_sem.at[step, 2, 1], at.side_x),
            remote(own2, own2, z_sem.at[step, 3, 0], z_sem.at[step, 3, 1], at.side_y),
        )

    def across(step):
        both1 = w1_all.at[step, half1]
        own2 = w2_all.at[step, q2]
        next2 = w2_all.at[step, far2]
        return (
            remote(both1, both1, z_sem.at[step, 4, 0], z_sem.at[step, 4, 1], at.side_y),
            remote(own2, own2, z_sem.at[step, 5, 0], z_sem.at[step, 5, 1], at.side_x),
            remote(next2, next2, z_sem.at[step, 6, 0], z_sem.at[step, 6, 1], at.side_x),
        )

    def start(group):
        for copy in group:
            copy.start()

    def finish(group):
        for copy in group:
            copy.wait()

    along_0, along_2 = (along(0), along(2))
    across_0, across_1, across_2 = (across(0), across(1), across(2))
    start(along_0)
    loads[2].wait()

    @pl.loop(0, 2)
    def _(i):
        span = tile(i, tokens // 2)
        r_s[span, :] = jax.nn.sigmoid(dot(mr_s[span, :], wr[...]))

    put(r_s, r_out)

    pair = lax.div(mp, 2) * 2
    decay_all = jnp.exp(-float(rows) * jnp.exp(vec_ref[2:3, :]))
    core_copy.wait()

    def last_of(device):
        return wide(segs_s[lax.rem(device + at.count, at.count), 0 : 2 * micros, :], 1024)

    even = jnp.where(core == 0, state_own[...], state_other[...])
    odd = jnp.where(core == 0, state_other[...], state_own[...])
    state_chip[...] = odd + jnp.where(last_of(pair) == last_of(pair + 1), decay_all * even, 0.0)
    chip_copies = [
        remote(state_chip, state_in.at[step - 1], s_sem.at[step, 0], s_sem.at[step, 1], at.plane(step))
        for step in range(1, planes)
    ]
    start(chip_copies)
    finish(along_0)
    start(across_0)
    finish(chip_copies)
    onward_1.start()
    total = jnp.zeros_like(state_chip[...])
    power = jnp.ones_like(decay_all)
    for step in range(1, planes):
        fits = jnp.logical_and(
            last_of(pair - 2 * step + 1) == last_of(pair - 1), z >= step
        )
        total = total + jnp.where(fits, power * state_in[step - 1], 0.0)
        power = power * decay_all * decay_all
    joined = state_other[...] + jnp.where(last_of(pair) == last_of(pair - 1), decay_all * total, 0.0)
    carry_s[...] = jnp.where(core == 0, total, joined)

    @pl.loop(0, 1024 // width)
    def _(i):
        cols = tile(i, width)
        rate = jnp.exp(vec_ref[2:3, cols])
        falling = jnp.exp(-place * rate)
        extra = vec_ref[3:4, cols]
        for m in range(micros):
            span = slice(m * rows, (m + 1) * rows)
            fits = jnp.logical_and(
                segcol_ref[span, :] == segs_s[before, m : m + 1, :], has_before
            ).astype(F32)
            carried = wide(fits, width) * falling
            num = num_s[span, cols] + carried * carry_s[m : m + 1, cols]
            den = den_s[span, cols] + carried * carry_s[micros + m : micros + m + 1, cols]
            bonus = jnp.exp(extra + k_s[span, cols])
            mixed = (num + bonus * v_s[span, cols]) / (den + bonus)
            num_s[span, cols] = num
            den_s[span, cols] = den
            gated_s[span, cols] = (r_s[span, cols] * mixed).astype(BF)

    finish(z_copies[2])
    start(along_2)
    put(num_s, num_out)
    put(den_s, den_out)
    put(gated_s, gated_out)
    loads[3].wait()

    @pl.loop(0, 2)
    def _(i):
        span = tile(i, tokens // 2)
        mid_s[span, :] = x_ref[span, :].astype(F32) + dot(gated_s[span, :], wo[...])

    put(mid_s, mid_out)
    gain_b, bias_b = (vec_ref[7:8, :], vec_ref[8:9, :])

    def norm_b(b):
        span = tile(b, block)
        xb_s[span, :] = unit_of(mid_s[span, :])[0] * gain_b + bias_b

    for m in range(micros):
        norm_b((m + 1) * (rows // block) - 1)
        pay_b[m : m + 1, :] = xb_s[(m + 1) * rows - 1 : (m + 1) * rows, :]
    pay_b[micros:, :] = jnp.zeros((8 - micros, 1024), F32)
    halo_b_copy = remote(pay_b, halo_b, s_sem.at[planes, 0], s_sem.at[planes, 1], at.ahead(1))
    halo_b_copy.start()
    for m in range(micros):

        @pl.loop(m * (rows // block), (m + 1) * (rows // block) - 1)
        def _(b):
            norm_b(b)

    halo_b_copy.wait()
    start(onward_2)
    for m in range(micros):

        def mix_b(b, prev, m=m):
            span = tile(m * (rows // block) + b, block)
            normed = xb_s[span, :]
            shifted = jnp.where(at_first, prev, pltpu.roll(normed, 1, 0)) * wide(
                keep_s[span, :], 1024
            )
            delta = normed - shifted
            xb_s[span, :] = delta
            mh2[span, :] = (shifted + delta * vec_ref[9:10, :]).astype(BF)
            mg_s[span, :] = (shifted + delta * vec_ref[10:11, :]).astype(BF)
            return normed[block - 1 : block, :]

        lax.fori_loop(0, rows // block, mix_b, halo_b[m : m + 1, :])

    own, far = (slice(0, tokens), slice(tokens, 2 * tokens))
    mh_copy = remote(
        mh2.at[own], mh2.at[far], s_sem.at[planes + 1, 0], s_sem.at[planes + 1, 1], at.other
    )
    mh_copy.start()
    put(mg_s, mg_out)
    put(xb_s, db_out)
    loads[4].wait()

    @pl.loop(0, 2)
    def _(i):
        span = tile(i, tokens // 2)
        gate = jax.nn.sigmoid(dot(mg_s[span, :], wg[...]))
        gate_s[span, :] = gate
        gr2[span, :] = (adj_ref[span, :].astype(F32) * gate).astype(BF)

    ret_copy = remote(
        gr2.at[own], gr2.at[far], s_sem.at[planes + 2, 0], s_sem.at[planes + 2, 1], at.other
    )
    ret_copy.start()
    put(gate_s, gate_out)
    finish(along_2)
    start(across_2)
    hidden = w1_ref.shape[1]
    w1_own, w2_own = (wk.at[:, 0:hidden], wv.at[0:hidden])
    w1_next, w2_next = (wk.at[:, hidden : 2 * hidden], wv.at[hidden : 2 * hidden])
    ff_loads = [
        pltpu.make_async_copy(source, target, ff_sem.at[index])
        for index, (source, target) in enumerate(
            ((w1_ref, w1_own), (w2_ref, w2_own), (w1_all.at[0], w1_next), (w2_all.at[0], w2_next))
        )
    ]
    ff_loads[0].start()
    ff_loads[1].start()
    ff_loads[0].wait()
    ff_loads[1].wait()
    half = tokens // 256
    step = feed_rows(w1_own, w2_own, mh2, gr2, sq_s, gp_s, ret_acc, gmh_acc, True)
    pl.loop(0, half)(step)
    mh_copy.wait()
    ret_copy.wait()
    put(mh2, mh_all)
    put(gr2, ret_all)
    finish(across_0)
    ff_loads[2].start()
    ff_loads[3].start()
    pl.loop(half, 2 * half)(step)
    finish(onward_2)
    onward_1.wait()
    start(across_1)
    feed_grads(mh2, gr2, sq_s, gp_s, parts1.at[0], parts2.at[0])
    put(parts1.at[0], parts1_out.at[0])
    put(parts2.at[0], parts2_out.at[0])
    ff_loads[2].wait()
    ff_loads[3].wait()
    pl.loop(0, 2 * half)(
        feed_rows(w1_next, w2_next, mh2, gr2, sq_s, gp_s, ret_acc, gmh_acc, False)
    )
    put(ret_acc, ret_acc_out)
    put(gmh_acc, gmh_acc_out)
    feed_grads(mh2, gr2, sq_s, gp_s, parts1.at[1], parts2.at[1])
    put(parts1.at[1], parts1_out.at[1])
    put(parts2.at[1], parts2_out.at[1])
    finish(across_2)
    finish(across_1)
    for copy in outs:
        copy.wait()


ANY = pl.BlockSpec(memory_space=pl.ANY)
VM = pl.BlockSpec(memory_space=pltpu.VMEM)


def forward_call(planes, micros, rows, operands):
    tokens = micros * rows
    hidden = operands[-1].shape[0]

    def big(kind):
        return jax.ShapeDtypeStruct((tokens, 1024), kind)

    def hold(kind):
        return pltpu.VMEM((tokens, 1024), kind)

    square = pltpu.VMEM((1024, 1024), BF)
    few = pltpu.VMEM((8, 1024), F32)
    pair = pltpu.SemaphoreType.DMA
    return pl.pallas_call(
        functools.partial(forward_kernel, planes, micros, rows),
        out_shape=[big(F32)] * 7
        + [big(BF)] * 5
        + [big(F32)] * 2
        + [
            jax.ShapeDtypeStruct((tokens, 128), F32),
            jax.ShapeDtypeStruct((2 * planes, 16, 128), F32),
            jax.ShapeDtypeStruct((16, 1024), F32),
            jax.ShapeDtypeStruct((tokens, 128), F32),
            jax.ShapeDtypeStruct((8, rows), F32),
        ]
        + [jax.ShapeDtypeStruct((2 * tokens, 1024), BF)] * 2
        + [
            jax.ShapeDtypeStruct((planes - 1, 1024, hidden), BF),
            jax.ShapeDtypeStruct((planes - 1, hidden, 1024), BF),
        ]
        + [jax.ShapeDtypeStruct((2 * tokens, 1024), F32)] * 2
        + [jax.ShapeDtypeStruct((2, 2, 2, 256, hidden), BF)] * 2,
        in_specs=[VM] * 14 + [ANY] * 7,
        out_specs=[ANY] * 27,
        scratch_shapes=[square] * 5
        + [hold(F32)] * 9
        + [hold(BF)] * 5
        + [
            pltpu.VMEM((tokens, 128), F32),
            pltpu.VMEM((tokens, 128), F32),
            pltpu.VMEM((8, rows), F32),
            pltpu.VMEM((4 * micros, 128), F32),
            few,
            pltpu.VMEM((micros, rows, rows), BF),
            few,
            few,
            few,
            few,
            pltpu.VMEM((2 * planes, 16, 128), F32),
            few,
            few,
            few,
            pltpu.VMEM((planes - 1, 8, 1024), F32),
            few,
            pair((5,)),
            pair((29,)),
            pair((2 * planes + 1, 2)),
            pair((planes - 1, 7, 2)),
            pair((planes + 3, 2)),
            pltpu.VMEM((16, 1024), F32),
            pltpu.VMEM((2 * tokens, 1024), BF),
            pltpu.VMEM((2 * tokens, 1024), BF),
            pltpu.VMEM((2 * tokens, hidden), BF),
            pltpu.VMEM((2 * tokens, hidden), BF),
            pltpu.VMEM((2 * tokens, 1024), F32),
            pltpu.VMEM((2 * tokens, 1024), F32),
            pltpu.VMEM((2, 2, 2, 256, hidden), BF),
            pltpu.VMEM((2, 2, 2, 256, hidden), BF),
            pair((4,)),
        ],
        compiler_params=pltpu.CompilerParams(
            collective_id=0, has_side_effects=True, vmem_limit_bytes=62 << 20
        ),
        cost_estimate=pl.CostEstimate(
            flops=36 * tokens * 1024 * 1024, bytes_accessed=40 << 20, transcendentals=6 * tokens * 1024
        ),
        name="time_mix_forward",
    )(*operands)


class Reduce:
    def __init__(self, at, parts, first, second, far, sems, slot, x_first):
        self.at, self.parts, self.slot = (at, parts, slot if far is not None else 0)
        side = lax.rem(at.dp, 2)
        line = lax.div(at.dp, 2)
        self.one, self.two = (side, line) if x_first else (line, side)
        near, next_to = (at.side_x, at.side_y) if x_first else (at.side_y, at.side_x)
        self.first, self.second, self.far = (first, second, far)
        self.copy_1 = remote(parts.at[1 - self.one], first, sems.at[0, 0], sems.at[0, 1], near)
        self.copy_2 = remote(
            parts.at[self.one, 1 - self.two], second, sems.at[1, 0], sems.at[1, 1], next_to
        )
        if self.slot:
            self.copy_3 = remote(
                parts.at[self.one, self.two], far, sems.at[2, 0], sems.at[2, 1], at.plane(slot)
            )

    def start(self):
        self.copy_1.start()

    def add(self, half, other):
        mine = self.parts.at[self.one, half]

        @pl.loop(0, mine.shape[0] // 64)
        def _(i):
            span = tile(i, 64)
            mine[span, :] = (mine[span, :].astype(F32) + other[span, :].astype(F32)).astype(BF)

    def middle(self):
        self.copy_1.wait()
        self.add(1 - self.two, self.first.at[1 - self.two])
        self.copy_2.start()
        self.add(self.two, self.first.at[self.two])

    def last(self):
        self.copy_2.wait()
        self.add(self.two, self.second)
        if self.slot:
            self.copy_3.start()

    def close(self):
        if self.slot:
            self.copy_3.wait()


def sum_rows(into, index, values):
    total = values[0:8]
    for start in range(8, values.shape[0], 8):
        total = total + values[start : start + 8]
    into[index] = into[index] + total


def norm_back_rows(grad, unit, inverse, gain):
    scaled = grad * gain
    return inverse * (
        scaled
        - jnp.mean(scaled, axis=-1, keepdims=True)
        - unit * jnp.mean(scaled * unit, axis=-1, keepdims=True)
    )


def middle_kernel(
    planes,
    micros,
    rows,
    vec_ref,
    keep_ref,
    segs_ref,
    segcol_ref,
    segrow_ref,
    w1_all,
    w2_all,
    mh_all,
    ret_all,
    ret_acc_ref,
    gmh_acc_ref,
    parts1_ref,
    parts2_ref,
    mid_ref,
    gate_ref,
    adj_ref,
    db_ref,
    k_ref,
    v_ref,
    r_ref,
    num_ref,
    den_ref,
    gate_w,
    output_w,
    out_ref,
    gmid_out,
    ggp_out,
    gatt_out,
    grp_out,
    gk_out,
    gv_out,
    sums_out,
    own1_out,
    own2_out,
    rest1_out,
    rest2_out,
    parts1,
    parts2,
    first1,
    first2,
    second1,
    second2,
    far1,
    far2,
    ret_acc,
    gmh_acc,
    ret_send,
    gmh_send,
    ret_recv,
    gmh_recv,
    mid_s,
    gate_s,
    adj_s,
    db_s,
    sums_s,
    sums_flat,
    mask_s,
    pay_b,
    halo_b,
    state_own,
    state_other,
    state_chip,
    state_in,
    carry_s,
    own1_s,
    own2_s,
    load_sem,
    out_sem,
    rs_sem,
    s_sem,
):
    at = Place(planes)
    dp, mp, z, core = (at.dp, at.mp, at.z, at.core)
    tokens = micros * rows
    hidden = w1_all.shape[2]
    outs = []

    def put(source, target):
        copy = pltpu.make_async_copy(source, target, out_sem.at[len(outs)])
        copy.start()
        outs.append(copy)

    loaded = []

    def load(source, target):
        copy = pltpu.make_async_copy(source, target, load_sem.at[len(loaded)])
        copy.start()
        loaded.append(copy)
        return copy

    greet(
        [at.other, at.side_x, at.side_y]
        + [at.plane(step) for step in range(1, planes)]
        + [at.ahead(1), at.ahead(-1)]
    )
    reduces = []
    for slot in range(planes):
        reduces.append(
            (
                Reduce(at, parts1.at[slot], first1.at[slot], second1.at[slot],
                       far1 if slot == 1 else None, rs_sem.at[slot, 0], slot, True),
                Reduce(at, parts2.at[slot], first2.at[slot], second2.at[slot],
                       far2 if slot == 1 else None, rs_sem.at[slot, 1], slot, False),
            )
        )
    ret_copy = remote(ret_send, ret_recv, s_sem.at[0, 0], s_sem.at[0, 1], at.other)
    gmh_copy = remote(gmh_send, gmh_recv, s_sem.at[1, 0], s_sem.at[1, 1], at.other)

    part_loads = []
    for slot in (1, 0):
        part_loads.append(
            (load(parts1_ref.at[slot], parts1.at[slot]), load(parts2_ref.at[slot], parts2.at[slot]))
        )
    acc_loads = [load(ret_acc_ref, ret_acc), load(gmh_acc_ref, gmh_acc)]

    def begin(slot):
        for reduce in reduces[slot]:
            reduce.start()

    def middle(slot):
        for reduce in reduces[slot]:
            reduce.middle()

    def last(slot):
        for reduce in reduces[slot]:
            reduce.last()

    def feed_forward(w1, w2, mh2, gr2, sq_s, gp_s):
        mh_load = [load(mh_all, mh2), load(ret_all, gr2)]
        order = (planes - 1, planes - 2)
        slots = [
            (load(w1_all.at[slot - 1], w1.at[index]), load(w2_all.at[slot - 1], w2.at[index]))
            for index, slot in enumerate(order)
        ]
        late = [load(mid_ref, mid_s), load(gate_ref, gate_s), load(adj_ref, adj_s), load(db_ref, db_s)]
        for index, slot in enumerate((1, 0)):
            for copy in part_loads[index]:
                copy.wait()
            begin(slot)
        for copy in mh_load + acc_loads:
            copy.wait()
        half = tokens // 256
        for index, slot in enumerate(order):
            for copy in slots[index]:
                copy.wait()
            step = feed_rows(
                w1.at[index], w2.at[index], mh2, gr2, sq_s, gp_s, ret_acc, gmh_acc, False
            )
            pl.loop(half, 2 * half)(step)
            if index == 1:

                @pl.loop(0, tokens // 64)
                def _(i):
                    span = tile(i, 64)
                    far_span = tile(tokens // 64 + i, 64)
                    ret_send[span, :] = ret_acc[far_span, :].astype(BF)
                    gmh_send[span, :] = gmh_acc[far_span, :].astype(BF)

                ret_copy.start()
                gmh_copy.start()
            pl.loop(0, half)(step)
            feed_grads(mh2, gr2, sq_s, gp_s, parts1.at[slot], parts2.at[slot])
            if index == 0:
                middle(1)
            begin(slot)
        for copy in late:
            copy.wait()

    pl.run_scoped(
        feed_forward,
        pltpu.VMEM((2, 1024, hidden), BF),
        pltpu.VMEM((2, hidden, 1024), BF),
        pltpu.VMEM((2 * tokens, 1024), BF),
        pltpu.VMEM((2 * tokens, 1024), BF),
        pltpu.VMEM((2 * tokens, hidden), BF),
        pltpu.VMEM((2 * tokens, hidden), BF),
    )
    own = slice(0, tokens)
    far = slice(tokens, 2 * tokens)
    block = 16

    def attention(k_s, v_s, r_s, num_s, den_s, wg, wo, ggp_s, gatt_s, grp_s, gk_s, gv_s):
        need_wg = load(gate_w, wg)
        need_wo = load(output_w, wo)
        need = [
            load(k_ref, k_s),
            load(v_ref, v_s),
            load(r_ref, r_s),
            load(num_ref, num_s),
            load(den_ref, den_s),
        ]
        sums_s[...] = jnp.zeros_like(sums_s)
        row_at = lax.broadcasted_iota(jnp.int32, (rows, rows), 0)
        col_at = lax.broadcasted_iota(jnp.int32, (rows, rows), 1)
        for m in range(micros):
            mask_s[m] = jnp.logical_and(
                segcol_ref[m * rows : (m + 1) * rows, :] == segrow_ref[m : m + 1, :],
                col_at > row_at,
            ).astype(F32).astype(BF)
        ret_copy.wait()

        @pl.loop(0, tokens // block)
        def _(b):
            span = tile(b, block)
            returned = ret_acc[span, :] + ret_recv[span, :].astype(F32)
            gate = gate_s[span, :]
            product_in = gate * returned
            ret_acc[span, :] = mid_s[span, :] + product_in
            ggp_s[span, :] = (adj_s[span, :].astype(F32) * product_in * (1.0 - gate)).astype(BF)

        put(ret_acc.at[own], out_ref)
        put(ggp_s, ggp_out)
        need_wg.wait()

        @pl.loop(0, 2)
        def _(i):
            span = tile(i, tokens // 2)
            ret_acc[tile(2 + i, tokens // 2), :] = dot(ggp_s[span, :], wg[...], NT)

        middle(0)
        gmg = ret_acc.at[far]
        gmh_copy.wait()
        mix_h, mix_g = (vec_ref[9:10, :], vec_ref[10:11, :])
        gain = vec_ref[7:8, :]

        def combine(b):
            span = tile(b, block)
            grad_h = gmh_acc[span, :] + gmh_recv[span, :].astype(F32)
            grad_g = gmg[span, :]
            shift = (grad_h * (1.0 - mix_h) + grad_g * (1.0 - mix_g)) * wide(keep_ref[span, :], 1024)
            return (span, grad_h, grad_g, shift)

        for m in range(micros):
            pay_b[m : m + 1, :] = combine(m * (rows // block))[3][0:1, :]
        pay_b[micros:, :] = jnp.zeros((8 - micros, 1024), F32)
        halo_copy = remote(pay_b, halo_b, s_sem.at[2, 0], s_sem.at[2, 1], at.ahead(-1))
        halo_copy.start()
        at_last = lax.broadcasted_iota(jnp.int32, (block, 1024), 0) == block - 1
        halo_copy.wait()
        last(1)
        for m in range(micros):

            def back_b(i, after, m=m):
                span, grad_h, grad_g, shift = combine((m + 1) * (rows // block) - 1 - i)
                delta = db_s[span, :]
                sum_rows(sums_s, 9, grad_h * delta)
                sum_rows(sums_s, 10, grad_g * delta)
                moved = jnp.where(at_last, after, pltpu.roll(shift, block - 1, 0))
                grad = grad_h * mix_h + grad_g * mix_g + moved
                unit, inverse = unit_of(mid_s[span, :])
                sum_rows(sums_s, 7, grad * unit)
                sum_rows(sums_s, 8, grad)
                total = adj_s[span, :].astype(F32) + norm_back_rows(grad, unit, inverse, gain)
                gmh_acc[span, :] = total
                gatt_s[span, :] = total.astype(BF)
                return shift[0:1, :]

            lax.fori_loop(0, rows // block, back_b, halo_b[m : m + 1, :])

        put(gmh_acc.at[own], gmid_out)
        put(gatt_s, gatt_out)
        need_wo.wait()

        @pl.loop(0, 2)
        def _(i):
            span = tile(i, tokens // 2)
            gmh_acc[tile(2 + i, tokens // 2), :] = dot(gatt_s[span, :], wo[...], NT)

        for copy in need:
            copy.wait()
        width = 256
        place = lax.broadcasted_iota(jnp.int32, (rows, width), 0).astype(F32)

        @pl.loop(0, 1024 // width)
        def _(i):
            cols = tile(i, width)
            rate = jnp.exp(vec_ref[2:3, cols])
            rising = jnp.exp(place * rate)
            falling = jnp.exp((1.0 - place) * rate)
            step_back = jnp.exp(-rate)
            extra = vec_ref[3:4, cols]
            for m in range(micros):
                span = slice(m * rows, (m + 1) * rows)
                far_span = slice(tokens + m * rows, tokens + (m + 1) * rows)
                bonus = jnp.exp(extra + k_s[span, cols])
                recept = r_s[span, cols]
                inverse = 1.0 / (den_s[span, cols] + bonus)
                mixed = (num_s[span, cols] + bonus * v_s[span, cols]) * inverse
                grad_gated = gmh_acc[far_span, cols]
                grad_mixed = grad_gated * recept
                grp_s[span, cols] = (grad_mixed * mixed * (1.0 - recept)).astype(BF)
                up = grad_mixed * inverse
                down = -up * mixed
                up_sum = rising * dot_exact_left(mask_s[m], falling * up)
                down_sum = rising * dot_exact_left(mask_s[m], falling * down)
                gmh_acc[far_span, cols] = up
                db_s[span, cols] = down
                mid_s[span, cols] = up_sum
                gate_s[span, cols] = down_sum
                state_own[m : m + 1, cols] = up[0:1] + step_back * up_sum[0:1]
                state_own[micros + m : micros + m + 1, cols] = down[0:1] + step_back * down_sum[0:1]

        put(grp_s, grp_out)
        core_copy = remote(state_own, state_other, s_sem.at[3, 0], s_sem.at[3, 1], at.other)
        core_copy.start()
        pair = lax.div(mp, 2) * 2
        decay_all = jnp.exp(-float(rows) * jnp.exp(vec_ref[2:3, :]))

        def seen(device, last):
            index = lax.rem(device + at.count, at.count)
            start = 0 if last else 2 * micros
            return wide(segs_ref[index, start : start + 2 * micros, :], 1024)

        core_copy.wait()
        even = jnp.where(core == 0, state_own[...], state_other[...])
        odd = jnp.where(core == 0, state_other[...], state_own[...])
        state_chip[...] = even + jnp.where(
            seen(pair, False) == seen(pair + 1, False), decay_all * odd, 0.0
        )
        chip_copies = [
            remote(state_chip, state_in.at[step - 1], s_sem.at[3 + step, 0], s_sem.at[3 + step, 1], at.plane(-step))
            for step in range(1, planes)
        ]
        for copy in chip_copies:
            copy.start()
        for copy in chip_copies:
            copy.wait()
        total = jnp.zeros_like(state_chip[...])
        power = jnp.ones_like(decay_all)
        for step in range(1, planes):
            fits = jnp.logical_and(
                seen(pair + 2 * step, False) == seen(mp, True), z + step < planes
            )
            total = total + jnp.where(fits, power * state_in[step - 1], 0.0)
            power = power * decay_all * decay_all
        joined = decay_all * total + jnp.where(
            seen(pair + 1, False) == seen(pair, True), state_other[...], 0.0
        )
        carry_s[...] = jnp.where(core == 0, joined, total)
        middle(3)
        last(0)

        @pl.loop(0, 1024 // width)
        def _(i):
            cols = tile(i, width)
            rate = jnp.exp(vec_ref[2:3, cols])
            tail = jnp.exp((place - (rows - 1.0)) * rate)
            extra = vec_ref[3:4, cols]
            step_back = jnp.exp(-rate)
            for m in range(micros):
                span = slice(m * rows, (m + 1) * rows)
                far_span = slice(tokens + m * rows, tokens + (m + 1) * rows)
                fits = (segcol_ref[span, :] == segs_ref[mp, m : m + 1, :]).astype(F32)
                carried = wide(fits, width) * tail
                up_sum = mid_s[span, cols] + carried * carry_s[m : m + 1, cols]
                down_sum = gate_s[span, cols] + carried * carry_s[micros + m : micros + m + 1, cols]
                up, down = (gmh_acc[far_span, cols], db_s[span, cols])
                key, value = (k_s[span, cols], v_s[span, cols])
                bonus = jnp.exp(extra + key)
                raised = jnp.exp(key)
                direct = (up * value + down) * bonus
                gk_s[span, cols] = (direct + raised * (value * up_sum + down_sum)).astype(BF)
                gv_s[span, cols] = (up * bonus + raised * up_sum).astype(BF)
                rate_part = -rate * step_back * (up_sum * num_s[span, cols] + down_sum * den_s[span, cols])
                for index, part in ((2, rate_part), (3, direct)):
                    summed = part[0:8]
                    for start in range(8, rows, 8):
                        summed = summed + part[start : start + 8]
                    sums_s[index, :, cols] = sums_s[index, :, cols] + summed

        put(gk_s, gk_out)
        put(gv_s, gv_out)
        for index in range(16):
            sums_flat[index : index + 1, :] = jnp.sum(sums_s[index], axis=0, keepdims=True)
        put(sums_flat, sums_out)
        for reduce in reduces[1]:
            reduce.close()
        middle(2)
        last(3)
        for parts, far_parts, own_s, own_out, rest_out, one, two in (
            (parts1, far1, own1_s, own1_out, rest1_out, lax.rem(dp, 2), lax.div(dp, 2)),
            (parts2, far2, own2_s, own2_out, rest2_out, lax.div(dp, 2), lax.rem(dp, 2)),
        ):
            own_s[...] = parts[0, one, two].astype(F32) + far_parts[...].astype(F32)
            put(own_s, own_out)
            put(parts.at[3, one, two], rest_out.at[1])
        last(2)
        put(parts1.at[2, lax.rem(dp, 2), lax.div(dp, 2)], rest1_out.at[0])
        put(parts2.at[2, lax.div(dp, 2), lax.rem(dp, 2)], rest2_out.at[0])
        for copy in outs:
            copy.wait()

    def hold(kind):
        return pltpu.VMEM((tokens, 1024), kind)

    square = pltpu.VMEM((1024, 1024), BF)
    pl.run_scoped(attention, *([hold(F32)] * 5), square, square, *([hold(BF)] * 5))


def middle_call(planes, micros, rows, operands):
    tokens = micros * rows
    hidden = operands[5].shape[2]

    def big(kind):
        return jax.ShapeDtypeStruct((tokens, 1024), kind)

    def hold(count, kind):
        return pltpu.VMEM((count, 1024), kind)

    few = hold(8, F32)
    quarter = (256, hidden)
    sems = pltpu.SemaphoreType.DMA
    return pl.pallas_call(
        functools.partial(middle_kernel, planes, micros, rows),
        out_shape=[big(F32)] * 2
        + [big(BF)] * 5
        + [jax.ShapeDtypeStruct((16, 1024), F32)]
        + [jax.ShapeDtypeStruct(quarter, F32)] * 2
        + [jax.ShapeDtypeStruct((2,) + quarter, BF)] * 2,
        in_specs=[VM] * 5 + [ANY] * 19,
        out_specs=[ANY] * 12,
        scratch_shapes=[pltpu.VMEM((planes, 2, 2) + quarter, BF)] * 2
        + [pltpu.VMEM((planes, 2) + quarter, BF)] * 2
        + [pltpu.VMEM((planes,) + quarter, BF)] * 2
        + [pltpu.VMEM(quarter, BF)] * 2
        + [hold(2 * tokens, F32)] * 2
        + [hold(tokens, BF)] * 4
        + [hold(tokens, F32), hold(tokens, F32), hold(tokens, BF), hold(tokens, F32)]
        + [
            pltpu.VMEM((16, 8, 1024), F32),
            pltpu.VMEM((16, 1024), F32),
            pltpu.VMEM((micros, rows, rows), BF),
            few,
            few,
            few,
            few,
            few,
            pltpu.VMEM((planes - 1, 8, 1024), F32),
            few,
            pltpu.VMEM(quarter, F32),
            pltpu.VMEM(quarter, F32),
            sems((23,)),
            sems((14,)),
            sems((planes, 2, 3, 2)),
            sems((3 + planes, 2)),
        ],
        compiler_params=pltpu.CompilerParams(
            collective_id=1, has_side_effects=True, vmem_limit_bytes=62 << 20
        ),
        cost_estimate=pl.CostEstimate(
            flops=52 * tokens * 1024 * 1024, bytes_accessed=60 << 20, transcendentals=6 * tokens * 1024
        ),
        name="channel_mix_and_adjoint",
    )(*operands)


class ReduceSquare:
    def __init__(self, at, parts, across, first, second, far, sems, x_first):
        self.at, self.across, self.first, self.second, self.far = (at, across, first, second, far)
        self.x_first = x_first
        side = lax.rem(at.dp, 2)
        line = lax.div(at.dp, 2)
        self.one, self.two = (side, line) if x_first else (line, side)
        near, next_to = (at.side_x, at.side_y) if x_first else (at.side_y, at.side_x)
        self.parts = parts
        self.mine = parts.at[at.core]
        self.copy_0 = remote(parts.at[1 - at.core], across, sems.at[0, 0], sems.at[0, 1], at.other)
        self.copy_1 = remote(self.mine.at[1 - self.one], first, sems.at[1, 0], sems.at[1, 1], near)
        self.copy_2 = remote(
            self.mine.at[self.one, 1 - self.two], second, sems.at[2, 0], sems.at[2, 1], next_to
        )
        self.copies_3 = [
            remote(
                self.mine.at[self.one, self.two, lax.rem(at.z + step, at.planes)],
                far.at[step - 1],
                sems.at[2 + step, 0],
                sems.at[2 + step, 1],
                at.plane(step),
            )
            for step in range(1, at.planes)
        ]

    def fill(self, left, right):
        planes = self.at.planes

        @pl.loop(0, 4)
        def _(q):
            line, side = (lax.div(q, 2), lax.rem(q, 2))
            one, two = (side, line) if self.x_first else (line, side)
            made = dot(left[:, tile(q, 256)], right[...], TN).astype(BF)
            split = made.reshape(planes, 2, 256 // (2 * planes), 1024)
            self.parts[0, one, two] = split[:, 0]
            self.parts[1, one, two] = split[:, 1]

        self.copy_0.start()

    def add(self, one, two, other):
        @pl.loop(0, self.at.planes)
        def _(i):
            self.mine[one, two, i] = (
                self.mine[one, two, i].astype(F32) + other[i].astype(F32)
            ).astype(BF)

    def begin(self):
        self.copy_0.wait()
        for two in range(2):
            self.add(1 - self.one, two, self.across.at[1 - self.one, two])
        self.copy_1.start()
        for two in range(2):
            self.add(self.one, two, self.across.at[self.one, two])

    def middle(self):
        self.copy_1.wait()
        self.add(self.one, 1 - self.two, self.first.at[1 - self.two])
        self.copy_2.start()
        self.add(self.one, self.two, self.first.at[self.two])

    def last(self):
        self.copy_2.wait()
        self.add(self.one, self.two, self.second)
        for copy in self.copies_3:
            copy.start()

    def close(self):
        for copy in self.copies_3:
            copy.wait()
        total = self.mine[self.one, self.two, self.at.z].astype(F32)
        for step in range(self.at.planes - 1):
            total = total + self.far[step].astype(F32)
        return total


def last_kernel(
    planes,
    micros,
    rows,
    vec_ref,
    keep_ref,
    sums_ref,
    gated_ref,
    gatt_ref,
    mg_ref,
    ggp_ref,
    mr_ref,
    grp_ref,
    mv_ref,
    gv_ref,
    mk_ref,
    gk_ref,
    recept_w,
    value_w,
    key_w,
    x_ref,
    da_ref,
    gmid_ref,
    part1_ref,
    part2_ref,
    rest1_ref,
    rest2_ref,
    grad_out,
    sums_out,
    own_output,
    own_gate,
    own_recept,
    own_value,
    own_key,
    own_hidden,
    own_return,
    left_s,
    right_s,
    w_s,
    x_s,
    da_s,
    total_s,
    g_s,
    sums_s,
    parts,
    across,
    first,
    second,
    far,
    own_s,
    pay_a,
    halo_a,
    flat_s,
    flat_recv,
    load_sem,
    out_sem,
    rs_sem,
    s_sem,
    ff_far,
    ff_total,
    own1_s,
    own2_s,
    ff_sem,
):
    at = Place(planes)
    tokens = micros * rows
    outs = []

    def put(source, target):
        copy = pltpu.make_async_copy(source, target, out_sem.at[len(outs)])
        copy.start()
        outs.append(copy)

    loaded = []

    def load(source, target):
        copy = pltpu.make_async_copy(source, target, load_sem.at[len(loaded)])
        copy.start()
        loaded.append(copy)
        return copy

    sides = (
        (gated_ref, gatt_ref),
        (mg_ref, ggp_ref),
        (mr_ref, grp_ref),
        (mv_ref, gv_ref),
        (mk_ref, gk_ref),
    )
    side_loads = [
        (load(left, left_s.at[index]), load(right, right_s.at[index]))
        for index, (left, right) in enumerate(sides)
    ]
    w_loads = [
        load(source, w_s.at[index]) for index, source in enumerate((recept_w, value_w, key_w))
    ]
    row_loads = [load(x_ref, x_s), load(da_ref, da_s), load(gmid_ref, total_s)]
    greet(
        [at.other, at.side_x, at.side_y]
        + [at.plane(step) for step in range(1, planes)]
        + [at.ahead(1), at.ahead(-1)]
    )
    reduces = [
        ReduceSquare(
            at, parts.at[index], across.at[index], first.at[index], second.at[index],
            far.at[index], rs_sem.at[index], index % 2 == 0,
        )
        for index in range(5)
    ]
    ff_loads = [load(part1_ref, ff_total.at[0]), load(part2_ref, ff_total.at[1])]
    ff_copies = [
        remote(rest.at[slot], ff_far.at[slot, index], ff_sem.at[slot, index, 0], ff_sem.at[slot, index, 1], at.plane(planes - 2 + slot))
        for slot in (1, 0)
        for index, rest in enumerate((rest1_ref, rest2_ref))
    ]
    for copy in ff_copies:
        copy.start()
    sums_s[...] = jnp.zeros_like(sums_s)
    def fill(index):
        for copy in side_loads[index]:
            copy.wait()
        reduces[index].fill(left_s.at[index], right_s.at[index])

    def back(index):
        w_loads[index].wait()

        @pl.loop(0, 2)
        def _(i):
            span = tile(i, tokens // 2)
            g_s[index, span, :] = dot(right_s[2 + index, span, :], w_s[index], NT)

    fill(0)
    fill(1)
    reduces[0].begin()
    fill(2)
    reduces[1].begin()
    fill(3)
    fill(4)
    back(0)
    back(1)
    reduces[0].middle()
    reduces[1].middle()
    reduces[2].begin()
    reduces[3].begin()
    back(2)
    for copy in row_loads:
        copy.wait()
    block = 16
    mixes = (vec_ref[6:7, :], vec_ref[5:6, :], vec_ref[4:5, :])
    gain = vec_ref[0:1, :]

    def combine(b):
        span = tile(b, block)
        grads = [g_s[index, span, :] for index in range(3)]
        shift = sum(grad * (1.0 - mix) for grad, mix in zip(grads, mixes))
        return (span, grads, shift * wide(keep_ref[span, :], 1024))

    for m in range(micros):
        pay_a[m : m + 1, :] = combine(m * (rows // block))[2][0:1, :]
    pay_a[micros:, :] = jnp.zeros((8 - micros, 1024), F32)
    halo_copy = remote(pay_a, halo_a, s_sem.at[0, 0], s_sem.at[0, 1], at.ahead(-1))
    halo_copy.start()
    at_last = lax.broadcasted_iota(jnp.int32, (block, 1024), 0) == block - 1
    halo_copy.wait()
    for m in range(micros):

        def back_a(i, after, m=m):
            span, grads, shift = combine((m + 1) * (rows // block) - 1 - i)
            delta = da_s[span, :]
            for index, grad in enumerate(grads):
                sum_rows(sums_s, 2 - index, grad * delta)
            moved = jnp.where(at_last, after, pltpu.roll(shift, block - 1, 0))
            grad = sum(part * mix for part, mix in zip(grads, mixes)) + moved
            unit, inverse = unit_of(x_s[span, :].astype(F32))
            sum_rows(sums_s, 3, grad * unit)
            sum_rows(sums_s, 4, grad)
            total_s[span, :] = total_s[span, :] + norm_back_rows(grad, unit, inverse, gain)
            return shift[0:1, :]

        lax.fori_loop(0, rows // block, back_a, halo_a[m : m + 1, :])
    put(total_s, grad_out)
    flat_s[0] = sums_ref[...]
    for index, row in enumerate((4, 5, 6, 0, 1)):
        flat_s[0, row : row + 1, :] = jnp.sum(sums_s[index], axis=0, keepdims=True)

    def flat_copy(level, slot, device):
        return remote(
            flat_s.at[level], flat_recv.at[slot], s_sem.at[1 + slot, 0], s_sem.at[1 + slot, 1], device
        )

    over_core = flat_copy(0, 0, at.other)
    over_core.start()
    reduces[0].last()
    reduces[1].last()
    reduces[4].begin()
    over_core.wait()
    flat_s[1] = flat_s[0] + flat_recv[0]
    flat_copies = [flat_copy(1, step, at.plane(step)) for step in range(1, planes)]
    for copy in flat_copies:
        copy.start()
    for copy in flat_copies:
        copy.wait()
    flat_s[2] = flat_s[1] + sum(flat_recv[step] for step in range(1, planes))
    reduces[2].middle()
    reduces[3].middle()
    over_x = flat_copy(2, planes, at.side_x)
    over_x.start()
    over_x.wait()
    flat_s[3] = flat_s[2] + flat_recv[planes]
    over_y = flat_copy(3, planes + 1, at.side_y)
    over_y.start()
    reduces[4].middle()
    reduces[2].last()
    reduces[3].last()
    over_y.wait()
    flat_s[0] = flat_s[3] + flat_recv[planes + 1]
    put(flat_s.at[0], sums_out)
    for copy in ff_loads + ff_copies:
        copy.wait()
    totals = [
        ff_total[index] + ff_far[0, index].astype(F32) + ff_far[1, index].astype(F32)
        for index in range(2)
    ]
    own1_s[...] = totals[0]
    own2_s[...] = totals[1].T
    put(own1_s, own_hidden)
    put(own2_s, own_return)
    reduces[4].last()
    for index, target in enumerate((own_output, own_gate, own_recept, own_value, own_key)):
        own_s[index] = reduces[index].close()
        put(own_s.at[index], target)
    for copy in outs:
        copy.wait()


def last_call(planes, micros, rows, operands):
    tokens = micros * rows

    def hold(count, kind):
        return pltpu.VMEM((count, tokens, 1024), kind)

    quarter = operands[-4].shape
    piece = (1024 // (8 * planes), 1024)
    sems = pltpu.SemaphoreType.DMA
    few = pltpu.VMEM((8, 1024), F32)
    return pl.pallas_call(
        functools.partial(last_kernel, planes, micros, rows),
        out_shape=[
            jax.ShapeDtypeStruct((tokens, 1024), F32),
            jax.ShapeDtypeStruct((16, 1024), F32),
        ]
        + [jax.ShapeDtypeStruct(piece, F32)] * 5
        + [jax.ShapeDtypeStruct(quarter, F32), jax.ShapeDtypeStruct(quarter[::-1], F32)],
        in_specs=[VM] * 3 + [ANY] * 20,
        out_specs=[ANY] * 9,
        scratch_shapes=[
            hold(5, BF),
            hold(5, BF),
            pltpu.VMEM((3, 1024, 1024), BF),
            pltpu.VMEM((tokens, 1024), BF),
            pltpu.VMEM((tokens, 1024), F32),
            pltpu.VMEM((tokens, 1024), F32),
            hold(3, F32),
            pltpu.VMEM((5, 8, 1024), F32),
            pltpu.VMEM((5, 2, 2, 2, planes) + piece, BF),
            pltpu.VMEM((5, 2, 2, planes) + piece, BF),
            pltpu.VMEM((5, 2, planes) + piece, BF),
            pltpu.VMEM((5, planes) + piece, BF),
            pltpu.VMEM((5, planes - 1) + piece, BF),
            pltpu.VMEM((5,) + piece, F32),
            few,
            few,
            pltpu.VMEM((4, 16, 1024), F32),
            pltpu.VMEM((2 + planes, 16, 1024), F32),
            sems((18,)),
            sems((9,)),
            sems((5, 2 + planes, 2)),
            sems((3 + planes, 2)),
            pltpu.VMEM((2, 2) + quarter, BF),
            pltpu.VMEM((2,) + quarter, F32),
            pltpu.VMEM(quarter, F32),
            pltpu.VMEM(quarter[::-1], F32),
            sems((2, 2, 2)),
        ],
        compiler_params=pltpu.CompilerParams(
            collective_id=2, has_side_effects=True, vmem_limit_bytes=62 << 20
        ),
        cost_estimate=pl.CostEstimate(
            flops=16 * tokens * 1024 * 1024, bytes_accessed=30 << 20, transcendentals=0
        ),
        name="time_mix_weights",
    )(*operands)


def one_micro(block_in, seg_ids, grad_out, vectors, matrices, hidden_w, return_w):
    (
        gain_one,
        bias_one,
        decay_vec,
        extra_array,
        mix_key,
        mix_value,
        mix_recept,
        gain_two,
        bias_two,
        mix_hidden,
        mix_gate,
    ) = vectors
    key_w, value_w, recept_w, output_w, gate_w = matrices
    row_count = block_in.shape[0]
    model_width = block_in.shape[1]
    seg_float = seg_ids.astype(jnp.float32)
    normed_a, unit_a, inv_a = layer_norm(block_in, gain_one, bias_one)
    prev_row, prev_seg = from_behind((normed_a[-1:], seg_float[-1:]), "mp", 1)
    same_row = jnp.concatenate(
        [
            (seg_float[:1] == prev_seg).astype(jnp.float32),
            (seg_ids[1:] == seg_ids[:-1]).astype(jnp.float32),
        ]
    )
    same_col = same_row[:, None]
    shifted_a = jnp.concatenate([prev_row, normed_a[:-1]], axis=0) * same_col
    delta_a = normed_a - shifted_a
    low_key = reduced_precision(shifted_a + delta_a * mix_key)
    low_value = reduced_precision(shifted_a + delta_a * mix_value)
    low_recept = reduced_precision(shifted_a + delta_a * mix_recept)
    lookup_start = product(low_key, key_w)
    content_start = product(low_value, value_w)
    recept = jax.nn.sigmoid(product(low_recept, recept_w))
    feature_fading = jnp.exp(decay_vec)
    positions = jnp.arange(row_count, dtype=jnp.float32)[:, None]
    rising = jnp.exp(positions * feature_fading)
    falling = jnp.exp(-(positions - 1.0) * feature_fading)
    falling_zero = jnp.exp(-positions * feature_fading)
    raised_lookup = jnp.exp(lookup_start)
    weighted_average = raised_lookup * content_start
    order_rows = jnp.arange(row_count)
    lower_tri = jnp.logical_and(
        seg_ids[:, None] == seg_ids[None, :], order_rows[None, :] < order_rows[:, None]
    ).astype(jnp.float32)
    last_mask = (seg_ids == seg_ids[-1]).astype(jnp.float32)
    first_mask = (seg_ids == seg_ids[0]).astype(jnp.float32) * same_row[0]
    forward_mat = jnp.concatenate([lower_tri, last_mask[None]], axis=0)
    stacked = jnp.concatenate(
        [
            rising * weighted_average,
            rising * raised_lookup,
            positions * rising * weighted_average,
            positions * rising * raised_lookup,
        ],
        axis=1,
    )
    summed = jnp.dot(forward_mat, stacked, precision=HIGH)
    inner_sums = summed[:row_count]
    closing = summed[row_count]
    num_loc = falling * inner_sums[:, :model_width]
    den_loc = falling * inner_sums[:, model_width : 2 * model_width]
    num_der = (
        -(positions - 1.0) * num_loc + falling * inner_sums[:, 2 * model_width : 3 * model_width]
    )
    den_der = -(positions - 1.0) * den_loc + falling * inner_sums[:, 3 * model_width :]
    end_fall = jnp.exp(-(row_count - 1.0) * feature_fading)
    state_num = end_fall * closing[:model_width]
    state_den = end_fall * closing[model_width : 2 * model_width]
    state_num_der = (
        -(row_count - 1.0) * state_num + end_fall * closing[2 * model_width : 3 * model_width]
    )
    state_den_der = -(row_count - 1.0) * state_den + end_fall * closing[3 * model_width :]
    uniform_flag = (seg_ids[-1] == seg_ids[0]).astype(jnp.float32) * same_row[0]
    carry_pass = uniform_flag * jnp.exp(-row_count * feature_fading)
    carry_der = -row_count * carry_pass
    zero_vec = jnp.zeros_like(feature_fading)
    one_vec = jnp.ones_like(feature_fading)
    in_num, in_den, in_num_der, in_den_der, pass_total, pass_der = carried_in(
        (state_num, state_den, state_num_der, state_den_der, carry_pass, carry_der),
        "mp",
        state_join,
        (zero_vec, zero_vec, zero_vec, zero_vec, one_vec, zero_vec),
        False,
    )
    carried = first_mask[:, None] * falling_zero
    dividend = num_loc + carried * in_num
    divisor_portion = den_loc + carried * in_den
    numer_der = num_der + carried * (in_num_der - positions * in_num)
    denom_der = den_der + carried * (in_den_der - positions * in_den)
    extra_summand = jnp.exp(extra_array + lookup_start)
    divisor_complete = divisor_portion + extra_summand
    mixture_result = (dividend + extra_summand * content_start) / divisor_complete
    gated = reduced_precision(recept * mixture_result)
    block_mid = block_in + product(gated, output_w)
    normed_b, unit_b, inv_b = layer_norm(block_mid, gain_two, bias_two)
    prev_mid = from_behind(normed_b[-1:], "mp", 1)
    shifted_b = jnp.concatenate([prev_mid, normed_b[:-1]], axis=0) * same_col
    delta_b = normed_b - shifted_b
    low_hidden = reduced_precision(shifted_b + delta_b * mix_hidden)
    low_gate = reduced_precision(shifted_b + delta_b * mix_gate)
    gate_two = jax.nn.sigmoid(product(low_gate, gate_w))
    hidden_rows = lax.all_gather(low_hidden, "mp", axis=0, tiled=True)
    pre_act = product(hidden_rows, hidden_w)
    rectified = jnp.maximum(pre_act, 0.0)
    squared = reduced_precision(rectified * rectified)
    returned = lax.psum_scatter(
        product(squared, return_w).astype(jnp.bfloat16), "mp", scatter_dimension=0, tiled=True
    ).astype(jnp.float32)
    output = block_mid + gate_two * returned
    grad_ret = reduced_precision(grad_out * gate_two)
    grad_gate_pre = reduced_precision(grad_out * returned * gate_two * (1.0 - gate_two))
    d_gate_w = (low_gate, grad_gate_pre)
    grad_low_gate = product_nt(grad_gate_pre, gate_w)
    grad_rows = lax.all_gather(grad_ret, "mp", axis=0, tiled=True)
    grad_squared = product_nt(grad_rows, return_w)
    d_return = (squared, grad_rows)
    grad_pre = reduced_precision(grad_squared * 2.0 * rectified)
    d_hidden = (hidden_rows, grad_pre)
    grad_low_hidden = lax.psum_scatter(
        product_nt(grad_pre, hidden_w).astype(jnp.bfloat16), "mp", scatter_dimension=0, tiled=True
    ).astype(jnp.float32)
    d_mix_hidden = jnp.sum(grad_low_hidden * delta_b, axis=0)
    d_mix_gate = jnp.sum(grad_low_gate * delta_b, axis=0)
    grad_shift_b = (
        grad_low_hidden * (1.0 - mix_hidden) + grad_low_gate * (1.0 - mix_gate)
    ) * same_col
    from_next_b = from_behind(grad_shift_b[:1], "mp", -1)
    grad_norm_b = (
        grad_low_hidden * mix_hidden
        + grad_low_gate * mix_gate
        + jnp.concatenate([grad_shift_b[1:], from_next_b], axis=0)
    )
    grad_mid_norm, d_gain_two, d_bias_two = norm_back(grad_norm_b, unit_b, inv_b, gain_two)
    grad_mid = grad_out + grad_mid_norm
    grad_att = reduced_precision(grad_mid)
    d_output_w = (gated, grad_att)
    grad_gated = product_nt(grad_att, output_w)
    grad_recept_pre = reduced_precision(grad_gated * mixture_result * recept * (1.0 - recept))
    grad_mixed = grad_gated * recept
    d_recept_w = (low_recept, grad_recept_pre)
    grad_low_recept = product_nt(grad_recept_pre, recept_w)
    dividend_adjoint = grad_mixed / divisor_complete
    divisor_adjoint = -dividend_adjoint * mixture_result
    extra_derivative_part = dividend_adjoint * content_start + divisor_adjoint
    extra_derivative = jnp.sum(extra_derivative_part * extra_summand, axis=0)
    d_rate = jnp.sum(dividend_adjoint * numer_der + divisor_adjoint * denom_der, axis=0)
    backward_mat = jnp.concatenate([lower_tri.T, first_mask[None]], axis=0)
    back_sum = jnp.dot(
        backward_mat,
        jnp.concatenate([falling * dividend_adjoint, falling * divisor_adjoint], axis=1),
        precision=HIGH,
    )
    step_back = jnp.exp(-feature_fading)
    from_num = step_back * back_sum[row_count, :model_width]
    from_den = step_back * back_sum[row_count, model_width:]
    out_num, out_den, out_pass = carried_in(
        (from_num, from_den, carry_pass), "mp", suffix_join, (zero_vec, zero_vec, one_vec), True
    )
    tail_fall = last_mask[:, None] * jnp.exp(-(row_count - 1.0 - positions) * feature_fading)
    cumulative_dividend = rising * back_sum[:row_count, :model_width] + tail_fall * out_num
    running_denominator = rising * back_sum[:row_count, model_width:] + tail_fall * out_den
    value_gradient = reduced_precision(
        dividend_adjoint * extra_summand + cumulative_dividend * raised_lookup
    )
    key_gradient = reduced_precision(
        extra_derivative_part * extra_summand
        + cumulative_dividend * weighted_average
        + running_denominator * raised_lookup
    )
    d_key_w = (low_key, key_gradient)
    d_value_w = (low_value, value_gradient)
    grad_low_key = product_nt(key_gradient, key_w)
    grad_low_value = product_nt(value_gradient, value_w)
    d_mix_key = jnp.sum(grad_low_key * delta_a, axis=0)
    d_mix_value = jnp.sum(grad_low_value * delta_a, axis=0)
    d_mix_recept = jnp.sum(grad_low_recept * delta_a, axis=0)
    grad_shift_a = (
        grad_low_key * (1.0 - mix_key)
        + grad_low_value * (1.0 - mix_value)
        + grad_low_recept * (1.0 - mix_recept)
    ) * same_col
    from_next_a = from_behind(grad_shift_a[:1], "mp", -1)
    grad_norm_a = (
        grad_low_key * mix_key
        + grad_low_value * mix_value
        + grad_low_recept * mix_recept
        + jnp.concatenate([grad_shift_a[1:], from_next_a], axis=0)
    )
    grad_in_norm, d_gain_one, d_bias_one = norm_back(grad_norm_a, unit_a, inv_a, gain_one)
    input_grad = grad_mid + grad_in_norm
    grads = (
        d_gain_one,
        d_bias_one,
        d_rate * feature_fading,
        extra_derivative,
        d_mix_key,
        d_mix_value,
        d_mix_recept,
        d_key_w,
        d_value_w,
        d_recept_w,
        d_output_w,
        d_gain_two,
        d_bias_two,
        d_mix_hidden,
        d_mix_gate,
        d_hidden,
        d_return,
        d_gate_w,
    )
    return (output, input_grad, grads)


def generic_body(
    incoming_signal,
    series_number_table,
    upstream_adjoint,
    first_scaling_factor,
    first_scaling_offset,
    logarithmic_fading_speeds,
    present_step_extra,
    lookup_shift_mixture,
    content_shift_mixture,
    admit_lookup_shift_mixture,
    attention_lookup_matrix,
    attention_content_matrix,
    attention_admit_matrix,
    attention_result_matrix,
    second_scaling_factor,
    second_scaling_offset,
    inner_shift_mixture,
    admit_shift_mixture,
    feedforward_lookup_matrix,
    feedforward_content_matrix,
    feedforward_admit_matrix,
):
    hidden_full, return_full = (feedforward_lookup_matrix, feedforward_content_matrix)
    vectors = tuple(
        (
            start_item.astype(jnp.float32)
            for start_item in (
                first_scaling_factor,
                first_scaling_offset,
                logarithmic_fading_speeds,
                present_step_extra,
                lookup_shift_mixture,
                content_shift_mixture,
                admit_lookup_shift_mixture,
                second_scaling_factor,
                second_scaling_offset,
                inner_shift_mixture,
                admit_shift_mixture,
            )
        )
    )
    matrices = (
        attention_lookup_matrix,
        attention_content_matrix,
        attention_admit_matrix,
        attention_result_matrix,
        feedforward_admit_matrix,
    )
    output, input_grad, grads = jax.vmap(
        lambda rows, ids, adjoint: one_micro(
            rows, ids, adjoint, vectors, matrices, hidden_full, return_full
        )
    )(
        incoming_signal[:, 0].astype(jnp.float32),
        series_number_table[:, 0],
        upstream_adjoint[:, 0].astype(jnp.float32),
    )
    totals = tuple(
        product_tn(*(side.reshape(-1, side.shape[-1]) for side in grad))
        if isinstance(grad, tuple)
        else jnp.sum(grad, axis=0)
        for grad in grads
    )
    square = [index for index in range(18) if totals[index].shape == totals[7].shape]
    lines = [index for index in range(18) if totals[index].ndim == 1]
    wide = lax.psum_scatter(
        jnp.concatenate([reduced_precision(totals[index]) for index in square], axis=1),
        ("dp", "mp"),
        scatter_dimension=0,
        tiled=True,
    ).astype(jnp.float32)
    thin = lax.psum_scatter(
        jnp.stack([totals[index] for index in lines], axis=1),
        ("dp", "mp"),
        scatter_dimension=0,
        tiled=True,
    )
    held = dict(zip(square, jnp.split(wide, len(square), axis=1)))
    held.update({index: thin[:, place] for place, index in enumerate(lines)})
    output, input_grad = (output[:, None], input_grad[:, None])
    owned = tuple(held[index] for index in sorted(held))
    hidden_own, return_own = (
        lax.psum_scatter(
            totals[15].astype(jnp.bfloat16), "dp", scatter_dimension=0, tiled=True
        ).astype(jnp.float32),
        lax.psum_scatter(
            totals[16].astype(jnp.bfloat16), "dp", scatter_dimension=1, tiled=True
        ).astype(jnp.float32),
    )
    return (
        output,
        input_grad,
        owned[0],
        owned[1],
        owned[2],
        owned[3],
        owned[4],
        owned[5],
        owned[6],
        owned[7],
        owned[8],
        owned[9],
        owned[10],
        owned[11],
        owned[12],
        owned[13],
        owned[14],
        hidden_own,
        return_own,
        owned[15],
    )


def hand_over(count, *refs):
    sems = refs[3 * count]
    ins, outs = ([], [])
    for index in range(count):
        held = refs[2 * count + index]
        ins.append(pltpu.make_async_copy(refs[index], held, sems.at[0, index]))
        outs.append(pltpu.make_async_copy(held, refs[count + index], sems.at[1, index]))
        ins[-1].start()
    for index in range(count):
        ins[index].wait()
        outs[index].start()
    for copy in outs:
        copy.wait()


def hand_call(arrays):
    count = len(arrays)
    return pl.pallas_call(
        functools.partial(hand_over, count),
        out_shape=[jax.ShapeDtypeStruct(part.shape, part.dtype) for part in arrays],
        in_specs=[ANY] * count,
        out_specs=[ANY] * count,
        scratch_shapes=[pltpu.VMEM(part.shape, part.dtype) for part in arrays]
        + [pltpu.SemaphoreType.DMA((2, count))],
        compiler_params=pltpu.CompilerParams(vmem_limit_bytes=60 << 20),
        name="hand_over",
    )(*arrays)


def kernel_body(
    incoming_signal,
    series_number_table,
    upstream_adjoint,
    first_scaling_factor,
    first_scaling_offset,
    logarithmic_fading_speeds,
    present_step_extra,
    lookup_shift_mixture,
    content_shift_mixture,
    admit_lookup_shift_mixture,
    attention_lookup_matrix,
    attention_content_matrix,
    attention_admit_matrix,
    attention_result_matrix,
    second_scaling_factor,
    second_scaling_offset,
    inner_shift_mixture,
    admit_shift_mixture,
    feedforward_lookup_matrix,
    feedforward_content_matrix,
    feedforward_admit_matrix,
):
    hidden_full, return_full = (feedforward_lookup_matrix, feedforward_content_matrix)
    matrices = (
        attention_lookup_matrix,
        attention_content_matrix,
        attention_admit_matrix,
        attention_result_matrix,
        feedforward_admit_matrix,
    )
    micros, _, rows, depth = incoming_signal.shape
    planes = lax.axis_size("mp") // 2
    x = incoming_signal.reshape(micros * rows, depth)
    adjoint = upstream_adjoint.reshape(micros * rows, depth)
    operands = (
        x,
        series_number_table.reshape(micros, rows),
        adjoint,
        first_scaling_factor,
        first_scaling_offset,
        logarithmic_fading_speeds,
        present_step_extra,
        lookup_shift_mixture,
        content_shift_mixture,
        admit_lookup_shift_mixture,
        second_scaling_factor,
        second_scaling_offset,
        inner_shift_mixture,
        admit_shift_mixture,
        *matrices,
        hidden_full,
        return_full,
    )
    (
        keys, values, recept, num, den, mid, gate, mk, mv, mr, gated, mg, delta_a, delta_b,
        keep, segs, table, segcol, segrow, mh_all, ret_all, w1_all, w2_all, ret_acc, gmh_acc,
        parts1, parts2,
    ) = forward_call(planes, micros, rows, operands)
    key_w, value_w, recept_w, output_w, gate_w = matrices
    (
        output, grad_mid, grad_gate, grad_att, grad_recept, grad_key, grad_value, sums,
        part1, part2, rest1, rest2,
    ) = middle_call(
        planes,
        micros,
        rows,
        (
            table, keep, segs, segcol, segrow, w1_all, w2_all, mh_all, ret_all, ret_acc, gmh_acc,
            parts1, parts2, mid, gate, adjoint, delta_b, keys, values, recept, num, den,
            gate_w, output_w,
        ),
    )
    (
        input_grad, sums, own_output, own_gate, own_recept, own_value, own_key, own_hidden,
        own_return,
    ) = last_call(
        planes,
        micros,
        rows,
        (
            table, keep, sums, gated, grad_att, mg, grad_gate, mr, grad_recept, mv, grad_value,
            mk, grad_key, recept_w, value_w, key_w, x, delta_a, grad_mid,
            part1, part2, rest1, rest2,
        ),
    )
    (
        output, input_grad, own_key, own_value, own_recept, own_output, own_hidden, own_return,
        own_gate,
    ) = hand_call(
        (
            output, input_grad, own_key, own_value, own_recept, own_output, own_hidden,
            own_return, own_gate,
        )
    )
    span = depth // (lax.axis_size("dp") * lax.axis_size("mp"))
    mine = lax.dynamic_slice_in_dim(
        sums, lax.axis_index(("dp", "mp")) * span, span, axis=1
    )
    line = [mine[index] for index in range(11)]
    shape = incoming_signal.shape
    return (
        output.reshape(shape),
        input_grad.reshape(shape),
        *line[:7],
        own_key,
        own_value,
        own_recept,
        own_output,
        *line[7:],
        own_hidden,
        own_return,
        own_gate,
    )


def solution(mesh):
    placed = (
        P(None, "dp", "mp", None),
        P(None, "dp", "mp"),
        P(None, "dp", "mp", None),
        P(),
        P(),
        P(),
        P(),
        P(),
        P(),
        P(),
        P(),
        P(),
        P(),
        P(),
        P(),
        P(),
        P(),
        P(),
        P(None, "mp"),
        P("mp", None),
        P(),
    )
    fits = mesh.shape["dp"] == 4 and mesh.shape["mp"] == 8
    return jax.shard_map(
        kernel_body if fits else generic_body,
        mesh=mesh,
        in_specs=placed,
        out_specs=(
            P(None, "dp", "mp", None),
            P(None, "dp", "mp", None),
            P(("dp", "mp")),
            P(("dp", "mp")),
            P(("dp", "mp")),
            P(("dp", "mp")),
            P(("dp", "mp")),
            P(("dp", "mp")),
            P(("dp", "mp")),
            P(("dp", "mp"), None),
            P(("dp", "mp"), None),
            P(("dp", "mp"), None),
            P(("dp", "mp"), None),
            P(("dp", "mp")),
            P(("dp", "mp")),
            P(("dp", "mp")),
            P(("dp", "mp")),
            P("dp", "mp"),
            P("mp", "dp"),
            P(("dp", "mp"), None),
        ),
        check_vma=False,
    )
```

```python
import functools

import jax
import jax.numpy as jnp
from jax import lax
from jax.experimental import pallas as pl
from jax.experimental.pallas import tpu as pltpu
from jax.sharding import PartitionSpec as P

EPS = 1e-05
HIGH = lax.Precision.HIGHEST


def from_behind(block, axis, distance):
    devices = range(lax.axis_size(axis))
    route = [(i - distance, i) for i in devices if i - distance in devices]
    return lax.ppermute(block, axis, route)


def carried_in(shard, axis, combine, identity, reverse):
    length, mine = (lax.axis_size(axis), lax.axis_index(axis))
    everything = jax.tree.map(lambda part: lax.all_gather(part, axis), shard)
    start = jax.tree.map(
        lambda part, zero: jnp.broadcast_to(jnp.asarray(zero, part.dtype), part.shape),
        shard,
        identity,
    )

    def step(k, before):
        at = length - 1 - k if reverse else k
        reached = at > mine if reverse else at < mine
        new = combine(before, jax.tree.map(lambda part: part[at], everything))
        return jax.tree.map(lambda a, b: jnp.where(reached, a, b), new, before)

    return lax.fori_loop(0, length, step, start)


def reduced_precision(values):
    return values.astype(jnp.bfloat16)


def product(left, right):
    return jnp.dot(left, right, preferred_element_type=jnp.float32)


def product_tn(left, right):
    return lax.dot_general(
        left, right, (((0,), (0,)), ((), ())), preferred_element_type=jnp.float32
    )


def product_nt(left, right):
    return lax.dot_general(
        left, right, (((1,), (1,)), ((), ())), preferred_element_type=jnp.float32
    )


def layer_norm(values, gain, bias):
    average = jnp.mean(values, axis=-1, keepdims=True)
    centre = values - average
    inverse = lax.rsqrt(jnp.mean(centre * centre, axis=-1, keepdims=True) + EPS)
    unit = centre * inverse
    return (unit * gain + bias, unit, inverse)


def norm_back(grad_in, unit, inverse, gain):
    scaled = grad_in * gain
    grad_values = inverse * (
        scaled
        - jnp.mean(scaled, axis=-1, keepdims=True)
        - unit * jnp.mean(scaled * unit, axis=-1, keepdims=True)
    )
    return (grad_values, jnp.sum(grad_in * unit, axis=0), jnp.sum(grad_in, axis=0))


def state_join(earlier, latter):
    return (
        latter[4] * earlier[0] + latter[0],
        latter[4] * earlier[1] + latter[1],
        latter[4] * earlier[2] + latter[5] * earlier[0] + latter[2],
        latter[4] * earlier[3] + latter[5] * earlier[1] + latter[3],
        earlier[4] * latter[4],
        earlier[5] * latter[4] + earlier[4] * latter[5],
    )


def suffix_join(earlier, latter):
    return (
        latter[0] + latter[2] * earlier[0],
        latter[1] + latter[2] * earlier[1],
        latter[2] * earlier[2],
    )


BF = jnp.bfloat16
F32 = jnp.float32
MESH = pl.DeviceIdType.MESH
NN = (((1,), (0,)), ((), ()))
NT = (((1,), (1,)), ((), ()))
TN = (((0,), (0,)), ((), ()))


def dot(left, right, form=NN):
    return lax.dot_general(left, right, form, preferred_element_type=F32)


def dot_exact_left(left, right):
    high = right.astype(BF)
    rest = (right - high.astype(F32)).astype(BF)
    return dot(left, high) + dot(left, rest)


def wide(lanes, width):
    return jnp.concatenate([lanes] * (width // 128), axis=1)


def tile(index, size):
    return pl.ds(pl.multiple_of(index * size, size), size)


def unit_of(values):
    average = jnp.mean(values, axis=-1, keepdims=True)
    centre = values - average
    inverse = lax.rsqrt(jnp.mean(centre * centre, axis=-1, keepdims=True) + EPS)
    return (centre * inverse, inverse)


def remote(source, target, send, receive, device):
    return pltpu.make_async_remote_copy(
        src_ref=source,
        dst_ref=target,
        send_sem=send,
        recv_sem=receive,
        device_id=device,
        device_id_type=MESH,
    )


class Place:
    def __init__(self, planes):
        self.planes = planes
        self.dp, self.mp = (lax.axis_index("dp"), lax.axis_index("mp"))
        self.z = lax.div(self.mp, 2)
        self.core = lax.rem(self.mp, 2)
        self.count = 2 * planes
        self.other = (self.dp, self.mp + 1 - 2 * self.core)
        self.side_x = (self.dp + 1 - 2 * lax.rem(self.dp, 2), self.mp)
        self.side_y = (lax.rem(self.dp + 2, 4), self.mp)

    def ahead(self, steps):
        return (self.dp, lax.rem(self.mp + steps + self.count, self.count))

    def plane(self, steps):
        return (self.dp, lax.rem(self.z + steps + self.planes, self.planes) * 2 + self.core)


def greet(devices):
    barrier = pltpu.get_barrier_semaphore()
    for device in devices:
        pl.semaphore_signal(barrier, inc=1, device_id=device, device_id_type=MESH)
    pl.semaphore_wait(barrier, len(devices))


def feed_rows(w1, w2, mh2, gr2, sq_s, gp_s, ret_acc, gmh_acc, fresh):
    def rows_of(i):
        span = tile(i, 256)
        pre = dot(mh2[span, :], w1[...])
        rectified = jnp.maximum(pre, 0.0)
        squared = (rectified * rectified).astype(BF)
        sq_s[span, :] = squared
        grad_squared = dot(gr2[span, :], w2[...], NT)
        grad_pre = (grad_squared * 2.0 * rectified).astype(BF)
        gp_s[span, :] = grad_pre
        if fresh:
            ret_acc[span, :] = dot(squared, w2[...])
            gmh_acc[span, :] = dot(grad_pre, w1[...], NT)
        else:
            ret_acc[span, :] += dot(squared, w2[...])
            gmh_acc[span, :] += dot(grad_pre, w1[...], NT)

    return rows_of


def feed_grads(mh2, gr2, sq_s, gp_s, parts1, parts2):
    @pl.loop(0, 4)
    def _(q):
        line, side = (lax.div(q, 2), lax.rem(q, 2))
        cols = tile(q, 256)
        parts1[side, line] = dot(mh2[:, cols], gp_s[...], TN).astype(BF)
        parts2[line, side] = dot(gr2[:, cols], sq_s[...], TN).astype(BF)


def forward_kernel(
    planes,
    micros,
    rows,
    x_ref,
    table_ref,
    adj_ref,
    *refs,
):
    (
    lines, refs) = (refs[:11], refs[11:])
    (
    key_w,
    value_w,
    recept_w,
    output_w,
    gate_w,
    w1_ref,
    w2_ref,
    k_out,
    v_out,
    r_out,
    num_out,
    den_out,
    mid_out,
    gate_out,
    mk_out,
    mv_out,
    mr_out,
    gated_out,
    mg_out,
    da_out,
    db_out,
    keep_out,
    segs_out,
    vec_out,
    segcol_out,
    segrow_out,
    mh_all,
    ret_all,
    w1_all,
    w2_all,
    ret_acc_out,
    gmh_acc_out,
    parts1_out,
    parts2_out,
    wk,
    wv,
    wr,
    wo,
    wg,
    k_s,
    v_s,
    r_s,
    num_s,
    den_s,
    mid_s,
    gate_s,
    xb_s,
    da_s,
    mk_s,
    mv_s,
    mr_s,
    gated_s,
    mg_s,
    keep_s,
    segcol_ref,
    segrow_ref,
    segpay_ref,
    last_ref,
    mask_s,
    halo_a,
    near_a,
    pay_b,
    halo_b,
    segs_s,
    state_own,
    state_other,
    state_chip,
    state_in,
    carry_s,
    w_sem,
    out_sem,
    small_sem,
    z_sem,
    s_sem,
    vec_ref,
    mh2,
    gr2,
    sq_s,
    gp_s,
    ret_acc,
    gmh_acc,
    parts1,
    parts2,
    ff_sem,
    ) = refs
    at = Place(planes)
    dp, mp, z, core = (at.dp, at.mp, at.z, at.core)
    tokens = micros * rows
    peers = [at.ahead(step) for step in range(1, at.count)]
    greet(peers + [at.side_x, at.side_y])

    for index, line in enumerate(lines):
        vec_ref[index : index + 1, :] = line[...].astype(F32).reshape(1, 1024)
    vec_ref[11:16, :] = jnp.zeros((5, 1024), F32)

    numbers = table_ref[...].astype(F32)
    rest = jnp.zeros((8 - micros, rows), F32)
    segrow_ref[...] = jnp.concatenate([numbers, rest], axis=0)
    columns = segrow_ref[...].T
    ends = [jnp.broadcast_to(numbers[:, at_end], (micros, 128)) for at_end in (slice(rows - 1, rows), slice(0, 1))]
    segpay_ref[...] = jnp.concatenate([ends[0], ends[0], ends[1], ends[1]], axis=0)
    last_ref[...] = jnp.zeros((8, 1024), F32)
    for m in range(micros):
        segcol_ref[m * rows : (m + 1) * rows, :] = jnp.broadcast_to(columns[:, m : m + 1], (rows, 128))
        last_ref[m : m + 1, :] = x_ref[(m + 1) * rows - 16 : (m + 1) * rows, :].astype(F32)[15:16]

    quarter1, quarter2 = (w1_ref.shape[0] // 4, w2_ref.shape[0] // 4)
    q1, q2 = (tile(dp, quarter1), tile(dp, quarter2))
    z_copies = {}
    for step in (1, planes - 1):
        to = at.plane(-step)
        z_copies[step - 1] = (
            remote(w1_ref.at[q1], w1_all.at[step - 1, q1], z_sem.at[step - 1, 0, 0], z_sem.at[step - 1, 0, 1], to),
            remote(w2_ref.at[q2], w2_all.at[step - 1, q2], z_sem.at[step - 1, 1, 0], z_sem.at[step - 1, 1, 1], to),
        )
    half1 = tile(lax.div(dp, 2), 2 * quarter1)
    far2 = tile(lax.rem(dp + 2, 4), quarter2)
    back = at.plane(-1)
    onward_1 = remote(w1_all.at[0, half1], w1_all.at[1, half1], z_sem.at[1, 0, 0], z_sem.at[1, 0, 1], back)
    onward_2 = (
        remote(w2_all.at[0, q2], w2_all.at[1, q2], z_sem.at[1, 1, 0], z_sem.at[1, 1, 1], back),
        remote(w2_all.at[0, far2], w2_all.at[1, far2], z_sem.at[1, 2, 0], z_sem.at[1, 2, 1], back),
    )

    halo_copy = remote(last_ref, halo_a, small_sem.at[0, 0], small_sem.at[0, 1], at.ahead(1))
    halo_copy.start()
    seg_copies = [
        remote(segpay_ref, segs_s.at[mp], small_sem.at[1 + step, 0], small_sem.at[1 + step, 1], device)
        for step, device in enumerate(peers)
    ]
    for copy in seg_copies:
        copy.start()
    segs_s[mp] = segpay_ref[...]
    loads = []
    for index, (source, target) in enumerate(
        ((key_w, wk), (value_w, wv), (recept_w, wr), (output_w, wo), (gate_w, wg))
    ):
        loads.append(pltpu.make_async_copy(source, target, w_sem.at[index]))
        loads[-1].start()
    for copy in z_copies[0]:
        copy.start()
    halo_copy.wait()
    for copy in seg_copies:
        copy.wait()

    def along(step):
        group = []
        own1, own2 = (w1_all.at[step, q1], w2_all.at[step, q2])
        return (
            remote(own1, own1, z_sem.at[step, 2, 0], z_sem.at[step, 2, 1], at.side_x),
            remote(own2, own2, z_sem.at[step, 3, 0], z_sem.at[step, 3, 1], at.side_y),
        )

    def across(step):
        both1 = w1_all.at[step, half1]
        own2 = w2_all.at[step, q2]
        next2 = w2_all.at[step, far2]
        return (
            remote(both1, both1, z_sem.at[step, 4, 0], z_sem.at[step, 4, 1], at.side_y),
            remote(own2, own2, z_sem.at[step, 5, 0], z_sem.at[step, 5, 1], at.side_x),
            remote(next2, next2, z_sem.at[step, 6, 0], z_sem.at[step, 6, 1], at.side_x),
        )

    def start(group):
        for copy in group:
            copy.start()

    def finish(group):
        for copy in group:
            copy.wait()

    along_0, along_2 = (along(0), along(2))
    across_0, across_1, across_2 = (across(0), across(1), across(2))

    before = lax.rem(mp + at.count - 1, at.count)
    has_before = mp > 0
    first_row = lax.broadcasted_iota(jnp.int32, (rows, 128), 0) == 0
    row_at = lax.broadcasted_iota(jnp.int32, (rows, rows), 0)
    col_at = lax.broadcasted_iota(jnp.int32, (rows, rows), 1)
    for m in range(micros):
        here = segcol_ref[m * rows : (m + 1) * rows, :]
        behind = jnp.where(
            first_row, segs_s[before, m : m + 1, :], pltpu.roll(here, 1, 0)
        )
        same = jnp.logical_and(
            here == behind, jnp.logical_or(jnp.logical_not(first_row), has_before)
        )
        keep_s[m * rows : (m + 1) * rows, :] = same.astype(F32)
        mask_s[m] = jnp.logical_and(
            here == segrow_ref[m : m + 1, :], col_at < row_at
        ).astype(F32).astype(BF)

    block = 32
    at_first = lax.broadcasted_iota(jnp.int32, (block, 1024), 0) == 0
    gain, bias = (vec_ref[0:1, :], vec_ref[1:2, :])
    near_a[...] = unit_of(halo_a[...])[0] * gain + bias
    for m in range(micros):

        def mix_a(b, prev, m=m):
            span = tile(m * (rows // block) + b, block)
            normed = unit_of(x_ref[span, :].astype(F32))[0] * gain + bias
            shifted = jnp.where(at_first, prev, pltpu.roll(normed, 1, 0)) * wide(
                keep_s[span, :], 1024
            )
            delta = normed - shifted
            da_s[span, :] = delta
            mk_s[span, :] = (shifted + delta * vec_ref[4:5, :]).astype(BF)
            mv_s[span, :] = (shifted + delta * vec_ref[5:6, :]).astype(BF)
            mr_s[span, :] = (shifted + delta * vec_ref[6:7, :]).astype(BF)
            return normed[block - 1 : block, :]

        lax.fori_loop(0, rows // block, mix_a, near_a[m : m + 1, :], unroll=2)

    outs = []

    def put(source, target):
        copy = pltpu.make_async_copy(source, target, out_sem.at[len(outs)])
        copy.start()
        outs.append(copy)

    put(da_s, da_out)
    put(keep_s, keep_out)
    put(segs_s, segs_out)
    put(segcol_ref, segcol_out)
    put(vec_ref, vec_out)
    put(segrow_ref, segrow_out)
    put(mk_s, mk_out)
    put(mv_s, mv_out)
    put(mr_s, mr_out)

    loads[0].wait()
    loads[1].wait()
    width = 256
    place = lax.broadcasted_iota(jnp.int32, (rows, width), 0).astype(F32)

    @pl.loop(0, 1024 // width)
    def _(i):
        cols = tile(i, width)
        rate = jnp.exp(vec_ref[2:3, cols])
        rising = jnp.exp(place * rate)
        falling = jnp.exp((1.0 - place) * rate)
        step_back = jnp.exp(-rate)
        keys = dot(mk_s[...], wk[:, cols])
        values = dot(mv_s[...], wv[:, cols])
        for m in range(micros):
            span = slice(m * rows, (m + 1) * rows)
            key, value = (keys[span], values[span])
            raised = jnp.exp(key)
            weighted = raised * value
            num = falling * dot_exact_left(mask_s[m], rising * weighted)
            den = falling * dot_exact_left(mask_s[m], rising * raised)
            k_s[span, cols] = key
            v_s[span, cols] = value
            num_s[span, cols] = num
            den_s[span, cols] = den
            state_own[m : m + 1, cols] = step_back * num[rows - 1 :] + weighted[rows - 1 :]
            state_own[micros + m : micros + m + 1, cols] = (
                step_back * den[rows - 1 :] + raised[rows - 1 :]
            )

    put(k_s, k_out)
    put(v_s, v_out)
    core_copy = remote(state_own, state_other, s_sem.at[0, 0], s_sem.at[0, 1], at.other)
    core_copy.start()
    finish(z_copies[0])
    start(along_0)
    z_copies[2][0].start()

    loads[2].wait()

    @pl.loop(0, 2)
    def _(i):
        span = tile(i, tokens // 2)
        r_s[span, :] = jax.nn.sigmoid(dot(mr_s[span, :], wr[...]))

    put(r_s, r_out)

    pair = lax.div(mp, 2) * 2
    decay_all = jnp.exp(-float(rows) * jnp.exp(vec_ref[2:3, :]))
    core_copy.wait()

    def last_of(device):
        return wide(segs_s[lax.rem(device + at.count, at.count), 0 : 2 * micros, :], 1024)

    even = jnp.where(core == 0, state_own[...], state_other[...])
    odd = jnp.where(core == 0, state_other[...], state_own[...])
    state_chip[...] = odd + jnp.where(last_of(pair) == last_of(pair + 1), decay_all * even, 0.0)
    chip_copies = [
        remote(state_chip, state_in.at[step - 1], s_sem.at[step, 0], s_sem.at[step, 1], at.plane(step))
        for step in range(1, planes)
    ]
    start(chip_copies)
    finish(chip_copies)
    z_copies[2][1].start()
    finish(along_0)
    start(across_0)
    total = jnp.zeros_like(state_chip[...])
    power = jnp.ones_like(decay_all)
    for step in range(1, planes):
        fits = jnp.logical_and(
            last_of(pair - 2 * step + 1) == last_of(pair - 1), z >= step
        )
        total = total + jnp.where(fits, power * state_in[step - 1], 0.0)
        power = power * decay_all * decay_all
    joined = state_other[...] + jnp.where(last_of(pair) == last_of(pair - 1), decay_all * total, 0.0)
    carry_s[...] = jnp.where(core == 0, total, joined)

    @pl.loop(0, 1024 // width)
    def _(i):
        cols = tile(i, width)
        rate = jnp.exp(vec_ref[2:3, cols])
        falling = jnp.exp(-place * rate)
        extra = vec_ref[3:4, cols]
        for m in range(micros):
            span = slice(m * rows, (m + 1) * rows)
            fits = jnp.logical_and(
                segcol_ref[span, :] == segs_s[before, m : m + 1, :], has_before
            ).astype(F32)
            carried = wide(fits, width) * falling
            num = num_s[span, cols] + carried * carry_s[m : m + 1, cols]
            den = den_s[span, cols] + carried * carry_s[micros + m : micros + m + 1, cols]
            bonus = jnp.exp(extra + k_s[span, cols])
            mixed = (num + bonus * v_s[span, cols]) / (den + bonus)
            num_s[span, cols] = num
            den_s[span, cols] = den
            gated_s[span, cols] = (r_s[span, cols] * mixed).astype(BF)

    put(num_s, num_out)
    put(den_s, den_out)
    put(gated_s, gated_out)
    loads[3].wait()

    @pl.loop(0, 2)
    def _(i):
        span = tile(i, tokens // 2)
        mid_s[span, :] = x_ref[span, :].astype(F32) + dot(gated_s[span, :], wo[...])

    put(mid_s, mid_out)
    gain_b, bias_b = (vec_ref[7:8, :], vec_ref[8:9, :])

    def norm_b(b):
        span = tile(b, block)
        xb_s[span, :] = unit_of(mid_s[span, :])[0] * gain_b + bias_b

    for m in range(micros):
        norm_b((m + 1) * (rows // block) - 1)
        pay_b[m : m + 1, :] = xb_s[(m + 1) * rows - 1 : (m + 1) * rows, :]
    pay_b[micros:, :] = jnp.zeros((8 - micros, 1024), F32)
    halo_b_copy = remote(pay_b, halo_b, s_sem.at[planes, 0], s_sem.at[planes, 1], at.ahead(1))
    halo_b_copy.start()
    for m in range(micros):

        @pl.loop(m * (rows // block), (m + 1) * (rows // block) - 1)
        def _(b):
            norm_b(b)

    halo_b_copy.wait()
    onward_1.start()
    start(onward_2)
    finish(z_copies[2])
    start(along_2)
    for m in range(micros):

        def mix_b(b, prev, m=m):
            span = tile(m * (rows // block) + b, block)
            normed = xb_s[span, :]
            shifted = jnp.where(at_first, prev, pltpu.roll(normed, 1, 0)) * wide(
                keep_s[span, :], 1024
            )
            delta = normed - shifted
            xb_s[span, :] = delta
            mh2[span, :] = (shifted + delta * vec_ref[9:10, :]).astype(BF)
            mg_s[span, :] = (shifted + delta * vec_ref[10:11, :]).astype(BF)
            return normed[block - 1 : block, :]

        lax.fori_loop(0, rows // block, mix_b, halo_b[m : m + 1, :], unroll=2)

    own, far = (slice(0, tokens), slice(tokens, 2 * tokens))
    mh_copy = remote(
        mh2.at[own], mh2.at[far], s_sem.at[planes + 1, 0], s_sem.at[planes + 1, 1], at.other
    )
    mh_copy.start()
    put(mg_s, mg_out)
    put(xb_s, db_out)
    loads[4].wait()

    @pl.loop(0, 2)
    def _(i):
        span = tile(i, tokens // 2)
        gate = jax.nn.sigmoid(dot(mg_s[span, :], wg[...]))
        gate_s[span, :] = gate
        gr2[span, :] = (adj_ref[span, :].astype(F32) * gate).astype(BF)

    ret_copy = remote(
        gr2.at[own], gr2.at[far], s_sem.at[planes + 2, 0], s_sem.at[planes + 2, 1], at.other
    )
    ret_copy.start()
    put(gate_s, gate_out)
    hidden = w1_ref.shape[1]
    w1_own, w2_own = (wk.at[:, 0:hidden], wv.at[0:hidden])
    w1_next, w2_next = (wk.at[:, hidden : 2 * hidden], wv.at[hidden : 2 * hidden])
    ff_loads = [
        pltpu.make_async_copy(source, target, ff_sem.at[index])
        for index, (source, target) in enumerate(
            ((w1_ref, w1_own), (w2_ref, w2_own), (w1_all.at[0], w1_next), (w2_all.at[0], w2_next))
        )
    ]
    ff_loads[0].start()
    ff_loads[1].start()
    ff_loads[0].wait()
    ff_loads[1].wait()
    half = tokens // 256
    step = feed_rows(w1_own, w2_own, mh2, gr2, sq_s, gp_s, ret_acc, gmh_acc, True)
    pl.loop(0, half)(step)
    mh_copy.wait()
    ret_copy.wait()
    finish(along_2)
    start(across_2)
    put(mh2, mh_all)
    put(gr2, ret_all)
    finish(across_0)
    ff_loads[2].start()
    ff_loads[3].start()
    pl.loop(half, 2 * half)(step)
    feed_grads(mh2, gr2, sq_s, gp_s, parts1.at[0], parts2.at[0])
    onward_1.wait()
    across_1[0].start()
    put(parts1.at[0], parts1_out.at[0])
    put(parts2.at[0], parts2_out.at[0])
    ff_loads[2].wait()
    ff_loads[3].wait()
    step = feed_rows(w1_next, w2_next, mh2, gr2, sq_s, gp_s, ret_acc, gmh_acc, False)
    pl.loop(0, half)(step)
    onward_2[0].wait()
    across_1[1].start()
    pl.loop(half, 2 * half)(step)
    onward_2[1].wait()
    across_1[2].start()
    put(ret_acc, ret_acc_out)
    put(gmh_acc, gmh_acc_out)
    feed_grads(mh2, gr2, sq_s, gp_s, parts1.at[1], parts2.at[1])
    put(parts1.at[1], parts1_out.at[1])
    put(parts2.at[1], parts2_out.at[1])
    finish(across_2)
    finish(across_1)
    for copy in outs:
        copy.wait()


ANY = pl.BlockSpec(memory_space=pl.ANY)
VM = pl.BlockSpec(memory_space=pltpu.VMEM)


def forward_call(planes, micros, rows, operands):
    tokens = micros * rows
    hidden = operands[-1].shape[0]

    def big(kind):
        return jax.ShapeDtypeStruct((tokens, 1024), kind)

    def hold(kind):
        return pltpu.VMEM((tokens, 1024), kind)

    square = pltpu.VMEM((1024, 1024), BF)
    few = pltpu.VMEM((8, 1024), F32)
    pair = pltpu.SemaphoreType.DMA
    return pl.pallas_call(
        functools.partial(forward_kernel, planes, micros, rows),
        out_shape=[big(F32)] * 7
        + [big(BF)] * 5
        + [big(F32)] * 2
        + [
            jax.ShapeDtypeStruct((tokens, 128), F32),
            jax.ShapeDtypeStruct((2 * planes, 16, 128), F32),
            jax.ShapeDtypeStruct((16, 1024), F32),
            jax.ShapeDtypeStruct((tokens, 128), F32),
            jax.ShapeDtypeStruct((8, rows), F32),
        ]
        + [jax.ShapeDtypeStruct((2 * tokens, 1024), BF)] * 2
        + [
            jax.ShapeDtypeStruct((planes - 1, 1024, hidden), BF),
            jax.ShapeDtypeStruct((planes - 1, hidden, 1024), BF),
        ]
        + [jax.ShapeDtypeStruct((2 * tokens, 1024), F32)] * 2
        + [jax.ShapeDtypeStruct((2, 2, 2, 256, hidden), BF)] * 2,
        in_specs=[VM] * 14 + [ANY] * 7,
        out_specs=[ANY] * 27,
        scratch_shapes=[square] * 5
        + [hold(F32)] * 9
        + [hold(BF)] * 5
        + [
            pltpu.VMEM((tokens, 128), F32),
            pltpu.VMEM((tokens, 128), F32),
            pltpu.VMEM((8, rows), F32),
            pltpu.VMEM((4 * micros, 128), F32),
            few,
            pltpu.VMEM((micros, rows, rows), BF),
            few,
            few,
            few,
            few,
            pltpu.VMEM((2 * planes, 16, 128), F32),
            few,
            few,
            few,
            pltpu.VMEM((planes - 1, 8, 1024), F32),
            few,
            pair((5,)),
            pair((29,)),
            pair((2 * planes + 1, 2)),
            pair((planes - 1, 7, 2)),
            pair((planes + 3, 2)),
            pltpu.VMEM((16, 1024), F32),
            pltpu.VMEM((2 * tokens, 1024), BF),
            pltpu.VMEM((2 * tokens, 1024), BF),
            pltpu.VMEM((2 * tokens, hidden), BF),
            pltpu.VMEM((2 * tokens, hidden), BF),
            pltpu.VMEM((2 * tokens, 1024), F32),
            pltpu.VMEM((2 * tokens, 1024), F32),
            pltpu.VMEM((2, 2, 2, 256, hidden), BF),
            pltpu.VMEM((2, 2, 2, 256, hidden), BF),
            pair((4,)),
        ],
        compiler_params=pltpu.CompilerParams(
            collective_id=0, has_side_effects=True, vmem_limit_bytes=62 << 20
        ),
        cost_estimate=pl.CostEstimate(
            flops=36 * tokens * 1024 * 1024, bytes_accessed=40 << 20, transcendentals=6 * tokens * 1024
        ),
        name="time_mix_forward",
    )(*operands)


class Reduce:
    def __init__(self, at, parts, first, second, far, sems, slot, x_first):
        self.at, self.parts, self.slot = (at, parts, slot if far is not None else 0)
        side = lax.rem(at.dp, 2)
        line = lax.div(at.dp, 2)
        self.one, self.two = (side, line) if x_first else (line, side)
        near, next_to = (at.side_x, at.side_y) if x_first else (at.side_y, at.side_x)
        self.first, self.second, self.far = (first, second, far)
        self.copy_1 = remote(parts.at[1 - self.one], first, sems.at[0, 0], sems.at[0, 1], near)
        self.copy_2 = remote(
            parts.at[self.one, 1 - self.two], second, sems.at[1, 0], sems.at[1, 1], next_to
        )
        if self.slot:
            self.copy_3 = remote(
                parts.at[self.one, self.two], far, sems.at[2, 0], sems.at[2, 1], at.plane(slot)
            )

    def start(self):
        self.copy_1.start()

    def add(self, half, other):
        mine = self.parts.at[self.one, half]

        @pl.loop(0, mine.shape[0] // 64)
        def _(i):
            span = tile(i, 64)
            mine[span, :] = (mine[span, :].astype(F32) + other[span, :].astype(F32)).astype(BF)

    def middle(self):
        self.copy_1.wait()
        self.add(1 - self.two, self.first.at[1 - self.two])
        self.copy_2.start()
        self.add(self.two, self.first.at[self.two])

    def last(self):
        self.copy_2.wait()
        self.add(self.two, self.second)
        if self.slot:
            self.copy_3.start()

    def close(self):
        if self.slot:
            self.copy_3.wait()


def sum_rows(into, index, values):
    total = values[0:8]
    for start in range(8, values.shape[0], 8):
        total = total + values[start : start + 8]
    into[index] = into[index] + total


def norm_back_rows(grad, unit, inverse, gain):
    scaled = grad * gain
    return inverse * (
        scaled
        - jnp.mean(scaled, axis=-1, keepdims=True)
        - unit * jnp.mean(scaled * unit, axis=-1, keepdims=True)
    )


def fill_square(parts, left, right, planes, split):
    @pl.loop(0, 4)
    def _(q):
        line, side = (lax.div(q, 2), lax.rem(q, 2))
        made = dot(left[:, tile(q, 256)], right[...], TN).astype(BF)
        pieces = made.reshape(planes, 2, 256 // (2 * planes), 1024)
        for core in range(2):
            if split > 0:
                parts[core, side, line, :, :, 0:split] = pieces[:, core, :, 0:split]
            if split < 1024:
                parts[core, line, side, :, :, split:1024] = pieces[:, core, :, split:1024]


def add_square(mine, other, planes):
    for one in range(2):
        for two in range(2):

            @pl.loop(0, planes)
            def _(i):
                mine[one, two, i] = (
                    mine[one, two, i].astype(F32) + other[one, two, i].astype(F32)
                ).astype(BF)


def middle_kernel(
    planes,
    micros,
    rows,
    vec_ref,
    keep_ref,
    segs_ref,
    segcol_ref,
    segrow_ref,
    w1_all,
    w2_all,
    mh_all,
    ret_all,
    ret_acc_ref,
    gmh_acc_ref,
    parts1_ref,
    parts2_ref,
    mid_ref,
    gate_ref,
    adj_ref,
    db_ref,
    k_ref,
    v_ref,
    r_ref,
    num_ref,
    den_ref,
    gate_w,
    output_w,
    gated_ref,
    mg_ref,
    out_ref,
    gmid_out,
    ggp_out,
    gatt_out,
    grp_out,
    gk_out,
    gv_out,
    sums_out,
    own1_out,
    own2_out,
    rest1_out,
    rest2_out,
    square_out,
    parts1,
    parts2,
    first1,
    first2,
    second1,
    second2,
    far1,
    far2,
    ret_acc,
    gmh_acc,
    ret_send,
    gmh_send,
    ret_recv,
    gmh_recv,
    mid_s,
    gate_s,
    adj_s,
    db_s,
    sums_s,
    sums_flat,
    mask_s,
    pay_b,
    halo_b,
    state_own,
    state_other,
    state_chip,
    state_in,
    carry_s,
    load_sem,
    out_sem,
    rs_sem,
    s_sem,
    square_parts,
    square_across,
    square_sem,
):
    at = Place(planes)
    dp, mp, z, core = (at.dp, at.mp, at.z, at.core)
    tokens = micros * rows
    hidden = w1_all.shape[2]
    outs = []

    def put(source, target):
        copy = pltpu.make_async_copy(source, target, out_sem.at[len(outs)])
        copy.start()
        outs.append(copy)

    loaded = []

    def load(source, target):
        copy = pltpu.make_async_copy(source, target, load_sem.at[len(loaded)])
        copy.start()
        loaded.append(copy)
        return copy

    greet(
        [at.other, at.side_x, at.side_y]
        + [at.plane(step) for step in range(1, planes)]
        + [at.ahead(1), at.ahead(-1)]
    )
    reduces = []
    for slot in range(planes):
        reduces.append(
            (
                Reduce(at, parts1.at[slot], first1.at[slot], second1.at[slot],
                       far1.at[slot // 2] if slot % 2 else None, rs_sem.at[slot, 0], slot, True),
                Reduce(at, parts2.at[slot], first2.at[slot], second2.at[slot],
                       far2.at[slot // 2] if slot % 2 else None, rs_sem.at[slot, 1], slot, False),
            )
        )
    ret_copy = remote(ret_send, ret_recv, s_sem.at[0, 0], s_sem.at[0, 1], at.other)
    gmh_copy = remote(gmh_send, gmh_recv, s_sem.at[1, 0], s_sem.at[1, 1], at.other)

    part_loads = []
    for slot in (1, 0):
        part_loads.append(
            (load(parts1_ref.at[slot], parts1.at[slot]), load(parts2_ref.at[slot], parts2.at[slot]))
        )
    acc_loads = [load(ret_acc_ref, ret_acc), load(gmh_acc_ref, gmh_acc)]

    def begin(slot):
        for reduce in reduces[slot]:
            reduce.start()

    def middle(slot):
        for reduce in reduces[slot]:
            reduce.middle()

    def last(slot):
        for reduce in reduces[slot]:
            reduce.last()

    def feed_forward(w1, w2, mh2, gr2, sq_s, gp_s):
        mh_load = [load(mh_all, mh2), load(ret_all, gr2)]
        order = (planes - 1, planes - 2)
        slots = [
            (load(w1_all.at[slot - 1], w1.at[index]), load(w2_all.at[slot - 1], w2.at[index]))
            for index, slot in enumerate(order)
        ]
        late = [load(mid_ref, mid_s), load(gate_ref, gate_s), load(adj_ref, adj_s), load(db_ref, db_s)]
        for index, slot in enumerate((1, 0)):
            for copy in part_loads[index]:
                copy.wait()
            begin(slot)
        for copy in mh_load + acc_loads:
            copy.wait()
        half = tokens // 256
        for index, slot in enumerate(order):
            for copy in slots[index]:
                copy.wait()
            step = feed_rows(
                w1.at[index], w2.at[index], mh2, gr2, sq_s, gp_s, ret_acc, gmh_acc, False
            )
            pl.loop(half, 2 * half)(step)
            if index == 1:

                @pl.loop(0, tokens // 64)
                def _(i):
                    span = tile(i, 64)
                    far_span = tile(tokens // 64 + i, 64)
                    ret_send[span, :] = ret_acc[far_span, :].astype(BF)
                    gmh_send[span, :] = gmh_acc[far_span, :].astype(BF)

                ret_copy.start()
                gmh_copy.start()
            pl.loop(0, half)(step)
            feed_grads(mh2, gr2, sq_s, gp_s, parts1.at[slot], parts2.at[slot])
            if index == 0:
                middle(1)
                begin(slot)
        for copy in late:
            copy.wait()

    pl.run_scoped(
        feed_forward,
        pltpu.VMEM((2, 1024, hidden), BF),
        pltpu.VMEM((2, hidden, 1024), BF),
        pltpu.VMEM((2 * tokens, 1024), BF),
        pltpu.VMEM((2 * tokens, 1024), BF),
        pltpu.VMEM((2 * tokens, hidden), BF),
        pltpu.VMEM((2 * tokens, hidden), BF),
    )
    own = slice(0, tokens)
    far = slice(tokens, 2 * tokens)
    block = 32

    def attention(k_s, v_s, r_s, num_s, den_s, wg, wo, ggp_s, gatt_s, grp_s, gk_s, gv_s):
        need_wg = load(gate_w, wg)
        need_wo = load(output_w, wo)
        need = [
            load(k_ref, k_s),
            load(v_ref, v_s),
            load(r_ref, r_s),
            load(num_ref, num_s),
            load(den_ref, den_s),
        ]
        sums_s[...] = jnp.zeros_like(sums_s)
        row_at = lax.broadcasted_iota(jnp.int32, (rows, rows), 0)
        col_at = lax.broadcasted_iota(jnp.int32, (rows, rows), 1)
        for m in range(micros):
            mask_s[m] = jnp.logical_and(
                segcol_ref[m * rows : (m + 1) * rows, :] == segrow_ref[m : m + 1, :],
                col_at > row_at,
            ).astype(F32).astype(BF)
        ret_copy.wait()
        need_gated = load(gated_ref, ret_send)

        @pl.loop(0, tokens // block)
        def _(b):
            span = tile(b, block)
            returned = ret_acc[span, :] + ret_recv[span, :].astype(F32)
            gate = gate_s[span, :]
            product_in = gate * returned
            ret_acc[span, :] = mid_s[span, :] + product_in
            ggp_s[span, :] = (adj_s[span, :].astype(F32) * product_in * (1.0 - gate)).astype(BF)

        put(ret_acc.at[own], out_ref)
        put(ggp_s, ggp_out)
        need_wg.wait()

        @pl.loop(0, 2)
        def _(i):
            span = tile(i, tokens // 2)
            ret_acc[tile(2 + i, tokens // 2), :] = dot(ggp_s[span, :], wg[...], NT)

        middle(0)
        gmg = ret_acc.at[far]
        gmh_copy.wait()
        need_mg = load(mg_ref, gmh_send)
        mix_h, mix_g = (vec_ref[9:10, :], vec_ref[10:11, :])
        gain = vec_ref[7:8, :]

        def combine(b):
            span = tile(b, block)
            grad_h = gmh_acc[span, :] + gmh_recv[span, :].astype(F32)
            grad_g = gmg[span, :]
            shift = (grad_h * (1.0 - mix_h) + grad_g * (1.0 - mix_g)) * wide(keep_ref[span, :], 1024)
            return (span, grad_h, grad_g, shift)

        for m in range(micros):
            pay_b[m : m + 1, :] = combine(m * (rows // block))[3][0:1, :]
        pay_b[micros:, :] = jnp.zeros((8 - micros, 1024), F32)
        halo_copy = remote(pay_b, halo_b, s_sem.at[2, 0], s_sem.at[2, 1], at.ahead(-1))
        halo_copy.start()
        at_last = lax.broadcasted_iota(jnp.int32, (block, 1024), 0) == block - 1
        halo_copy.wait()
        last(1)
        for m in range(micros):

            def back_b(i, after, m=m):
                span, grad_h, grad_g, shift = combine((m + 1) * (rows // block) - 1 - i)
                delta = db_s[span, :]
                sum_rows(sums_s, 9, grad_h * delta)
                sum_rows(sums_s, 10, grad_g * delta)
                moved = jnp.where(at_last, after, pltpu.roll(shift, block - 1, 0))
                grad = grad_h * mix_h + grad_g * mix_g + moved
                unit, inverse = unit_of(mid_s[span, :])
                sum_rows(sums_s, 7, grad * unit)
                sum_rows(sums_s, 8, grad)
                total = adj_s[span, :].astype(F32) + norm_back_rows(grad, unit, inverse, gain)
                gmh_acc[span, :] = total
                gatt_s[span, :] = total.astype(BF)
                return shift[0:1, :]

            lax.fori_loop(0, rows // block, back_b, halo_b[m : m + 1, :], unroll=2)

        put(gmh_acc.at[own], gmid_out)
        put(gatt_s, gatt_out)
        need_wo.wait()

        @pl.loop(0, 2)
        def _(i):
            span = tile(i, tokens // 2)
            gmh_acc[tile(2 + i, tokens // 2), :] = dot(gatt_s[span, :], wo[...], NT)

        for copy in need:
            copy.wait()
        width = 256
        place = lax.broadcasted_iota(jnp.int32, (rows, width), 0).astype(F32)

        @pl.loop(0, 1024 // width)
        def _(i):
            cols = tile(i, width)
            rate = jnp.exp(vec_ref[2:3, cols])
            rising = jnp.exp(place * rate)
            falling = jnp.exp((1.0 - place) * rate)
            step_back = jnp.exp(-rate)
            extra = vec_ref[3:4, cols]
            for m in range(micros):
                span = slice(m * rows, (m + 1) * rows)
                far_span = slice(tokens + m * rows, tokens + (m + 1) * rows)
                bonus = jnp.exp(extra + k_s[span, cols])
                recept = r_s[span, cols]
                inverse = 1.0 / (den_s[span, cols] + bonus)
                mixed = (num_s[span, cols] + bonus * v_s[span, cols]) * inverse
                grad_gated = gmh_acc[far_span, cols]
                grad_mixed = grad_gated * recept
                grp_s[span, cols] = (grad_mixed * mixed * (1.0 - recept)).astype(BF)
                up = grad_mixed * inverse
                down = -up * mixed
                up_sum = rising * dot_exact_left(mask_s[m], falling * up)
                down_sum = rising * dot_exact_left(mask_s[m], falling * down)
                gmh_acc[far_span, cols] = up
                db_s[span, cols] = down
                mid_s[span, cols] = up_sum
                gate_s[span, cols] = down_sum
                state_own[m : m + 1, cols] = up[0:1] + step_back * up_sum[0:1]
                state_own[micros + m : micros + m + 1, cols] = down[0:1] + step_back * down_sum[0:1]

        put(grp_s, grp_out)
        core_copy = remote(state_own, state_other, s_sem.at[3, 0], s_sem.at[3, 1], at.other)
        core_copy.start()
        middle(3)
        begin(2)
        pair = lax.div(mp, 2) * 2
        decay_all = jnp.exp(-float(rows) * jnp.exp(vec_ref[2:3, :]))

        def seen(device, last):
            index = lax.rem(device + at.count, at.count)
            start = 0 if last else 2 * micros
            return wide(segs_ref[index, start : start + 2 * micros, :], 1024)

        core_copy.wait()
        even = jnp.where(core == 0, state_own[...], state_other[...])
        odd = jnp.where(core == 0, state_other[...], state_own[...])
        state_chip[...] = even + jnp.where(
            seen(pair, False) == seen(pair + 1, False), decay_all * odd, 0.0
        )
        chip_copies = [
            remote(state_chip, state_in.at[step - 1], s_sem.at[3 + step, 0], s_sem.at[3 + step, 1], at.plane(-step))
            for step in range(1, planes)
        ]
        for copy in chip_copies:
            copy.start()
        for copy in chip_copies:
            copy.wait()
        total = jnp.zeros_like(state_chip[...])
        power = jnp.ones_like(decay_all)
        for step in range(1, planes):
            fits = jnp.logical_and(
                seen(pair + 2 * step, False) == seen(mp, True), z + step < planes
            )
            total = total + jnp.where(fits, power * state_in[step - 1], 0.0)
            power = power * decay_all * decay_all
        joined = decay_all * total + jnp.where(
            seen(pair + 1, False) == seen(pair, True), state_other[...], 0.0
        )
        carry_s[...] = jnp.where(core == 0, joined, total)
        last(0)

        @pl.loop(0, 1024 // width)
        def _(i):
            cols = tile(i, width)
            rate = jnp.exp(vec_ref[2:3, cols])
            tail = jnp.exp((place - (rows - 1.0)) * rate)
            extra = vec_ref[3:4, cols]
            step_back = jnp.exp(-rate)
            for m in range(micros):
                span = slice(m * rows, (m + 1) * rows)
                far_span = slice(tokens + m * rows, tokens + (m + 1) * rows)
                fits = (segcol_ref[span, :] == segs_ref[mp, m : m + 1, :]).astype(F32)
                carried = wide(fits, width) * tail
                up_sum = mid_s[span, cols] + carried * carry_s[m : m + 1, cols]
                down_sum = gate_s[span, cols] + carried * carry_s[micros + m : micros + m + 1, cols]
                up, down = (gmh_acc[far_span, cols], db_s[span, cols])
                key, value = (k_s[span, cols], v_s[span, cols])
                bonus = jnp.exp(extra + key)
                raised = jnp.exp(key)
                direct = (up * value + down) * bonus
                gk_s[span, cols] = (direct + raised * (value * up_sum + down_sum)).astype(BF)
                gv_s[span, cols] = (up * bonus + raised * up_sum).astype(BF)
                rate_part = -rate * step_back * (up_sum * num_s[span, cols] + down_sum * den_s[span, cols])
                for index, part in ((2, rate_part), (3, direct)):
                    summed = part[0:8]
                    for start in range(8, rows, 8):
                        summed = summed + part[start : start + 8]
                    sums_s[index, :, cols] = sums_s[index, :, cols] + summed

        put(gk_s, gk_out)
        put(gv_s, gv_out)
        for index in range(16):
            sums_flat[index : index + 1, :] = jnp.sum(sums_s[index], axis=0, keepdims=True)
        put(sums_flat, sums_out)
        last(3)
        need_gated.wait()
        need_mg.wait()
        square_copies = []
        for index, (left, right) in enumerate(((ret_send, gatt_s), (gmh_send, ggp_s))):
            fill_square(square_parts.at[index], left, right, planes, 1024 * (1 - index))
            square_copies.append(
                remote(
                    square_parts.at[index, 1 - core],
                    square_across.at[index],
                    square_sem.at[index, 0],
                    square_sem.at[index, 1],
                    at.other,
                )
            )
            square_copies[index].start()
        for index in range(2):
            square_copies[index].wait()
            add_square(square_parts.at[index, core], square_across.at[index], planes)
            put(square_parts.at[index, core], square_out.at[index])
        middle(2)
        for slot in (1, 3):
            for reduce in reduces[slot]:
                reduce.close()
        for parts, far_parts, own_s, own_out, one, two in (
            (parts1, far1, mid_s, own1_out, lax.rem(dp, 2), lax.div(dp, 2)),
            (parts2, far2, gate_s, own2_out, lax.div(dp, 2), lax.rem(dp, 2)),
        ):
            own_s[0:256, 0:hidden] = (
                parts[0, one, two].astype(F32)
                + far_parts[0].astype(F32)
                + far_parts[1].astype(F32)
            )
            put(own_s.at[0:256, 0:hidden], own_out)
        last(2)
        put(parts1.at[2, lax.rem(dp, 2), lax.div(dp, 2)], rest1_out)
        put(parts2.at[2, lax.div(dp, 2), lax.rem(dp, 2)], rest2_out)
        for copy in outs:
            copy.wait()

    def hold(kind):
        return pltpu.VMEM((tokens, 1024), kind)

    square = pltpu.VMEM((1024, 1024), BF)
    pl.run_scoped(attention, *([hold(F32)] * 5), square, square, *([hold(BF)] * 5))


def middle_call(planes, micros, rows, operands):
    tokens = micros * rows
    hidden = operands[5].shape[2]

    def big(kind):
        return jax.ShapeDtypeStruct((tokens, 1024), kind)

    def hold(count, kind):
        return pltpu.VMEM((count, 1024), kind)

    few = hold(8, F32)
    quarter = (256, hidden)
    piece = (planes, 256 // (2 * planes), 1024)
    sems = pltpu.SemaphoreType.DMA
    return pl.pallas_call(
        functools.partial(middle_kernel, planes, micros, rows),
        out_shape=[big(F32)] * 2
        + [big(BF)] * 5
        + [jax.ShapeDtypeStruct((16, 1024), F32)]
        + [jax.ShapeDtypeStruct(quarter, F32)] * 2
        + [jax.ShapeDtypeStruct(quarter, BF)] * 2
        + [jax.ShapeDtypeStruct((2, 2, 2) + piece, BF)],
        in_specs=[VM] * 5 + [ANY] * 21,
        out_specs=[ANY] * 13,
        scratch_shapes=[pltpu.VMEM((planes, 2, 2) + quarter, BF)] * 2
        + [pltpu.VMEM((planes, 2) + quarter, BF)] * 2
        + [pltpu.VMEM((planes,) + quarter, BF)] * 2
        + [pltpu.VMEM((2,) + quarter, BF)] * 2
        + [hold(2 * tokens, F32)] * 2
        + [hold(tokens, BF)] * 4
        + [hold(tokens, F32), hold(tokens, F32), hold(tokens, BF), hold(tokens, F32)]
        + [
            pltpu.VMEM((16, 8, 1024), F32),
            pltpu.VMEM((16, 1024), F32),
            pltpu.VMEM((micros, rows, rows), BF),
            few,
            few,
            few,
            few,
            few,
            pltpu.VMEM((planes - 1, 8, 1024), F32),
            few,
            sems((25,)),
            sems((14,)),
            sems((planes, 2, 3, 2)),
            sems((3 + planes, 2)),
            pltpu.VMEM((2, 2, 2, 2) + piece, BF),
            pltpu.VMEM((2, 2, 2) + piece, BF),
            sems((2, 2)),
        ],
        compiler_params=pltpu.CompilerParams(
            collective_id=1, has_side_effects=True, vmem_limit_bytes=62 << 20
        ),
        cost_estimate=pl.CostEstimate(
            flops=52 * tokens * 1024 * 1024, bytes_accessed=60 << 20, transcendentals=6 * tokens * 1024
        ),
        name="channel_mix_and_adjoint",
    )(*operands)


class ReduceSquare:
    def __init__(self, at, mine, first, second, far, sems, x_first):
        self.at, self.mine, self.first, self.second, self.far = (at, mine, first, second, far)
        side = lax.rem(at.dp, 2)
        line = lax.div(at.dp, 2)
        self.one, self.two = (side, line) if x_first else (line, side)
        near, next_to = (at.side_x, at.side_y) if x_first else (at.side_y, at.side_x)
        self.copy_1 = remote(mine.at[1 - self.one], first, sems.at[0, 0], sems.at[0, 1], near)
        self.copy_2 = remote(
            mine.at[self.one, 1 - self.two], second, sems.at[1, 0], sems.at[1, 1], next_to
        )
        self.copies_3 = [
            remote(
                mine.at[self.one, self.two, lax.rem(at.z + step, at.planes)],
                far.at[step - 1],
                sems.at[1 + step, 0],
                sems.at[1 + step, 1],
                at.plane(step),
            )
            for step in range(1, at.planes)
        ]

    def add(self, one, two, other):
        @pl.loop(0, self.at.planes)
        def _(i):
            self.mine[one, two, i] = (
                self.mine[one, two, i].astype(F32) + other[i].astype(F32)
            ).astype(BF)

    def begin(self):
        self.copy_1.start()

    def middle(self):
        self.copy_1.wait()
        self.add(self.one, 1 - self.two, self.first.at[1 - self.two])
        self.copy_2.start()
        self.add(self.one, self.two, self.first.at[self.two])

    def last(self):
        self.copy_2.wait()
        self.add(self.one, self.two, self.second)

    def send(self):
        for copy in self.copies_3:
            copy.start()

    def close(self):
        for copy in self.copies_3:
            copy.wait()
        total = self.mine[self.one, self.two, self.at.z].astype(F32)
        for step in range(self.at.planes - 1):
            total = total + self.far[step].astype(F32)
        return total


def last_kernel(
    planes,
    micros,
    rows,
    vec_ref,
    keep_ref,
    sums_ref,
    square_ref,
    mr_ref,
    grp_ref,
    mv_ref,
    gv_ref,
    mk_ref,
    gk_ref,
    recept_w,
    value_w,
    key_w,
    x_ref,
    da_ref,
    gmid_ref,
    part1_ref,
    part2_ref,
    rest1_ref,
    rest2_ref,
    grad_out,
    sums_out,
    own_output,
    own_gate,
    own_recept,
    own_value,
    own_key,
    own_hidden,
    own_return,
    left_s,
    right_s,
    w_s,
    x_s,
    da_s,
    total_s,
    g_s,
    sums_s,
    parts,
    across,
    first,
    second,
    far,
    own_s,
    pay_a,
    halo_a,
    flat_s,
    flat_recv,
    load_sem,
    out_sem,
    rs_sem,
    s_sem,
    ff_far,
    ff_total,
    own1_s,
    own2_s,
    ff_sem,
    ready_s,
    core_sem,
):
    at = Place(planes)
    tokens = micros * rows
    outs = []

    def put(source, target):
        copy = pltpu.make_async_copy(source, target, out_sem.at[len(outs)])
        copy.start()
        outs.append(copy)

    loaded = []

    def load(source, target):
        copy = pltpu.make_async_copy(source, target, load_sem.at[len(loaded)])
        copy.start()
        loaded.append(copy)
        return copy

    sides = (
        (mr_ref, grp_ref),
        (mv_ref, gv_ref),
        (mk_ref, gk_ref),
    )
    ready_load = load(square_ref, ready_s)
    side_loads = [
        (load(left, left_s.at[index]), load(right, right_s.at[index]))
        for index, (left, right) in enumerate(sides)
    ]
    w_loads = [
        load(source, w_s.at[index]) for index, source in enumerate((recept_w, value_w, key_w))
    ]
    row_loads = [load(x_ref, x_s), load(da_ref, da_s), load(gmid_ref, total_s)]
    greet(
        [at.other, at.side_x, at.side_y]
        + [at.plane(step) for step in range(1, planes)]
        + [at.ahead(1), at.ahead(-1)]
    )
    core = at.core
    lefts, rights = (slice(0, 512), slice(512, 1024))
    reduces = []
    for index, (cols, x_first) in enumerate(
        ((None, True), (None, False), (None, True), (None, False), (lefts, True), (rights, False))
    ):
        place = min(index, 4)
        mine = ready_s.at[index] if index < 2 else parts.at[place - 2, core]
        refs = (mine, first.at[place], second.at[place], far.at[place])
        if cols is not None:
            refs = (
                mine.at[:, :, :, :, cols],
                first.at[place, :, :, :, cols],
                second.at[place, :, :, cols],
                far.at[place, :, :, cols],
            )
        reduces.append(ReduceSquare(at, *refs, rs_sem.at[index], x_first))
    core_copies = [
        remote(
            parts.at[index, 1 - core],
            across.at[index],
            core_sem.at[index, 0],
            core_sem.at[index, 1],
            at.other,
        )
        for index in range(3)
    ]
    ff_loads = [load(part1_ref, ff_total.at[0]), load(part2_ref, ff_total.at[1])]
    ff_copies = [
        remote(rest, ff_far.at[index], ff_sem.at[index, 0], ff_sem.at[index, 1], at.plane(2))
        for index, rest in enumerate((rest1_ref, rest2_ref))
    ]
    ready_load.wait()
    reduces[0].begin()
    reduces[1].begin()
    mixes = (vec_ref[6:7, :], vec_ref[5:6, :], vec_ref[4:5, :])
    heads = jnp.zeros((16 * micros, 1024), F32)
    for index in range(3):
        side_loads[index][1].wait()
        w_loads[index].wait()
        picked = jnp.concatenate(
            [right_s[index, m * rows : m * rows + 16, :] for m in range(micros)], axis=0
        )
        heads = heads + dot(picked, w_s[index], NT) * (1.0 - mixes[index])
    for m in range(micros):
        pay_a[m : m + 1, :] = heads[16 * m : 16 * m + 1] * wide(
            keep_ref[m * rows : m * rows + 8, :], 1024
        )[0:1]
    pay_a[micros:, :] = jnp.zeros((8 - micros, 1024), F32)
    halo_copy = remote(pay_a, halo_a, s_sem.at[0, 0], s_sem.at[0, 1], at.ahead(-1))
    halo_copy.start()
    for copy in ff_copies:
        copy.start()
    sums_s[...] = jnp.zeros_like(sums_s)

    def fill(index, split):
        side_loads[index][0].wait()
        fill_square(parts.at[index], left_s.at[index], right_s.at[index], planes, split)
        core_copies[index].start()

    def settle(index):
        core_copies[index].wait()
        add_square(parts.at[index, core], across.at[index], planes)

    def back(index):
        @pl.loop(0, 2)
        def _(i):
            span = tile(i, tokens // 2)
            g_s[index, span, :] = dot(right_s[index, span, :], w_s[index], NT)

    fill(0, 1024)
    fill(1, 0)
    settle(0)
    fill(2, 512)
    settle(1)
    back(0)
    reduces[0].middle()
    reduces[1].middle()
    reduces[2].begin()
    reduces[3].begin()
    settle(2)
    back(1)
    back(2)
    for copy in row_loads:
        copy.wait()
    block = 32
    gain = vec_ref[0:1, :]

    def combine(b):
        span = tile(b, block)
        grads = [g_s[index, span, :] for index in range(3)]
        shift = sum(grad * (1.0 - mix) for grad, mix in zip(grads, mixes))
        return (span, grads, shift * wide(keep_ref[span, :], 1024))

    at_last = lax.broadcasted_iota(jnp.int32, (block, 1024), 0) == block - 1
    halo_copy.wait()
    for index in range(2):
        reduces[index].last()
        reduces[index].send()
    for m in range(micros):

        def back_a(i, after, m=m):
            span, grads, shift = combine((m + 1) * (rows // block) - 1 - i)
            delta = da_s[span, :]
            for index, grad in enumerate(grads):
                sum_rows(sums_s, 2 - index, grad * delta)
            moved = jnp.where(at_last, after, pltpu.roll(shift, block - 1, 0))
            grad = sum(part * mix for part, mix in zip(grads, mixes)) + moved
            unit, inverse = unit_of(x_s[span, :].astype(F32))
            sum_rows(sums_s, 3, grad * unit)
            sum_rows(sums_s, 4, grad)
            total_s[span, :] = total_s[span, :] + norm_back_rows(grad, unit, inverse, gain)
            return shift[0:1, :]

        lax.fori_loop(0, rows // block, back_a, halo_a[m : m + 1, :], unroll=2)
    put(total_s, grad_out)
    flat_s[0] = sums_ref[...]
    for index, row in enumerate((4, 5, 6, 0, 1)):
        flat_s[0, row : row + 1, :] = jnp.sum(sums_s[index], axis=0, keepdims=True)

    def flat_copy(level, slot, device):
        return remote(
            flat_s.at[level], flat_recv.at[slot], s_sem.at[1 + slot, 0], s_sem.at[1 + slot, 1], device
        )

    over_core = flat_copy(0, 0, at.other)
    over_core.start()
    over_core.wait()
    flat_s[1] = flat_s[0] + flat_recv[0]
    over_x = flat_copy(1, 1, at.side_x)
    over_x.start()
    reduces[2].middle()
    reduces[3].middle()
    over_x.wait()
    flat_s[2] = flat_s[1] + flat_recv[1]
    over_y = flat_copy(2, 2, at.side_y)
    over_y.start()
    reduces[4].begin()
    reduces[5].begin()
    for index in range(2, 4):
        reduces[index].last()
        reduces[index].send()
    over_y.wait()
    flat_s[3] = flat_s[2] + flat_recv[2]
    flat_copies = [flat_copy(3, 2 + step, at.plane(step)) for step in range(1, planes)]
    for copy in flat_copies:
        copy.start()
    for copy in ff_loads + ff_copies:
        copy.wait()
    own1_s[...] = ff_total[0] + ff_far[0].astype(F32)
    own2_s[...] = (ff_total[1] + ff_far[1].astype(F32)).T
    put(own1_s, own_hidden)
    put(own2_s, own_return)
    reduces[4].middle()
    reduces[5].middle()
    for index in range(4, 6):
        reduces[index].last()
        reduces[index].send()
    for index, target in enumerate((own_output, own_gate, own_recept, own_value)):
        own_s[index] = reduces[index].close()
        put(own_s.at[index], target)
    for copy in flat_copies:
        copy.wait()
    flat_s[0] = flat_s[3] + sum(flat_recv[2 + step] for step in range(1, planes))
    put(flat_s.at[0], sums_out)
    own_s[4, :, lefts] = reduces[4].close()
    own_s[4, :, rights] = reduces[5].close()
    put(own_s.at[4], own_key)
    for copy in outs:
        copy.wait()


def last_call(planes, micros, rows, operands):
    tokens = micros * rows

    def hold(count, kind):
        return pltpu.VMEM((count, tokens, 1024), kind)

    quarter = operands[-4].shape
    piece = (1024 // (8 * planes), 1024)
    sems = pltpu.SemaphoreType.DMA
    few = pltpu.VMEM((8, 1024), F32)
    return pl.pallas_call(
        functools.partial(last_kernel, planes, micros, rows),
        out_shape=[
            jax.ShapeDtypeStruct((tokens, 1024), F32),
            jax.ShapeDtypeStruct((16, 1024), F32),
        ]
        + [jax.ShapeDtypeStruct(piece, F32)] * 5
        + [jax.ShapeDtypeStruct(quarter, F32), jax.ShapeDtypeStruct(quarter[::-1], F32)],
        in_specs=[VM] * 3 + [ANY] * 17,
        out_specs=[ANY] * 9,
        scratch_shapes=[
            hold(3, BF),
            hold(3, BF),
            pltpu.VMEM((3, 1024, 1024), BF),
            pltpu.VMEM((tokens, 1024), BF),
            pltpu.VMEM((tokens, 1024), F32),
            pltpu.VMEM((tokens, 1024), F32),
            hold(3, F32),
            pltpu.VMEM((5, 8, 1024), F32),
            pltpu.VMEM((3, 2, 2, 2, planes) + piece, BF),
            pltpu.VMEM((3, 2, 2, planes) + piece, BF),
            pltpu.VMEM((5, 2, planes) + piece, BF),
            pltpu.VMEM((5, planes) + piece, BF),
            pltpu.VMEM((5, planes - 1) + piece, BF),
            pltpu.VMEM((5,) + piece, F32),
            few,
            few,
            pltpu.VMEM((4, 16, 1024), F32),
            pltpu.VMEM((2 + planes, 16, 1024), F32),
            sems((18,)),
            sems((9,)),
            sems((6, 1 + planes, 2)),
            sems((3 + planes, 2)),
            pltpu.VMEM((2,) + quarter, BF),
            pltpu.VMEM((2,) + quarter, F32),
            pltpu.VMEM(quarter, F32),
            pltpu.VMEM(quarter[::-1], F32),
            sems((2, 2)),
            pltpu.VMEM((2, 2, 2, planes) + piece, BF),
            sems((3, 2)),
        ],
        compiler_params=pltpu.CompilerParams(
            collective_id=2, has_side_effects=True, vmem_limit_bytes=62 << 20
        ),
        cost_estimate=pl.CostEstimate(
            flops=16 * tokens * 1024 * 1024, bytes_accessed=30 << 20, transcendentals=0
        ),
        name="time_mix_weights",
    )(*operands)


def one_micro(block_in, seg_ids, grad_out, vectors, matrices, hidden_w, return_w):
    (
        gain_one,
        bias_one,
        decay_vec,
        extra_array,
        mix_key,
        mix_value,
        mix_recept,
        gain_two,
        bias_two,
        mix_hidden,
        mix_gate,
    ) = vectors
    key_w, value_w, recept_w, output_w, gate_w = matrices
    row_count = block_in.shape[0]
    model_width = block_in.shape[1]
    seg_float = seg_ids.astype(jnp.float32)
    normed_a, unit_a, inv_a = layer_norm(block_in, gain_one, bias_one)
    prev_row, prev_seg = from_behind((normed_a[-1:], seg_float[-1:]), "mp", 1)
    same_row = jnp.concatenate(
        [
            (seg_float[:1] == prev_seg).astype(jnp.float32),
            (seg_ids[1:] == seg_ids[:-1]).astype(jnp.float32),
        ]
    )
    same_col = same_row[:, None]
    shifted_a = jnp.concatenate([prev_row, normed_a[:-1]], axis=0) * same_col
    delta_a = normed_a - shifted_a
    low_key = reduced_precision(shifted_a + delta_a * mix_key)
    low_value = reduced_precision(shifted_a + delta_a * mix_value)
    low_recept = reduced_precision(shifted_a + delta_a * mix_recept)
    lookup_start = product(low_key, key_w)
    content_start = product(low_value, value_w)
    recept = jax.nn.sigmoid(product(low_recept, recept_w))
    feature_fading = jnp.exp(decay_vec)
    positions = jnp.arange(row_count, dtype=jnp.float32)[:, None]
    rising = jnp.exp(positions * feature_fading)
    falling = jnp.exp(-(positions - 1.0) * feature_fading)
    falling_zero = jnp.exp(-positions * feature_fading)
    raised_lookup = jnp.exp(lookup_start)
    weighted_average = raised_lookup * content_start
    order_rows = jnp.arange(row_count)
    lower_tri = jnp.logical_and(
        seg_ids[:, None] == seg_ids[None, :], order_rows[None, :] < order_rows[:, None]
    ).astype(jnp.float32)
    last_mask = (seg_ids == seg_ids[-1]).astype(jnp.float32)
    first_mask = (seg_ids == seg_ids[0]).astype(jnp.float32) * same_row[0]
    forward_mat = jnp.concatenate([lower_tri, last_mask[None]], axis=0)
    stacked = jnp.concatenate(
        [
            rising * weighted_average,
            rising * raised_lookup,
            positions * rising * weighted_average,
            positions * rising * raised_lookup,
        ],
        axis=1,
    )
    summed = jnp.dot(forward_mat, stacked, precision=HIGH)
    inner_sums = summed[:row_count]
    closing = summed[row_count]
    num_loc = falling * inner_sums[:, :model_width]
    den_loc = falling * inner_sums[:, model_width : 2 * model_width]
    num_der = (
        -(positions - 1.0) * num_loc + falling * inner_sums[:, 2 * model_width : 3 * model_width]
    )
    den_der = -(positions - 1.0) * den_loc + falling * inner_sums[:, 3 * model_width :]
    end_fall = jnp.exp(-(row_count - 1.0) * feature_fading)
    state_num = end_fall * closing[:model_width]
    state_den = end_fall * closing[model_width : 2 * model_width]
    state_num_der = (
        -(row_count - 1.0) * state_num + end_fall * closing[2 * model_width : 3 * model_width]
    )
    state_den_der = -(row_count - 1.0) * state_den + end_fall * closing[3 * model_width :]
    uniform_flag = (seg_ids[-1] == seg_ids[0]).astype(jnp.float32) * same_row[0]
    carry_pass = uniform_flag * jnp.exp(-row_count * feature_fading)
    carry_der = -row_count * carry_pass
    zero_vec = jnp.zeros_like(feature_fading)
    one_vec = jnp.ones_like(feature_fading)
    in_num, in_den, in_num_der, in_den_der, pass_total, pass_der = carried_in(
        (state_num, state_den, state_num_der, state_den_der, carry_pass, carry_der),
        "mp",
        state_join,
        (zero_vec, zero_vec, zero_vec, zero_vec, one_vec, zero_vec),
        False,
    )
    carried = first_mask[:, None] * falling_zero
    dividend = num_loc + carried * in_num
    divisor_portion = den_loc + carried * in_den
    numer_der = num_der + carried * (in_num_der - positions * in_num)
    denom_der = den_der + carried * (in_den_der - positions * in_den)
    extra_summand = jnp.exp(extra_array + lookup_start)
    divisor_complete = divisor_portion + extra_summand
    mixture_result = (dividend + extra_summand * content_start) / divisor_complete
    gated = reduced_precision(recept * mixture_result)
    block_mid = block_in + product(gated, output_w)
    normed_b, unit_b, inv_b = layer_norm(block_mid, gain_two, bias_two)
    prev_mid = from_behind(normed_b[-1:], "mp", 1)
    shifted_b = jnp.concatenate([prev_mid, normed_b[:-1]], axis=0) * same_col
    delta_b = normed_b - shifted_b
    low_hidden = reduced_precision(shifted_b + delta_b * mix_hidden)
    low_gate = reduced_precision(shifted_b + delta_b * mix_gate)
    gate_two = jax.nn.sigmoid(product(low_gate, gate_w))
    hidden_rows = lax.all_gather(low_hidden, "mp", axis=0, tiled=True)
    pre_act = product(hidden_rows, hidden_w)
    rectified = jnp.maximum(pre_act, 0.0)
    squared = reduced_precision(rectified * rectified)
    returned = lax.psum_scatter(
        product(squared, return_w).astype(jnp.bfloat16), "mp", scatter_dimension=0, tiled=True
    ).astype(jnp.float32)
    output = block_mid + gate_two * returned
    grad_ret = reduced_precision(grad_out * gate_two)
    grad_gate_pre = reduced_precision(grad_out * returned * gate_two * (1.0 - gate_two))
    d_gate_w = (low_gate, grad_gate_pre)
    grad_low_gate = product_nt(grad_gate_pre, gate_w)
    grad_rows = lax.all_gather(grad_ret, "mp", axis=0, tiled=True)
    grad_squared = product_nt(grad_rows, return_w)
    d_return = (squared, grad_rows)
    grad_pre = reduced_precision(grad_squared * 2.0 * rectified)
    d_hidden = (hidden_rows, grad_pre)
    grad_low_hidden = lax.psum_scatter(
        product_nt(grad_pre, hidden_w).astype(jnp.bfloat16), "mp", scatter_dimension=0, tiled=True
    ).astype(jnp.float32)
    d_mix_hidden = jnp.sum(grad_low_hidden * delta_b, axis=0)
    d_mix_gate = jnp.sum(grad_low_gate * delta_b, axis=0)
    grad_shift_b = (
        grad_low_hidden * (1.0 - mix_hidden) + grad_low_gate * (1.0 - mix_gate)
    ) * same_col
    from_next_b = from_behind(grad_shift_b[:1], "mp", -1)
    grad_norm_b = (
        grad_low_hidden * mix_hidden
        + grad_low_gate * mix_gate
        + jnp.concatenate([grad_shift_b[1:], from_next_b], axis=0)
    )
    grad_mid_norm, d_gain_two, d_bias_two = norm_back(grad_norm_b, unit_b, inv_b, gain_two)
    grad_mid = grad_out + grad_mid_norm
    grad_att = reduced_precision(grad_mid)
    d_output_w = (gated, grad_att)
    grad_gated = product_nt(grad_att, output_w)
    grad_recept_pre = reduced_precision(grad_gated * mixture_result * recept * (1.0 - recept))
    grad_mixed = grad_gated * recept
    d_recept_w = (low_recept, grad_recept_pre)
    grad_low_recept = product_nt(grad_recept_pre, recept_w)
    dividend_adjoint = grad_mixed / divisor_complete
    divisor_adjoint = -dividend_adjoint * mixture_result
    extra_derivative_part = dividend_adjoint * content_start + divisor_adjoint
    extra_derivative = jnp.sum(extra_derivative_part * extra_summand, axis=0)
    d_rate = jnp.sum(dividend_adjoint * numer_der + divisor_adjoint * denom_der, axis=0)
    backward_mat = jnp.concatenate([lower_tri.T, first_mask[None]], axis=0)
    back_sum = jnp.dot(
        backward_mat,
        jnp.concatenate([falling * dividend_adjoint, falling * divisor_adjoint], axis=1),
        precision=HIGH,
    )
    step_back = jnp.exp(-feature_fading)
    from_num = step_back * back_sum[row_count, :model_width]
    from_den = step_back * back_sum[row_count, model_width:]
    out_num, out_den, out_pass = carried_in(
        (from_num, from_den, carry_pass), "mp", suffix_join, (zero_vec, zero_vec, one_vec), True
    )
    tail_fall = last_mask[:, None] * jnp.exp(-(row_count - 1.0 - positions) * feature_fading)
    cumulative_dividend = rising * back_sum[:row_count, :model_width] + tail_fall * out_num
    running_denominator = rising * back_sum[:row_count, model_width:] + tail_fall * out_den
    value_gradient = reduced_precision(
        dividend_adjoint * extra_summand + cumulative_dividend * raised_lookup
    )
    key_gradient = reduced_precision(
        extra_derivative_part * extra_summand
        + cumulative_dividend * weighted_average
        + running_denominator * raised_lookup
    )
    d_key_w = (low_key, key_gradient)
    d_value_w = (low_value, value_gradient)
    grad_low_key = product_nt(key_gradient, key_w)
    grad_low_value = product_nt(value_gradient, value_w)
    d_mix_key = jnp.sum(grad_low_key * delta_a, axis=0)
    d_mix_value = jnp.sum(grad_low_value * delta_a, axis=0)
    d_mix_recept = jnp.sum(grad_low_recept * delta_a, axis=0)
    grad_shift_a = (
        grad_low_key * (1.0 - mix_key)
        + grad_low_value * (1.0 - mix_value)
        + grad_low_recept * (1.0 - mix_recept)
    ) * same_col
    from_next_a = from_behind(grad_shift_a[:1], "mp", -1)
    grad_norm_a = (
        grad_low_key * mix_key
        + grad_low_value * mix_value
        + grad_low_recept * mix_recept
        + jnp.concatenate([grad_shift_a[1:], from_next_a], axis=0)
    )
    grad_in_norm, d_gain_one, d_bias_one = norm_back(grad_norm_a, unit_a, inv_a, gain_one)
    input_grad = grad_mid + grad_in_norm
    grads = (
        d_gain_one,
        d_bias_one,
        d_rate * feature_fading,
        extra_derivative,
        d_mix_key,
        d_mix_value,
        d_mix_recept,
        d_key_w,
        d_value_w,
        d_recept_w,
        d_output_w,
        d_gain_two,
        d_bias_two,
        d_mix_hidden,
        d_mix_gate,
        d_hidden,
        d_return,
        d_gate_w,
    )
    return (output, input_grad, grads)


def generic_body(
    incoming_signal,
    series_number_table,
    upstream_adjoint,
    first_scaling_factor,
    first_scaling_offset,
    logarithmic_fading_speeds,
    present_step_extra,
    lookup_shift_mixture,
    content_shift_mixture,
    admit_lookup_shift_mixture,
    attention_lookup_matrix,
    attention_content_matrix,
    attention_admit_matrix,
    attention_result_matrix,
    second_scaling_factor,
    second_scaling_offset,
    inner_shift_mixture,
    admit_shift_mixture,
    feedforward_lookup_matrix,
    feedforward_content_matrix,
    feedforward_admit_matrix,
):
    hidden_full, return_full = (feedforward_lookup_matrix, feedforward_content_matrix)
    vectors = tuple(
        (
            start_item.astype(jnp.float32)
            for start_item in (
                first_scaling_factor,
                first_scaling_offset,
                logarithmic_fading_speeds,
                present_step_extra,
                lookup_shift_mixture,
                content_shift_mixture,
                admit_lookup_shift_mixture,
                second_scaling_factor,
                second_scaling_offset,
                inner_shift_mixture,
                admit_shift_mixture,
            )
        )
    )
    matrices = (
        attention_lookup_matrix,
        attention_content_matrix,
        attention_admit_matrix,
        attention_result_matrix,
        feedforward_admit_matrix,
    )
    output, input_grad, grads = jax.vmap(
        lambda rows, ids, adjoint: one_micro(
            rows, ids, adjoint, vectors, matrices, hidden_full, return_full
        )
    )(
        incoming_signal[:, 0].astype(jnp.float32),
        series_number_table[:, 0],
        upstream_adjoint[:, 0].astype(jnp.float32),
    )
    totals = tuple(
        product_tn(*(side.reshape(-1, side.shape[-1]) for side in grad))
        if isinstance(grad, tuple)
        else jnp.sum(grad, axis=0)
        for grad in grads
    )
    square = [index for index in range(18) if totals[index].shape == totals[7].shape]
    lines = [index for index in range(18) if totals[index].ndim == 1]
    wide = lax.psum_scatter(
        jnp.concatenate([reduced_precision(totals[index]) for index in square], axis=1),
        ("dp", "mp"),
        scatter_dimension=0,
        tiled=True,
    ).astype(jnp.float32)
    thin = lax.psum_scatter(
        jnp.stack([totals[index] for index in lines], axis=1),
        ("dp", "mp"),
        scatter_dimension=0,
        tiled=True,
    )
    held = dict(zip(square, jnp.split(wide, len(square), axis=1)))
    held.update({index: thin[:, place] for place, index in enumerate(lines)})
    output, input_grad = (output[:, None], input_grad[:, None])
    owned = tuple(held[index] for index in sorted(held))
    hidden_own, return_own = (
        lax.psum_scatter(
            totals[15].astype(jnp.bfloat16), "dp", scatter_dimension=0, tiled=True
        ).astype(jnp.float32),
        lax.psum_scatter(
            totals[16].astype(jnp.bfloat16), "dp", scatter_dimension=1, tiled=True
        ).astype(jnp.float32),
    )
    return (
        output,
        input_grad,
        owned[0],
        owned[1],
        owned[2],
        owned[3],
        owned[4],
        owned[5],
        owned[6],
        owned[7],
        owned[8],
        owned[9],
        owned[10],
        owned[11],
        owned[12],
        owned[13],
        owned[14],
        hidden_own,
        return_own,
        owned[15],
    )


def hand_over(count, *refs):
    sems = refs[3 * count]
    ins, outs = ([], [])
    for index in range(count):
        held = refs[2 * count + index]
        ins.append(pltpu.make_async_copy(refs[index], held, sems.at[0, index]))
        outs.append(pltpu.make_async_copy(held, refs[count + index], sems.at[1, index]))
        ins[-1].start()
    for index in range(count):
        ins[index].wait()
        outs[index].start()
    for copy in outs:
        copy.wait()


def hand_call(arrays):
    count = len(arrays)
    return pl.pallas_call(
        functools.partial(hand_over, count),
        out_shape=[jax.ShapeDtypeStruct(part.shape, part.dtype) for part in arrays],
        in_specs=[ANY] * count,
        out_specs=[ANY] * count,
        scratch_shapes=[pltpu.VMEM(part.shape, part.dtype) for part in arrays]
        + [pltpu.SemaphoreType.DMA((2, count))],
        compiler_params=pltpu.CompilerParams(vmem_limit_bytes=60 << 20),
        name="hand_over",
    )(*arrays)


def kernel_body(
    incoming_signal,
    series_number_table,
    upstream_adjoint,
    first_scaling_factor,
    first_scaling_offset,
    logarithmic_fading_speeds,
    present_step_extra,
    lookup_shift_mixture,
    content_shift_mixture,
    admit_lookup_shift_mixture,
    attention_lookup_matrix,
    attention_content_matrix,
    attention_admit_matrix,
    attention_result_matrix,
    second_scaling_factor,
    second_scaling_offset,
    inner_shift_mixture,
    admit_shift_mixture,
    feedforward_lookup_matrix,
    feedforward_content_matrix,
    feedforward_admit_matrix,
):
    hidden_full, return_full = (feedforward_lookup_matrix, feedforward_content_matrix)
    matrices = (
        attention_lookup_matrix,
        attention_content_matrix,
        attention_admit_matrix,
        attention_result_matrix,
        feedforward_admit_matrix,
    )
    micros, _, rows, depth = incoming_signal.shape
    planes = lax.axis_size("mp") // 2
    x = incoming_signal.reshape(micros * rows, depth)
    adjoint = upstream_adjoint.reshape(micros * rows, depth)
    operands = (
        x,
        series_number_table.reshape(micros, rows),
        adjoint,
        first_scaling_factor,
        first_scaling_offset,
        logarithmic_fading_speeds,
        present_step_extra,
        lookup_shift_mixture,
        content_shift_mixture,
        admit_lookup_shift_mixture,
        second_scaling_factor,
        second_scaling_offset,
        inner_shift_mixture,
        admit_shift_mixture,
        *matrices,
        hidden_full,
        return_full,
    )
    (
        keys, values, recept, num, den, mid, gate, mk, mv, mr, gated, mg, delta_a, delta_b,
        keep, segs, table, segcol, segrow, mh_all, ret_all, w1_all, w2_all, ret_acc, gmh_acc,
        parts1, parts2,
    ) = forward_call(planes, micros, rows, operands)
    key_w, value_w, recept_w, output_w, gate_w = matrices
    (
        output, grad_mid, grad_gate, grad_att, grad_recept, grad_key, grad_value, sums,
        part1, part2, rest1, rest2, squares,
    ) = middle_call(
        planes,
        micros,
        rows,
        (
            table, keep, segs, segcol, segrow, w1_all, w2_all, mh_all, ret_all, ret_acc, gmh_acc,
            parts1, parts2, mid, gate, adjoint, delta_b, keys, values, recept, num, den,
            gate_w, output_w, gated, mg,
        ),
    )
    (
        input_grad, sums, own_output, own_gate, own_recept, own_value, own_key, own_hidden,
        own_return,
    ) = last_call(
        planes,
        micros,
        rows,
        (
            table, keep, sums, squares, mr, grad_recept, mv, grad_value,
            mk, grad_key, recept_w, value_w, key_w, x, delta_a, grad_mid,
            part1, part2, rest1, rest2,
        ),
    )
    (
        output, input_grad, own_key, own_value, own_recept, own_output, own_hidden, own_return,
        own_gate,
    ) = hand_call(
        (
            output, input_grad, own_key, own_value, own_recept, own_output, own_hidden,
            own_return, own_gate,
        )
    )
    span = depth // (lax.axis_size("dp") * lax.axis_size("mp"))
    mine = lax.dynamic_slice_in_dim(
        sums, lax.axis_index(("dp", "mp")) * span, span, axis=1
    )
    line = [mine[index] for index in range(11)]
    shape = incoming_signal.shape
    return (
        output.reshape(shape),
        input_grad.reshape(shape),
        *line[:7],
        own_key,
        own_value,
        own_recept,
        own_output,
        *line[7:],
        own_hidden,
        own_return,
        own_gate,
    )


def solution(mesh):
    placed = (
        P(None, "dp", "mp", None),
        P(None, "dp", "mp"),
        P(None, "dp", "mp", None),
        P(),
        P(),
        P(),
        P(),
        P(),
        P(),
        P(),
        P(),
        P(),
        P(),
        P(),
        P(),
        P(),
        P(),
        P(),
        P(None, "mp"),
        P("mp", None),
        P(),
    )
    fits = mesh.shape["dp"] == 4 and mesh.shape["mp"] == 8
    return jax.shard_map(
        kernel_body if fits else generic_body,
        mesh=mesh,
        in_specs=placed,
        out_specs=(
            P(None, "dp", "mp", None),
            P(None, "dp", "mp", None),
            P(("dp", "mp")),
            P(("dp", "mp")),
            P(("dp", "mp")),
            P(("dp", "mp")),
            P(("dp", "mp")),
            P(("dp", "mp")),
            P(("dp", "mp")),
            P(("dp", "mp"), None),
            P(("dp", "mp"), None),
            P(("dp", "mp"), None),
            P(("dp", "mp"), None),
            P(("dp", "mp")),
            P(("dp", "mp")),
            P(("dp", "mp")),
            P(("dp", "mp")),
            P("dp", "mp"),
            P("mp", "dp"),
            P(("dp", "mp"), None),
        ),
        check_vma=False,
    )
```

```python
import functools

import jax
import jax.numpy as jnp
from jax import lax
from jax.experimental import pallas as pl
from jax.experimental.pallas import tpu as pltpu
from jax.sharding import PartitionSpec as P

EPS = 1e-05
HIGH = lax.Precision.HIGHEST


def from_behind(block, axis, distance):
    devices = range(lax.axis_size(axis))
    route = [(i - distance, i) for i in devices if i - distance in devices]
    return lax.ppermute(block, axis, route)


def carried_in(shard, axis, combine, identity, reverse):
    length, mine = (lax.axis_size(axis), lax.axis_index(axis))
    everything = jax.tree.map(lambda part: lax.all_gather(part, axis), shard)
    start = jax.tree.map(
        lambda part, zero: jnp.broadcast_to(jnp.asarray(zero, part.dtype), part.shape),
        shard,
        identity,
    )

    def step(k, before):
        at = length - 1 - k if reverse else k
        reached = at > mine if reverse else at < mine
        new = combine(before, jax.tree.map(lambda part: part[at], everything))
        return jax.tree.map(lambda a, b: jnp.where(reached, a, b), new, before)

    return lax.fori_loop(0, length, step, start)


def reduced_precision(values):
    return values.astype(jnp.bfloat16)


def product(left, right):
    return jnp.dot(left, right, preferred_element_type=jnp.float32)


def product_tn(left, right):
    return lax.dot_general(
        left, right, (((0,), (0,)), ((), ())), preferred_element_type=jnp.float32
    )


def product_nt(left, right):
    return lax.dot_general(
        left, right, (((1,), (1,)), ((), ())), preferred_element_type=jnp.float32
    )


def layer_norm(values, gain, bias):
    average = jnp.mean(values, axis=-1, keepdims=True)
    centre = values - average
    inverse = lax.rsqrt(jnp.mean(centre * centre, axis=-1, keepdims=True) + EPS)
    unit = centre * inverse
    return (unit * gain + bias, unit, inverse)


def norm_back(grad_in, unit, inverse, gain):
    scaled = grad_in * gain
    grad_values = inverse * (
        scaled
        - jnp.mean(scaled, axis=-1, keepdims=True)
        - unit * jnp.mean(scaled * unit, axis=-1, keepdims=True)
    )
    return (grad_values, jnp.sum(grad_in * unit, axis=0), jnp.sum(grad_in, axis=0))


def state_join(earlier, latter):
    return (
        latter[4] * earlier[0] + latter[0],
        latter[4] * earlier[1] + latter[1],
        latter[4] * earlier[2] + latter[5] * earlier[0] + latter[2],
        latter[4] * earlier[3] + latter[5] * earlier[1] + latter[3],
        earlier[4] * latter[4],
        earlier[5] * latter[4] + earlier[4] * latter[5],
    )


def suffix_join(earlier, latter):
    return (
        latter[0] + latter[2] * earlier[0],
        latter[1] + latter[2] * earlier[1],
        latter[2] * earlier[2],
    )


BF = jnp.bfloat16
F32 = jnp.float32
MESH = pl.DeviceIdType.MESH
NN = (((1,), (0,)), ((), ()))
NT = (((1,), (1,)), ((), ()))
TN = (((0,), (0,)), ((), ()))


def dot(left, right, form=NN):
    return lax.dot_general(left, right, form, preferred_element_type=F32)


def dot_exact_left(left, right):
    high = right.astype(BF)
    rest = (right - high.astype(F32)).astype(BF)
    return dot(left, high) + dot(left, rest)


def wide(lanes, width):
    return jnp.concatenate([lanes] * (width // 128), axis=1)


def tile(index, size):
    return pl.ds(pl.multiple_of(index * size, size), size)


def unit_of(values):
    average = jnp.mean(values, axis=-1, keepdims=True)
    centre = values - average
    inverse = lax.rsqrt(jnp.mean(centre * centre, axis=-1, keepdims=True) + EPS)
    return (centre * inverse, inverse)


def remote(source, target, send, receive, device):
    return pltpu.make_async_remote_copy(
        src_ref=source,
        dst_ref=target,
        send_sem=send,
        recv_sem=receive,
        device_id=device,
        device_id_type=MESH,
    )


class Place:
    def __init__(self, planes):
        self.planes = planes
        self.dp, self.mp = (lax.axis_index("dp"), lax.axis_index("mp"))
        self.z = lax.div(self.mp, 2)
        self.core = lax.rem(self.mp, 2)
        self.count = 2 * planes
        self.other = (self.dp, self.mp + 1 - 2 * self.core)
        self.side_x = (self.dp + 1 - 2 * lax.rem(self.dp, 2), self.mp)
        self.side_y = (lax.rem(self.dp + 2, 4), self.mp)

    def ahead(self, steps):
        return (self.dp, lax.rem(self.mp + steps + self.count, self.count))

    def plane(self, steps):
        return (self.dp, lax.rem(self.z + steps + self.planes, self.planes) * 2 + self.core)


def greet(devices):
    barrier = pltpu.get_barrier_semaphore()
    for device in devices:
        pl.semaphore_signal(barrier, inc=1, device_id=device, device_id_type=MESH)
    pl.semaphore_wait(barrier, len(devices))


def feed_rows(w1, w2, mh2, gr2, sq_s, gp_s, ret_acc, gmh_acc, fresh):
    def rows_of(i):
        span = tile(i, 256)
        pre = dot(mh2[span, :], w1[...])
        rectified = jnp.maximum(pre, 0.0)
        squared = (rectified * rectified).astype(BF)
        sq_s[span, :] = squared
        grad_squared = dot(gr2[span, :], w2[...], NT)
        grad_pre = (grad_squared * 2.0 * rectified).astype(BF)
        gp_s[span, :] = grad_pre
        if fresh:
            ret_acc[span, :] = dot(squared, w2[...])
            gmh_acc[span, :] = dot(grad_pre, w1[...], NT)
        else:
            ret_acc[span, :] += dot(squared, w2[...])
            gmh_acc[span, :] += dot(grad_pre, w1[...], NT)

    return rows_of


def feed_grads(mh2, gr2, sq_s, gp_s, parts1, parts2):
    @pl.loop(0, 4)
    def _(q):
        line, side = (lax.div(q, 2), lax.rem(q, 2))
        cols = tile(q, 256)
        parts1[side, line] = dot(mh2[:, cols], gp_s[...], TN).astype(BF)
        parts2[line, side] = dot(gr2[:, cols], sq_s[...], TN).astype(BF)


def forward_kernel(
    planes,
    micros,
    rows,
    x_ref,
    table_ref,
    adj_ref,
    *refs,
):
    (
    lines, refs) = (refs[:11], refs[11:])
    (
    key_w,
    value_w,
    recept_w,
    output_w,
    gate_w,
    w1_ref,
    w2_ref,
    k_out,
    v_out,
    r_out,
    num_out,
    den_out,
    mid_out,
    gate_out,
    mk_out,
    mv_out,
    mr_out,
    gated_out,
    mg_out,
    da_out,
    db_out,
    keep_out,
    segs_out,
    vec_out,
    segcol_out,
    segrow_out,
    mh_all,
    ret_all,
    w1_all,
    w2_all,
    ret_acc_out,
    gmh_acc_out,
    parts1_out,
    parts2_out,
    wk,
    wv,
    wr,
    wo,
    wg,
    k_s,
    v_s,
    r_s,
    num_s,
    den_s,
    mid_s,
    gate_s,
    xb_s,
    da_s,
    mk_s,
    mv_s,
    mr_s,
    gated_s,
    mg_s,
    keep_s,
    segcol_ref,
    segrow_ref,
    segpay_ref,
    last_ref,
    mask_s,
    halo_a,
    near_a,
    pay_b,
    halo_b,
    segs_s,
    state_own,
    state_other,
    state_chip,
    state_in,
    carry_s,
    w_sem,
    out_sem,
    small_sem,
    z_sem,
    s_sem,
    vec_ref,
    mh2,
    gr2,
    sq_s,
    gp_s,
    ret_acc,
    gmh_acc,
    parts1,
    parts2,
    ff_sem,
    ) = refs
    at = Place(planes)
    dp, mp, z, core = (at.dp, at.mp, at.z, at.core)
    tokens = micros * rows
    peers = [at.ahead(step) for step in range(1, at.count)]
    greet(peers + [at.side_x, at.side_y])

    for index, line in enumerate(lines):
        vec_ref[index : index + 1, :] = line[...].astype(F32).reshape(1, 1024)
    vec_ref[11:16, :] = jnp.zeros((5, 1024), F32)

    numbers = table_ref[...].astype(F32)
    rest = jnp.zeros((8 - micros, rows), F32)
    segrow_ref[...] = jnp.concatenate([numbers, rest], axis=0)
    columns = segrow_ref[...].T
    ends = [jnp.broadcast_to(numbers[:, at_end], (micros, 128)) for at_end in (slice(rows - 1, rows), slice(0, 1))]
    segpay_ref[...] = jnp.concatenate([ends[0], ends[0], ends[1], ends[1]], axis=0)
    last_ref[...] = jnp.zeros((8, 1024), F32)
    for m in range(micros):
        segcol_ref[m * rows : (m + 1) * rows, :] = jnp.broadcast_to(columns[:, m : m + 1], (rows, 128))
        last_ref[m : m + 1, :] = x_ref[(m + 1) * rows - 16 : (m + 1) * rows, :].astype(F32)[15:16]

    quarter1, quarter2 = (w1_ref.shape[0] // 4, w2_ref.shape[0] // 4)
    q1, q2 = (tile(dp, quarter1), tile(dp, quarter2))
    z_copies = {}
    for step in (1, planes - 1):
        to = at.plane(-step)
        z_copies[step - 1] = (
            remote(w1_ref.at[q1], w1_all.at[step - 1, q1], z_sem.at[step - 1, 0, 0], z_sem.at[step - 1, 0, 1], to),
            remote(w2_ref.at[q2], w2_all.at[step - 1, q2], z_sem.at[step - 1, 1, 0], z_sem.at[step - 1, 1, 1], to),
        )
    half1 = tile(lax.div(dp, 2), 2 * quarter1)
    far2 = tile(lax.rem(dp + 2, 4), quarter2)
    back = at.plane(-1)
    onward_1 = remote(w1_all.at[0, half1], w1_all.at[1, half1], z_sem.at[1, 0, 0], z_sem.at[1, 0, 1], back)
    onward_2 = (
        remote(w2_all.at[0, q2], w2_all.at[1, q2], z_sem.at[1, 1, 0], z_sem.at[1, 1, 1], back),
        remote(w2_all.at[0, far2], w2_all.at[1, far2], z_sem.at[1, 2, 0], z_sem.at[1, 2, 1], back),
    )

    halo_copy = remote(last_ref, halo_a, small_sem.at[0, 0], small_sem.at[0, 1], at.ahead(1))
    halo_copy.start()
    seg_copies = [
        remote(segpay_ref, segs_s.at[mp], small_sem.at[1 + step, 0], small_sem.at[1 + step, 1], device)
        for step, device in enumerate(peers)
    ]
    for copy in seg_copies:
        copy.start()
    segs_s[mp] = segpay_ref[...]
    loads = []
    for index, (source, target) in enumerate(
        ((key_w, wk), (value_w, wv), (recept_w, wr), (output_w, wo), (gate_w, wg))
    ):
        loads.append(pltpu.make_async_copy(source, target, w_sem.at[index]))
        loads[-1].start()
    for copy in z_copies[0]:
        copy.start()
    halo_copy.wait()
    for copy in seg_copies:
        copy.wait()

    def along(step):
        group = []
        own1, own2 = (w1_all.at[step, q1], w2_all.at[step, q2])
        return (
            remote(own1, own1, z_sem.at[step, 2, 0], z_sem.at[step, 2, 1], at.side_x),
            remote(own2, own2, z_sem.at[step, 3, 0], z_sem.at[step, 3, 1], at.side_y),
        )

    def across(step):
        both1 = w1_all.at[step, half1]
        own2 = w2_all.at[step, q2]
        next2 = w2_all.at[step, far2]
        return (
            remote(both1, both1, z_sem.at[step, 4, 0], z_sem.at[step, 4, 1], at.side_y),
            remote(own2, own2, z_sem.at[step, 5, 0], z_sem.at[step, 5, 1], at.side_x),
            remote(next2, next2, z_sem.at[step, 6, 0], z_sem.at[step, 6, 1], at.side_x),
        )

    def start(group):
        for copy in group:
            copy.start()

    def finish(group):
        for copy in group:
            copy.wait()

    along_0, along_2 = (along(0), along(2))
    across_0, across_1, across_2 = (across(0), across(1), across(2))

    before = lax.rem(mp + at.count - 1, at.count)
    has_before = mp > 0
    first_row = lax.broadcasted_iota(jnp.int32, (rows, 128), 0) == 0
    row_at = lax.broadcasted_iota(jnp.int32, (rows, rows), 0)
    col_at = lax.broadcasted_iota(jnp.int32, (rows, rows), 1)
    for m in range(micros):
        here = segcol_ref[m * rows : (m + 1) * rows, :]
        behind = jnp.where(
            first_row, segs_s[before, m : m + 1, :], pltpu.roll(here, 1, 0)
        )
        same = jnp.logical_and(
            here == behind, jnp.logical_or(jnp.logical_not(first_row), has_before)
        )
        keep_s[m * rows : (m + 1) * rows, :] = same.astype(F32)
        mask_s[m] = jnp.logical_and(
            here == segrow_ref[m : m + 1, :], col_at < row_at
        ).astype(F32).astype(BF)

    block = 32
    at_first = lax.broadcasted_iota(jnp.int32, (block, 1024), 0) == 0
    gain, bias = (vec_ref[0:1, :], vec_ref[1:2, :])
    near_a[...] = unit_of(halo_a[...])[0] * gain + bias
    for m in range(micros):

        def mix_a(b, prev, m=m):
            span = tile(m * (rows // block) + b, block)
            normed = unit_of(x_ref[span, :].astype(F32))[0] * gain + bias
            shifted = jnp.where(at_first, prev, pltpu.roll(normed, 1, 0)) * wide(
                keep_s[span, :], 1024
            )
            delta = normed - shifted
            da_s[span, :] = delta
            mk_s[span, :] = (shifted + delta * vec_ref[4:5, :]).astype(BF)
            mv_s[span, :] = (shifted + delta * vec_ref[5:6, :]).astype(BF)
            mr_s[span, :] = (shifted + delta * vec_ref[6:7, :]).astype(BF)
            return normed[block - 1 : block, :]

        lax.fori_loop(0, rows // block, mix_a, near_a[m : m + 1, :], unroll=2)

    outs = []

    def put(source, target):
        copy = pltpu.make_async_copy(source, target, out_sem.at[len(outs)])
        copy.start()
        outs.append(copy)

    put(da_s, da_out)
    put(keep_s, keep_out)
    put(segs_s, segs_out)
    put(segcol_ref, segcol_out)
    put(vec_ref, vec_out)
    put(segrow_ref, segrow_out)
    put(mk_s, mk_out)
    put(mv_s, mv_out)
    put(mr_s, mr_out)

    loads[0].wait()
    loads[1].wait()
    width = 256
    place = lax.broadcasted_iota(jnp.int32, (rows, width), 0).astype(F32)

    @pl.loop(0, 1024 // width)
    def _(i):
        cols = tile(i, width)
        rate = jnp.exp(vec_ref[2:3, cols])
        rising = jnp.exp(place * rate)
        falling = jnp.exp((1.0 - place) * rate)
        step_back = jnp.exp(-rate)
        keys = dot(mk_s[...], wk[:, cols])
        values = dot(mv_s[...], wv[:, cols])
        for m in range(micros):
            span = slice(m * rows, (m + 1) * rows)
            key, value = (keys[span], values[span])
            raised = jnp.exp(key)
            weighted = raised * value
            num = falling * dot_exact_left(mask_s[m], rising * weighted)
            den = falling * dot_exact_left(mask_s[m], rising * raised)
            k_s[span, cols] = key
            v_s[span, cols] = value
            num_s[span, cols] = num
            den_s[span, cols] = den
            state_own[m : m + 1, cols] = step_back * num[rows - 1 :] + weighted[rows - 1 :]
            state_own[micros + m : micros + m + 1, cols] = (
                step_back * den[rows - 1 :] + raised[rows - 1 :]
            )

    put(k_s, k_out)
    put(v_s, v_out)
    core_copy = remote(state_own, state_other, s_sem.at[0, 0], s_sem.at[0, 1], at.other)
    core_copy.start()
    finish(z_copies[0])
    start(along_0)
    z_copies[2][0].start()

    loads[2].wait()

    @pl.loop(0, 2)
    def _(i):
        span = tile(i, tokens // 2)
        r_s[span, :] = jax.nn.sigmoid(dot(mr_s[span, :], wr[...]))

    put(r_s, r_out)

    pair = lax.div(mp, 2) * 2
    decay_all = jnp.exp(-float(rows) * jnp.exp(vec_ref[2:3, :]))
    core_copy.wait()

    def last_of(device):
        return wide(segs_s[lax.rem(device + at.count, at.count), 0 : 2 * micros, :], 1024)

    even = jnp.where(core == 0, state_own[...], state_other[...])
    odd = jnp.where(core == 0, state_other[...], state_own[...])
    state_chip[...] = odd + jnp.where(last_of(pair) == last_of(pair + 1), decay_all * even, 0.0)
    chip_copies = [
        remote(state_chip, state_in.at[step - 1], s_sem.at[step, 0], s_sem.at[step, 1], at.plane(step))
        for step in range(1, planes)
    ]
    start(chip_copies)
    finish(chip_copies)
    z_copies[2][1].start()
    finish(along_0)
    start(across_0)
    total = jnp.zeros_like(state_chip[...])
    power = jnp.ones_like(decay_all)
    for step in range(1, planes):
        fits = jnp.logical_and(
            last_of(pair - 2 * step + 1) == last_of(pair - 1), z >= step
        )
        total = total + jnp.where(fits, power * state_in[step - 1], 0.0)
        power = power * decay_all * decay_all
    joined = state_other[...] + jnp.where(last_of(pair) == last_of(pair - 1), decay_all * total, 0.0)
    carry_s[...] = jnp.where(core == 0, total, joined)

    @pl.loop(0, 1024 // width)
    def _(i):
        cols = tile(i, width)
        rate = jnp.exp(vec_ref[2:3, cols])
        falling = jnp.exp(-place * rate)
        extra = vec_ref[3:4, cols]
        for m in range(micros):
            span = slice(m * rows, (m + 1) * rows)
            fits = jnp.logical_and(
                segcol_ref[span, :] == segs_s[before, m : m + 1, :], has_before
            ).astype(F32)
            carried = wide(fits, width) * falling
            num = num_s[span, cols] + carried * carry_s[m : m + 1, cols]
            den = den_s[span, cols] + carried * carry_s[micros + m : micros + m + 1, cols]
            bonus = jnp.exp(extra + k_s[span, cols])
            mixed = (num + bonus * v_s[span, cols]) / (den + bonus)
            num_s[span, cols] = num
            den_s[span, cols] = den
            gated_s[span, cols] = (r_s[span, cols] * mixed).astype(BF)

    put(num_s, num_out)
    put(den_s, den_out)
    put(gated_s, gated_out)
    loads[3].wait()

    @pl.loop(0, 2)
    def _(i):
        span = tile(i, tokens // 2)
        mid_s[span, :] = x_ref[span, :].astype(F32) + dot(gated_s[span, :], wo[...])

    put(mid_s, mid_out)
    gain_b, bias_b = (vec_ref[7:8, :], vec_ref[8:9, :])

    def norm_b(b):
        span = tile(b, block)
        xb_s[span, :] = unit_of(mid_s[span, :])[0] * gain_b + bias_b

    for m in range(micros):
        norm_b((m + 1) * (rows // block) - 1)
        pay_b[m : m + 1, :] = xb_s[(m + 1) * rows - 1 : (m + 1) * rows, :]
    pay_b[micros:, :] = jnp.zeros((8 - micros, 1024), F32)
    halo_b_copy = remote(pay_b, halo_b, s_sem.at[planes, 0], s_sem.at[planes, 1], at.ahead(1))
    halo_b_copy.start()
    for m in range(micros):

        @pl.loop(m * (rows // block), (m + 1) * (rows // block) - 1)
        def _(b):
            norm_b(b)

    halo_b_copy.wait()
    onward_1.start()
    start(onward_2)
    finish(z_copies[2])
    start(along_2)
    for m in range(micros):

        def mix_b(b, prev, m=m):
            span = tile(m * (rows // block) + b, block)
            normed = xb_s[span, :]
            shifted = jnp.where(at_first, prev, pltpu.roll(normed, 1, 0)) * wide(
                keep_s[span, :], 1024
            )
            delta = normed - shifted
            xb_s[span, :] = delta
            mh2[span, :] = (shifted + delta * vec_ref[9:10, :]).astype(BF)
            mg_s[span, :] = (shifted + delta * vec_ref[10:11, :]).astype(BF)
            return normed[block - 1 : block, :]

        lax.fori_loop(0, rows // block, mix_b, halo_b[m : m + 1, :], unroll=2)

    own, far = (slice(0, tokens), slice(tokens, 2 * tokens))
    mh_copy = remote(
        mh2.at[own], mh2.at[far], s_sem.at[planes + 1, 0], s_sem.at[planes + 1, 1], at.other
    )
    mh_copy.start()
    put(mg_s, mg_out)
    put(xb_s, db_out)
    loads[4].wait()

    @pl.loop(0, 2)
    def _(i):
        span = tile(i, tokens // 2)
        gate = jax.nn.sigmoid(dot(mg_s[span, :], wg[...]))
        gate_s[span, :] = gate
        gr2[span, :] = (adj_ref[span, :].astype(F32) * gate).astype(BF)

    ret_copy = remote(
        gr2.at[own], gr2.at[far], s_sem.at[planes + 2, 0], s_sem.at[planes + 2, 1], at.other
    )
    ret_copy.start()
    put(gate_s, gate_out)
    hidden = w1_ref.shape[1]
    w1_own, w2_own = (wk.at[:, 0:hidden], wv.at[0:hidden])
    w1_next, w2_next = (wk.at[:, hidden : 2 * hidden], wv.at[hidden : 2 * hidden])
    ff_loads = [
        pltpu.make_async_copy(source, target, ff_sem.at[index])
        for index, (source, target) in enumerate(
            ((w1_ref, w1_own), (w2_ref, w2_own), (w1_all.at[0], w1_next), (w2_all.at[0], w2_next))
        )
    ]
    ff_loads[0].start()
    ff_loads[1].start()
    ff_loads[0].wait()
    ff_loads[1].wait()
    half = tokens // 256
    step = feed_rows(w1_own, w2_own, mh2, gr2, sq_s, gp_s, ret_acc, gmh_acc, True)
    pl.loop(0, half)(step)
    mh_copy.wait()
    ret_copy.wait()
    finish(along_2)
    start(across_2)
    put(mh2, mh_all)
    put(gr2, ret_all)
    finish(across_0)
    ff_loads[2].start()
    ff_loads[3].start()
    pl.loop(half, 2 * half)(step)
    feed_grads(mh2, gr2, sq_s, gp_s, parts1.at[0], parts2.at[0])
    onward_1.wait()
    across_1[0].start()
    put(parts1.at[0], parts1_out.at[0])
    put(parts2.at[0], parts2_out.at[0])
    ff_loads[2].wait()
    ff_loads[3].wait()
    step = feed_rows(w1_next, w2_next, mh2, gr2, sq_s, gp_s, ret_acc, gmh_acc, False)
    pl.loop(0, half)(step)
    onward_2[0].wait()
    across_1[1].start()
    pl.loop(half, 2 * half)(step)
    onward_2[1].wait()
    across_1[2].start()
    put(ret_acc, ret_acc_out)
    put(gmh_acc, gmh_acc_out)
    feed_grads(mh2, gr2, sq_s, gp_s, parts1.at[1], parts2.at[1])
    put(parts1.at[1], parts1_out.at[1])
    put(parts2.at[1], parts2_out.at[1])
    finish(across_2)
    finish(across_1)
    for copy in outs:
        copy.wait()


ANY = pl.BlockSpec(memory_space=pl.ANY)
VM = pl.BlockSpec(memory_space=pltpu.VMEM)


def forward_call(planes, micros, rows, operands):
    tokens = micros * rows
    hidden = operands[-1].shape[0]

    def big(kind):
        return jax.ShapeDtypeStruct((tokens, 1024), kind)

    def hold(kind):
        return pltpu.VMEM((tokens, 1024), kind)

    square = pltpu.VMEM((1024, 1024), BF)
    few = pltpu.VMEM((8, 1024), F32)
    pair = pltpu.SemaphoreType.DMA
    return pl.pallas_call(
        functools.partial(forward_kernel, planes, micros, rows),
        out_shape=[big(F32)] * 7
        + [big(BF)] * 5
        + [big(F32)] * 2
        + [
            jax.ShapeDtypeStruct((tokens, 128), F32),
            jax.ShapeDtypeStruct((2 * planes, 16, 128), F32),
            jax.ShapeDtypeStruct((16, 1024), F32),
            jax.ShapeDtypeStruct((tokens, 128), F32),
            jax.ShapeDtypeStruct((8, rows), F32),
        ]
        + [jax.ShapeDtypeStruct((2 * tokens, 1024), BF)] * 2
        + [
            jax.ShapeDtypeStruct((planes - 1, 1024, hidden), BF),
            jax.ShapeDtypeStruct((planes - 1, hidden, 1024), BF),
        ]
        + [jax.ShapeDtypeStruct((2 * tokens, 1024), F32)] * 2
        + [jax.ShapeDtypeStruct((2, 2, 2, 256, hidden), BF)] * 2,
        in_specs=[VM] * 14 + [ANY] * 7,
        out_specs=[ANY] * 27,
        scratch_shapes=[square] * 5
        + [hold(F32)] * 9
        + [hold(BF)] * 5
        + [
            pltpu.VMEM((tokens, 128), F32),
            pltpu.VMEM((tokens, 128), F32),
            pltpu.VMEM((8, rows), F32),
            pltpu.VMEM((4 * micros, 128), F32),
            few,
            pltpu.VMEM((micros, rows, rows), BF),
            few,
            few,
            few,
            few,
            pltpu.VMEM((2 * planes, 16, 128), F32),
            few,
            few,
            few,
            pltpu.VMEM((planes - 1, 8, 1024), F32),
            few,
            pair((5,)),
            pair((29,)),
            pair((2 * planes + 1, 2)),
            pair((planes - 1, 7, 2)),
            pair((planes + 3, 2)),
            pltpu.VMEM((16, 1024), F32),
            pltpu.VMEM((2 * tokens, 1024), BF),
            pltpu.VMEM((2 * tokens, 1024), BF),
            pltpu.VMEM((2 * tokens, hidden), BF),
            pltpu.VMEM((2 * tokens, hidden), BF),
            pltpu.VMEM((2 * tokens, 1024), F32),
            pltpu.VMEM((2 * tokens, 1024), F32),
            pltpu.VMEM((2, 2, 2, 256, hidden), BF),
            pltpu.VMEM((2, 2, 2, 256, hidden), BF),
            pair((4,)),
        ],
        compiler_params=pltpu.CompilerParams(
            collective_id=0, has_side_effects=True, vmem_limit_bytes=62 << 20
        ),
        cost_estimate=pl.CostEstimate(
            flops=36 * tokens * 1024 * 1024, bytes_accessed=40 << 20, transcendentals=6 * tokens * 1024
        ),
        name="time_mix_forward",
    )(*operands)


class Reduce:
    def __init__(self, at, parts, first, second, far, sems, slot, x_first, source=None):
        self.at, self.parts, self.slot = (at, parts, slot if far is not None else 0)
        side = lax.rem(at.dp, 2)
        line = lax.div(at.dp, 2)
        self.one, self.two = (side, line) if x_first else (line, side)
        near, next_to = (at.side_x, at.side_y) if x_first else (at.side_y, at.side_x)
        self.first, self.second, self.far = (first, second, far)
        self.copy_1 = remote(
            (parts if source is None else source).at[1 - self.one],
            first,
            sems.at[0, 0],
            sems.at[0, 1],
            near,
        )
        self.copy_2 = remote(
            parts.at[self.one, 1 - self.two], second, sems.at[1, 0], sems.at[1, 1], next_to
        )
        if self.slot:
            self.copy_3 = remote(
                parts.at[self.one, self.two], far, sems.at[2, 0], sems.at[2, 1], at.plane(slot)
            )

    def start(self):
        self.copy_1.start()

    def add(self, half, other):
        mine = self.parts.at[self.one, half]

        @pl.loop(0, mine.shape[0] // 64)
        def _(i):
            span = tile(i, 64)
            mine[span, :] = (mine[span, :].astype(F32) + other[span, :].astype(F32)).astype(BF)

    def middle(self):
        self.copy_1.wait()
        self.add(1 - self.two, self.first.at[1 - self.two])
        self.copy_2.start()
        self.add(self.two, self.first.at[self.two])

    def last(self):
        self.copy_2.wait()
        self.add(self.two, self.second)
        if self.slot:
            self.copy_3.start()

    def close(self):
        if self.slot:
            self.copy_3.wait()


def sum_rows(into, index, values):
    total = values[0:8]
    for start in range(8, values.shape[0], 8):
        total = total + values[start : start + 8]
    into[index] = into[index] + total


def norm_back_rows(grad, unit, inverse, gain):
    scaled = grad * gain
    return inverse * (
        scaled
        - jnp.mean(scaled, axis=-1, keepdims=True)
        - unit * jnp.mean(scaled * unit, axis=-1, keepdims=True)
    )


def fill_square(parts, left, right, planes, split):
    @pl.loop(0, 4)
    def _(q):
        line, side = (lax.div(q, 2), lax.rem(q, 2))
        made = dot(left[:, tile(q, 256)], right[...], TN).astype(BF)
        pieces = made.reshape(planes, 2, 256 // (2 * planes), 1024)
        for core in range(2):
            if split > 0:
                parts[core, side, line, :, :, 0:split] = pieces[:, core, :, 0:split]
            if split < 1024:
                parts[core, line, side, :, :, split:1024] = pieces[:, core, :, split:1024]


def add_square(mine, other, planes):
    for one in range(2):
        for two in range(2):

            @pl.loop(0, planes)
            def _(i):
                mine[one, two, i] = (
                    mine[one, two, i].astype(F32) + other[one, two, i].astype(F32)
                ).astype(BF)


def middle_kernel(
    planes,
    micros,
    rows,
    vec_ref,
    keep_ref,
    segs_ref,
    segcol_ref,
    segrow_ref,
    w1_all,
    w2_all,
    mh_all,
    ret_all,
    ret_acc_ref,
    gmh_acc_ref,
    parts1_ref,
    parts2_ref,
    mid_ref,
    gate_ref,
    adj_ref,
    db_ref,
    k_ref,
    v_ref,
    r_ref,
    num_ref,
    den_ref,
    gate_w,
    output_w,
    gated_ref,
    mg_ref,
    out_ref,
    gmid_out,
    ggp_out,
    gatt_out,
    grp_out,
    gk_out,
    gv_out,
    sums_out,
    own1_out,
    own2_out,
    rest1_out,
    rest2_out,
    square_out,
    parts1,
    parts2,
    first1,
    first2,
    second1,
    second2,
    far1,
    far2,
    ret_acc,
    gmh_acc,
    ret_send,
    gmh_send,
    ret_recv,
    gmh_recv,
    mid_s,
    gate_s,
    adj_s,
    db_s,
    sums_s,
    sums_flat,
    mask_s,
    pay_b,
    halo_b,
    state_own,
    state_other,
    state_chip,
    state_in,
    carry_s,
    load_sem,
    out_sem,
    rs_sem,
    s_sem,
    square_parts,
    square_across,
    square_sem,
    ahead_s,
    ahead_sem,
):
    at = Place(planes)
    dp, mp, z, core = (at.dp, at.mp, at.z, at.core)
    tokens = micros * rows
    hidden = w1_all.shape[2]
    outs = []

    def put(source, target):
        copy = pltpu.make_async_copy(source, target, out_sem.at[len(outs)])
        copy.start()
        outs.append(copy)

    loaded = []

    def load(source, target):
        copy = pltpu.make_async_copy(source, target, load_sem.at[len(loaded)])
        copy.start()
        loaded.append(copy)
        return copy

    greet(
        [at.other, at.side_x, at.side_y]
        + [at.plane(step) for step in range(1, planes)]
        + [at.ahead(1), at.ahead(-1)]
    )
    half_cols = hidden // 2
    early, late_half = (slice(0, half_cols), slice(half_cols, hidden))

    def group(slot, cols, sem, source):
        made = []
        for kind, (parts, first, second, far, parts_ref) in enumerate(
            (
                (parts1, first1, second1, far1, parts1_ref),
                (parts2, first2, second2, far2, parts2_ref),
            )
        ):
            made.append(
                Reduce(
                    at,
                    parts.at[slot, :, :, :, cols],
                    first.at[slot, :, :, cols],
                    second.at[slot, :, cols],
                    far.at[slot // 2, :, cols] if slot % 2 else None,
                    rs_sem.at[sem, kind],
                    slot,
                    kind == 0,
                    parts_ref.at[slot, :, :, :, cols] if source else None,
                )
            )
        return made

    everything = slice(0, hidden)
    reduces = {
        "near": group(1, late_half, 0, True),
        "own": group(0, late_half, 1, True),
        "joined": group(0, early, 2, False),
        3: group(3, everything, 3, False),
        2: group(2, everything, 4, False),
    }
    ahead_copies = [
        remote(
            parts_ref.at[1, :, :, :, early],
            ahead_s.at[kind],
            ahead_sem.at[kind, 0],
            ahead_sem.at[kind, 1],
            at.plane(1),
        )
        for kind, parts_ref in enumerate((parts1_ref, parts2_ref))
    ]
    ret_copy = remote(ret_send, ret_recv, s_sem.at[0, 0], s_sem.at[0, 1], at.other)
    gmh_copy = remote(gmh_send, gmh_recv, s_sem.at[1, 0], s_sem.at[1, 1], at.other)

    def begin(name):
        for reduce in reduces[name]:
            reduce.start()

    def middle(name):
        for reduce in reduces[name]:
            reduce.middle()

    def last(name):
        for reduce in reduces[name]:
            reduce.last()

    begin("near")
    begin("own")
    for copy in ahead_copies:
        copy.start()
    part_loads = []
    for slot in (1, 0):
        part_loads.append(
            (load(parts1_ref.at[slot], parts1.at[slot]), load(parts2_ref.at[slot], parts2.at[slot]))
        )
    acc_loads = [load(ret_acc_ref, ret_acc), load(gmh_acc_ref, gmh_acc)]

    def feed_forward(w1, w2, mh2, gr2, sq_s, gp_s):
        mh_load = [load(mh_all, mh2), load(ret_all, gr2)]
        order = (planes - 1, planes - 2)
        slots = [
            (load(w1_all.at[slot - 1], w1.at[index]), load(w2_all.at[slot - 1], w2.at[index]))
            for index, slot in enumerate(order)
        ]
        late = [load(mid_ref, mid_s), load(gate_ref, gate_s), load(adj_ref, adj_s), load(db_ref, db_s)]
        for copies in part_loads:
            for copy in copies:
                copy.wait()
        for copy in mh_load + acc_loads:
            copy.wait()
        half = tokens // 256
        for index, slot in enumerate(order):
            for copy in slots[index]:
                copy.wait()
            step = feed_rows(
                w1.at[index], w2.at[index], mh2, gr2, sq_s, gp_s, ret_acc, gmh_acc, False
            )
            pl.loop(half, 2 * half)(step)
            if index == 1:

                @pl.loop(0, tokens // 64)
                def _(i):
                    span = tile(i, 64)
                    far_span = tile(tokens // 64 + i, 64)
                    ret_send[span, :] = ret_acc[far_span, :].astype(BF)
                    gmh_send[span, :] = gmh_acc[far_span, :].astype(BF)

                ret_copy.start()
                gmh_copy.start()
            pl.loop(0, half)(step)
            feed_grads(mh2, gr2, sq_s, gp_s, parts1.at[slot], parts2.at[slot])
            if index == 0:
                middle("near")
                middle("own")
                begin(slot)
        for copy in late:
            copy.wait()

    pl.run_scoped(
        feed_forward,
        pltpu.VMEM((2, 1024, hidden), BF),
        pltpu.VMEM((2, hidden, 1024), BF),
        pltpu.VMEM((2 * tokens, 1024), BF),
        pltpu.VMEM((2 * tokens, 1024), BF),
        pltpu.VMEM((2 * tokens, hidden), BF),
        pltpu.VMEM((2 * tokens, hidden), BF),
    )
    own = slice(0, tokens)
    far = slice(tokens, 2 * tokens)
    block = 32

    def attention(k_s, v_s, r_s, num_s, den_s, wg, wo, ggp_s, gatt_s, grp_s, gk_s, gv_s):
        need_wg = load(gate_w, wg)
        need_wo = load(output_w, wo)
        need = [
            load(k_ref, k_s),
            load(v_ref, v_s),
            load(r_ref, r_s),
            load(num_ref, num_s),
            load(den_ref, den_s),
        ]
        sums_s[...] = jnp.zeros_like(sums_s)
        row_at = lax.broadcasted_iota(jnp.int32, (rows, rows), 0)
        col_at = lax.broadcasted_iota(jnp.int32, (rows, rows), 1)
        for m in range(micros):
            mask_s[m] = jnp.logical_and(
                segcol_ref[m * rows : (m + 1) * rows, :] == segrow_ref[m : m + 1, :],
                col_at > row_at,
            ).astype(F32).astype(BF)
        ret_copy.wait()
        need_gated = load(gated_ref, ret_send)

        @pl.loop(0, tokens // block)
        def _(b):
            span = tile(b, block)
            returned = ret_acc[span, :] + ret_recv[span, :].astype(F32)
            gate = gate_s[span, :]
            product_in = gate * returned
            ret_acc[span, :] = mid_s[span, :] + product_in
            ggp_s[span, :] = (adj_s[span, :].astype(F32) * product_in * (1.0 - gate)).astype(BF)

        put(ret_acc.at[own], out_ref)
        put(ggp_s, ggp_out)
        need_wg.wait()

        @pl.loop(0, 2)
        def _(i):
            span = tile(i, tokens // 2)
            ret_acc[tile(2 + i, tokens // 2), :] = dot(ggp_s[span, :], wg[...], NT)

        for kind, parts in enumerate((parts1, parts2)):
            ahead_copies[kind].wait()
            for one in range(2):
                for two in range(2):

                    @pl.loop(0, 4)
                    def _(i, kind=kind, parts=parts, one=one, two=two):
                        span = tile(i, 64)
                        parts[0, one, two, span, early] = (
                            parts[0, one, two, span, early].astype(F32)
                            + ahead_s[kind, one, two, span, :].astype(F32)
                        ).astype(BF)

        begin("joined")
        gmg = ret_acc.at[far]
        gmh_copy.wait()
        need_mg = load(mg_ref, gmh_send)
        mix_h, mix_g = (vec_ref[9:10, :], vec_ref[10:11, :])
        gain = vec_ref[7:8, :]

        def combine(b):
            span = tile(b, block)
            grad_h = gmh_acc[span, :] + gmh_recv[span, :].astype(F32)
            grad_g = gmg[span, :]
            shift = (grad_h * (1.0 - mix_h) + grad_g * (1.0 - mix_g)) * wide(keep_ref[span, :], 1024)
            return (span, grad_h, grad_g, shift)

        for m in range(micros):
            pay_b[m : m + 1, :] = combine(m * (rows // block))[3][0:1, :]
        pay_b[micros:, :] = jnp.zeros((8 - micros, 1024), F32)
        halo_copy = remote(pay_b, halo_b, s_sem.at[2, 0], s_sem.at[2, 1], at.ahead(-1))
        halo_copy.start()
        at_last = lax.broadcasted_iota(jnp.int32, (block, 1024), 0) == block - 1
        halo_copy.wait()
        last("near")
        last("own")
        for m in range(micros):

            def back_b(i, after, m=m):
                span, grad_h, grad_g, shift = combine((m + 1) * (rows // block) - 1 - i)
                delta = db_s[span, :]
                sum_rows(sums_s, 9, grad_h * delta)
                sum_rows(sums_s, 10, grad_g * delta)
                moved = jnp.where(at_last, after, pltpu.roll(shift, block - 1, 0))
                grad = grad_h * mix_h + grad_g * mix_g + moved
                unit, inverse = unit_of(mid_s[span, :])
                sum_rows(sums_s, 7, grad * unit)
                sum_rows(sums_s, 8, grad)
                total = adj_s[span, :].astype(F32) + norm_back_rows(grad, unit, inverse, gain)
                gmh_acc[span, :] = total
                gatt_s[span, :] = total.astype(BF)
                return shift[0:1, :]

            lax.fori_loop(0, rows // block, back_b, halo_b[m : m + 1, :], unroll=2)

        put(gmh_acc.at[own], gmid_out)
        put(gatt_s, gatt_out)
        need_wo.wait()

        @pl.loop(0, 2)
        def _(i):
            span = tile(i, tokens // 2)
            gmh_acc[tile(2 + i, tokens // 2), :] = dot(gatt_s[span, :], wo[...], NT)

        middle(3)
        begin(2)
        for copy in need:
            copy.wait()
        width = 256
        place = lax.broadcasted_iota(jnp.int32, (rows, width), 0).astype(F32)

        @pl.loop(0, 1024 // width)
        def _(i):
            cols = tile(i, width)
            rate = jnp.exp(vec_ref[2:3, cols])
            rising = jnp.exp(place * rate)
            falling = jnp.exp((1.0 - place) * rate)
            step_back = jnp.exp(-rate)
            extra = vec_ref[3:4, cols]
            for m in range(micros):
                span = slice(m * rows, (m + 1) * rows)
                far_span = slice(tokens + m * rows, tokens + (m + 1) * rows)
                bonus = jnp.exp(extra + k_s[span, cols])
                recept = r_s[span, cols]
                inverse = 1.0 / (den_s[span, cols] + bonus)
                mixed = (num_s[span, cols] + bonus * v_s[span, cols]) * inverse
                grad_gated = gmh_acc[far_span, cols]
                grad_mixed = grad_gated * recept
                grp_s[span, cols] = (grad_mixed * mixed * (1.0 - recept)).astype(BF)
                up = grad_mixed * inverse
                down = -up * mixed
                up_sum = rising * dot_exact_left(mask_s[m], falling * up)
                down_sum = rising * dot_exact_left(mask_s[m], falling * down)
                gmh_acc[far_span, cols] = up
                db_s[span, cols] = down
                mid_s[span, cols] = up_sum
                gate_s[span, cols] = down_sum
                state_own[m : m + 1, cols] = up[0:1] + step_back * up_sum[0:1]
                state_own[micros + m : micros + m + 1, cols] = down[0:1] + step_back * down_sum[0:1]

        put(grp_s, grp_out)
        core_copy = remote(state_own, state_other, s_sem.at[3, 0], s_sem.at[3, 1], at.other)
        core_copy.start()
        middle("joined")
        pair = lax.div(mp, 2) * 2
        decay_all = jnp.exp(-float(rows) * jnp.exp(vec_ref[2:3, :]))

        def seen(device, last):
            index = lax.rem(device + at.count, at.count)
            start = 0 if last else 2 * micros
            return wide(segs_ref[index, start : start + 2 * micros, :], 1024)

        core_copy.wait()
        even = jnp.where(core == 0, state_own[...], state_other[...])
        odd = jnp.where(core == 0, state_other[...], state_own[...])
        state_chip[...] = even + jnp.where(
            seen(pair, False) == seen(pair + 1, False), decay_all * odd, 0.0
        )
        chip_copies = [
            remote(state_chip, state_in.at[step - 1], s_sem.at[3 + step, 0], s_sem.at[3 + step, 1], at.plane(-step))
            for step in range(1, planes)
        ]
        for copy in chip_copies:
            copy.start()
        for copy in chip_copies:
            copy.wait()
        total = jnp.zeros_like(state_chip[...])
        power = jnp.ones_like(decay_all)
        for step in range(1, planes):
            fits = jnp.logical_and(
                seen(pair + 2 * step, False) == seen(mp, True), z + step < planes
            )
            total = total + jnp.where(fits, power * state_in[step - 1], 0.0)
            power = power * decay_all * decay_all
        joined = decay_all * total + jnp.where(
            seen(pair + 1, False) == seen(pair, True), state_other[...], 0.0
        )
        carry_s[...] = jnp.where(core == 0, joined, total)
        last(3)

        @pl.loop(0, 1024 // width)
        def _(i):
            cols = tile(i, width)
            rate = jnp.exp(vec_ref[2:3, cols])
            tail = jnp.exp((place - (rows - 1.0)) * rate)
            extra = vec_ref[3:4, cols]
            step_back = jnp.exp(-rate)
            for m in range(micros):
                span = slice(m * rows, (m + 1) * rows)
                far_span = slice(tokens + m * rows, tokens + (m + 1) * rows)
                fits = (segcol_ref[span, :] == segs_ref[mp, m : m + 1, :]).astype(F32)
                carried = wide(fits, width) * tail
                up_sum = mid_s[span, cols] + carried * carry_s[m : m + 1, cols]
                down_sum = gate_s[span, cols] + carried * carry_s[micros + m : micros + m + 1, cols]
                up, down = (gmh_acc[far_span, cols], db_s[span, cols])
                key, value = (k_s[span, cols], v_s[span, cols])
                bonus = jnp.exp(extra + key)
                raised = jnp.exp(key)
                direct = (up * value + down) * bonus
                gk_s[span, cols] = (direct + raised * (value * up_sum + down_sum)).astype(BF)
                gv_s[span, cols] = (up * bonus + raised * up_sum).astype(BF)
                rate_part = -rate * step_back * (up_sum * num_s[span, cols] + down_sum * den_s[span, cols])
                for index, part in ((2, rate_part), (3, direct)):
                    summed = part[0:8]
                    for start in range(8, rows, 8):
                        summed = summed + part[start : start + 8]
                    sums_s[index, :, cols] = sums_s[index, :, cols] + summed

        put(gk_s, gk_out)
        put(gv_s, gv_out)
        for index in range(16):
            sums_flat[index : index + 1, :] = jnp.sum(sums_s[index], axis=0, keepdims=True)
        put(sums_flat, sums_out)
        need_gated.wait()
        need_mg.wait()
        square_copies = []
        for index, (left, right) in enumerate(((ret_send, gatt_s), (gmh_send, ggp_s))):
            fill_square(square_parts.at[index], left, right, planes, 1024 * (1 - index))
            square_copies.append(
                remote(
                    square_parts.at[index, 1 - core],
                    square_across.at[index],
                    square_sem.at[index, 0],
                    square_sem.at[index, 1],
                    at.other,
                )
            )
            square_copies[index].start()
        for index in range(2):
            square_copies[index].wait()
            add_square(square_parts.at[index, core], square_across.at[index], planes)
            put(square_parts.at[index, core], square_out.at[index])
        middle(2)
        last("joined")
        for name in ("near", 3):
            for reduce in reduces[name]:
                reduce.close()
        for parts, far_parts, own_s, own_out, one, two in (
            (parts1, far1, mid_s, own1_out, lax.rem(dp, 2), lax.div(dp, 2)),
            (parts2, far2, gate_s, own2_out, lax.div(dp, 2), lax.rem(dp, 2)),
        ):
            total = parts[0, one, two].astype(F32) + far_parts[1].astype(F32)
            own_s[0:256, early] = total[:, early]
            own_s[0:256, late_half] = total[:, late_half] + far_parts[0, :, late_half].astype(F32)
            put(own_s.at[0:256, 0:hidden], own_out)
        last(2)
        put(parts1.at[2, lax.rem(dp, 2), lax.div(dp, 2)], rest1_out)
        put(parts2.at[2, lax.div(dp, 2), lax.rem(dp, 2)], rest2_out)
        for copy in outs:
            copy.wait()

    def hold(kind):
        return pltpu.VMEM((tokens, 1024), kind)

    square = pltpu.VMEM((1024, 1024), BF)
    pl.run_scoped(attention, *([hold(F32)] * 5), square, square, *([hold(BF)] * 5))


def middle_call(planes, micros, rows, operands):
    tokens = micros * rows
    hidden = operands[5].shape[2]

    def big(kind):
        return jax.ShapeDtypeStruct((tokens, 1024), kind)

    def hold(count, kind):
        return pltpu.VMEM((count, 1024), kind)

    few = hold(8, F32)
    quarter = (256, hidden)
    piece = (planes, 256 // (2 * planes), 1024)
    sems = pltpu.SemaphoreType.DMA
    return pl.pallas_call(
        functools.partial(middle_kernel, planes, micros, rows),
        out_shape=[big(F32)] * 2
        + [big(BF)] * 5
        + [jax.ShapeDtypeStruct((16, 1024), F32)]
        + [jax.ShapeDtypeStruct(quarter, F32)] * 2
        + [jax.ShapeDtypeStruct(quarter, BF)] * 2
        + [jax.ShapeDtypeStruct((2, 2, 2) + piece, BF)],
        in_specs=[VM] * 5 + [ANY] * 21,
        out_specs=[ANY] * 13,
        scratch_shapes=[pltpu.VMEM((planes, 2, 2) + quarter, BF)] * 2
        + [pltpu.VMEM((planes, 2) + quarter, BF)] * 2
        + [pltpu.VMEM((planes,) + quarter, BF)] * 2
        + [pltpu.VMEM((2,) + quarter, BF)] * 2
        + [hold(2 * tokens, F32)] * 2
        + [hold(tokens, BF)] * 4
        + [hold(tokens, F32), hold(tokens, F32), hold(tokens, BF), hold(tokens, F32)]
        + [
            pltpu.VMEM((16, 8, 1024), F32),
            pltpu.VMEM((16, 1024), F32),
            pltpu.VMEM((micros, rows, rows), BF),
            few,
            few,
            few,
            few,
            few,
            pltpu.VMEM((planes - 1, 8, 1024), F32),
            few,
            sems((25,)),
            sems((14,)),
            sems((planes + 1, 2, 3, 2)),
            sems((3 + planes, 2)),
            pltpu.VMEM((2, 2, 2, 2) + piece, BF),
            pltpu.VMEM((2, 2, 2) + piece, BF),
            sems((2, 2)),
            pltpu.VMEM((2, 2, 2, 256, hidden // 2), BF),
            sems((2, 2)),
        ],
        compiler_params=pltpu.CompilerParams(
            collective_id=1, has_side_effects=True, vmem_limit_bytes=63 << 20
        ),
        cost_estimate=pl.CostEstimate(
            flops=52 * tokens * 1024 * 1024, bytes_accessed=60 << 20, transcendentals=6 * tokens * 1024
        ),
        name="channel_mix_and_adjoint",
    )(*operands)


class ReduceSquare:
    def __init__(self, at, mine, first, second, far, sems, x_first, source=None):
        self.at, self.mine, self.first, self.second, self.far = (at, mine, first, second, far)
        side = lax.rem(at.dp, 2)
        line = lax.div(at.dp, 2)
        self.one, self.two = (side, line) if x_first else (line, side)
        near, next_to = (at.side_x, at.side_y) if x_first else (at.side_y, at.side_x)
        self.copy_1 = remote(
            (mine if source is None else source).at[1 - self.one],
            first,
            sems.at[0, 0],
            sems.at[0, 1],
            near,
        )
        self.copy_2 = remote(
            mine.at[self.one, 1 - self.two], second, sems.at[1, 0], sems.at[1, 1], next_to
        )
        self.copies_3 = [
            remote(
                mine.at[self.one, self.two, lax.rem(at.z + step, at.planes)],
                far.at[step - 1],
                sems.at[1 + step, 0],
                sems.at[1 + step, 1],
                at.plane(step),
            )
            for step in range(1, at.planes)
        ]

    def add(self, one, two, other):
        @pl.loop(0, self.at.planes)
        def _(i):
            self.mine[one, two, i] = (
                self.mine[one, two, i].astype(F32) + other[i].astype(F32)
            ).astype(BF)

    def begin(self):
        self.copy_1.start()

    def middle(self):
        self.copy_1.wait()
        self.add(self.one, 1 - self.two, self.first.at[1 - self.two])
        self.copy_2.start()
        self.add(self.one, self.two, self.first.at[self.two])

    def last(self):
        self.copy_2.wait()
        self.add(self.one, self.two, self.second)

    def send(self):
        for copy in self.copies_3:
            copy.start()

    def close(self):
        for copy in self.copies_3:
            copy.wait()
        total = self.mine[self.one, self.two, self.at.z].astype(F32)
        for step in range(self.at.planes - 1):
            total = total + self.far[step].astype(F32)
        return total


def last_kernel(
    planes,
    micros,
    rows,
    vec_ref,
    keep_ref,
    sums_ref,
    square_ref,
    mr_ref,
    grp_ref,
    mv_ref,
    gv_ref,
    mk_ref,
    gk_ref,
    recept_w,
    value_w,
    key_w,
    x_ref,
    da_ref,
    gmid_ref,
    part1_ref,
    part2_ref,
    rest1_ref,
    rest2_ref,
    grad_out,
    sums_out,
    own_output,
    own_gate,
    own_recept,
    own_value,
    own_key,
    own_hidden,
    own_return,
    left_s,
    right_s,
    w_s,
    x_s,
    da_s,
    total_s,
    g_s,
    sums_s,
    parts,
    across,
    first,
    second,
    far,
    own_s,
    pay_a,
    halo_a,
    flat_s,
    flat_recv,
    load_sem,
    out_sem,
    rs_sem,
    s_sem,
    ff_far,
    ff_total,
    own1_s,
    own2_s,
    ff_sem,
    ready_s,
    core_sem,
):
    at = Place(planes)
    tokens = micros * rows
    outs = []

    def put(source, target):
        copy = pltpu.make_async_copy(source, target, out_sem.at[len(outs)])
        copy.start()
        outs.append(copy)

    loaded = []

    def load(source, target):
        copy = pltpu.make_async_copy(source, target, load_sem.at[len(loaded)])
        copy.start()
        loaded.append(copy)
        return copy

    sides = (
        (mr_ref, grp_ref),
        (mv_ref, gv_ref),
        (mk_ref, gk_ref),
    )
    ready_load = load(square_ref, ready_s)
    side_loads = [
        (load(left, left_s.at[index]), load(right, right_s.at[index]))
        for index, (left, right) in enumerate(sides)
    ]
    w_loads = [
        load(source, w_s.at[index]) for index, source in enumerate((recept_w, value_w, key_w))
    ]
    row_loads = [load(x_ref, x_s), load(da_ref, da_s), load(gmid_ref, total_s)]
    greet(
        [at.other, at.side_x, at.side_y]
        + [at.plane(step) for step in range(1, planes)]
        + [at.ahead(1), at.ahead(-1)]
    )
    core = at.core
    lefts, rights = (slice(0, 512), slice(512, 1024))
    reduces = []
    for index, (cols, x_first) in enumerate(
        ((None, True), (None, False), (None, True), (None, False), (lefts, True), (rights, False))
    ):
        place = min(index, 4)
        mine = ready_s.at[index] if index < 2 else parts.at[place - 2, core]
        refs = (mine, first.at[place], second.at[place], far.at[place])
        if cols is not None:
            refs = (
                mine.at[:, :, :, :, cols],
                first.at[place, :, :, :, cols],
                second.at[place, :, :, cols],
                far.at[place, :, :, cols],
            )
        source = square_ref.at[index] if index < 2 else None
        reduces.append(ReduceSquare(at, *refs, rs_sem.at[index], x_first, source))
    core_copies = [
        remote(
            parts.at[index, 1 - core],
            across.at[index],
            core_sem.at[index, 0],
            core_sem.at[index, 1],
            at.other,
        )
        for index in range(3)
    ]
    ff_loads = [load(part1_ref, ff_total.at[0]), load(part2_ref, ff_total.at[1])]
    ff_copies = [
        remote(rest, ff_far.at[index], ff_sem.at[index, 0], ff_sem.at[index, 1], at.plane(2))
        for index, rest in enumerate((rest1_ref, rest2_ref))
    ]
    reduces[0].begin()
    reduces[1].begin()
    ready_load.wait()
    mixes = (vec_ref[6:7, :], vec_ref[5:6, :], vec_ref[4:5, :])
    heads = jnp.zeros((16 * micros, 1024), F32)
    for index in range(3):
        side_loads[index][1].wait()
        w_loads[index].wait()
        picked = jnp.concatenate(
            [right_s[index, m * rows : m * rows + 16, :] for m in range(micros)], axis=0
        )
        heads = heads + dot(picked, w_s[index], NT) * (1.0 - mixes[index])
    for m in range(micros):
        pay_a[m : m + 1, :] = heads[16 * m : 16 * m + 1] * wide(
            keep_ref[m * rows : m * rows + 8, :], 1024
        )[0:1]
    pay_a[micros:, :] = jnp.zeros((8 - micros, 1024), F32)
    halo_copy = remote(pay_a, halo_a, s_sem.at[0, 0], s_sem.at[0, 1], at.ahead(-1))
    halo_copy.start()
    for copy in ff_copies:
        copy.start()
    sums_s[...] = jnp.zeros_like(sums_s)

    def fill(index, split):
        side_loads[index][0].wait()
        fill_square(parts.at[index], left_s.at[index], right_s.at[index], planes, split)
        core_copies[index].start()

    def settle(index):
        core_copies[index].wait()
        add_square(parts.at[index, core], across.at[index], planes)

    def back(index):
        @pl.loop(0, 2)
        def _(i):
            span = tile(i, tokens // 2)
            g_s[index, span, :] = dot(right_s[index, span, :], w_s[index], NT)

    fill(0, 1024)
    fill(1, 0)
    settle(0)
    fill(2, 512)
    settle(1)
    back(0)
    reduces[0].middle()
    reduces[1].middle()
    reduces[2].begin()
    reduces[3].begin()
    settle(2)
    back(1)
    back(2)
    for copy in row_loads:
        copy.wait()
    block = 32
    gain = vec_ref[0:1, :]

    def combine(b):
        span = tile(b, block)
        grads = [g_s[index, span, :] for index in range(3)]
        shift = sum(grad * (1.0 - mix) for grad, mix in zip(grads, mixes))
        return (span, grads, shift * wide(keep_ref[span, :], 1024))

    at_last = lax.broadcasted_iota(jnp.int32, (block, 1024), 0) == block - 1
    halo_copy.wait()
    for index in range(2):
        reduces[index].last()
        reduces[index].send()
    for m in range(micros):

        def back_a(i, after, m=m):
            span, grads, shift = combine((m + 1) * (rows // block) - 1 - i)
            delta = da_s[span, :]
            for index, grad in enumerate(grads):
                sum_rows(sums_s, 2 - index, grad * delta)
            moved = jnp.where(at_last, after, pltpu.roll(shift, block - 1, 0))
            grad = sum(part * mix for part, mix in zip(grads, mixes)) + moved
            unit, inverse = unit_of(x_s[span, :].astype(F32))
            sum_rows(sums_s, 3, grad * unit)
            sum_rows(sums_s, 4, grad)
            total_s[span, :] = total_s[span, :] + norm_back_rows(grad, unit, inverse, gain)
            return shift[0:1, :]

        lax.fori_loop(0, rows // block, back_a, halo_a[m : m + 1, :], unroll=2)
    put(total_s, grad_out)
    flat_s[0] = sums_ref[...]
    for index, row in enumerate((4, 5, 6, 0, 1)):
        flat_s[0, row : row + 1, :] = jnp.sum(sums_s[index], axis=0, keepdims=True)

    def flat_copy(level, slot, device):
        return remote(
            flat_s.at[level], flat_recv.at[slot], s_sem.at[1 + slot, 0], s_sem.at[1 + slot, 1], device
        )

    over_core = flat_copy(0, 0, at.other)
    over_core.start()
    over_core.wait()
    flat_s[1] = flat_s[0] + flat_recv[0]
    over_x = flat_copy(1, 1, at.side_x)
    over_x.start()
    reduces[2].middle()
    reduces[3].middle()
    over_x.wait()
    flat_s[2] = flat_s[1] + flat_recv[1]
    over_y = flat_copy(2, 2, at.side_y)
    over_y.start()
    reduces[4].begin()
    reduces[5].begin()
    for index in range(2, 4):
        reduces[index].last()
        reduces[index].send()
    over_y.wait()
    flat_s[3] = flat_s[2] + flat_recv[2]
    flat_copies = [flat_copy(3, 2 + step, at.plane(step)) for step in range(1, planes)]
    for copy in flat_copies:
        copy.start()
    for copy in ff_loads + ff_copies:
        copy.wait()
    own1_s[...] = ff_total[0] + ff_far[0].astype(F32)
    own2_s[...] = (ff_total[1] + ff_far[1].astype(F32)).T
    put(own1_s, own_hidden)
    put(own2_s, own_return)
    reduces[4].middle()
    reduces[5].middle()
    for index in range(4, 6):
        reduces[index].last()
        reduces[index].send()
    for index, target in enumerate((own_output, own_gate, own_recept, own_value)):
        own_s[index] = reduces[index].close()
        put(own_s.at[index], target)
    for copy in flat_copies:
        copy.wait()
    flat_s[0] = flat_s[3] + sum(flat_recv[2 + step] for step in range(1, planes))
    put(flat_s.at[0], sums_out)
    own_s[4, :, lefts] = reduces[4].close()
    own_s[4, :, rights] = reduces[5].close()
    put(own_s.at[4], own_key)
    for copy in outs:
        copy.wait()


def last_call(planes, micros, rows, operands):
    tokens = micros * rows

    def hold(count, kind):
        return pltpu.VMEM((count, tokens, 1024), kind)

    quarter = operands[-4].shape
    piece = (1024 // (8 * planes), 1024)
    sems = pltpu.SemaphoreType.DMA
    few = pltpu.VMEM((8, 1024), F32)
    return pl.pallas_call(
        functools.partial(last_kernel, planes, micros, rows),
        out_shape=[
            jax.ShapeDtypeStruct((tokens, 1024), F32),
            jax.ShapeDtypeStruct((16, 1024), F32),
        ]
        + [jax.ShapeDtypeStruct(piece, F32)] * 5
        + [jax.ShapeDtypeStruct(quarter, F32), jax.ShapeDtypeStruct(quarter[::-1], F32)],
        in_specs=[VM] * 3 + [ANY] * 17,
        out_specs=[ANY] * 9,
        scratch_shapes=[
            hold(3, BF),
            hold(3, BF),
            pltpu.VMEM((3, 1024, 1024), BF),
            pltpu.VMEM((tokens, 1024), BF),
            pltpu.VMEM((tokens, 1024), F32),
            pltpu.VMEM((tokens, 1024), F32),
            hold(3, F32),
            pltpu.VMEM((5, 8, 1024), F32),
            pltpu.VMEM((3, 2, 2, 2, planes) + piece, BF),
            pltpu.VMEM((3, 2, 2, planes) + piece, BF),
            pltpu.VMEM((5, 2, planes) + piece, BF),
            pltpu.VMEM((5, planes) + piece, BF),
            pltpu.VMEM((5, planes - 1) + piece, BF),
            pltpu.VMEM((5,) + piece, F32),
            few,
            few,
            pltpu.VMEM((4, 16, 1024), F32),
            pltpu.VMEM((2 + planes, 16, 1024), F32),
            sems((18,)),
            sems((9,)),
            sems((6, 1 + planes, 2)),
            sems((3 + planes, 2)),
            pltpu.VMEM((2,) + quarter, BF),
            pltpu.VMEM((2,) + quarter, F32),
            pltpu.VMEM(quarter, F32),
            pltpu.VMEM(quarter[::-1], F32),
            sems((2, 2)),
            pltpu.VMEM((2, 2, 2, planes) + piece, BF),
            sems((3, 2)),
        ],
        compiler_params=pltpu.CompilerParams(
            collective_id=2, has_side_effects=True, vmem_limit_bytes=62 << 20
        ),
        cost_estimate=pl.CostEstimate(
            flops=16 * tokens * 1024 * 1024, bytes_accessed=30 << 20, transcendentals=0
        ),
        name="time_mix_weights",
    )(*operands)


def one_micro(block_in, seg_ids, grad_out, vectors, matrices, hidden_w, return_w):
    (
        gain_one,
        bias_one,
        decay_vec,
        extra_array,
        mix_key,
        mix_value,
        mix_recept,
        gain_two,
        bias_two,
        mix_hidden,
        mix_gate,
    ) = vectors
    key_w, value_w, recept_w, output_w, gate_w = matrices
    row_count = block_in.shape[0]
    model_width = block_in.shape[1]
    seg_float = seg_ids.astype(jnp.float32)
    normed_a, unit_a, inv_a = layer_norm(block_in, gain_one, bias_one)
    prev_row, prev_seg = from_behind((normed_a[-1:], seg_float[-1:]), "mp", 1)
    same_row = jnp.concatenate(
        [
            (seg_float[:1] == prev_seg).astype(jnp.float32),
            (seg_ids[1:] == seg_ids[:-1]).astype(jnp.float32),
        ]
    )
    same_col = same_row[:, None]
    shifted_a = jnp.concatenate([prev_row, normed_a[:-1]], axis=0) * same_col
    delta_a = normed_a - shifted_a
    low_key = reduced_precision(shifted_a + delta_a * mix_key)
    low_value = reduced_precision(shifted_a + delta_a * mix_value)
    low_recept = reduced_precision(shifted_a + delta_a * mix_recept)
    lookup_start = product(low_key, key_w)
    content_start = product(low_value, value_w)
    recept = jax.nn.sigmoid(product(low_recept, recept_w))
    feature_fading = jnp.exp(decay_vec)
    positions = jnp.arange(row_count, dtype=jnp.float32)[:, None]
    rising = jnp.exp(positions * feature_fading)
    falling = jnp.exp(-(positions - 1.0) * feature_fading)
    falling_zero = jnp.exp(-positions * feature_fading)
    raised_lookup = jnp.exp(lookup_start)
    weighted_average = raised_lookup * content_start
    order_rows = jnp.arange(row_count)
    lower_tri = jnp.logical_and(
        seg_ids[:, None] == seg_ids[None, :], order_rows[None, :] < order_rows[:, None]
    ).astype(jnp.float32)
    last_mask = (seg_ids == seg_ids[-1]).astype(jnp.float32)
    first_mask = (seg_ids == seg_ids[0]).astype(jnp.float32) * same_row[0]
    forward_mat = jnp.concatenate([lower_tri, last_mask[None]], axis=0)
    stacked = jnp.concatenate(
        [
            rising * weighted_average,
            rising * raised_lookup,
            positions * rising * weighted_average,
            positions * rising * raised_lookup,
        ],
        axis=1,
    )
    summed = jnp.dot(forward_mat, stacked, precision=HIGH)
    inner_sums = summed[:row_count]
    closing = summed[row_count]
    num_loc = falling * inner_sums[:, :model_width]
    den_loc = falling * inner_sums[:, model_width : 2 * model_width]
    num_der = (
        -(positions - 1.0) * num_loc + falling * inner_sums[:, 2 * model_width : 3 * model_width]
    )
    den_der = -(positions - 1.0) * den_loc + falling * inner_sums[:, 3 * model_width :]
    end_fall = jnp.exp(-(row_count - 1.0) * feature_fading)
    state_num = end_fall * closing[:model_width]
    state_den = end_fall * closing[model_width : 2 * model_width]
    state_num_der = (
        -(row_count - 1.0) * state_num + end_fall * closing[2 * model_width : 3 * model_width]
    )
    state_den_der = -(row_count - 1.0) * state_den + end_fall * closing[3 * model_width :]
    uniform_flag = (seg_ids[-1] == seg_ids[0]).astype(jnp.float32) * same_row[0]
    carry_pass = uniform_flag * jnp.exp(-row_count * feature_fading)
    carry_der = -row_count * carry_pass
    zero_vec = jnp.zeros_like(feature_fading)
    one_vec = jnp.ones_like(feature_fading)
    in_num, in_den, in_num_der, in_den_der, pass_total, pass_der = carried_in(
        (state_num, state_den, state_num_der, state_den_der, carry_pass, carry_der),
        "mp",
        state_join,
        (zero_vec, zero_vec, zero_vec, zero_vec, one_vec, zero_vec),
        False,
    )
    carried = first_mask[:, None] * falling_zero
    dividend = num_loc + carried * in_num
    divisor_portion = den_loc + carried * in_den
    numer_der = num_der + carried * (in_num_der - positions * in_num)
    denom_der = den_der + carried * (in_den_der - positions * in_den)
    extra_summand = jnp.exp(extra_array + lookup_start)
    divisor_complete = divisor_portion + extra_summand
    mixture_result = (dividend + extra_summand * content_start) / divisor_complete
    gated = reduced_precision(recept * mixture_result)
    block_mid = block_in + product(gated, output_w)
    normed_b, unit_b, inv_b = layer_norm(block_mid, gain_two, bias_two)
    prev_mid = from_behind(normed_b[-1:], "mp", 1)
    shifted_b = jnp.concatenate([prev_mid, normed_b[:-1]], axis=0) * same_col
    delta_b = normed_b - shifted_b
    low_hidden = reduced_precision(shifted_b + delta_b * mix_hidden)
    low_gate = reduced_precision(shifted_b + delta_b * mix_gate)
    gate_two = jax.nn.sigmoid(product(low_gate, gate_w))
    hidden_rows = lax.all_gather(low_hidden, "mp", axis=0, tiled=True)
    pre_act = product(hidden_rows, hidden_w)
    rectified = jnp.maximum(pre_act, 0.0)
    squared = reduced_precision(rectified * rectified)
    returned = lax.psum_scatter(
        product(squared, return_w).astype(jnp.bfloat16), "mp", scatter_dimension=0, tiled=True
    ).astype(jnp.float32)
    output = block_mid + gate_two * returned
    grad_ret = reduced_precision(grad_out * gate_two)
    grad_gate_pre = reduced_precision(grad_out * returned * gate_two * (1.0 - gate_two))
    d_gate_w = (low_gate, grad_gate_pre)
    grad_low_gate = product_nt(grad_gate_pre, gate_w)
    grad_rows = lax.all_gather(grad_ret, "mp", axis=0, tiled=True)
    grad_squared = product_nt(grad_rows, return_w)
    d_return = (squared, grad_rows)
    grad_pre = reduced_precision(grad_squared * 2.0 * rectified)
    d_hidden = (hidden_rows, grad_pre)
    grad_low_hidden = lax.psum_scatter(
        product_nt(grad_pre, hidden_w).astype(jnp.bfloat16), "mp", scatter_dimension=0, tiled=True
    ).astype(jnp.float32)
    d_mix_hidden = jnp.sum(grad_low_hidden * delta_b, axis=0)
    d_mix_gate = jnp.sum(grad_low_gate * delta_b, axis=0)
    grad_shift_b = (
        grad_low_hidden * (1.0 - mix_hidden) + grad_low_gate * (1.0 - mix_gate)
    ) * same_col
    from_next_b = from_behind(grad_shift_b[:1], "mp", -1)
    grad_norm_b = (
        grad_low_hidden * mix_hidden
        + grad_low_gate * mix_gate
        + jnp.concatenate([grad_shift_b[1:], from_next_b], axis=0)
    )
    grad_mid_norm, d_gain_two, d_bias_two = norm_back(grad_norm_b, unit_b, inv_b, gain_two)
    grad_mid = grad_out + grad_mid_norm
    grad_att = reduced_precision(grad_mid)
    d_output_w = (gated, grad_att)
    grad_gated = product_nt(grad_att, output_w)
    grad_recept_pre = reduced_precision(grad_gated * mixture_result * recept * (1.0 - recept))
    grad_mixed = grad_gated * recept
    d_recept_w = (low_recept, grad_recept_pre)
    grad_low_recept = product_nt(grad_recept_pre, recept_w)
    dividend_adjoint = grad_mixed / divisor_complete
    divisor_adjoint = -dividend_adjoint * mixture_result
    extra_derivative_part = dividend_adjoint * content_start + divisor_adjoint
    extra_derivative = jnp.sum(extra_derivative_part * extra_summand, axis=0)
    d_rate = jnp.sum(dividend_adjoint * numer_der + divisor_adjoint * denom_der, axis=0)
    backward_mat = jnp.concatenate([lower_tri.T, first_mask[None]], axis=0)
    back_sum = jnp.dot(
        backward_mat,
        jnp.concatenate([falling * dividend_adjoint, falling * divisor_adjoint], axis=1),
        precision=HIGH,
    )
    step_back = jnp.exp(-feature_fading)
    from_num = step_back * back_sum[row_count, :model_width]
    from_den = step_back * back_sum[row_count, model_width:]
    out_num, out_den, out_pass = carried_in(
        (from_num, from_den, carry_pass), "mp", suffix_join, (zero_vec, zero_vec, one_vec), True
    )
    tail_fall = last_mask[:, None] * jnp.exp(-(row_count - 1.0 - positions) * feature_fading)
    cumulative_dividend = rising * back_sum[:row_count, :model_width] + tail_fall * out_num
    running_denominator = rising * back_sum[:row_count, model_width:] + tail_fall * out_den
    value_gradient = reduced_precision(
        dividend_adjoint * extra_summand + cumulative_dividend * raised_lookup
    )
    key_gradient = reduced_precision(
        extra_derivative_part * extra_summand
        + cumulative_dividend * weighted_average
        + running_denominator * raised_lookup
    )
    d_key_w = (low_key, key_gradient)
    d_value_w = (low_value, value_gradient)
    grad_low_key = product_nt(key_gradient, key_w)
    grad_low_value = product_nt(value_gradient, value_w)
    d_mix_key = jnp.sum(grad_low_key * delta_a, axis=0)
    d_mix_value = jnp.sum(grad_low_value * delta_a, axis=0)
    d_mix_recept = jnp.sum(grad_low_recept * delta_a, axis=0)
    grad_shift_a = (
        grad_low_key * (1.0 - mix_key)
        + grad_low_value * (1.0 - mix_value)
        + grad_low_recept * (1.0 - mix_recept)
    ) * same_col
    from_next_a = from_behind(grad_shift_a[:1], "mp", -1)
    grad_norm_a = (
        grad_low_key * mix_key
        + grad_low_value * mix_value
        + grad_low_recept * mix_recept
        + jnp.concatenate([grad_shift_a[1:], from_next_a], axis=0)
    )
    grad_in_norm, d_gain_one, d_bias_one = norm_back(grad_norm_a, unit_a, inv_a, gain_one)
    input_grad = grad_mid + grad_in_norm
    grads = (
        d_gain_one,
        d_bias_one,
        d_rate * feature_fading,
        extra_derivative,
        d_mix_key,
        d_mix_value,
        d_mix_recept,
        d_key_w,
        d_value_w,
        d_recept_w,
        d_output_w,
        d_gain_two,
        d_bias_two,
        d_mix_hidden,
        d_mix_gate,
        d_hidden,
        d_return,
        d_gate_w,
    )
    return (output, input_grad, grads)


def generic_body(
    incoming_signal,
    series_number_table,
    upstream_adjoint,
    first_scaling_factor,
    first_scaling_offset,
    logarithmic_fading_speeds,
    present_step_extra,
    lookup_shift_mixture,
    content_shift_mixture,
    admit_lookup_shift_mixture,
    attention_lookup_matrix,
    attention_content_matrix,
    attention_admit_matrix,
    attention_result_matrix,
    second_scaling_factor,
    second_scaling_offset,
    inner_shift_mixture,
    admit_shift_mixture,
    feedforward_lookup_matrix,
    feedforward_content_matrix,
    feedforward_admit_matrix,
):
    hidden_full, return_full = (feedforward_lookup_matrix, feedforward_content_matrix)
    vectors = tuple(
        (
            start_item.astype(jnp.float32)
            for start_item in (
                first_scaling_factor,
                first_scaling_offset,
                logarithmic_fading_speeds,
                present_step_extra,
                lookup_shift_mixture,
                content_shift_mixture,
                admit_lookup_shift_mixture,
                second_scaling_factor,
                second_scaling_offset,
                inner_shift_mixture,
                admit_shift_mixture,
            )
        )
    )
    matrices = (
        attention_lookup_matrix,
        attention_content_matrix,
        attention_admit_matrix,
        attention_result_matrix,
        feedforward_admit_matrix,
    )
    output, input_grad, grads = jax.vmap(
        lambda rows, ids, adjoint: one_micro(
            rows, ids, adjoint, vectors, matrices, hidden_full, return_full
        )
    )(
        incoming_signal[:, 0].astype(jnp.float32),
        series_number_table[:, 0],
        upstream_adjoint[:, 0].astype(jnp.float32),
    )
    totals = tuple(
        product_tn(*(side.reshape(-1, side.shape[-1]) for side in grad))
        if isinstance(grad, tuple)
        else jnp.sum(grad, axis=0)
        for grad in grads
    )
    square = [index for index in range(18) if totals[index].shape == totals[7].shape]
    lines = [index for index in range(18) if totals[index].ndim == 1]
    wide = lax.psum_scatter(
        jnp.concatenate([reduced_precision(totals[index]) for index in square], axis=1),
        ("dp", "mp"),
        scatter_dimension=0,
        tiled=True,
    ).astype(jnp.float32)
    thin = lax.psum_scatter(
        jnp.stack([totals[index] for index in lines], axis=1),
        ("dp", "mp"),
        scatter_dimension=0,
        tiled=True,
    )
    held = dict(zip(square, jnp.split(wide, len(square), axis=1)))
    held.update({index: thin[:, place] for place, index in enumerate(lines)})
    output, input_grad = (output[:, None], input_grad[:, None])
    owned = tuple(held[index] for index in sorted(held))
    hidden_own, return_own = (
        lax.psum_scatter(
            totals[15].astype(jnp.bfloat16), "dp", scatter_dimension=0, tiled=True
        ).astype(jnp.float32),
        lax.psum_scatter(
            totals[16].astype(jnp.bfloat16), "dp", scatter_dimension=1, tiled=True
        ).astype(jnp.float32),
    )
    return (
        output,
        input_grad,
        owned[0],
        owned[1],
        owned[2],
        owned[3],
        owned[4],
        owned[5],
        owned[6],
        owned[7],
        owned[8],
        owned[9],
        owned[10],
        owned[11],
        owned[12],
        owned[13],
        owned[14],
        hidden_own,
        return_own,
        owned[15],
    )


def hand_over(count, *refs):
    sems = refs[3 * count]
    ins, outs = ([], [])
    for index in range(count):
        held = refs[2 * count + index]
        ins.append(pltpu.make_async_copy(refs[index], held, sems.at[0, index]))
        outs.append(pltpu.make_async_copy(held, refs[count + index], sems.at[1, index]))
        ins[-1].start()
    for index in range(count):
        ins[index].wait()
        outs[index].start()
    for copy in outs:
        copy.wait()


def hand_call(arrays):
    count = len(arrays)
    return pl.pallas_call(
        functools.partial(hand_over, count),
        out_shape=[jax.ShapeDtypeStruct(part.shape, part.dtype) for part in arrays],
        in_specs=[ANY] * count,
        out_specs=[ANY] * count,
        scratch_shapes=[pltpu.VMEM(part.shape, part.dtype) for part in arrays]
        + [pltpu.SemaphoreType.DMA((2, count))],
        compiler_params=pltpu.CompilerParams(vmem_limit_bytes=60 << 20),
        name="hand_over",
    )(*arrays)


def kernel_body(
    incoming_signal,
    series_number_table,
    upstream_adjoint,
    first_scaling_factor,
    first_scaling_offset,
    logarithmic_fading_speeds,
    present_step_extra,
    lookup_shift_mixture,
    content_shift_mixture,
    admit_lookup_shift_mixture,
    attention_lookup_matrix,
    attention_content_matrix,
    attention_admit_matrix,
    attention_result_matrix,
    second_scaling_factor,
    second_scaling_offset,
    inner_shift_mixture,
    admit_shift_mixture,
    feedforward_lookup_matrix,
    feedforward_content_matrix,
    feedforward_admit_matrix,
):
    hidden_full, return_full = (feedforward_lookup_matrix, feedforward_content_matrix)
    matrices = (
        attention_lookup_matrix,
        attention_content_matrix,
        attention_admit_matrix,
        attention_result_matrix,
        feedforward_admit_matrix,
    )
    micros, _, rows, depth = incoming_signal.shape
    planes = lax.axis_size("mp") // 2
    x = incoming_signal.reshape(micros * rows, depth)
    adjoint = upstream_adjoint.reshape(micros * rows, depth)
    operands = (
        x,
        series_number_table.reshape(micros, rows),
        adjoint,
        first_scaling_factor,
        first_scaling_offset,
        logarithmic_fading_speeds,
        present_step_extra,
        lookup_shift_mixture,
        content_shift_mixture,
        admit_lookup_shift_mixture,
        second_scaling_factor,
        second_scaling_offset,
        inner_shift_mixture,
        admit_shift_mixture,
        *matrices,
        hidden_full,
        return_full,
    )
    (
        keys, values, recept, num, den, mid, gate, mk, mv, mr, gated, mg, delta_a, delta_b,
        keep, segs, table, segcol, segrow, mh_all, ret_all, w1_all, w2_all, ret_acc, gmh_acc,
        parts1, parts2,
    ) = forward_call(planes, micros, rows, operands)
    key_w, value_w, recept_w, output_w, gate_w = matrices
    (
        output, grad_mid, grad_gate, grad_att, grad_recept, grad_key, grad_value, sums,
        part1, part2, rest1, rest2, squares,
    ) = middle_call(
        planes,
        micros,
        rows,
        (
            table, keep, segs, segcol, segrow, w1_all, w2_all, mh_all, ret_all, ret_acc, gmh_acc,
            parts1, parts2, mid, gate, adjoint, delta_b, keys, values, recept, num, den,
            gate_w, output_w, gated, mg,
        ),
    )
    (
        input_grad, sums, own_output, own_gate, own_recept, own_value, own_key, own_hidden,
        own_return,
    ) = last_call(
        planes,
        micros,
        rows,
        (
            table, keep, sums, squares, mr, grad_recept, mv, grad_value,
            mk, grad_key, recept_w, value_w, key_w, x, delta_a, grad_mid,
            part1, part2, rest1, rest2,
        ),
    )
    (
        output, input_grad, own_key, own_value, own_recept, own_output, own_hidden, own_return,
        own_gate,
    ) = hand_call(
        (
            output, input_grad, own_key, own_value, own_recept, own_output, own_hidden,
            own_return, own_gate,
        )
    )
    span = depth // (lax.axis_size("dp") * lax.axis_size("mp"))
    mine = lax.dynamic_slice_in_dim(
        sums, lax.axis_index(("dp", "mp")) * span, span, axis=1
    )
    line = [mine[index] for index in range(11)]
    shape = incoming_signal.shape
    return (
        output.reshape(shape),
        input_grad.reshape(shape),
        *line[:7],
        own_key,
        own_value,
        own_recept,
        own_output,
        *line[7:],
        own_hidden,
        own_return,
        own_gate,
    )


def solution(mesh):
    placed = (
        P(None, "dp", "mp", None),
        P(None, "dp", "mp"),
        P(None, "dp", "mp", None),
        P(),
        P(),
        P(),
        P(),
        P(),
        P(),
        P(),
        P(),
        P(),
        P(),
        P(),
        P(),
        P(),
        P(),
        P(),
        P(None, "mp"),
        P("mp", None),
        P(),
    )
    fits = mesh.shape["dp"] == 4 and mesh.shape["mp"] == 8
    return jax.shard_map(
        kernel_body if fits else generic_body,
        mesh=mesh,
        in_specs=placed,
        out_specs=(
            P(None, "dp", "mp", None),
            P(None, "dp", "mp", None),
            P(("dp", "mp")),
            P(("dp", "mp")),
            P(("dp", "mp")),
            P(("dp", "mp")),
            P(("dp", "mp")),
            P(("dp", "mp")),
            P(("dp", "mp")),
            P(("dp", "mp"), None),
            P(("dp", "mp"), None),
            P(("dp", "mp"), None),
            P(("dp", "mp"), None),
            P(("dp", "mp")),
            P(("dp", "mp")),
            P(("dp", "mp")),
            P(("dp", "mp")),
            P("dp", "mp"),
            P("mp", "dp"),
            P(("dp", "mp"), None),
        ),
        check_vma=False,
    )
```

```python
import functools

import jax
import jax.numpy as jnp
from jax import lax
from jax.experimental import pallas as pl
from jax.experimental.pallas import tpu as pltpu
from jax.sharding import PartitionSpec as P

EPS = 1e-05
HIGH = lax.Precision.HIGHEST


def from_behind(block, axis, distance):
    devices = range(lax.axis_size(axis))
    route = [(i - distance, i) for i in devices if i - distance in devices]
    return lax.ppermute(block, axis, route)


def carried_in(shard, axis, combine, identity, reverse):
    length, mine = (lax.axis_size(axis), lax.axis_index(axis))
    everything = jax.tree.map(lambda part: lax.all_gather(part, axis), shard)
    start = jax.tree.map(
        lambda part, zero: jnp.broadcast_to(jnp.asarray(zero, part.dtype), part.shape),
        shard,
        identity,
    )

    def step(k, before):
        at = length - 1 - k if reverse else k
        reached = at > mine if reverse else at < mine
        new = combine(before, jax.tree.map(lambda part: part[at], everything))
        return jax.tree.map(lambda a, b: jnp.where(reached, a, b), new, before)

    return lax.fori_loop(0, length, step, start)


def reduced_precision(values):
    return values.astype(jnp.bfloat16)


def product(left, right):
    return jnp.dot(left, right, preferred_element_type=jnp.float32)


def product_tn(left, right):
    return lax.dot_general(
        left, right, (((0,), (0,)), ((), ())), preferred_element_type=jnp.float32
    )


def product_nt(left, right):
    return lax.dot_general(
        left, right, (((1,), (1,)), ((), ())), preferred_element_type=jnp.float32
    )


def layer_norm(values, gain, bias):
    average = jnp.mean(values, axis=-1, keepdims=True)
    centre = values - average
    inverse = lax.rsqrt(jnp.mean(centre * centre, axis=-1, keepdims=True) + EPS)
    unit = centre * inverse
    return (unit * gain + bias, unit, inverse)


def norm_back(grad_in, unit, inverse, gain):
    scaled = grad_in * gain
    grad_values = inverse * (
        scaled
        - jnp.mean(scaled, axis=-1, keepdims=True)
        - unit * jnp.mean(scaled * unit, axis=-1, keepdims=True)
    )
    return (grad_values, jnp.sum(grad_in * unit, axis=0), jnp.sum(grad_in, axis=0))


def state_join(earlier, latter):
    return (
        latter[4] * earlier[0] + latter[0],
        latter[4] * earlier[1] + latter[1],
        latter[4] * earlier[2] + latter[5] * earlier[0] + latter[2],
        latter[4] * earlier[3] + latter[5] * earlier[1] + latter[3],
        earlier[4] * latter[4],
        earlier[5] * latter[4] + earlier[4] * latter[5],
    )


def suffix_join(earlier, latter):
    return (
        latter[0] + latter[2] * earlier[0],
        latter[1] + latter[2] * earlier[1],
        latter[2] * earlier[2],
    )


BF = jnp.bfloat16
F32 = jnp.float32
MESH = pl.DeviceIdType.MESH
NN = (((1,), (0,)), ((), ()))
NT = (((1,), (1,)), ((), ()))
TN = (((0,), (0,)), ((), ()))


def dot(left, right, form=NN):
    return lax.dot_general(left, right, form, preferred_element_type=F32)


def dot_exact_left(left, right):
    high = right.astype(BF)
    rest = (right - high.astype(F32)).astype(BF)
    return dot(left, high) + dot(left, rest)


def wide(lanes, width):
    return jnp.concatenate([lanes] * (width // 128), axis=1)


def tile(index, size):
    return pl.ds(pl.multiple_of(index * size, size), size)


def unit_of(values):
    average = jnp.mean(values, axis=-1, keepdims=True)
    centre = values - average
    inverse = lax.rsqrt(jnp.mean(centre * centre, axis=-1, keepdims=True) + EPS)
    return (centre * inverse, inverse)


def remote(source, target, send, receive, device):
    return pltpu.make_async_remote_copy(
        src_ref=source,
        dst_ref=target,
        send_sem=send,
        recv_sem=receive,
        device_id=device,
        device_id_type=MESH,
    )


class Place:
    def __init__(self, planes):
        self.planes = planes
        self.dp, self.mp = (lax.axis_index("dp"), lax.axis_index("mp"))
        self.z = lax.div(self.mp, 2)
        self.core = lax.rem(self.mp, 2)
        self.count = 2 * planes
        self.other = (self.dp, self.mp + 1 - 2 * self.core)
        self.side_x = (self.dp + 1 - 2 * lax.rem(self.dp, 2), self.mp)
        self.side_y = (lax.rem(self.dp + 2, 4), self.mp)

    def ahead(self, steps):
        return (self.dp, lax.rem(self.mp + steps + self.count, self.count))

    def plane(self, steps):
        return (self.dp, lax.rem(self.z + steps + self.planes, self.planes) * 2 + self.core)


def greet(devices):
    barrier = pltpu.get_barrier_semaphore()
    for device in devices:
        pl.semaphore_signal(barrier, inc=1, device_id=device, device_id_type=MESH)
    pl.semaphore_wait(barrier, len(devices))


def feed_rows(w1, w2, mh2, gr2, sq_s, gp_s, ret_acc, gmh_acc, fresh):
    def rows_of(i):
        span = tile(i, 256)
        pre = dot(mh2[span, :], w1[...])
        rectified = jnp.maximum(pre, 0.0)
        squared = (rectified * rectified).astype(BF)
        sq_s[span, :] = squared
        grad_squared = dot(gr2[span, :], w2[...], NT)
        grad_pre = (grad_squared * 2.0 * rectified).astype(BF)
        gp_s[span, :] = grad_pre
        if fresh:
            ret_acc[span, :] = dot(squared, w2[...])
            gmh_acc[span, :] = dot(grad_pre, w1[...], NT)
        else:
            ret_acc[span, :] += dot(squared, w2[...])
            gmh_acc[span, :] += dot(grad_pre, w1[...], NT)

    return rows_of


def feed_grads(mh2, gr2, sq_s, gp_s, parts1, parts2):
    @pl.loop(0, 4)
    def _(q):
        line, side = (lax.div(q, 2), lax.rem(q, 2))
        cols = tile(q, 256)
        parts1[side, line] = dot(mh2[:, cols], gp_s[...], TN).astype(BF)
        parts2[line, side] = dot(gr2[:, cols], sq_s[...], TN).astype(BF)


def forward_kernel(
    planes,
    micros,
    rows,
    x_ref,
    table_ref,
    adj_ref,
    *refs,
):
    (
    lines, refs) = (refs[:11], refs[11:])
    (
    key_w,
    value_w,
    recept_w,
    output_w,
    gate_w,
    w1_ref,
    w2_ref,
    k_out,
    v_out,
    r_out,
    num_out,
    den_out,
    mid_out,
    gate_out,
    mk_out,
    mv_out,
    mr_out,
    gated_out,
    mg_out,
    da_out,
    db_out,
    keep_out,
    segs_out,
    vec_out,
    segcol_out,
    segrow_out,
    mh_all,
    ret_all,
    w1_all,
    w2_all,
    ret_acc_out,
    gmh_acc_out,
    parts1_out,
    parts2_out,
    wk,
    wv,
    wr,
    wo,
    wg,
    k_s,
    v_s,
    r_s,
    num_s,
    den_s,
    mid_s,
    gate_s,
    xb_s,
    da_s,
    mk_s,
    mv_s,
    mr_s,
    gated_s,
    mg_s,
    keep_s,
    segcol_ref,
    segrow_ref,
    segpay_ref,
    last_ref,
    mask_s,
    halo_a,
    near_a,
    pay_b,
    halo_b,
    segs_s,
    state_own,
    state_other,
    state_chip,
    state_in,
    carry_s,
    w_sem,
    out_sem,
    small_sem,
    z_sem,
    s_sem,
    vec_ref,
    mh2,
    gr2,
    sq_s,
    gp_s,
    ret_acc,
    gmh_acc,
    parts1,
    parts2,
    ff_sem,
    ) = refs
    at = Place(planes)
    dp, mp, z, core = (at.dp, at.mp, at.z, at.core)
    tokens = micros * rows
    peers = [at.ahead(step) for step in range(1, at.count)]
    greet(peers + [at.side_x, at.side_y])

    for index, line in enumerate(lines):
        vec_ref[index : index + 1, :] = line[...].astype(F32).reshape(1, 1024)
    vec_ref[11:16, :] = jnp.zeros((5, 1024), F32)

    numbers = table_ref[...].astype(F32)
    rest = jnp.zeros((8 - micros, rows), F32)
    segrow_ref[...] = jnp.concatenate([numbers, rest], axis=0)
    columns = segrow_ref[...].T
    ends = [jnp.broadcast_to(numbers[:, at_end], (micros, 128)) for at_end in (slice(rows - 1, rows), slice(0, 1))]
    segpay_ref[...] = jnp.concatenate([ends[0], ends[0], ends[1], ends[1]], axis=0)
    last_ref[...] = jnp.zeros((8, 1024), F32)
    for m in range(micros):
        segcol_ref[m * rows : (m + 1) * rows, :] = jnp.broadcast_to(columns[:, m : m + 1], (rows, 128))
        last_ref[m : m + 1, :] = x_ref[(m + 1) * rows - 16 : (m + 1) * rows, :].astype(F32)[15:16]

    quarter1, quarter2 = (w1_ref.shape[0] // 4, w2_ref.shape[0] // 4)
    q1, q2 = (tile(dp, quarter1), tile(dp, quarter2))
    z_copies = {}
    for step in (1, planes - 1):
        to = at.plane(-step)
        z_copies[step - 1] = (
            remote(w1_ref.at[q1], w1_all.at[step - 1, q1], z_sem.at[step - 1, 0, 0], z_sem.at[step - 1, 0, 1], to),
            remote(w2_ref.at[q2], w2_all.at[step - 1, q2], z_sem.at[step - 1, 1, 0], z_sem.at[step - 1, 1, 1], to),
        )
    half1 = tile(lax.div(dp, 2), 2 * quarter1)
    far2 = tile(lax.rem(dp + 2, 4), quarter2)
    back = at.plane(-1)
    onward_1 = remote(w1_all.at[0, half1], w1_all.at[1, half1], z_sem.at[1, 0, 0], z_sem.at[1, 0, 1], back)
    onward_2 = (
        remote(w2_all.at[0, q2], w2_all.at[1, q2], z_sem.at[1, 1, 0], z_sem.at[1, 1, 1], back),
        remote(w2_all.at[0, far2], w2_all.at[1, far2], z_sem.at[1, 2, 0], z_sem.at[1, 2, 1], back),
    )

    halo_copy = remote(last_ref, halo_a, small_sem.at[0, 0], small_sem.at[0, 1], at.ahead(1))
    halo_copy.start()
    seg_copies = [
        remote(segpay_ref, segs_s.at[mp], small_sem.at[1 + step, 0], small_sem.at[1 + step, 1], device)
        for step, device in enumerate(peers)
    ]
    for copy in seg_copies:
        copy.start()
    segs_s[mp] = segpay_ref[...]
    loads = []
    for index, (source, target) in enumerate(
        ((key_w, wk), (value_w, wv), (recept_w, wr), (output_w, wo), (gate_w, wg))
    ):
        loads.append(pltpu.make_async_copy(source, target, w_sem.at[index]))
        loads[-1].start()
    for copy in z_copies[0]:
        copy.start()
    halo_copy.wait()
    for copy in seg_copies:
        copy.wait()

    def along(step):
        group = []
        own1, own2 = (w1_all.at[step, q1], w2_all.at[step, q2])
        return (
            remote(own1, own1, z_sem.at[step, 2, 0], z_sem.at[step, 2, 1], at.side_x),
            remote(own2, own2, z_sem.at[step, 3, 0], z_sem.at[step, 3, 1], at.side_y),
        )

    def across(step):
        both1 = w1_all.at[step, half1]
        own2 = w2_all.at[step, q2]
        next2 = w2_all.at[step, far2]
        return (
            remote(both1, both1, z_sem.at[step, 4, 0], z_sem.at[step, 4, 1], at.side_y),
            remote(own2, own2, z_sem.at[step, 5, 0], z_sem.at[step, 5, 1], at.side_x),
            remote(next2, next2, z_sem.at[step, 6, 0], z_sem.at[step, 6, 1], at.side_x),
        )

    def start(group):
        for copy in group:
            copy.start()

    def finish(group):
        for copy in group:
            copy.wait()

    along_0, along_2 = (along(0), along(2))
    across_0, across_1, across_2 = (across(0), across(1), across(2))

    before = lax.rem(mp + at.count - 1, at.count)
    has_before = mp > 0
    first_row = lax.broadcasted_iota(jnp.int32, (rows, 128), 0) == 0
    row_at = lax.broadcasted_iota(jnp.int32, (rows, rows), 0)
    col_at = lax.broadcasted_iota(jnp.int32, (rows, rows), 1)
    for m in range(micros):
        here = segcol_ref[m * rows : (m + 1) * rows, :]
        behind = jnp.where(
            first_row, segs_s[before, m : m + 1, :], pltpu.roll(here, 1, 0)
        )
        same = jnp.logical_and(
            here == behind, jnp.logical_or(jnp.logical_not(first_row), has_before)
        )
        keep_s[m * rows : (m + 1) * rows, :] = same.astype(F32)
        mask_s[m] = jnp.logical_and(
            here == segrow_ref[m : m + 1, :], col_at < row_at
        ).astype(F32).astype(BF)

    block = 32
    at_first = lax.broadcasted_iota(jnp.int32, (block, 1024), 0) == 0
    gain, bias = (vec_ref[0:1, :], vec_ref[1:2, :])
    near_a[...] = unit_of(halo_a[...])[0] * gain + bias
    for m in range(micros):

        def mix_a(b, prev, m=m):
            span = tile(m * (rows // block) + b, block)
            normed = unit_of(x_ref[span, :].astype(F32))[0] * gain + bias
            shifted = jnp.where(at_first, prev, pltpu.roll(normed, 1, 0)) * wide(
                keep_s[span, :], 1024
            )
            delta = normed - shifted
            da_s[span, :] = delta
            mk_s[span, :] = (shifted + delta * vec_ref[4:5, :]).astype(BF)
            mv_s[span, :] = (shifted + delta * vec_ref[5:6, :]).astype(BF)
            mr_s[span, :] = (shifted + delta * vec_ref[6:7, :]).astype(BF)
            return normed[block - 1 : block, :]

        lax.fori_loop(0, rows // block, mix_a, near_a[m : m + 1, :], unroll=2)

    outs = []

    def put(source, target):
        copy = pltpu.make_async_copy(source, target, out_sem.at[len(outs)])
        copy.start()
        outs.append(copy)

    put(da_s, da_out)
    put(keep_s, keep_out)
    put(segs_s, segs_out)
    put(segcol_ref, segcol_out)
    put(vec_ref, vec_out)
    put(segrow_ref, segrow_out)
    put(mk_s, mk_out)
    put(mv_s, mv_out)
    put(mr_s, mr_out)

    loads[0].wait()
    loads[1].wait()
    width = 256
    place = lax.broadcasted_iota(jnp.int32, (rows, width), 0).astype(F32)

    @pl.loop(0, 1024 // width)
    def _(i):
        cols = tile(i, width)
        rate = jnp.exp(vec_ref[2:3, cols])
        rising = jnp.exp(place * rate)
        falling = jnp.exp((1.0 - place) * rate)
        step_back = jnp.exp(-rate)
        keys = dot(mk_s[...], wk[:, cols])
        values = dot(mv_s[...], wv[:, cols])
        for m in range(micros):
            span = slice(m * rows, (m + 1) * rows)
            key, value = (keys[span], values[span])
            raised = jnp.exp(key)
            weighted = raised * value
            num = falling * dot_exact_left(mask_s[m], rising * weighted)
            den = falling * dot_exact_left(mask_s[m], rising * raised)
            k_s[span, cols] = key
            v_s[span, cols] = value
            num_s[span, cols] = num
            den_s[span, cols] = den
            state_own[m : m + 1, cols] = step_back * num[rows - 1 :] + weighted[rows - 1 :]
            state_own[micros + m : micros + m + 1, cols] = (
                step_back * den[rows - 1 :] + raised[rows - 1 :]
            )

    put(k_s, k_out)
    put(v_s, v_out)
    core_copy = remote(state_own, state_other, s_sem.at[0, 0], s_sem.at[0, 1], at.other)
    core_copy.start()
    finish(z_copies[0])
    start(along_0)
    z_copies[2][0].start()

    loads[2].wait()

    @pl.loop(0, 2)
    def _(i):
        span = tile(i, tokens // 2)
        r_s[span, :] = jax.nn.sigmoid(dot(mr_s[span, :], wr[...]))

    put(r_s, r_out)

    pair = lax.div(mp, 2) * 2
    decay_all = jnp.exp(-float(rows) * jnp.exp(vec_ref[2:3, :]))
    core_copy.wait()

    def last_of(device):
        return wide(segs_s[lax.rem(device + at.count, at.count), 0 : 2 * micros, :], 1024)

    even = jnp.where(core == 0, state_own[...], state_other[...])
    odd = jnp.where(core == 0, state_other[...], state_own[...])
    state_chip[...] = odd + jnp.where(last_of(pair) == last_of(pair + 1), decay_all * even, 0.0)
    chip_copies = [
        remote(state_chip, state_in.at[step - 1], s_sem.at[step, 0], s_sem.at[step, 1], at.plane(step))
        for step in range(1, planes)
    ]
    start(chip_copies)
    finish(chip_copies)
    z_copies[2][1].start()
    finish(along_0)
    start(across_0)
    total = jnp.zeros_like(state_chip[...])
    power = jnp.ones_like(decay_all)
    for step in range(1, planes):
        fits = jnp.logical_and(
            last_of(pair - 2 * step + 1) == last_of(pair - 1), z >= step
        )
        total = total + jnp.where(fits, power * state_in[step - 1], 0.0)
        power = power * decay_all * decay_all
    joined = state_other[...] + jnp.where(last_of(pair) == last_of(pair - 1), decay_all * total, 0.0)
    carry_s[...] = jnp.where(core == 0, total, joined)

    @pl.loop(0, 1024 // width)
    def _(i):
        cols = tile(i, width)
        rate = jnp.exp(vec_ref[2:3, cols])
        falling = jnp.exp(-place * rate)
        extra = vec_ref[3:4, cols]
        for m in range(micros):
            span = slice(m * rows, (m + 1) * rows)
            fits = jnp.logical_and(
                segcol_ref[span, :] == segs_s[before, m : m + 1, :], has_before
            ).astype(F32)
            carried = wide(fits, width) * falling
            num = num_s[span, cols] + carried * carry_s[m : m + 1, cols]
            den = den_s[span, cols] + carried * carry_s[micros + m : micros + m + 1, cols]
            bonus = jnp.exp(extra + k_s[span, cols])
            mixed = (num + bonus * v_s[span, cols]) / (den + bonus)
            num_s[span, cols] = num
            den_s[span, cols] = den
            gated_s[span, cols] = (r_s[span, cols] * mixed).astype(BF)

    put(num_s, num_out)
    put(den_s, den_out)
    put(gated_s, gated_out)
    loads[3].wait()

    @pl.loop(0, 2)
    def _(i):
        span = tile(i, tokens // 2)
        mid_s[span, :] = x_ref[span, :].astype(F32) + dot(gated_s[span, :], wo[...])

    put(mid_s, mid_out)
    gain_b, bias_b = (vec_ref[7:8, :], vec_ref[8:9, :])

    def norm_b(b):
        span = tile(b, block)
        xb_s[span, :] = unit_of(mid_s[span, :])[0] * gain_b + bias_b

    for m in range(micros):
        norm_b((m + 1) * (rows // block) - 1)
        pay_b[m : m + 1, :] = xb_s[(m + 1) * rows - 1 : (m + 1) * rows, :]
    pay_b[micros:, :] = jnp.zeros((8 - micros, 1024), F32)
    halo_b_copy = remote(pay_b, halo_b, s_sem.at[planes, 0], s_sem.at[planes, 1], at.ahead(1))
    halo_b_copy.start()
    for m in range(micros):

        @pl.loop(m * (rows // block), (m + 1) * (rows // block) - 1)
        def _(b):
            norm_b(b)

    halo_b_copy.wait()
    onward_1.start()
    start(onward_2)
    finish(z_copies[2])
    start(along_2)
    for m in range(micros):

        def mix_b(b, prev, m=m):
            span = tile(m * (rows // block) + b, block)
            normed = xb_s[span, :]
            shifted = jnp.where(at_first, prev, pltpu.roll(normed, 1, 0)) * wide(
                keep_s[span, :], 1024
            )
            delta = normed - shifted
            xb_s[span, :] = delta
            mh2[span, :] = (shifted + delta * vec_ref[9:10, :]).astype(BF)
            mg_s[span, :] = (shifted + delta * vec_ref[10:11, :]).astype(BF)
            return normed[block - 1 : block, :]

        lax.fori_loop(0, rows // block, mix_b, halo_b[m : m + 1, :], unroll=2)

    own, far = (slice(0, tokens), slice(tokens, 2 * tokens))
    mh_copy = remote(
        mh2.at[own], mh2.at[far], s_sem.at[planes + 1, 0], s_sem.at[planes + 1, 1], at.other
    )
    mh_copy.start()
    put(mg_s, mg_out)
    put(xb_s, db_out)
    loads[4].wait()

    @pl.loop(0, 2)
    def _(i):
        span = tile(i, tokens // 2)
        gate = jax.nn.sigmoid(dot(mg_s[span, :], wg[...]))
        gate_s[span, :] = gate
        gr2[span, :] = (adj_ref[span, :].astype(F32) * gate).astype(BF)

    ret_copy = remote(
        gr2.at[own], gr2.at[far], s_sem.at[planes + 2, 0], s_sem.at[planes + 2, 1], at.other
    )
    ret_copy.start()
    put(gate_s, gate_out)
    hidden = w1_ref.shape[1]
    w1_own, w2_own = (wk.at[:, 0:hidden], wv.at[0:hidden])
    w1_next, w2_next = (wk.at[:, hidden : 2 * hidden], wv.at[hidden : 2 * hidden])
    ff_loads = [
        pltpu.make_async_copy(source, target, ff_sem.at[index])
        for index, (source, target) in enumerate(
            ((w1_ref, w1_own), (w2_ref, w2_own), (w1_all.at[0], w1_next), (w2_all.at[0], w2_next))
        )
    ]
    ff_loads[0].start()
    ff_loads[1].start()
    ff_loads[0].wait()
    ff_loads[1].wait()
    half = tokens // 256
    step = feed_rows(w1_own, w2_own, mh2, gr2, sq_s, gp_s, ret_acc, gmh_acc, True)
    pl.loop(0, half)(step)
    mh_copy.wait()
    ret_copy.wait()
    finish(along_2)
    start(across_2)
    put(mh2, mh_all)
    put(gr2, ret_all)
    finish(across_0)
    ff_loads[2].start()
    ff_loads[3].start()
    pl.loop(half, 2 * half)(step)
    feed_grads(mh2, gr2, sq_s, gp_s, parts1.at[0], parts2.at[0])
    onward_1.wait()
    across_1[0].start()
    put(parts1.at[0], parts1_out.at[0])
    put(parts2.at[0], parts2_out.at[0])
    ff_loads[2].wait()
    ff_loads[3].wait()
    step = feed_rows(w1_next, w2_next, mh2, gr2, sq_s, gp_s, ret_acc, gmh_acc, False)
    pl.loop(0, half)(step)
    onward_2[0].wait()
    across_1[1].start()
    pl.loop(half, 2 * half)(step)
    onward_2[1].wait()
    across_1[2].start()
    put(ret_acc, ret_acc_out)
    put(gmh_acc, gmh_acc_out)
    feed_grads(mh2, gr2, sq_s, gp_s, parts1.at[1], parts2.at[1])
    put(parts1.at[1], parts1_out.at[1])
    put(parts2.at[1], parts2_out.at[1])
    finish(across_2)
    finish(across_1)
    for copy in outs:
        copy.wait()


ANY = pl.BlockSpec(memory_space=pl.ANY)
VM = pl.BlockSpec(memory_space=pltpu.VMEM)


def forward_call(planes, micros, rows, operands):
    tokens = micros * rows
    hidden = operands[-1].shape[0]

    def big(kind):
        return jax.ShapeDtypeStruct((tokens, 1024), kind)

    def hold(kind):
        return pltpu.VMEM((tokens, 1024), kind)

    square = pltpu.VMEM((1024, 1024), BF)
    few = pltpu.VMEM((8, 1024), F32)
    pair = pltpu.SemaphoreType.DMA
    return pl.pallas_call(
        functools.partial(forward_kernel, planes, micros, rows),
        out_shape=[big(F32)] * 7
        + [big(BF)] * 5
        + [big(F32)] * 2
        + [
            jax.ShapeDtypeStruct((tokens, 128), F32),
            jax.ShapeDtypeStruct((2 * planes, 16, 128), F32),
            jax.ShapeDtypeStruct((16, 1024), F32),
            jax.ShapeDtypeStruct((tokens, 128), F32),
            jax.ShapeDtypeStruct((8, rows), F32),
        ]
        + [jax.ShapeDtypeStruct((2 * tokens, 1024), BF)] * 2
        + [
            jax.ShapeDtypeStruct((planes - 1, 1024, hidden), BF),
            jax.ShapeDtypeStruct((planes - 1, hidden, 1024), BF),
        ]
        + [jax.ShapeDtypeStruct((2 * tokens, 1024), F32)] * 2
        + [jax.ShapeDtypeStruct((2, 2, 2, 256, hidden), BF)] * 2,
        in_specs=[VM] * 14 + [ANY] * 7,
        out_specs=[ANY] * 27,
        scratch_shapes=[square] * 5
        + [hold(F32)] * 9
        + [hold(BF)] * 5
        + [
            pltpu.VMEM((tokens, 128), F32),
            pltpu.VMEM((tokens, 128), F32),
            pltpu.VMEM((8, rows), F32),
            pltpu.VMEM((4 * micros, 128), F32),
            few,
            pltpu.VMEM((micros, rows, rows), BF),
            few,
            few,
            few,
            few,
            pltpu.VMEM((2 * planes, 16, 128), F32),
            few,
            few,
            few,
            pltpu.VMEM((planes - 1, 8, 1024), F32),
            few,
            pair((5,)),
            pair((29,)),
            pair((2 * planes + 1, 2)),
            pair((planes - 1, 7, 2)),
            pair((planes + 3, 2)),
            pltpu.VMEM((16, 1024), F32),
            pltpu.VMEM((2 * tokens, 1024), BF),
            pltpu.VMEM((2 * tokens, 1024), BF),
            pltpu.VMEM((2 * tokens, hidden), BF),
            pltpu.VMEM((2 * tokens, hidden), BF),
            pltpu.VMEM((2 * tokens, 1024), F32),
            pltpu.VMEM((2 * tokens, 1024), F32),
            pltpu.VMEM((2, 2, 2, 256, hidden), BF),
            pltpu.VMEM((2, 2, 2, 256, hidden), BF),
            pair((4,)),
        ],
        compiler_params=pltpu.CompilerParams(
            collective_id=0, has_side_effects=True, vmem_limit_bytes=62 << 20
        ),
        cost_estimate=pl.CostEstimate(
            flops=36 * tokens * 1024 * 1024, bytes_accessed=40 << 20, transcendentals=6 * tokens * 1024
        ),
        name="time_mix_forward",
    )(*operands)


class Reduce:
    def __init__(self, at, parts, first, second, far, sems, slot, x_first, source=None):
        self.at, self.parts, self.slot = (at, parts, slot if far is not None else 0)
        side = lax.rem(at.dp, 2)
        line = lax.div(at.dp, 2)
        self.one, self.two = (side, line) if x_first else (line, side)
        near, next_to = (at.side_x, at.side_y) if x_first else (at.side_y, at.side_x)
        self.first, self.second, self.far = (first, second, far)
        self.copy_1 = remote(
            (parts if source is None else source).at[1 - self.one],
            first,
            sems.at[0, 0],
            sems.at[0, 1],
            near,
        )
        self.copy_2 = remote(
            parts.at[self.one, 1 - self.two], second, sems.at[1, 0], sems.at[1, 1], next_to
        )
        if self.slot:
            self.copy_3 = remote(
                parts.at[self.one, self.two], far, sems.at[2, 0], sems.at[2, 1], at.plane(slot)
            )

    def start(self):
        self.copy_1.start()

    def add(self, half, other):
        mine = self.parts.at[self.one, half]

        @pl.loop(0, mine.shape[0] // 64)
        def _(i):
            span = tile(i, 64)
            mine[span, :] = (mine[span, :].astype(F32) + other[span, :].astype(F32)).astype(BF)

    def middle(self):
        self.copy_1.wait()
        self.add(1 - self.two, self.first.at[1 - self.two])
        self.copy_2.start()
        self.add(self.two, self.first.at[self.two])

    def last(self):
        self.copy_2.wait()
        self.add(self.two, self.second)
        if self.slot:
            self.copy_3.start()

    def close(self):
        if self.slot:
            self.copy_3.wait()


def sum_rows(into, index, values):
    total = values[0:8]
    for start in range(8, values.shape[0], 8):
        total = total + values[start : start + 8]
    into[index] = into[index] + total


def norm_back_rows(grad, unit, inverse, gain):
    scaled = grad * gain
    return inverse * (
        scaled
        - jnp.mean(scaled, axis=-1, keepdims=True)
        - unit * jnp.mean(scaled * unit, axis=-1, keepdims=True)
    )


def fill_square(parts, left, right, planes, split):
    @pl.loop(0, 4)
    def _(q):
        line, side = (lax.div(q, 2), lax.rem(q, 2))
        made = dot(left[:, tile(q, 256)], right[...], TN).astype(BF)
        pieces = made.reshape(planes, 2, 256 // (2 * planes), 1024)
        for core in range(2):
            if split > 0:
                parts[core, side, line, :, :, 0:split] = pieces[:, core, :, 0:split]
            if split < 1024:
                parts[core, line, side, :, :, split:1024] = pieces[:, core, :, split:1024]


def add_square(mine, other, planes):
    for one in range(2):
        for two in range(2):

            @pl.loop(0, planes)
            def _(i):
                mine[one, two, i] = (
                    mine[one, two, i].astype(F32) + other[one, two, i].astype(F32)
                ).astype(BF)


def middle_kernel(
    planes,
    micros,
    rows,
    vec_ref,
    keep_ref,
    segs_ref,
    segcol_ref,
    segrow_ref,
    w1_all,
    w2_all,
    mh_all,
    ret_all,
    ret_acc_ref,
    gmh_acc_ref,
    parts1_ref,
    parts2_ref,
    mid_ref,
    gate_ref,
    adj_ref,
    db_ref,
    k_ref,
    v_ref,
    r_ref,
    num_ref,
    den_ref,
    gate_w,
    output_w,
    gated_ref,
    mg_ref,
    out_ref,
    gmid_out,
    ggp_out,
    gatt_out,
    grp_out,
    gk_out,
    gv_out,
    sums_out,
    own1_out,
    own2_out,
    rest1_out,
    rest2_out,
    square_out,
    parts1,
    parts2,
    first1,
    first2,
    second1,
    second2,
    far1,
    far2,
    ret_acc,
    gmh_acc,
    ret_send,
    gmh_send,
    ret_recv,
    gmh_recv,
    mid_s,
    gate_s,
    adj_s,
    db_s,
    sums_s,
    sums_flat,
    mask_s,
    pay_b,
    halo_b,
    state_own,
    state_other,
    state_chip,
    state_in,
    carry_s,
    load_sem,
    out_sem,
    rs_sem,
    s_sem,
    square_parts,
    square_across,
    square_sem,
    ahead_s,
    ahead_sem,
):
    at = Place(planes)
    dp, mp, z, core = (at.dp, at.mp, at.z, at.core)
    tokens = micros * rows
    hidden = w1_all.shape[2]
    outs = []

    def put(source, target):
        copy = pltpu.make_async_copy(source, target, out_sem.at[len(outs)])
        copy.start()
        outs.append(copy)

    loaded = []

    def load(source, target):
        copy = pltpu.make_async_copy(source, target, load_sem.at[len(loaded)])
        copy.start()
        loaded.append(copy)
        return copy

    greet(
        [at.other, at.side_x, at.side_y]
        + [at.plane(step) for step in range(1, planes)]
        + [at.ahead(1), at.ahead(-1)]
    )
    half_cols = hidden // 2
    early, late_half = (slice(0, half_cols), slice(half_cols, hidden))

    def group(slot, cols, sem, source):
        made = []
        for kind, (parts, first, second, far, parts_ref) in enumerate(
            (
                (parts1, first1, second1, far1, parts1_ref),
                (parts2, first2, second2, far2, parts2_ref),
            )
        ):
            made.append(
                Reduce(
                    at,
                    parts.at[slot, :, :, :, cols],
                    first.at[slot, :, :, cols],
                    second.at[slot, :, cols],
                    far.at[slot // 2, :, cols] if slot % 2 else None,
                    rs_sem.at[sem, kind],
                    slot,
                    kind == 0,
                    parts_ref.at[slot, :, :, :, cols] if source else None,
                )
            )
        return made

    everything = slice(0, hidden)
    reduces = {
        "near": group(1, late_half, 0, True),
        "own": group(0, late_half, 1, True),
        "joined": group(0, early, 2, False),
        3: group(3, everything, 3, False),
        2: group(2, everything, 4, False),
    }
    ahead_copies = [
        remote(
            parts_ref.at[1, :, :, :, early],
            ahead_s.at[kind],
            ahead_sem.at[kind, 0],
            ahead_sem.at[kind, 1],
            at.plane(1),
        )
        for kind, parts_ref in enumerate((parts1_ref, parts2_ref))
    ]
    ret_copy = remote(ret_send, ret_recv, s_sem.at[0, 0], s_sem.at[0, 1], at.other)
    gmh_copy = remote(gmh_send, gmh_recv, s_sem.at[1, 0], s_sem.at[1, 1], at.other)

    def begin(name):
        for reduce in reduces[name]:
            reduce.start()

    def middle(name):
        for reduce in reduces[name]:
            reduce.middle()

    def last(name):
        for reduce in reduces[name]:
            reduce.last()

    begin("near")
    begin("own")
    for copy in ahead_copies:
        copy.start()

    def feed_forward(w1, w2, mh2, gr2, sq_s, gp_s):
        mh_load = [load(mh_all, mh2), load(ret_all, gr2)]
        order = (planes - 1, planes - 2)
        slots = []
        part_loads = []
        for index, slot in enumerate(order):
            slots.append(
                (load(w1_all.at[slot - 1], w1.at[index]), load(w2_all.at[slot - 1], w2.at[index]))
            )
            if index == 0:
                mh_load += [load(ret_acc_ref, ret_acc), load(gmh_acc_ref, gmh_acc)]
                for part in (1, 0):
                    part_loads.append(load(parts1_ref.at[part], parts1.at[part]))
                    part_loads.append(load(parts2_ref.at[part], parts2.at[part]))
        late = [load(mid_ref, mid_s), load(gate_ref, gate_s), load(adj_ref, adj_s), load(db_ref, db_s)]
        for copy in mh_load:
            copy.wait()
        half = tokens // 256
        for index, slot in enumerate(order):
            for copy in slots[index]:
                copy.wait()
            step = feed_rows(
                w1.at[index], w2.at[index], mh2, gr2, sq_s, gp_s, ret_acc, gmh_acc, False
            )
            pl.loop(half, 2 * half)(step)
            if index == 0:
                for copy in part_loads:
                    copy.wait()
                middle("near")
            else:

                @pl.loop(0, tokens // 64)
                def _(i):
                    span = tile(i, 64)
                    far_span = tile(tokens // 64 + i, 64)
                    ret_send[span, :] = ret_acc[far_span, :].astype(BF)
                    gmh_send[span, :] = gmh_acc[far_span, :].astype(BF)

                ret_copy.start()
                gmh_copy.start()
            pl.loop(0, half)(step)
            if index == 0:
                middle("own")
            feed_grads(mh2, gr2, sq_s, gp_s, parts1.at[slot], parts2.at[slot])
            if index == 0:
                begin(slot)
        for copy in late:
            copy.wait()

    pl.run_scoped(
        feed_forward,
        pltpu.VMEM((2, 1024, hidden), BF),
        pltpu.VMEM((2, hidden, 1024), BF),
        pltpu.VMEM((2 * tokens, 1024), BF),
        pltpu.VMEM((2 * tokens, 1024), BF),
        pltpu.VMEM((2 * tokens, hidden), BF),
        pltpu.VMEM((2 * tokens, hidden), BF),
    )
    own = slice(0, tokens)
    far = slice(tokens, 2 * tokens)
    block = 32

    def attention(k_s, v_s, r_s, num_s, den_s, wg, wo, ggp_s, gatt_s, grp_s, gk_s, gv_s):
        need_wg = load(gate_w, wg)
        need_wo = load(output_w, wo)
        need = [
            load(k_ref, k_s),
            load(v_ref, v_s),
            load(r_ref, r_s),
            load(num_ref, num_s),
            load(den_ref, den_s),
        ]
        sums_s[...] = jnp.zeros_like(sums_s)
        row_at = lax.broadcasted_iota(jnp.int32, (rows, rows), 0)
        col_at = lax.broadcasted_iota(jnp.int32, (rows, rows), 1)
        for m in range(micros):
            mask_s[m] = jnp.logical_and(
                segcol_ref[m * rows : (m + 1) * rows, :] == segrow_ref[m : m + 1, :],
                col_at > row_at,
            ).astype(F32).astype(BF)
        ret_copy.wait()
        need_gated = load(gated_ref, ret_send)

        @pl.loop(0, tokens // block)
        def _(b):
            span = tile(b, block)
            returned = ret_acc[span, :] + ret_recv[span, :].astype(F32)
            gate = gate_s[span, :]
            product_in = gate * returned
            ret_acc[span, :] = mid_s[span, :] + product_in
            ggp_s[span, :] = (adj_s[span, :].astype(F32) * product_in * (1.0 - gate)).astype(BF)

        put(ret_acc.at[own], out_ref)
        put(ggp_s, ggp_out)
        need_wg.wait()

        @pl.loop(0, 2)
        def _(i):
            span = tile(i, tokens // 2)
            ret_acc[tile(2 + i, tokens // 2), :] = dot(ggp_s[span, :], wg[...], NT)

        for kind, parts in enumerate((parts1, parts2)):
            ahead_copies[kind].wait()
            for one in range(2):
                for two in range(2):

                    @pl.loop(0, 4)
                    def _(i, kind=kind, parts=parts, one=one, two=two):
                        span = tile(i, 64)
                        parts[0, one, two, span, early] = (
                            parts[0, one, two, span, early].astype(F32)
                            + ahead_s[kind, one, two, span, :].astype(F32)
                        ).astype(BF)

        begin("joined")
        gmg = ret_acc.at[far]
        gmh_copy.wait()
        need_mg = load(mg_ref, gmh_send)
        mix_h, mix_g = (vec_ref[9:10, :], vec_ref[10:11, :])
        gain = vec_ref[7:8, :]

        def combine(b):
            span = tile(b, block)
            grad_h = gmh_acc[span, :] + gmh_recv[span, :].astype(F32)
            grad_g = gmg[span, :]
            shift = (grad_h * (1.0 - mix_h) + grad_g * (1.0 - mix_g)) * wide(keep_ref[span, :], 1024)
            return (span, grad_h, grad_g, shift)

        for m in range(micros):
            pay_b[m : m + 1, :] = combine(m * (rows // block))[3][0:1, :]
        pay_b[micros:, :] = jnp.zeros((8 - micros, 1024), F32)
        halo_copy = remote(pay_b, halo_b, s_sem.at[2, 0], s_sem.at[2, 1], at.ahead(-1))
        halo_copy.start()
        at_last = lax.broadcasted_iota(jnp.int32, (block, 1024), 0) == block - 1
        halo_copy.wait()
        last("near")
        last("own")
        middle(3)
        begin(2)
        for m in range(micros):

            def back_b(i, after, m=m):
                span, grad_h, grad_g, shift = combine((m + 1) * (rows // block) - 1 - i)
                delta = db_s[span, :]
                sum_rows(sums_s, 9, grad_h * delta)
                sum_rows(sums_s, 10, grad_g * delta)
                moved = jnp.where(at_last, after, pltpu.roll(shift, block - 1, 0))
                grad = grad_h * mix_h + grad_g * mix_g + moved
                unit, inverse = unit_of(mid_s[span, :])
                sum_rows(sums_s, 7, grad * unit)
                sum_rows(sums_s, 8, grad)
                total = adj_s[span, :].astype(F32) + norm_back_rows(grad, unit, inverse, gain)
                gmh_acc[span, :] = total
                gatt_s[span, :] = total.astype(BF)
                return shift[0:1, :]

            lax.fori_loop(0, rows // block, back_b, halo_b[m : m + 1, :], unroll=2)

        put(gmh_acc.at[own], gmid_out)
        put(gatt_s, gatt_out)
        need_wo.wait()

        @pl.loop(0, 2)
        def _(i):
            span = tile(i, tokens // 2)
            gmh_acc[tile(2 + i, tokens // 2), :] = dot(gatt_s[span, :], wo[...], NT)

        middle("joined")
        for copy in need:
            copy.wait()
        width = 256
        place = lax.broadcasted_iota(jnp.int32, (rows, width), 0).astype(F32)

        @pl.loop(0, 1024 // width)
        def _(i):
            cols = tile(i, width)
            rate = jnp.exp(vec_ref[2:3, cols])
            rising = jnp.exp(place * rate)
            falling = jnp.exp((1.0 - place) * rate)
            step_back = jnp.exp(-rate)
            extra = vec_ref[3:4, cols]
            for m in range(micros):
                span = slice(m * rows, (m + 1) * rows)
                far_span = slice(tokens + m * rows, tokens + (m + 1) * rows)
                bonus = jnp.exp(extra + k_s[span, cols])
                recept = r_s[span, cols]
                inverse = 1.0 / (den_s[span, cols] + bonus)
                mixed = (num_s[span, cols] + bonus * v_s[span, cols]) * inverse
                grad_gated = gmh_acc[far_span, cols]
                grad_mixed = grad_gated * recept
                grp_s[span, cols] = (grad_mixed * mixed * (1.0 - recept)).astype(BF)
                up = grad_mixed * inverse
                down = -up * mixed
                up_sum = rising * dot_exact_left(mask_s[m], falling * up)
                down_sum = rising * dot_exact_left(mask_s[m], falling * down)
                gmh_acc[far_span, cols] = up
                db_s[span, cols] = down
                mid_s[span, cols] = up_sum
                gate_s[span, cols] = down_sum
                state_own[m : m + 1, cols] = up[0:1] + step_back * up_sum[0:1]
                state_own[micros + m : micros + m + 1, cols] = down[0:1] + step_back * down_sum[0:1]

        put(grp_s, grp_out)
        core_copy = remote(state_own, state_other, s_sem.at[3, 0], s_sem.at[3, 1], at.other)
        core_copy.start()
        pair = lax.div(mp, 2) * 2
        decay_all = jnp.exp(-float(rows) * jnp.exp(vec_ref[2:3, :]))

        def seen(device, last):
            index = lax.rem(device + at.count, at.count)
            start = 0 if last else 2 * micros
            return wide(segs_ref[index, start : start + 2 * micros, :], 1024)

        core_copy.wait()
        even = jnp.where(core == 0, state_own[...], state_other[...])
        odd = jnp.where(core == 0, state_other[...], state_own[...])
        state_chip[...] = even + jnp.where(
            seen(pair, False) == seen(pair + 1, False), decay_all * odd, 0.0
        )
        chip_copies = [
            remote(state_chip, state_in.at[step - 1], s_sem.at[3 + step, 0], s_sem.at[3 + step, 1], at.plane(-step))
            for step in range(1, planes)
        ]
        for copy in chip_copies:
            copy.start()
        for copy in chip_copies:
            copy.wait()
        total = jnp.zeros_like(state_chip[...])
        power = jnp.ones_like(decay_all)
        for step in range(1, planes):
            fits = jnp.logical_and(
                seen(pair + 2 * step, False) == seen(mp, True), z + step < planes
            )
            total = total + jnp.where(fits, power * state_in[step - 1], 0.0)
            power = power * decay_all * decay_all
        joined = decay_all * total + jnp.where(
            seen(pair + 1, False) == seen(pair, True), state_other[...], 0.0
        )
        carry_s[...] = jnp.where(core == 0, joined, total)
        last(3)

        @pl.loop(0, 1024 // width)
        def _(i):
            cols = tile(i, width)
            rate = jnp.exp(vec_ref[2:3, cols])
            tail = jnp.exp((place - (rows - 1.0)) * rate)
            extra = vec_ref[3:4, cols]
            step_back = jnp.exp(-rate)
            for m in range(micros):
                span = slice(m * rows, (m + 1) * rows)
                far_span = slice(tokens + m * rows, tokens + (m + 1) * rows)
                fits = (segcol_ref[span, :] == segs_ref[mp, m : m + 1, :]).astype(F32)
                carried = wide(fits, width) * tail
                up_sum = mid_s[span, cols] + carried * carry_s[m : m + 1, cols]
                down_sum = gate_s[span, cols] + carried * carry_s[micros + m : micros + m + 1, cols]
                up, down = (gmh_acc[far_span, cols], db_s[span, cols])
                key, value = (k_s[span, cols], v_s[span, cols])
                bonus = jnp.exp(extra + key)
                raised = jnp.exp(key)
                direct = (up * value + down) * bonus
                gk_s[span, cols] = (direct + raised * (value * up_sum + down_sum)).astype(BF)
                gv_s[span, cols] = (up * bonus + raised * up_sum).astype(BF)
                rate_part = -rate * step_back * (up_sum * num_s[span, cols] + down_sum * den_s[span, cols])
                for index, part in ((2, rate_part), (3, direct)):
                    summed = part[0:8]
                    for start in range(8, rows, 8):
                        summed = summed + part[start : start + 8]
                    sums_s[index, :, cols] = sums_s[index, :, cols] + summed

        put(gk_s, gk_out)
        put(gv_s, gv_out)
        for index in range(16):
            sums_flat[index : index + 1, :] = jnp.sum(sums_s[index], axis=0, keepdims=True)
        put(sums_flat, sums_out)
        need_gated.wait()
        need_mg.wait()
        square_copies = []
        for index, (left, right) in enumerate(((ret_send, gatt_s), (gmh_send, ggp_s))):
            fill_square(square_parts.at[index], left, right, planes, 512)
            square_copies.append(
                remote(
                    square_parts.at[index, 1 - core],
                    square_across.at[index],
                    square_sem.at[index, 0],
                    square_sem.at[index, 1],
                    at.other,
                )
            )
            square_copies[index].start()
        middle(2)
        for index in range(2):
            square_copies[index].wait()
            add_square(square_parts.at[index, core], square_across.at[index], planes)
            put(square_parts.at[index, core], square_out.at[index])
        last("joined")
        for name in ("near", 3):
            for reduce in reduces[name]:
                reduce.close()
        for parts, far_parts, own_s, own_out, one, two in (
            (parts1, far1, mid_s, own1_out, lax.rem(dp, 2), lax.div(dp, 2)),
            (parts2, far2, gate_s, own2_out, lax.div(dp, 2), lax.rem(dp, 2)),
        ):
            total = parts[0, one, two].astype(F32) + far_parts[1].astype(F32)
            own_s[0:256, early] = total[:, early]
            own_s[0:256, late_half] = total[:, late_half] + far_parts[0, :, late_half].astype(F32)
            put(own_s.at[0:256, 0:hidden], own_out)
        last(2)
        put(parts1.at[2, lax.rem(dp, 2), lax.div(dp, 2)], rest1_out)
        put(parts2.at[2, lax.div(dp, 2), lax.rem(dp, 2)], rest2_out)
        for copy in outs:
            copy.wait()

    def hold(kind):
        return pltpu.VMEM((tokens, 1024), kind)

    square = pltpu.VMEM((1024, 1024), BF)
    pl.run_scoped(attention, *([hold(F32)] * 5), square, square, *([hold(BF)] * 5))


def middle_call(planes, micros, rows, operands):
    tokens = micros * rows
    hidden = operands[5].shape[2]

    def big(kind):
        return jax.ShapeDtypeStruct((tokens, 1024), kind)

    def hold(count, kind):
        return pltpu.VMEM((count, 1024), kind)

    few = hold(8, F32)
    quarter = (256, hidden)
    piece = (planes, 256 // (2 * planes), 1024)
    sems = pltpu.SemaphoreType.DMA
    return pl.pallas_call(
        functools.partial(middle_kernel, planes, micros, rows),
        out_shape=[big(F32)] * 2
        + [big(BF)] * 5
        + [jax.ShapeDtypeStruct((16, 1024), F32)]
        + [jax.ShapeDtypeStruct(quarter, F32)] * 2
        + [jax.ShapeDtypeStruct(quarter, BF)] * 2
        + [jax.ShapeDtypeStruct((2, 2, 2) + piece, BF)],
        in_specs=[VM] * 5 + [ANY] * 21,
        out_specs=[ANY] * 13,
        scratch_shapes=[pltpu.VMEM((planes, 2, 2) + quarter, BF)] * 2
        + [pltpu.VMEM((planes, 2) + quarter, BF)] * 2
        + [pltpu.VMEM((planes,) + quarter, BF)] * 2
        + [pltpu.VMEM((2,) + quarter, BF)] * 2
        + [hold(2 * tokens, F32)] * 2
        + [hold(tokens, BF)] * 4
        + [hold(tokens, F32), hold(tokens, F32), hold(tokens, BF), hold(tokens, F32)]
        + [
            pltpu.VMEM((16, 8, 1024), F32),
            pltpu.VMEM((16, 1024), F32),
            pltpu.VMEM((micros, rows, rows), BF),
            few,
            few,
            few,
            few,
            few,
            pltpu.VMEM((planes - 1, 8, 1024), F32),
            few,
            sems((25,)),
            sems((14,)),
            sems((planes + 1, 2, 3, 2)),
            sems((3 + planes, 2)),
            pltpu.VMEM((2, 2, 2, 2) + piece, BF),
            pltpu.VMEM((2, 2, 2) + piece, BF),
            sems((2, 2)),
            pltpu.VMEM((2, 2, 2, 256, hidden // 2), BF),
            sems((2, 2)),
        ],
        compiler_params=pltpu.CompilerParams(
            collective_id=1, has_side_effects=True, vmem_limit_bytes=63 << 20
        ),
        cost_estimate=pl.CostEstimate(
            flops=52 * tokens * 1024 * 1024, bytes_accessed=60 << 20, transcendentals=6 * tokens * 1024
        ),
        name="channel_mix_and_adjoint",
    )(*operands)


class ReduceSquare:
    def __init__(self, at, mine, first, second, far, sems, x_first, source=None):
        self.at, self.mine, self.first, self.second, self.far = (at, mine, first, second, far)
        side = lax.rem(at.dp, 2)
        line = lax.div(at.dp, 2)
        self.one, self.two = (side, line) if x_first else (line, side)
        near, next_to = (at.side_x, at.side_y) if x_first else (at.side_y, at.side_x)
        self.copy_1 = remote(
            (mine if source is None else source).at[1 - self.one],
            first,
            sems.at[0, 0],
            sems.at[0, 1],
            near,
        )
        self.copy_2 = remote(
            mine.at[self.one, 1 - self.two], second, sems.at[1, 0], sems.at[1, 1], next_to
        )
        self.copies_3 = [
            remote(
                mine.at[self.one, self.two, lax.rem(at.z + step, at.planes)],
                far.at[step - 1],
                sems.at[1 + step, 0],
                sems.at[1 + step, 1],
                at.plane(step),
            )
            for step in range(1, at.planes)
        ]

    def add(self, one, two, other):
        @pl.loop(0, self.at.planes)
        def _(i):
            self.mine[one, two, i] = (
                self.mine[one, two, i].astype(F32) + other[i].astype(F32)
            ).astype(BF)

    def begin(self):
        self.copy_1.start()

    def middle(self):
        self.copy_1.wait()
        self.add(self.one, 1 - self.two, self.first.at[1 - self.two])
        self.copy_2.start()
        self.add(self.one, self.two, self.first.at[self.two])

    def last(self):
        self.copy_2.wait()
        self.add(self.one, self.two, self.second)

    def send(self):
        for copy in self.copies_3:
            copy.start()

    def close(self):
        for copy in self.copies_3:
            copy.wait()
        total = self.mine[self.one, self.two, self.at.z].astype(F32)
        for step in range(self.at.planes - 1):
            total = total + self.far[step].astype(F32)
        return total


def last_kernel(
    planes,
    micros,
    rows,
    vec_ref,
    keep_ref,
    sums_ref,
    square_ref,
    mr_ref,
    grp_ref,
    mv_ref,
    gv_ref,
    mk_ref,
    gk_ref,
    recept_w,
    value_w,
    key_w,
    x_ref,
    da_ref,
    gmid_ref,
    part1_ref,
    part2_ref,
    rest1_ref,
    rest2_ref,
    grad_out,
    sums_out,
    own_output,
    own_gate,
    own_recept,
    own_value,
    own_key,
    own_hidden,
    own_return,
    left_s,
    right_s,
    w_s,
    x_s,
    da_s,
    total_s,
    g_s,
    sums_s,
    parts,
    across,
    first,
    second,
    far,
    own_s,
    pay_a,
    halo_a,
    flat_s,
    flat_recv,
    load_sem,
    out_sem,
    rs_sem,
    s_sem,
    ff_far,
    ff_total,
    own1_s,
    own2_s,
    ff_sem,
    ready_s,
    core_sem,
):
    at = Place(planes)
    tokens = micros * rows
    outs = []

    def put(source, target):
        copy = pltpu.make_async_copy(source, target, out_sem.at[len(outs)])
        copy.start()
        outs.append(copy)

    loaded = []

    def load(source, target):
        copy = pltpu.make_async_copy(source, target, load_sem.at[len(loaded)])
        copy.start()
        loaded.append(copy)
        return copy

    sides = (
        (mr_ref, grp_ref),
        (mv_ref, gv_ref),
        (mk_ref, gk_ref),
    )
    ready_load = load(square_ref, ready_s)
    side_loads = [
        (load(left, left_s.at[index]), load(right, right_s.at[index]))
        for index, (left, right) in enumerate(sides)
    ]
    w_loads = [
        load(source, w_s.at[index]) for index, source in enumerate((recept_w, value_w, key_w))
    ]
    row_loads = [load(x_ref, x_s), load(da_ref, da_s), load(gmid_ref, total_s)]
    greet(
        [at.other, at.side_x, at.side_y]
        + [at.plane(step) for step in range(1, planes)]
        + [at.ahead(1), at.ahead(-1)]
    )
    core = at.core
    lefts, rights = (slice(0, 512), slice(512, 1024))
    reduces = []
    for index in range(5):
        mine = ready_s.at[index] if index < 2 else parts.at[index - 2, core]
        halves = []
        for kind, cols in enumerate((lefts, rights)):
            halves.append(
                ReduceSquare(
                    at,
                    mine.at[:, :, :, :, cols],
                    first.at[index, :, :, :, cols],
                    second.at[index, :, :, cols],
                    far.at[index, :, :, cols],
                    rs_sem.at[index, kind],
                    kind == 0,
                    square_ref.at[index, :, :, :, :, cols] if index < 2 else None,
                )
            )
        reduces.append(halves)

    def begin(index):
        for half in reduces[index]:
            half.begin()

    def middle(index):
        for half in reduces[index]:
            half.middle()

    def last(index):
        for half in reduces[index]:
            half.last()
            half.send()

    def close(index, target):
        for half, cols in zip(reduces[index], (lefts, rights)):
            own_s[index, :, cols] = half.close()
        put(own_s.at[index], target)

    core_copies = [
        remote(
            parts.at[index, 1 - core],
            across.at[index],
            core_sem.at[index, 0],
            core_sem.at[index, 1],
            at.other,
        )
        for index in range(3)
    ]
    ff_loads = [load(part1_ref, ff_total.at[0]), load(part2_ref, ff_total.at[1])]
    ff_copies = [
        remote(rest, ff_far.at[index], ff_sem.at[index, 0], ff_sem.at[index, 1], at.plane(2))
        for index, rest in enumerate((rest1_ref, rest2_ref))
    ]
    begin(0)
    begin(1)
    ready_load.wait()
    mixes = (vec_ref[6:7, :], vec_ref[5:6, :], vec_ref[4:5, :])
    heads = jnp.zeros((16 * micros, 1024), F32)
    for index in range(3):
        side_loads[index][1].wait()
        w_loads[index].wait()
        picked = jnp.concatenate(
            [right_s[index, m * rows : m * rows + 16, :] for m in range(micros)], axis=0
        )
        heads = heads + dot(picked, w_s[index], NT) * (1.0 - mixes[index])
    for m in range(micros):
        pay_a[m : m + 1, :] = heads[16 * m : 16 * m + 1] * wide(
            keep_ref[m * rows : m * rows + 8, :], 1024
        )[0:1]
    pay_a[micros:, :] = jnp.zeros((8 - micros, 1024), F32)
    halo_copy = remote(pay_a, halo_a, s_sem.at[0, 0], s_sem.at[0, 1], at.ahead(-1))
    halo_copy.start()
    for copy in ff_copies:
        copy.start()
    sums_s[...] = jnp.zeros_like(sums_s)

    def fill(index):
        side_loads[index][0].wait()
        fill_square(parts.at[index], left_s.at[index], right_s.at[index], planes, 512)
        core_copies[index].start()

    def settle(index):
        core_copies[index].wait()
        add_square(parts.at[index, core], across.at[index], planes)

    def back(index):
        @pl.loop(0, 2)
        def _(i):
            span = tile(i, tokens // 2)
            g_s[index, span, :] = dot(right_s[index, span, :], w_s[index], NT)

    fill(0)
    middle(0)
    fill(1)
    settle(0)
    begin(2)
    fill(2)
    settle(1)
    middle(1)
    begin(3)
    settle(2)
    back(0)
    last(0)
    back(1)
    back(2)
    for copy in row_loads:
        copy.wait()
    block = 32
    gain = vec_ref[0:1, :]

    def combine(b):
        span = tile(b, block)
        grads = [g_s[index, span, :] for index in range(3)]
        shift = sum(grad * (1.0 - mix) for grad, mix in zip(grads, mixes))
        return (span, grads, shift * wide(keep_ref[span, :], 1024))

    at_last = lax.broadcasted_iota(jnp.int32, (block, 1024), 0) == block - 1
    halo_copy.wait()
    for m in range(micros):

        def back_a(i, after, m=m):
            span, grads, shift = combine((m + 1) * (rows // block) - 1 - i)
            delta = da_s[span, :]
            for index, grad in enumerate(grads):
                sum_rows(sums_s, 2 - index, grad * delta)
            moved = jnp.where(at_last, after, pltpu.roll(shift, block - 1, 0))
            grad = sum(part * mix for part, mix in zip(grads, mixes)) + moved
            unit, inverse = unit_of(x_s[span, :].astype(F32))
            sum_rows(sums_s, 3, grad * unit)
            sum_rows(sums_s, 4, grad)
            total_s[span, :] = total_s[span, :] + norm_back_rows(grad, unit, inverse, gain)
            return shift[0:1, :]

        lax.fori_loop(0, rows // block, back_a, halo_a[m : m + 1, :], unroll=2)
    put(total_s, grad_out)
    flat_s[0] = sums_ref[...]
    for index, row in enumerate((4, 5, 6, 0, 1)):
        flat_s[0, row : row + 1, :] = jnp.sum(sums_s[index], axis=0, keepdims=True)

    def flat_copy(level, slot, device):
        return remote(
            flat_s.at[level], flat_recv.at[slot], s_sem.at[1 + slot, 0], s_sem.at[1 + slot, 1], device
        )

    over_core = flat_copy(0, 0, at.other)
    over_core.start()
    over_core.wait()
    flat_s[1] = flat_s[0] + flat_recv[0]
    over_x = flat_copy(1, 1, at.side_x)
    middle(2)
    over_x.start()
    begin(4)
    last(1)
    middle(3)
    over_x.wait()
    flat_s[2] = flat_s[1] + flat_recv[1]
    over_y = flat_copy(2, 2, at.side_y)
    over_y.start()
    last(2)
    middle(4)
    over_y.wait()
    flat_s[3] = flat_s[2] + flat_recv[2]
    flat_copies = []
    for step in range(1, planes):
        to = lax.rem(at.z + step, planes)
        lanes = tile(at.dp * (planes // 2) + lax.div(to, 2), 128)
        slot = 2 + step
        flat_copies.append(
            remote(
                flat_s.at[3, :, lanes],
                flat_recv.at[slot, :, lanes],
                s_sem.at[1 + slot, 0],
                s_sem.at[1 + slot, 1],
                at.plane(step),
            )
        )
    for copy in flat_copies:
        copy.start()
    last(3)
    for copy in ff_loads + ff_copies:
        copy.wait()
    own1_s[...] = ff_total[0] + ff_far[0].astype(F32)
    own2_s[...] = (ff_total[1] + ff_far[1].astype(F32)).T
    put(own1_s, own_hidden)
    put(own2_s, own_return)
    last(4)
    close(0, own_output)
    close(1, own_gate)
    close(2, own_recept)
    for copy in flat_copies:
        copy.wait()
    lanes = tile(at.dp * (planes // 2) + lax.div(at.z, 2), 128)
    flat_s[0, :, lanes] = flat_s[3, :, lanes] + sum(
        flat_recv[2 + step, :, lanes] for step in range(1, planes)
    )
    put(flat_s.at[0], sums_out)
    close(3, own_value)
    close(4, own_key)
    for copy in outs:
        copy.wait()


def last_call(planes, micros, rows, operands):
    tokens = micros * rows

    def hold(count, kind):
        return pltpu.VMEM((count, tokens, 1024), kind)

    quarter = operands[-4].shape
    piece = (1024 // (8 * planes), 1024)
    sems = pltpu.SemaphoreType.DMA
    few = pltpu.VMEM((8, 1024), F32)
    return pl.pallas_call(
        functools.partial(last_kernel, planes, micros, rows),
        out_shape=[
            jax.ShapeDtypeStruct((tokens, 1024), F32),
            jax.ShapeDtypeStruct((16, 1024), F32),
        ]
        + [jax.ShapeDtypeStruct(piece, F32)] * 5
        + [jax.ShapeDtypeStruct(quarter, F32), jax.ShapeDtypeStruct(quarter[::-1], F32)],
        in_specs=[VM] * 3 + [ANY] * 17,
        out_specs=[ANY] * 9,
        scratch_shapes=[
            hold(3, BF),
            hold(3, BF),
            pltpu.VMEM((3, 1024, 1024), BF),
            pltpu.VMEM((tokens, 1024), BF),
            pltpu.VMEM((tokens, 1024), F32),
            pltpu.VMEM((tokens, 1024), F32),
            hold(3, F32),
            pltpu.VMEM((5, 8, 1024), F32),
            pltpu.VMEM((3, 2, 2, 2, planes) + piece, BF),
            pltpu.VMEM((3, 2, 2, planes) + piece, BF),
            pltpu.VMEM((5, 2, planes) + piece, BF),
            pltpu.VMEM((5, planes) + piece, BF),
            pltpu.VMEM((5, planes - 1) + piece, BF),
            pltpu.VMEM((5,) + piece, F32),
            few,
            few,
            pltpu.VMEM((4, 16, 1024), F32),
            pltpu.VMEM((2 + planes, 16, 1024), F32),
            sems((18,)),
            sems((9,)),
            sems((5, 2, 1 + planes, 2)),
            sems((3 + planes, 2)),
            pltpu.VMEM((2,) + quarter, BF),
            pltpu.VMEM((2,) + quarter, F32),
            pltpu.VMEM(quarter, F32),
            pltpu.VMEM(quarter[::-1], F32),
            sems((2, 2)),
            pltpu.VMEM((2, 2, 2, planes) + piece, BF),
            sems((3, 2)),
        ],
        compiler_params=pltpu.CompilerParams(
            collective_id=2, has_side_effects=True, vmem_limit_bytes=62 << 20
        ),
        cost_estimate=pl.CostEstimate(
            flops=16 * tokens * 1024 * 1024, bytes_accessed=30 << 20, transcendentals=0
        ),
        name="time_mix_weights",
    )(*operands)


def one_micro(block_in, seg_ids, grad_out, vectors, matrices, hidden_w, return_w):
    (
        gain_one,
        bias_one,
        decay_vec,
        extra_array,
        mix_key,
        mix_value,
        mix_recept,
        gain_two,
        bias_two,
        mix_hidden,
        mix_gate,
    ) = vectors
    key_w, value_w, recept_w, output_w, gate_w = matrices
    row_count = block_in.shape[0]
    model_width = block_in.shape[1]
    seg_float = seg_ids.astype(jnp.float32)
    normed_a, unit_a, inv_a = layer_norm(block_in, gain_one, bias_one)
    prev_row, prev_seg = from_behind((normed_a[-1:], seg_float[-1:]), "mp", 1)
    same_row = jnp.concatenate(
        [
            (seg_float[:1] == prev_seg).astype(jnp.float32),
            (seg_ids[1:] == seg_ids[:-1]).astype(jnp.float32),
        ]
    )
    same_col = same_row[:, None]
    shifted_a = jnp.concatenate([prev_row, normed_a[:-1]], axis=0) * same_col
    delta_a = normed_a - shifted_a
    low_key = reduced_precision(shifted_a + delta_a * mix_key)
    low_value = reduced_precision(shifted_a + delta_a * mix_value)
    low_recept = reduced_precision(shifted_a + delta_a * mix_recept)
    lookup_start = product(low_key, key_w)
    content_start = product(low_value, value_w)
    recept = jax.nn.sigmoid(product(low_recept, recept_w))
    feature_fading = jnp.exp(decay_vec)
    positions = jnp.arange(row_count, dtype=jnp.float32)[:, None]
    rising = jnp.exp(positions * feature_fading)
    falling = jnp.exp(-(positions - 1.0) * feature_fading)
    falling_zero = jnp.exp(-positions * feature_fading)
    raised_lookup = jnp.exp(lookup_start)
    weighted_average = raised_lookup * content_start
    order_rows = jnp.arange(row_count)
    lower_tri = jnp.logical_and(
        seg_ids[:, None] == seg_ids[None, :], order_rows[None, :] < order_rows[:, None]
    ).astype(jnp.float32)
    last_mask = (seg_ids == seg_ids[-1]).astype(jnp.float32)
    first_mask = (seg_ids == seg_ids[0]).astype(jnp.float32) * same_row[0]
    forward_mat = jnp.concatenate([lower_tri, last_mask[None]], axis=0)
    stacked = jnp.concatenate(
        [
            rising * weighted_average,
            rising * raised_lookup,
            positions * rising * weighted_average,
            positions * rising * raised_lookup,
        ],
        axis=1,
    )
    summed = jnp.dot(forward_mat, stacked, precision=HIGH)
    inner_sums = summed[:row_count]
    closing = summed[row_count]
    num_loc = falling * inner_sums[:, :model_width]
    den_loc = falling * inner_sums[:, model_width : 2 * model_width]
    num_der = (
        -(positions - 1.0) * num_loc + falling * inner_sums[:, 2 * model_width : 3 * model_width]
    )
    den_der = -(positions - 1.0) * den_loc + falling * inner_sums[:, 3 * model_width :]
    end_fall = jnp.exp(-(row_count - 1.0) * feature_fading)
    state_num = end_fall * closing[:model_width]
    state_den = end_fall * closing[model_width : 2 * model_width]
    state_num_der = (
        -(row_count - 1.0) * state_num + end_fall * closing[2 * model_width : 3 * model_width]
    )
    state_den_der = -(row_count - 1.0) * state_den + end_fall * closing[3 * model_width :]
    uniform_flag = (seg_ids[-1] == seg_ids[0]).astype(jnp.float32) * same_row[0]
    carry_pass = uniform_flag * jnp.exp(-row_count * feature_fading)
    carry_der = -row_count * carry_pass
    zero_vec = jnp.zeros_like(feature_fading)
    one_vec = jnp.ones_like(feature_fading)
    in_num, in_den, in_num_der, in_den_der, pass_total, pass_der = carried_in(
        (state_num, state_den, state_num_der, state_den_der, carry_pass, carry_der),
        "mp",
        state_join,
        (zero_vec, zero_vec, zero_vec, zero_vec, one_vec, zero_vec),
        False,
    )
    carried = first_mask[:, None] * falling_zero
    dividend = num_loc + carried * in_num
    divisor_portion = den_loc + carried * in_den
    numer_der = num_der + carried * (in_num_der - positions * in_num)
    denom_der = den_der + carried * (in_den_der - positions * in_den)
    extra_summand = jnp.exp(extra_array + lookup_start)
    divisor_complete = divisor_portion + extra_summand
    mixture_result = (dividend + extra_summand * content_start) / divisor_complete
    gated = reduced_precision(recept * mixture_result)
    block_mid = block_in + product(gated, output_w)
    normed_b, unit_b, inv_b = layer_norm(block_mid, gain_two, bias_two)
    prev_mid = from_behind(normed_b[-1:], "mp", 1)
    shifted_b = jnp.concatenate([prev_mid, normed_b[:-1]], axis=0) * same_col
    delta_b = normed_b - shifted_b
    low_hidden = reduced_precision(shifted_b + delta_b * mix_hidden)
    low_gate = reduced_precision(shifted_b + delta_b * mix_gate)
    gate_two = jax.nn.sigmoid(product(low_gate, gate_w))
    hidden_rows = lax.all_gather(low_hidden, "mp", axis=0, tiled=True)
    pre_act = product(hidden_rows, hidden_w)
    rectified = jnp.maximum(pre_act, 0.0)
    squared = reduced_precision(rectified * rectified)
    returned = lax.psum_scatter(
        product(squared, return_w).astype(jnp.bfloat16), "mp", scatter_dimension=0, tiled=True
    ).astype(jnp.float32)
    output = block_mid + gate_two * returned
    grad_ret = reduced_precision(grad_out * gate_two)
    grad_gate_pre = reduced_precision(grad_out * returned * gate_two * (1.0 - gate_two))
    d_gate_w = (low_gate, grad_gate_pre)
    grad_low_gate = product_nt(grad_gate_pre, gate_w)
    grad_rows = lax.all_gather(grad_ret, "mp", axis=0, tiled=True)
    grad_squared = product_nt(grad_rows, return_w)
    d_return = (squared, grad_rows)
    grad_pre = reduced_precision(grad_squared * 2.0 * rectified)
    d_hidden = (hidden_rows, grad_pre)
    grad_low_hidden = lax.psum_scatter(
        product_nt(grad_pre, hidden_w).astype(jnp.bfloat16), "mp", scatter_dimension=0, tiled=True
    ).astype(jnp.float32)
    d_mix_hidden = jnp.sum(grad_low_hidden * delta_b, axis=0)
    d_mix_gate = jnp.sum(grad_low_gate * delta_b, axis=0)
    grad_shift_b = (
        grad_low_hidden * (1.0 - mix_hidden) + grad_low_gate * (1.0 - mix_gate)
    ) * same_col
    from_next_b = from_behind(grad_shift_b[:1], "mp", -1)
    grad_norm_b = (
        grad_low_hidden * mix_hidden
        + grad_low_gate * mix_gate
        + jnp.concatenate([grad_shift_b[1:], from_next_b], axis=0)
    )
    grad_mid_norm, d_gain_two, d_bias_two = norm_back(grad_norm_b, unit_b, inv_b, gain_two)
    grad_mid = grad_out + grad_mid_norm
    grad_att = reduced_precision(grad_mid)
    d_output_w = (gated, grad_att)
    grad_gated = product_nt(grad_att, output_w)
    grad_recept_pre = reduced_precision(grad_gated * mixture_result * recept * (1.0 - recept))
    grad_mixed = grad_gated * recept
    d_recept_w = (low_recept, grad_recept_pre)
    grad_low_recept = product_nt(grad_recept_pre, recept_w)
    dividend_adjoint = grad_mixed / divisor_complete
    divisor_adjoint = -dividend_adjoint * mixture_result
    extra_derivative_part = dividend_adjoint * content_start + divisor_adjoint
    extra_derivative = jnp.sum(extra_derivative_part * extra_summand, axis=0)
    d_rate = jnp.sum(dividend_adjoint * numer_der + divisor_adjoint * denom_der, axis=0)
    backward_mat = jnp.concatenate([lower_tri.T, first_mask[None]], axis=0)
    back_sum = jnp.dot(
        backward_mat,
        jnp.concatenate([falling * dividend_adjoint, falling * divisor_adjoint], axis=1),
        precision=HIGH,
    )
    step_back = jnp.exp(-feature_fading)
    from_num = step_back * back_sum[row_count, :model_width]
    from_den = step_back * back_sum[row_count, model_width:]
    out_num, out_den, out_pass = carried_in(
        (from_num, from_den, carry_pass), "mp", suffix_join, (zero_vec, zero_vec, one_vec), True
    )
    tail_fall = last_mask[:, None] * jnp.exp(-(row_count - 1.0 - positions) * feature_fading)
    cumulative_dividend = rising * back_sum[:row_count, :model_width] + tail_fall * out_num
    running_denominator = rising * back_sum[:row_count, model_width:] + tail_fall * out_den
    value_gradient = reduced_precision(
        dividend_adjoint * extra_summand + cumulative_dividend * raised_lookup
    )
    key_gradient = reduced_precision(
        extra_derivative_part * extra_summand
        + cumulative_dividend * weighted_average
        + running_denominator * raised_lookup
    )
    d_key_w = (low_key, key_gradient)
    d_value_w = (low_value, value_gradient)
    grad_low_key = product_nt(key_gradient, key_w)
    grad_low_value = product_nt(value_gradient, value_w)
    d_mix_key = jnp.sum(grad_low_key * delta_a, axis=0)
    d_mix_value = jnp.sum(grad_low_value * delta_a, axis=0)
    d_mix_recept = jnp.sum(grad_low_recept * delta_a, axis=0)
    grad_shift_a = (
        grad_low_key * (1.0 - mix_key)
        + grad_low_value * (1.0 - mix_value)
        + grad_low_recept * (1.0 - mix_recept)
    ) * same_col
    from_next_a = from_behind(grad_shift_a[:1], "mp", -1)
    grad_norm_a = (
        grad_low_key * mix_key
        + grad_low_value * mix_value
        + grad_low_recept * mix_recept
        + jnp.concatenate([grad_shift_a[1:], from_next_a], axis=0)
    )
    grad_in_norm, d_gain_one, d_bias_one = norm_back(grad_norm_a, unit_a, inv_a, gain_one)
    input_grad = grad_mid + grad_in_norm
    grads = (
        d_gain_one,
        d_bias_one,
        d_rate * feature_fading,
        extra_derivative,
        d_mix_key,
        d_mix_value,
        d_mix_recept,
        d_key_w,
        d_value_w,
        d_recept_w,
        d_output_w,
        d_gain_two,
        d_bias_two,
        d_mix_hidden,
        d_mix_gate,
        d_hidden,
        d_return,
        d_gate_w,
    )
    return (output, input_grad, grads)


def generic_body(
    incoming_signal,
    series_number_table,
    upstream_adjoint,
    first_scaling_factor,
    first_scaling_offset,
    logarithmic_fading_speeds,
    present_step_extra,
    lookup_shift_mixture,
    content_shift_mixture,
    admit_lookup_shift_mixture,
    attention_lookup_matrix,
    attention_content_matrix,
    attention_admit_matrix,
    attention_result_matrix,
    second_scaling_factor,
    second_scaling_offset,
    inner_shift_mixture,
    admit_shift_mixture,
    feedforward_lookup_matrix,
    feedforward_content_matrix,
    feedforward_admit_matrix,
):
    hidden_full, return_full = (feedforward_lookup_matrix, feedforward_content_matrix)
    vectors = tuple(
        (
            start_item.astype(jnp.float32)
            for start_item in (
                first_scaling_factor,
                first_scaling_offset,
                logarithmic_fading_speeds,
                present_step_extra,
                lookup_shift_mixture,
                content_shift_mixture,
                admit_lookup_shift_mixture,
                second_scaling_factor,
                second_scaling_offset,
                inner_shift_mixture,
                admit_shift_mixture,
            )
        )
    )
    matrices = (
        attention_lookup_matrix,
        attention_content_matrix,
        attention_admit_matrix,
        attention_result_matrix,
        feedforward_admit_matrix,
    )
    output, input_grad, grads = jax.vmap(
        lambda rows, ids, adjoint: one_micro(
            rows, ids, adjoint, vectors, matrices, hidden_full, return_full
        )
    )(
        incoming_signal[:, 0].astype(jnp.float32),
        series_number_table[:, 0],
        upstream_adjoint[:, 0].astype(jnp.float32),
    )
    totals = tuple(
        product_tn(*(side.reshape(-1, side.shape[-1]) for side in grad))
        if isinstance(grad, tuple)
        else jnp.sum(grad, axis=0)
        for grad in grads
    )
    square = [index for index in range(18) if totals[index].shape == totals[7].shape]
    lines = [index for index in range(18) if totals[index].ndim == 1]
    wide = lax.psum_scatter(
        jnp.concatenate([reduced_precision(totals[index]) for index in square], axis=1),
        ("dp", "mp"),
        scatter_dimension=0,
        tiled=True,
    ).astype(jnp.float32)
    thin = lax.psum_scatter(
        jnp.stack([totals[index] for index in lines], axis=1),
        ("dp", "mp"),
        scatter_dimension=0,
        tiled=True,
    )
    held = dict(zip(square, jnp.split(wide, len(square), axis=1)))
    held.update({index: thin[:, place] for place, index in enumerate(lines)})
    output, input_grad = (output[:, None], input_grad[:, None])
    owned = tuple(held[index] for index in sorted(held))
    hidden_own, return_own = (
        lax.psum_scatter(
            totals[15].astype(jnp.bfloat16), "dp", scatter_dimension=0, tiled=True
        ).astype(jnp.float32),
        lax.psum_scatter(
            totals[16].astype(jnp.bfloat16), "dp", scatter_dimension=1, tiled=True
        ).astype(jnp.float32),
    )
    return (
        output,
        input_grad,
        owned[0],
        owned[1],
        owned[2],
        owned[3],
        owned[4],
        owned[5],
        owned[6],
        owned[7],
        owned[8],
        owned[9],
        owned[10],
        owned[11],
        owned[12],
        owned[13],
        owned[14],
        hidden_own,
        return_own,
        owned[15],
    )


def hand_over(count, *refs):
    sems = refs[3 * count]
    ins, outs = ([], [])
    for index in range(count):
        held = refs[2 * count + index]
        ins.append(pltpu.make_async_copy(refs[index], held, sems.at[0, index]))
        outs.append(pltpu.make_async_copy(held, refs[count + index], sems.at[1, index]))
        ins[-1].start()
    for index in range(count):
        ins[index].wait()
        outs[index].start()
    for copy in outs:
        copy.wait()


def hand_call(arrays):
    count = len(arrays)
    return pl.pallas_call(
        functools.partial(hand_over, count),
        out_shape=[jax.ShapeDtypeStruct(part.shape, part.dtype) for part in arrays],
        in_specs=[ANY] * count,
        out_specs=[ANY] * count,
        scratch_shapes=[pltpu.VMEM(part.shape, part.dtype) for part in arrays]
        + [pltpu.SemaphoreType.DMA((2, count))],
        compiler_params=pltpu.CompilerParams(vmem_limit_bytes=60 << 20),
        name="hand_over",
    )(*arrays)


def kernel_body(
    incoming_signal,
    series_number_table,
    upstream_adjoint,
    first_scaling_factor,
    first_scaling_offset,
    logarithmic_fading_speeds,
    present_step_extra,
    lookup_shift_mixture,
    content_shift_mixture,
    admit_lookup_shift_mixture,
    attention_lookup_matrix,
    attention_content_matrix,
    attention_admit_matrix,
    attention_result_matrix,
    second_scaling_factor,
    second_scaling_offset,
    inner_shift_mixture,
    admit_shift_mixture,
    feedforward_lookup_matrix,
    feedforward_content_matrix,
    feedforward_admit_matrix,
):
    hidden_full, return_full = (feedforward_lookup_matrix, feedforward_content_matrix)
    matrices = (
        attention_lookup_matrix,
        attention_content_matrix,
        attention_admit_matrix,
        attention_result_matrix,
        feedforward_admit_matrix,
    )
    micros, _, rows, depth = incoming_signal.shape
    planes = lax.axis_size("mp") // 2
    x = incoming_signal.reshape(micros * rows, depth)
    adjoint = upstream_adjoint.reshape(micros * rows, depth)
    operands = (
        x,
        series_number_table.reshape(micros, rows),
        adjoint,
        first_scaling_factor,
        first_scaling_offset,
        logarithmic_fading_speeds,
        present_step_extra,
        lookup_shift_mixture,
        content_shift_mixture,
        admit_lookup_shift_mixture,
        second_scaling_factor,
        second_scaling_offset,
        inner_shift_mixture,
        admit_shift_mixture,
        *matrices,
        hidden_full,
        return_full,
    )
    (
        keys, values, recept, num, den, mid, gate, mk, mv, mr, gated, mg, delta_a, delta_b,
        keep, segs, table, segcol, segrow, mh_all, ret_all, w1_all, w2_all, ret_acc, gmh_acc,
        parts1, parts2,
    ) = forward_call(planes, micros, rows, operands)
    key_w, value_w, recept_w, output_w, gate_w = matrices
    (
        output, grad_mid, grad_gate, grad_att, grad_recept, grad_key, grad_value, sums,
        part1, part2, rest1, rest2, squares,
    ) = middle_call(
        planes,
        micros,
        rows,
        (
            table, keep, segs, segcol, segrow, w1_all, w2_all, mh_all, ret_all, ret_acc, gmh_acc,
            parts1, parts2, mid, gate, adjoint, delta_b, keys, values, recept, num, den,
            gate_w, output_w, gated, mg,
        ),
    )
    (
        input_grad, sums, own_output, own_gate, own_recept, own_value, own_key, own_hidden,
        own_return,
    ) = last_call(
        planes,
        micros,
        rows,
        (
            table, keep, sums, squares, mr, grad_recept, mv, grad_value,
            mk, grad_key, recept_w, value_w, key_w, x, delta_a, grad_mid,
            part1, part2, rest1, rest2,
        ),
    )
    (
        output, input_grad, own_key, own_value, own_recept, own_output, own_hidden, own_return,
        own_gate,
    ) = hand_call(
        (
            output, input_grad, own_key, own_value, own_recept, own_output, own_hidden,
            own_return, own_gate,
        )
    )
    span = depth // (lax.axis_size("dp") * lax.axis_size("mp"))
    mine = lax.dynamic_slice_in_dim(
        sums, lax.axis_index(("dp", "mp")) * span, span, axis=1
    )
    line = [mine[index] for index in range(11)]
    shape = incoming_signal.shape
    return (
        output.reshape(shape),
        input_grad.reshape(shape),
        *line[:7],
        own_key,
        own_value,
        own_recept,
        own_output,
        *line[7:],
        own_hidden,
        own_return,
        own_gate,
    )


def solution(mesh):
    placed = (
        P(None, "dp", "mp", None),
        P(None, "dp", "mp"),
        P(None, "dp", "mp", None),
        P(),
        P(),
        P(),
        P(),
        P(),
        P(),
        P(),
        P(),
        P(),
        P(),
        P(),
        P(),
        P(),
        P(),
        P(),
        P(None, "mp"),
        P("mp", None),
        P(),
    )
    fits = mesh.shape["dp"] == 4 and mesh.shape["mp"] == 8
    return jax.shard_map(
        kernel_body if fits else generic_body,
        mesh=mesh,
        in_specs=placed,
        out_specs=(
            P(None, "dp", "mp", None),
            P(None, "dp", "mp", None),
            P(("dp", "mp")),
            P(("dp", "mp")),
            P(("dp", "mp")),
            P(("dp", "mp")),
            P(("dp", "mp")),
            P(("dp", "mp")),
            P(("dp", "mp")),
            P(("dp", "mp"), None),
            P(("dp", "mp"), None),
            P(("dp", "mp"), None),
            P(("dp", "mp"), None),
            P(("dp", "mp")),
            P(("dp", "mp")),
            P(("dp", "mp")),
            P(("dp", "mp")),
            P("dp", "mp"),
            P("mp", "dp"),
            P(("dp", "mp"), None),
        ),
        check_vma=False,
    )
```

```python
import functools

import jax
import jax.numpy as jnp
from jax import lax
from jax.experimental import pallas as pl
from jax.experimental.pallas import tpu as pltpu
from jax.sharding import PartitionSpec as P

EPS = 1e-05
HIGH = lax.Precision.HIGHEST


def from_behind(block, axis, distance):
    devices = range(lax.axis_size(axis))
    route = [(i - distance, i) for i in devices if i - distance in devices]
    return lax.ppermute(block, axis, route)


def carried_in(shard, axis, combine, identity, reverse):
    length, mine = (lax.axis_size(axis), lax.axis_index(axis))
    everything = jax.tree.map(lambda part: lax.all_gather(part, axis), shard)
    start = jax.tree.map(
        lambda part, zero: jnp.broadcast_to(jnp.asarray(zero, part.dtype), part.shape),
        shard,
        identity,
    )

    def step(k, before):
        at = length - 1 - k if reverse else k
        reached = at > mine if reverse else at < mine
        new = combine(before, jax.tree.map(lambda part: part[at], everything))
        return jax.tree.map(lambda a, b: jnp.where(reached, a, b), new, before)

    return lax.fori_loop(0, length, step, start)


def reduced_precision(values):
    return values.astype(jnp.bfloat16)


def product(left, right):
    return jnp.dot(left, right, preferred_element_type=jnp.float32)


def product_tn(left, right):
    return lax.dot_general(
        left, right, (((0,), (0,)), ((), ())), preferred_element_type=jnp.float32
    )


def product_nt(left, right):
    return lax.dot_general(
        left, right, (((1,), (1,)), ((), ())), preferred_element_type=jnp.float32
    )


def layer_norm(values, gain, bias):
    average = jnp.mean(values, axis=-1, keepdims=True)
    centre = values - average
    inverse = lax.rsqrt(jnp.mean(centre * centre, axis=-1, keepdims=True) + EPS)
    unit = centre * inverse
    return (unit * gain + bias, unit, inverse)


def norm_back(grad_in, unit, inverse, gain):
    scaled = grad_in * gain
    grad_values = inverse * (
        scaled
        - jnp.mean(scaled, axis=-1, keepdims=True)
        - unit * jnp.mean(scaled * unit, axis=-1, keepdims=True)
    )
    return (grad_values, jnp.sum(grad_in * unit, axis=0), jnp.sum(grad_in, axis=0))


def state_join(earlier, latter):
    return (
        latter[4] * earlier[0] + latter[0],
        latter[4] * earlier[1] + latter[1],
        latter[4] * earlier[2] + latter[5] * earlier[0] + latter[2],
        latter[4] * earlier[3] + latter[5] * earlier[1] + latter[3],
        earlier[4] * latter[4],
        earlier[5] * latter[4] + earlier[4] * latter[5],
    )


def suffix_join(earlier, latter):
    return (
        latter[0] + latter[2] * earlier[0],
        latter[1] + latter[2] * earlier[1],
        latter[2] * earlier[2],
    )


BF = jnp.bfloat16
F32 = jnp.float32
MESH = pl.DeviceIdType.MESH
NN = (((1,), (0,)), ((), ()))
NT = (((1,), (1,)), ((), ()))
TN = (((0,), (0,)), ((), ()))


def dot(left, right, form=NN):
    return lax.dot_general(left, right, form, preferred_element_type=F32)


def dot_exact_left(left, right):
    high = right.astype(BF)
    rest = (right - high.astype(F32)).astype(BF)
    return dot(left, high) + dot(left, rest)


def wide(lanes, width):
    return jnp.concatenate([lanes] * (width // 128), axis=1)


def tile(index, size):
    return pl.ds(pl.multiple_of(index * size, size), size)


def unit_of(values):
    average = jnp.mean(values, axis=-1, keepdims=True)
    centre = values - average
    inverse = lax.rsqrt(jnp.mean(centre * centre, axis=-1, keepdims=True) + EPS)
    return (centre * inverse, inverse)


def remote(source, target, send, receive, device):
    return pltpu.make_async_remote_copy(
        src_ref=source,
        dst_ref=target,
        send_sem=send,
        recv_sem=receive,
        device_id=device,
        device_id_type=MESH,
    )


class Place:
    def __init__(self, planes):
        self.planes = planes
        self.dp, self.mp = (lax.axis_index("dp"), lax.axis_index("mp"))
        self.z = lax.div(self.mp, 2)
        self.core = lax.rem(self.mp, 2)
        self.count = 2 * planes
        self.other = (self.dp, self.mp + 1 - 2 * self.core)
        self.side_x = (self.dp + 1 - 2 * lax.rem(self.dp, 2), self.mp)
        self.side_y = (lax.rem(self.dp + 2, 4), self.mp)

    def ahead(self, steps):
        return (self.dp, lax.rem(self.mp + steps + self.count, self.count))

    def plane(self, steps):
        return (self.dp, lax.rem(self.z + steps + self.planes, self.planes) * 2 + self.core)


def greet(devices):
    barrier = pltpu.get_barrier_semaphore()
    for device in devices:
        pl.semaphore_signal(barrier, inc=1, device_id=device, device_id_type=MESH)
    pl.semaphore_wait(barrier, len(devices))


def feed_rows(w1, w2, mh2, gr2, sq_s, gp_s, ret_acc, gmh_acc, fresh):
    def rows_of(i):
        span = tile(i, 256)
        pre = dot(mh2[span, :], w1[...])
        rectified = jnp.maximum(pre, 0.0)
        squared = (rectified * rectified).astype(BF)
        sq_s[span, :] = squared
        grad_squared = dot(gr2[span, :], w2[...], NT)
        grad_pre = (grad_squared * 2.0 * rectified).astype(BF)
        gp_s[span, :] = grad_pre
        if fresh:
            ret_acc[span, :] = dot(squared, w2[...])
            gmh_acc[span, :] = dot(grad_pre, w1[...], NT)
        else:
            ret_acc[span, :] += dot(squared, w2[...])
            gmh_acc[span, :] += dot(grad_pre, w1[...], NT)

    return rows_of


def feed_grads(mh2, gr2, sq_s, gp_s, parts1, parts2):
    @pl.loop(0, 4)
    def _(q):
        line, side = (lax.div(q, 2), lax.rem(q, 2))
        cols = tile(q, 256)
        parts1[side, line] = dot(mh2[:, cols], gp_s[...], TN).astype(BF)
        parts2[line, side] = dot(gr2[:, cols], sq_s[...], TN).astype(BF)


def forward_kernel(
    planes,
    micros,
    rows,
    x_ref,
    table_ref,
    adj_ref,
    *refs,
):
    (
    lines, refs) = (refs[:11], refs[11:])
    (
    key_w,
    value_w,
    recept_w,
    output_w,
    gate_w,
    w1_ref,
    w2_ref,
    k_out,
    v_out,
    r_out,
    num_out,
    den_out,
    mid_out,
    gate_out,
    mk_out,
    mv_out,
    mr_out,
    gated_out,
    mg_out,
    da_out,
    db_out,
    keep_out,
    segs_out,
    vec_out,
    segcol_out,
    segrow_out,
    mh_all,
    ret_all,
    w1_all,
    w2_all,
    ret_acc_out,
    gmh_acc_out,
    parts1_out,
    parts2_out,
    wk,
    wv,
    wr,
    wo,
    wg,
    k_s,
    v_s,
    r_s,
    num_s,
    den_s,
    mid_s,
    gate_s,
    xb_s,
    da_s,
    mk_s,
    mv_s,
    mr_s,
    gated_s,
    mg_s,
    keep_s,
    segcol_ref,
    segrow_ref,
    segpay_ref,
    last_ref,
    mask_s,
    halo_a,
    near_a,
    pay_b,
    halo_b,
    segs_s,
    state_own,
    state_other,
    state_chip,
    state_in,
    carry_s,
    w_sem,
    out_sem,
    small_sem,
    z_sem,
    s_sem,
    vec_ref,
    mh2,
    gr2,
    sq_s,
    gp_s,
    ret_acc,
    gmh_acc,
    parts1,
    parts2,
    ff_sem,
    ) = refs
    at = Place(planes)
    dp, mp, z, core = (at.dp, at.mp, at.z, at.core)
    tokens = micros * rows
    peers = [at.ahead(step) for step in range(1, at.count)]
    greet(peers + [at.side_x, at.side_y])

    for index, line in enumerate(lines):
        vec_ref[index : index + 1, :] = line[...].astype(F32).reshape(1, 1024)
    vec_ref[11:16, :] = jnp.zeros((5, 1024), F32)

    numbers = table_ref[...].astype(F32)
    rest = jnp.zeros((8 - micros, rows), F32)
    segrow_ref[...] = jnp.concatenate([numbers, rest], axis=0)
    columns = segrow_ref[...].T
    ends = [jnp.broadcast_to(numbers[:, at_end], (micros, 128)) for at_end in (slice(rows - 1, rows), slice(0, 1))]
    segpay_ref[...] = jnp.concatenate([ends[0], ends[0], ends[1], ends[1]], axis=0)
    last_ref[...] = jnp.zeros((8, 1024), F32)
    for m in range(micros):
        segcol_ref[m * rows : (m + 1) * rows, :] = jnp.broadcast_to(columns[:, m : m + 1], (rows, 128))
        last_ref[m : m + 1, :] = x_ref[(m + 1) * rows - 16 : (m + 1) * rows, :].astype(F32)[15:16]

    quarter1, quarter2 = (w1_ref.shape[0] // 4, w2_ref.shape[0] // 4)
    q1, q2 = (tile(dp, quarter1), tile(dp, quarter2))
    z_copies = {}
    for step in (1, planes - 1):
        to = at.plane(-step)
        z_copies[step - 1] = (
            remote(w1_ref.at[q1], w1_all.at[step - 1, q1], z_sem.at[step - 1, 0, 0], z_sem.at[step - 1, 0, 1], to),
            remote(w2_ref.at[q2], w2_all.at[step - 1, q2], z_sem.at[step - 1, 1, 0], z_sem.at[step - 1, 1, 1], to),
        )
    half1 = tile(lax.div(dp, 2), 2 * quarter1)
    far2 = tile(lax.rem(dp + 2, 4), quarter2)
    back = at.plane(-1)
    onward_1 = remote(w1_all.at[0, half1], w1_all.at[1, half1], z_sem.at[1, 0, 0], z_sem.at[1, 0, 1], back)
    onward_2 = (
        remote(w2_all.at[0, q2], w2_all.at[1, q2], z_sem.at[1, 1, 0], z_sem.at[1, 1, 1], back),
        remote(w2_all.at[0, far2], w2_all.at[1, far2], z_sem.at[1, 2, 0], z_sem.at[1, 2, 1], back),
    )

    halo_copy = remote(last_ref, halo_a, small_sem.at[0, 0], small_sem.at[0, 1], at.ahead(1))
    halo_copy.start()
    seg_copies = [
        remote(segpay_ref, segs_s.at[mp], small_sem.at[1 + step, 0], small_sem.at[1 + step, 1], device)
        for step, device in enumerate(peers)
    ]
    for copy in seg_copies:
        copy.start()
    segs_s[mp] = segpay_ref[...]
    loads = []
    for index, (source, target) in enumerate(
        ((key_w, wk), (value_w, wv), (recept_w, wr), (output_w, wo), (gate_w, wg))
    ):
        loads.append(pltpu.make_async_copy(source, target, w_sem.at[index]))
        loads[-1].start()
    for copy in z_copies[0]:
        copy.start()
    halo_copy.wait()
    for copy in seg_copies:
        copy.wait()

    side1 = tile(dp + 1 - 2 * lax.rem(dp, 2), quarter1)

    def hop(array, span, step, index, device):
        part = array.at[step, span]
        return remote(part, part, z_sem.at[step, index, 0], z_sem.at[step, index, 1], device)

    def early(step):
        return (
            hop(w1_all, q1, step, 2, at.side_x),
            hop(w2_all, q2, step, 3, at.side_y),
            hop(w2_all, q2, step, 5, at.side_x),
            hop(w1_all, q1, step, 4, at.side_y),
        )

    def late(step):
        return (
            hop(w1_all, side1, step, 7, at.side_y),
            hop(w2_all, far2, step, 6, at.side_x),
        )

    def across(step):
        return (
            hop(w1_all, half1, step, 4, at.side_y),
            hop(w2_all, q2, step, 5, at.side_x),
            hop(w2_all, far2, step, 6, at.side_x),
        )

    def start(group):
        for copy in group:
            copy.start()

    def finish(group):
        for copy in group:
            copy.wait()

    early_0, early_2 = (early(0), early(2))
    late_0, across_1, late_2 = (late(0), across(1), late(2))

    before = lax.rem(mp + at.count - 1, at.count)
    has_before = mp > 0
    first_row = lax.broadcasted_iota(jnp.int32, (rows, 128), 0) == 0
    row_at = lax.broadcasted_iota(jnp.int32, (rows, rows), 0)
    col_at = lax.broadcasted_iota(jnp.int32, (rows, rows), 1)
    for m in range(micros):
        here = segcol_ref[m * rows : (m + 1) * rows, :]
        behind = jnp.where(
            first_row, segs_s[before, m : m + 1, :], pltpu.roll(here, 1, 0)
        )
        same = jnp.logical_and(
            here == behind, jnp.logical_or(jnp.logical_not(first_row), has_before)
        )
        keep_s[m * rows : (m + 1) * rows, :] = same.astype(F32)
        mask_s[m] = jnp.logical_and(
            here == segrow_ref[m : m + 1, :], col_at < row_at
        ).astype(F32).astype(BF)

    block = 32
    at_first = lax.broadcasted_iota(jnp.int32, (block, 1024), 0) == 0
    gain, bias = (vec_ref[0:1, :], vec_ref[1:2, :])
    near_a[...] = unit_of(halo_a[...])[0] * gain + bias
    for m in range(micros):

        def mix_a(b, prev, m=m):
            span = tile(m * (rows // block) + b, block)
            normed = unit_of(x_ref[span, :].astype(F32))[0] * gain + bias
            shifted = jnp.where(at_first, prev, pltpu.roll(normed, 1, 0)) * wide(
                keep_s[span, :], 1024
            )
            delta = normed - shifted
            da_s[span, :] = delta
            mk_s[span, :] = (shifted + delta * vec_ref[4:5, :]).astype(BF)
            mv_s[span, :] = (shifted + delta * vec_ref[5:6, :]).astype(BF)
            mr_s[span, :] = (shifted + delta * vec_ref[6:7, :]).astype(BF)
            return normed[block - 1 : block, :]

        lax.fori_loop(0, rows // block, mix_a, near_a[m : m + 1, :], unroll=2)

    outs = []

    def put(source, target):
        copy = pltpu.make_async_copy(source, target, out_sem.at[len(outs)])
        copy.start()
        outs.append(copy)

    put(da_s, da_out)
    put(keep_s, keep_out)
    put(segs_s, segs_out)
    put(segcol_ref, segcol_out)
    put(vec_ref, vec_out)
    put(segrow_ref, segrow_out)
    put(mk_s, mk_out)
    put(mv_s, mv_out)
    put(mr_s, mr_out)

    loads[0].wait()
    loads[1].wait()
    width = 256
    place = lax.broadcasted_iota(jnp.int32, (rows, width), 0).astype(F32)

    @pl.loop(0, 1024 // width)
    def _(i):
        cols = tile(i, width)
        rate = jnp.exp(vec_ref[2:3, cols])
        rising = jnp.exp(place * rate)
        falling = jnp.exp((1.0 - place) * rate)
        step_back = jnp.exp(-rate)
        keys = dot(mk_s[...], wk[:, cols])
        values = dot(mv_s[...], wv[:, cols])
        for m in range(micros):
            span = slice(m * rows, (m + 1) * rows)
            key, value = (keys[span], values[span])
            raised = jnp.exp(key)
            weighted = raised * value
            num = falling * dot_exact_left(mask_s[m], rising * weighted)
            den = falling * dot_exact_left(mask_s[m], rising * raised)
            k_s[span, cols] = key
            v_s[span, cols] = value
            num_s[span, cols] = num
            den_s[span, cols] = den
            state_own[m : m + 1, cols] = step_back * num[rows - 1 :] + weighted[rows - 1 :]
            state_own[micros + m : micros + m + 1, cols] = (
                step_back * den[rows - 1 :] + raised[rows - 1 :]
            )

    put(k_s, k_out)
    put(v_s, v_out)
    core_copy = remote(state_own, state_other, s_sem.at[0, 0], s_sem.at[0, 1], at.other)
    core_copy.start()
    finish(z_copies[0])
    start(early_0)
    z_copies[2][0].start()

    loads[2].wait()

    @pl.loop(0, 2)
    def _(i):
        span = tile(i, tokens // 2)
        r_s[span, :] = jax.nn.sigmoid(dot(mr_s[span, :], wr[...]))

    put(r_s, r_out)

    pair = lax.div(mp, 2) * 2
    decay_all = jnp.exp(-float(rows) * jnp.exp(vec_ref[2:3, :]))
    core_copy.wait()

    def last_of(device):
        return wide(segs_s[lax.rem(device + at.count, at.count), 0 : 2 * micros, :], 1024)

    even = jnp.where(core == 0, state_own[...], state_other[...])
    odd = jnp.where(core == 0, state_other[...], state_own[...])
    state_chip[...] = odd + jnp.where(last_of(pair) == last_of(pair + 1), decay_all * even, 0.0)
    chip_copies = [
        remote(state_chip, state_in.at[step - 1], s_sem.at[step, 0], s_sem.at[step, 1], at.plane(step))
        for step in range(1, planes)
    ]
    start(chip_copies)
    finish(early_0[0:2])
    start(late_0)
    finish(chip_copies)
    z_copies[2][1].start()
    total = jnp.zeros_like(state_chip[...])
    power = jnp.ones_like(decay_all)
    for step in range(1, planes):
        fits = jnp.logical_and(
            last_of(pair - 2 * step + 1) == last_of(pair - 1), z >= step
        )
        total = total + jnp.where(fits, power * state_in[step - 1], 0.0)
        power = power * decay_all * decay_all
    joined = state_other[...] + jnp.where(last_of(pair) == last_of(pair - 1), decay_all * total, 0.0)
    carry_s[...] = jnp.where(core == 0, total, joined)

    @pl.loop(0, 1024 // width)
    def _(i):
        cols = tile(i, width)
        rate = jnp.exp(vec_ref[2:3, cols])
        falling = jnp.exp(-place * rate)
        extra = vec_ref[3:4, cols]
        for m in range(micros):
            span = slice(m * rows, (m + 1) * rows)
            fits = jnp.logical_and(
                segcol_ref[span, :] == segs_s[before, m : m + 1, :], has_before
            ).astype(F32)
            carried = wide(fits, width) * falling
            num = num_s[span, cols] + carried * carry_s[m : m + 1, cols]
            den = den_s[span, cols] + carried * carry_s[micros + m : micros + m + 1, cols]
            bonus = jnp.exp(extra + k_s[span, cols])
            mixed = (num + bonus * v_s[span, cols]) / (den + bonus)
            num_s[span, cols] = num
            den_s[span, cols] = den
            gated_s[span, cols] = (r_s[span, cols] * mixed).astype(BF)

    put(num_s, num_out)
    put(den_s, den_out)
    put(gated_s, gated_out)
    loads[3].wait()

    @pl.loop(0, 2)
    def _(i):
        span = tile(i, tokens // 2)
        mid_s[span, :] = x_ref[span, :].astype(F32) + dot(gated_s[span, :], wo[...])

    put(mid_s, mid_out)
    gain_b, bias_b = (vec_ref[7:8, :], vec_ref[8:9, :])

    def norm_b(b):
        span = tile(b, block)
        xb_s[span, :] = unit_of(mid_s[span, :])[0] * gain_b + bias_b

    for m in range(micros):
        norm_b((m + 1) * (rows // block) - 1)
        pay_b[m : m + 1, :] = xb_s[(m + 1) * rows - 1 : (m + 1) * rows, :]
    pay_b[micros:, :] = jnp.zeros((8 - micros, 1024), F32)
    halo_b_copy = remote(pay_b, halo_b, s_sem.at[planes, 0], s_sem.at[planes, 1], at.ahead(1))
    halo_b_copy.start()
    for m in range(micros):

        @pl.loop(m * (rows // block), (m + 1) * (rows // block) - 1)
        def _(b):
            norm_b(b)

    halo_b_copy.wait()
    onward_1.start()
    start(onward_2)
    finish(z_copies[2])
    start(early_2)
    for m in range(micros):

        def mix_b(b, prev, m=m):
            span = tile(m * (rows // block) + b, block)
            normed = xb_s[span, :]
            shifted = jnp.where(at_first, prev, pltpu.roll(normed, 1, 0)) * wide(
                keep_s[span, :], 1024
            )
            delta = normed - shifted
            xb_s[span, :] = delta
            mh2[span, :] = (shifted + delta * vec_ref[9:10, :]).astype(BF)
            mg_s[span, :] = (shifted + delta * vec_ref[10:11, :]).astype(BF)
            return normed[block - 1 : block, :]

        lax.fori_loop(0, rows // block, mix_b, halo_b[m : m + 1, :], unroll=2)

    own, far = (slice(0, tokens), slice(tokens, 2 * tokens))
    mh_copy = remote(
        mh2.at[own], mh2.at[far], s_sem.at[planes + 1, 0], s_sem.at[planes + 1, 1], at.other
    )
    mh_copy.start()
    put(mg_s, mg_out)
    put(xb_s, db_out)
    loads[4].wait()

    @pl.loop(0, 2)
    def _(i):
        span = tile(i, tokens // 2)
        gate = jax.nn.sigmoid(dot(mg_s[span, :], wg[...]))
        gate_s[span, :] = gate
        gr2[span, :] = (adj_ref[span, :].astype(F32) * gate).astype(BF)

    ret_copy = remote(
        gr2.at[own], gr2.at[far], s_sem.at[planes + 2, 0], s_sem.at[planes + 2, 1], at.other
    )
    ret_copy.start()
    put(gate_s, gate_out)
    hidden = w1_ref.shape[1]
    w1_own, w2_own = (wk.at[:, 0:hidden], wv.at[0:hidden])
    w1_next, w2_next = (wk.at[:, hidden : 2 * hidden], wv.at[hidden : 2 * hidden])
    ff_loads = [
        pltpu.make_async_copy(source, target, ff_sem.at[index])
        for index, (source, target) in enumerate(
            ((w1_ref, w1_own), (w2_ref, w2_own), (w1_all.at[0], w1_next), (w2_all.at[0], w2_next))
        )
    ]
    ff_loads[0].start()
    ff_loads[1].start()
    ff_loads[0].wait()
    ff_loads[1].wait()
    half = tokens // 256
    step = feed_rows(w1_own, w2_own, mh2, gr2, sq_s, gp_s, ret_acc, gmh_acc, True)
    pl.loop(0, half)(step)
    mh_copy.wait()
    ret_copy.wait()
    finish(early_2[0:2])
    start(late_2)
    put(mh2, mh_all)
    put(gr2, ret_all)
    finish(early_0[2:4] + late_0)
    ff_loads[2].start()
    ff_loads[3].start()
    pl.loop(half, 2 * half)(step)
    feed_grads(mh2, gr2, sq_s, gp_s, parts1.at[0], parts2.at[0])
    onward_1.wait()
    across_1[0].start()
    put(parts1.at[0], parts1_out.at[0])
    put(parts2.at[0], parts2_out.at[0])
    ff_loads[2].wait()
    ff_loads[3].wait()
    step = feed_rows(w1_next, w2_next, mh2, gr2, sq_s, gp_s, ret_acc, gmh_acc, False)
    pl.loop(0, half)(step)
    onward_2[0].wait()
    across_1[1].start()
    pl.loop(half, 2 * half)(step)
    onward_2[1].wait()
    across_1[2].start()
    put(ret_acc, ret_acc_out)
    put(gmh_acc, gmh_acc_out)
    feed_grads(mh2, gr2, sq_s, gp_s, parts1.at[1], parts2.at[1])
    put(parts1.at[1], parts1_out.at[1])
    put(parts2.at[1], parts2_out.at[1])
    finish(early_2[2:4] + late_2)
    finish(across_1)
    for copy in outs:
        copy.wait()


ANY = pl.BlockSpec(memory_space=pl.ANY)
VM = pl.BlockSpec(memory_space=pltpu.VMEM)


def forward_call(planes, micros, rows, operands):
    tokens = micros * rows
    hidden = operands[-1].shape[0]

    def big(kind):
        return jax.ShapeDtypeStruct((tokens, 1024), kind)

    def hold(kind):
        return pltpu.VMEM((tokens, 1024), kind)

    square = pltpu.VMEM((1024, 1024), BF)
    few = pltpu.VMEM((8, 1024), F32)
    pair = pltpu.SemaphoreType.DMA
    return pl.pallas_call(
        functools.partial(forward_kernel, planes, micros, rows),
        out_shape=[big(F32)] * 7
        + [big(BF)] * 5
        + [big(F32)] * 2
        + [
            jax.ShapeDtypeStruct((tokens, 128), F32),
            jax.ShapeDtypeStruct((2 * planes, 16, 128), F32),
            jax.ShapeDtypeStruct((16, 1024), F32),
            jax.ShapeDtypeStruct((tokens, 128), F32),
            jax.ShapeDtypeStruct((8, rows), F32),
        ]
        + [jax.ShapeDtypeStruct((2 * tokens, 1024), BF)] * 2
        + [
            jax.ShapeDtypeStruct((planes - 1, 1024, hidden), BF),
            jax.ShapeDtypeStruct((planes - 1, hidden, 1024), BF),
        ]
        + [jax.ShapeDtypeStruct((2 * tokens, 1024), F32)] * 2
        + [jax.ShapeDtypeStruct((2, 2, 2, 256, hidden), BF)] * 2,
        in_specs=[VM] * 14 + [ANY] * 7,
        out_specs=[ANY] * 27,
        scratch_shapes=[square] * 5
        + [hold(F32)] * 9
        + [hold(BF)] * 5
        + [
            pltpu.VMEM((tokens, 128), F32),
            pltpu.VMEM((tokens, 128), F32),
            pltpu.VMEM((8, rows), F32),
            pltpu.VMEM((4 * micros, 128), F32),
            few,
            pltpu.VMEM((micros, rows, rows), BF),
            few,
            few,
            few,
            few,
            pltpu.VMEM((2 * planes, 16, 128), F32),
            few,
            few,
            few,
            pltpu.VMEM((planes - 1, 8, 1024), F32),
            few,
            pair((5,)),
            pair((29,)),
            pair((2 * planes + 1, 2)),
            pair((planes - 1, 8, 2)),
            pair((planes + 3, 2)),
            pltpu.VMEM((16, 1024), F32),
            pltpu.VMEM((2 * tokens, 1024), BF),
            pltpu.VMEM((2 * tokens, 1024), BF),
            pltpu.VMEM((2 * tokens, hidden), BF),
            pltpu.VMEM((2 * tokens, hidden), BF),
            pltpu.VMEM((2 * tokens, 1024), F32),
            pltpu.VMEM((2 * tokens, 1024), F32),
            pltpu.VMEM((2, 2, 2, 256, hidden), BF),
            pltpu.VMEM((2, 2, 2, 256, hidden), BF),
            pair((4,)),
        ],
        compiler_params=pltpu.CompilerParams(
            collective_id=0, has_side_effects=True, vmem_limit_bytes=62 << 20
        ),
        cost_estimate=pl.CostEstimate(
            flops=36 * tokens * 1024 * 1024, bytes_accessed=40 << 20, transcendentals=6 * tokens * 1024
        ),
        name="time_mix_forward",
    )(*operands)


class Reduce:
    def __init__(self, at, parts, first, second, far, sems, slot, x_first, source=None):
        self.at, self.parts, self.slot = (at, parts, slot if far is not None else 0)
        side = lax.rem(at.dp, 2)
        line = lax.div(at.dp, 2)
        self.one, self.two = (side, line) if x_first else (line, side)
        near, next_to = (at.side_x, at.side_y) if x_first else (at.side_y, at.side_x)
        self.first, self.second, self.far = (first, second, far)
        self.copy_1 = remote(
            (parts if source is None else source).at[1 - self.one],
            first,
            sems.at[0, 0],
            sems.at[0, 1],
            near,
        )
        self.copy_2 = remote(
            parts.at[self.one, 1 - self.two], second, sems.at[1, 0], sems.at[1, 1], next_to
        )
        if self.slot:
            self.copy_3 = remote(
                parts.at[self.one, self.two], far, sems.at[2, 0], sems.at[2, 1], at.plane(slot)
            )

    def start(self):
        self.copy_1.start()

    def add(self, half, other):
        mine = self.parts.at[self.one, half]

        @pl.loop(0, mine.shape[0] // 64)
        def _(i):
            span = tile(i, 64)
            mine[span, :] = (mine[span, :].astype(F32) + other[span, :].astype(F32)).astype(BF)

    def middle(self):
        self.copy_1.wait()
        self.add(1 - self.two, self.first.at[1 - self.two])
        self.copy_2.start()
        self.add(self.two, self.first.at[self.two])

    def last(self):
        self.copy_2.wait()
        self.add(self.two, self.second)
        if self.slot:
            self.copy_3.start()

    def close(self):
        if self.slot:
            self.copy_3.wait()


def sum_rows(into, index, values):
    total = values[0:8]
    for start in range(8, values.shape[0], 8):
        total = total + values[start : start + 8]
    into[index] = into[index] + total


def norm_back_rows(grad, unit, inverse, gain):
    scaled = grad * gain
    return inverse * (
        scaled
        - jnp.mean(scaled, axis=-1, keepdims=True)
        - unit * jnp.mean(scaled * unit, axis=-1, keepdims=True)
    )


def fill_square(parts, left, right, planes, split):
    @pl.loop(0, 4)
    def _(q):
        line, side = (lax.div(q, 2), lax.rem(q, 2))
        made = dot(left[:, tile(q, 256)], right[...], TN).astype(BF)
        pieces = made.reshape(planes, 2, 256 // (2 * planes), 1024)
        for core in range(2):
            if split > 0:
                parts[core, side, line, :, :, 0:split] = pieces[:, core, :, 0:split]
            if split < 1024:
                parts[core, line, side, :, :, split:1024] = pieces[:, core, :, split:1024]


def add_square(mine, other, planes):
    for one in range(2):
        for two in range(2):

            @pl.loop(0, planes)
            def _(i):
                mine[one, two, i] = (
                    mine[one, two, i].astype(F32) + other[one, two, i].astype(F32)
                ).astype(BF)


def middle_kernel(
    planes,
    micros,
    rows,
    vec_ref,
    keep_ref,
    segs_ref,
    segcol_ref,
    segrow_ref,
    w1_all,
    w2_all,
    mh_all,
    ret_all,
    ret_acc_ref,
    gmh_acc_ref,
    parts1_ref,
    parts2_ref,
    mid_ref,
    gate_ref,
    adj_ref,
    db_ref,
    k_ref,
    v_ref,
    r_ref,
    num_ref,
    den_ref,
    gate_w,
    output_w,
    gated_ref,
    mg_ref,
    out_ref,
    gmid_out,
    ggp_out,
    gatt_out,
    grp_out,
    gk_out,
    gv_out,
    sums_out,
    own1_out,
    own2_out,
    rest1_out,
    rest2_out,
    square_out,
    parts1,
    parts2,
    first1,
    first2,
    second1,
    second2,
    far1,
    far2,
    ret_acc,
    gmh_acc,
    ret_send,
    gmh_send,
    ret_recv,
    gmh_recv,
    mid_s,
    gate_s,
    adj_s,
    db_s,
    sums_s,
    sums_flat,
    mask_s,
    pay_b,
    halo_b,
    state_own,
    state_other,
    state_chip,
    state_in,
    carry_s,
    load_sem,
    out_sem,
    rs_sem,
    s_sem,
    square_parts,
    square_across,
    square_sem,
    ahead_s,
    ahead_sem,
):
    at = Place(planes)
    dp, mp, z, core = (at.dp, at.mp, at.z, at.core)
    tokens = micros * rows
    hidden = w1_all.shape[2]
    outs = []

    def put(source, target):
        copy = pltpu.make_async_copy(source, target, out_sem.at[len(outs)])
        copy.start()
        outs.append(copy)

    loaded = []

    def load(source, target):
        copy = pltpu.make_async_copy(source, target, load_sem.at[len(loaded)])
        copy.start()
        loaded.append(copy)
        return copy

    greet(
        [at.other, at.side_x, at.side_y]
        + [at.plane(step) for step in range(1, planes)]
        + [at.ahead(1), at.ahead(-1)]
    )
    half_cols = hidden // 2
    early, late_half = (slice(0, half_cols), slice(half_cols, hidden))

    def group(slot, cols, sem, source):
        made = []
        for kind, (parts, first, second, far, parts_ref) in enumerate(
            (
                (parts1, first1, second1, far1, parts1_ref),
                (parts2, first2, second2, far2, parts2_ref),
            )
        ):
            made.append(
                Reduce(
                    at,
                    parts.at[slot, :, :, :, cols],
                    first.at[slot, :, :, cols],
                    second.at[slot, :, cols],
                    far.at[slot // 2, :, cols] if slot % 2 else None,
                    rs_sem.at[sem, kind],
                    slot,
                    kind == 0,
                    parts_ref.at[slot, :, :, :, cols] if source else None,
                )
            )
        return made

    everything = slice(0, hidden)
    reduces = {
        "near": group(1, late_half, 0, True),
        "own": group(0, late_half, 1, True),
        "joined": group(0, early, 2, False),
        3: group(3, everything, 3, False),
        2: group(2, everything, 4, False),
    }
    ahead_copies = [
        remote(
            parts_ref.at[1, :, :, :, early],
            ahead_s.at[kind],
            ahead_sem.at[kind, 0],
            ahead_sem.at[kind, 1],
            at.plane(1),
        )
        for kind, parts_ref in enumerate((parts1_ref, parts2_ref))
    ]
    ret_copy = remote(ret_send, ret_recv, s_sem.at[0, 0], s_sem.at[0, 1], at.other)
    gmh_copy = remote(gmh_send, gmh_recv, s_sem.at[1, 0], s_sem.at[1, 1], at.other)

    def begin(name):
        for reduce in reduces[name]:
            reduce.start()

    def middle(name):
        for reduce in reduces[name]:
            reduce.middle()

    def last(name):
        for reduce in reduces[name]:
            reduce.last()

    begin("near")
    begin("own")
    for copy in ahead_copies:
        copy.start()

    def feed_forward(w1, w2, mh2, gr2, sq_s, gp_s):
        mh_load = [load(mh_all, mh2), load(ret_all, gr2)]
        order = (planes - 1, planes - 2)
        slots = []
        part_loads = []
        for index, slot in enumerate(order):
            slots.append(
                (load(w1_all.at[slot - 1], w1.at[index]), load(w2_all.at[slot - 1], w2.at[index]))
            )
            if index == 0:
                mh_load += [load(ret_acc_ref, ret_acc), load(gmh_acc_ref, gmh_acc)]
                for part in (1, 0):
                    part_loads.append(load(parts1_ref.at[part], parts1.at[part]))
                    part_loads.append(load(parts2_ref.at[part], parts2.at[part]))
        late = [load(mid_ref, mid_s), load(gate_ref, gate_s), load(adj_ref, adj_s), load(db_ref, db_s)]
        for copy in mh_load:
            copy.wait()
        half = tokens // 256
        for index, slot in enumerate(order):
            for copy in slots[index]:
                copy.wait()
            step = feed_rows(
                w1.at[index], w2.at[index], mh2, gr2, sq_s, gp_s, ret_acc, gmh_acc, False
            )
            pl.loop(half, 2 * half)(step)
            if index == 0:
                for copy in part_loads:
                    copy.wait()
                middle("near")
            else:

                @pl.loop(0, tokens // 64)
                def _(i):
                    span = tile(i, 64)
                    far_span = tile(tokens // 64 + i, 64)
                    ret_send[span, :] = ret_acc[far_span, :].astype(BF)
                    gmh_send[span, :] = gmh_acc[far_span, :].astype(BF)

                ret_copy.start()
                gmh_copy.start()
            pl.loop(0, half)(step)
            if index == 0:
                middle("own")
            feed_grads(mh2, gr2, sq_s, gp_s, parts1.at[slot], parts2.at[slot])
            if index == 0:
                begin(slot)
        for copy in late:
            copy.wait()

    pl.run_scoped(
        feed_forward,
        pltpu.VMEM((2, 1024, hidden), BF),
        pltpu.VMEM((2, hidden, 1024), BF),
        pltpu.VMEM((2 * tokens, 1024), BF),
        pltpu.VMEM((2 * tokens, 1024), BF),
        pltpu.VMEM((2 * tokens, hidden), BF),
        pltpu.VMEM((2 * tokens, hidden), BF),
    )
    own = slice(0, tokens)
    far = slice(tokens, 2 * tokens)
    block = 32

    def attention(k_s, v_s, r_s, num_s, den_s, wg, wo, ggp_s, gatt_s, grp_s, gk_s, gv_s):
        need_wg = load(gate_w, wg)
        need_wo = load(output_w, wo)
        need = [
            load(k_ref, k_s),
            load(v_ref, v_s),
            load(r_ref, r_s),
            load(num_ref, num_s),
            load(den_ref, den_s),
        ]
        sums_s[...] = jnp.zeros_like(sums_s)
        row_at = lax.broadcasted_iota(jnp.int32, (rows, rows), 0)
        col_at = lax.broadcasted_iota(jnp.int32, (rows, rows), 1)
        for m in range(micros):
            mask_s[m] = jnp.logical_and(
                segcol_ref[m * rows : (m + 1) * rows, :] == segrow_ref[m : m + 1, :],
                col_at > row_at,
            ).astype(F32).astype(BF)
        ret_copy.wait()
        need_gated = load(gated_ref, ret_send)

        @pl.loop(0, tokens // block)
        def _(b):
            span = tile(b, block)
            returned = ret_acc[span, :] + ret_recv[span, :].astype(F32)
            gate = gate_s[span, :]
            product_in = gate * returned
            ret_acc[span, :] = mid_s[span, :] + product_in
            ggp_s[span, :] = (adj_s[span, :].astype(F32) * product_in * (1.0 - gate)).astype(BF)

        put(ret_acc.at[own], out_ref)
        put(ggp_s, ggp_out)
        need_wg.wait()

        @pl.loop(0, 2)
        def _(i):
            span = tile(i, tokens // 2)
            ret_acc[tile(2 + i, tokens // 2), :] = dot(ggp_s[span, :], wg[...], NT)

        for kind, parts in enumerate((parts1, parts2)):
            ahead_copies[kind].wait()
            for one in range(2):
                for two in range(2):

                    @pl.loop(0, 4)
                    def _(i, kind=kind, parts=parts, one=one, two=two):
                        span = tile(i, 64)
                        parts[0, one, two, span, early] = (
                            parts[0, one, two, span, early].astype(F32)
                            + ahead_s[kind, one, two, span, :].astype(F32)
                        ).astype(BF)

        begin("joined")
        gmg = ret_acc.at[far]
        gmh_copy.wait()
        need_mg = load(mg_ref, gmh_send)
        mix_h, mix_g = (vec_ref[9:10, :], vec_ref[10:11, :])
        gain = vec_ref[7:8, :]

        def combine(b):
            span = tile(b, block)
            grad_h = gmh_acc[span, :] + gmh_recv[span, :].astype(F32)
            grad_g = gmg[span, :]
            shift = (grad_h * (1.0 - mix_h) + grad_g * (1.0 - mix_g)) * wide(keep_ref[span, :], 1024)
            return (span, grad_h, grad_g, shift)

        for m in range(micros):
            pay_b[m : m + 1, :] = combine(m * (rows // block))[3][0:1, :]
        pay_b[micros:, :] = jnp.zeros((8 - micros, 1024), F32)
        halo_copy = remote(pay_b, halo_b, s_sem.at[2, 0], s_sem.at[2, 1], at.ahead(-1))
        halo_copy.start()
        at_last = lax.broadcasted_iota(jnp.int32, (block, 1024), 0) == block - 1
        halo_copy.wait()
        last("near")
        last("own")
        middle(3)
        begin(2)
        for m in range(micros):

            def back_b(i, after, m=m):
                span, grad_h, grad_g, shift = combine((m + 1) * (rows // block) - 1 - i)
                delta = db_s[span, :]
                sum_rows(sums_s, 9, grad_h * delta)
                sum_rows(sums_s, 10, grad_g * delta)
                moved = jnp.where(at_last, after, pltpu.roll(shift, block - 1, 0))
                grad = grad_h * mix_h + grad_g * mix_g + moved
                unit, inverse = unit_of(mid_s[span, :])
                sum_rows(sums_s, 7, grad * unit)
                sum_rows(sums_s, 8, grad)
                total = adj_s[span, :].astype(F32) + norm_back_rows(grad, unit, inverse, gain)
                gmh_acc[span, :] = total
                gatt_s[span, :] = total.astype(BF)
                return shift[0:1, :]

            lax.fori_loop(0, rows // block, back_b, halo_b[m : m + 1, :], unroll=2)

        put(gmh_acc.at[own], gmid_out)
        put(gatt_s, gatt_out)
        need_wo.wait()

        @pl.loop(0, 2)
        def _(i):
            span = tile(i, tokens // 2)
            gmh_acc[tile(2 + i, tokens // 2), :] = dot(gatt_s[span, :], wo[...], NT)

        middle("joined")
        for copy in need:
            copy.wait()
        width = 256
        place = lax.broadcasted_iota(jnp.int32, (rows, width), 0).astype(F32)

        @pl.loop(0, 1024 // width)
        def _(i):
            cols = tile(i, width)
            rate = jnp.exp(vec_ref[2:3, cols])
            rising = jnp.exp(place * rate)
            falling = jnp.exp((1.0 - place) * rate)
            step_back = jnp.exp(-rate)
            extra = vec_ref[3:4, cols]
            for m in range(micros):
                span = slice(m * rows, (m + 1) * rows)
                far_span = slice(tokens + m * rows, tokens + (m + 1) * rows)
                bonus = jnp.exp(extra + k_s[span, cols])
                recept = r_s[span, cols]
                inverse = 1.0 / (den_s[span, cols] + bonus)
                mixed = (num_s[span, cols] + bonus * v_s[span, cols]) * inverse
                grad_gated = gmh_acc[far_span, cols]
                grad_mixed = grad_gated * recept
                grp_s[span, cols] = (grad_mixed * mixed * (1.0 - recept)).astype(BF)
                up = grad_mixed * inverse
                down = -up * mixed
                up_sum = rising * dot_exact_left(mask_s[m], falling * up)
                down_sum = rising * dot_exact_left(mask_s[m], falling * down)
                gmh_acc[far_span, cols] = up
                db_s[span, cols] = down
                mid_s[span, cols] = up_sum
                gate_s[span, cols] = down_sum
                state_own[m : m + 1, cols] = up[0:1] + step_back * up_sum[0:1]
                state_own[micros + m : micros + m + 1, cols] = down[0:1] + step_back * down_sum[0:1]

        put(grp_s, grp_out)
        core_copy = remote(state_own, state_other, s_sem.at[3, 0], s_sem.at[3, 1], at.other)
        core_copy.start()
        pair = lax.div(mp, 2) * 2
        decay_all = jnp.exp(-float(rows) * jnp.exp(vec_ref[2:3, :]))

        def seen(device, last):
            index = lax.rem(device + at.count, at.count)
            start = 0 if last else 2 * micros
            return wide(segs_ref[index, start : start + 2 * micros, :], 1024)

        core_copy.wait()
        even = jnp.where(core == 0, state_own[...], state_other[...])
        odd = jnp.where(core == 0, state_other[...], state_own[...])
        state_chip[...] = even + jnp.where(
            seen(pair, False) == seen(pair + 1, False), decay_all * odd, 0.0
        )
        chip_copies = [
            remote(state_chip, state_in.at[step - 1], s_sem.at[3 + step, 0], s_sem.at[3 + step, 1], at.plane(-step))
            for step in range(1, planes)
        ]
        for copy in chip_copies:
            copy.start()
        for copy in chip_copies:
            copy.wait()
        total = jnp.zeros_like(state_chip[...])
        power = jnp.ones_like(decay_all)
        for step in range(1, planes):
            fits = jnp.logical_and(
                seen(pair + 2 * step, False) == seen(mp, True), z + step < planes
            )
            total = total + jnp.where(fits, power * state_in[step - 1], 0.0)
            power = power * decay_all * decay_all
        joined = decay_all * total + jnp.where(
            seen(pair + 1, False) == seen(pair, True), state_other[...], 0.0
        )
        carry_s[...] = jnp.where(core == 0, joined, total)
        last(3)

        @pl.loop(0, 1024 // width)
        def _(i):
            cols = tile(i, width)
            rate = jnp.exp(vec_ref[2:3, cols])
            tail = jnp.exp((place - (rows - 1.0)) * rate)
            extra = vec_ref[3:4, cols]
            step_back = jnp.exp(-rate)
            for m in range(micros):
                span = slice(m * rows, (m + 1) * rows)
                far_span = slice(tokens + m * rows, tokens + (m + 1) * rows)
                fits = (segcol_ref[span, :] == segs_ref[mp, m : m + 1, :]).astype(F32)
                carried = wide(fits, width) * tail
                up_sum = mid_s[span, cols] + carried * carry_s[m : m + 1, cols]
                down_sum = gate_s[span, cols] + carried * carry_s[micros + m : micros + m + 1, cols]
                up, down = (gmh_acc[far_span, cols], db_s[span, cols])
                key, value = (k_s[span, cols], v_s[span, cols])
                bonus = jnp.exp(extra + key)
                raised = jnp.exp(key)
                direct = (up * value + down) * bonus
                gk_s[span, cols] = (direct + raised * (value * up_sum + down_sum)).astype(BF)
                gv_s[span, cols] = (up * bonus + raised * up_sum).astype(BF)
                rate_part = -rate * step_back * (up_sum * num_s[span, cols] + down_sum * den_s[span, cols])
                for index, part in ((2, rate_part), (3, direct)):
                    summed = part[0:8]
                    for start in range(8, rows, 8):
                        summed = summed + part[start : start + 8]
                    sums_s[index, :, cols] = sums_s[index, :, cols] + summed

        put(gk_s, gk_out)
        put(gv_s, gv_out)
        for index in range(16):
            sums_flat[index : index + 1, :] = jnp.sum(sums_s[index], axis=0, keepdims=True)
        put(sums_flat, sums_out)
        need_gated.wait()
        need_mg.wait()
        square_copies = []
        for index, (left, right) in enumerate(((ret_send, gatt_s), (gmh_send, ggp_s))):
            fill_square(square_parts.at[index], left, right, planes, 512)
            square_copies.append(
                remote(
                    square_parts.at[index, 1 - core],
                    square_across.at[index],
                    square_sem.at[index, 0],
                    square_sem.at[index, 1],
                    at.other,
                )
            )
            square_copies[index].start()
        middle(2)
        for index in range(2):
            square_copies[index].wait()
            add_square(square_parts.at[index, core], square_across.at[index], planes)
            put(square_parts.at[index, core], square_out.at[index])
        last("joined")
        for name in ("near", 3):
            for reduce in reduces[name]:
                reduce.close()
        for parts, far_parts, own_s, own_out, one, two in (
            (parts1, far1, mid_s, own1_out, lax.rem(dp, 2), lax.div(dp, 2)),
            (parts2, far2, gate_s, own2_out, lax.div(dp, 2), lax.rem(dp, 2)),
        ):
            total = parts[0, one, two].astype(F32) + far_parts[1].astype(F32)
            own_s[0:256, early] = total[:, early]
            own_s[0:256, late_half] = total[:, late_half] + far_parts[0, :, late_half].astype(F32)
            put(own_s.at[0:256, 0:hidden], own_out)
        last(2)
        put(parts1.at[2, lax.rem(dp, 2), lax.div(dp, 2)], rest1_out)
        put(parts2.at[2, lax.div(dp, 2), lax.rem(dp, 2)], rest2_out)
        for copy in outs:
            copy.wait()

    def hold(kind):
        return pltpu.VMEM((tokens, 1024), kind)

    square = pltpu.VMEM((1024, 1024), BF)
    pl.run_scoped(attention, *([hold(F32)] * 5), square, square, *([hold(BF)] * 5))


def middle_call(planes, micros, rows, operands):
    tokens = micros * rows
    hidden = operands[5].shape[2]

    def big(kind):
        return jax.ShapeDtypeStruct((tokens, 1024), kind)

    def hold(count, kind):
        return pltpu.VMEM((count, 1024), kind)

    few = hold(8, F32)
    quarter = (256, hidden)
    piece = (planes, 256 // (2 * planes), 1024)
    sems = pltpu.SemaphoreType.DMA
    return pl.pallas_call(
        functools.partial(middle_kernel, planes, micros, rows),
        out_shape=[big(F32)] * 2
        + [big(BF)] * 5
        + [jax.ShapeDtypeStruct((16, 1024), F32)]
        + [jax.ShapeDtypeStruct(quarter, F32)] * 2
        + [jax.ShapeDtypeStruct(quarter, BF)] * 2
        + [jax.ShapeDtypeStruct((2, 2, 2) + piece, BF)],
        in_specs=[VM] * 5 + [ANY] * 21,
        out_specs=[ANY] * 13,
        scratch_shapes=[pltpu.VMEM((planes, 2, 2) + quarter, BF)] * 2
        + [pltpu.VMEM((planes, 2) + quarter, BF)] * 2
        + [pltpu.VMEM((planes,) + quarter, BF)] * 2
        + [pltpu.VMEM((2,) + quarter, BF)] * 2
        + [hold(2 * tokens, F32)] * 2
        + [hold(tokens, BF)] * 4
        + [hold(tokens, F32), hold(tokens, F32), hold(tokens, BF), hold(tokens, F32)]
        + [
            pltpu.VMEM((16, 8, 1024), F32),
            pltpu.VMEM((16, 1024), F32),
            pltpu.VMEM((micros, rows, rows), BF),
            few,
            few,
            few,
            few,
            few,
            pltpu.VMEM((planes - 1, 8, 1024), F32),
            few,
            sems((25,)),
            sems((14,)),
            sems((planes + 1, 2, 3, 2)),
            sems((3 + planes, 2)),
            pltpu.VMEM((2, 2, 2, 2) + piece, BF),
            pltpu.VMEM((2, 2, 2) + piece, BF),
            sems((2, 2)),
            pltpu.VMEM((2, 2, 2, 256, hidden // 2), BF),
            sems((2, 2)),
        ],
        compiler_params=pltpu.CompilerParams(
            collective_id=1, has_side_effects=True, vmem_limit_bytes=63 << 20
        ),
        cost_estimate=pl.CostEstimate(
            flops=52 * tokens * 1024 * 1024, bytes_accessed=60 << 20, transcendentals=6 * tokens * 1024
        ),
        name="channel_mix_and_adjoint",
    )(*operands)


class ReduceSquare:
    def __init__(self, at, mine, first, second, far, sems, x_first, source=None):
        self.at, self.mine, self.first, self.second, self.far = (at, mine, first, second, far)
        side = lax.rem(at.dp, 2)
        line = lax.div(at.dp, 2)
        self.one, self.two = (side, line) if x_first else (line, side)
        near, next_to = (at.side_x, at.side_y) if x_first else (at.side_y, at.side_x)
        self.copy_1 = remote(
            (mine if source is None else source).at[1 - self.one],
            first,
            sems.at[0, 0],
            sems.at[0, 1],
            near,
        )
        self.copy_2 = remote(
            mine.at[self.one, 1 - self.two], second, sems.at[1, 0], sems.at[1, 1], next_to
        )
        self.copies_3 = [
            remote(
                mine.at[self.one, self.two, lax.rem(at.z + step, at.planes)],
                far.at[step - 1],
                sems.at[1 + step, 0],
                sems.at[1 + step, 1],
                at.plane(step),
            )
            for step in range(1, at.planes)
        ]

    def add(self, one, two, other):
        @pl.loop(0, self.at.planes)
        def _(i):
            self.mine[one, two, i] = (
                self.mine[one, two, i].astype(F32) + other[i].astype(F32)
            ).astype(BF)

    def begin(self):
        self.copy_1.start()

    def middle(self):
        self.copy_1.wait()
        self.add(self.one, 1 - self.two, self.first.at[1 - self.two])
        self.copy_2.start()
        self.add(self.one, self.two, self.first.at[self.two])

    def last(self):
        self.copy_2.wait()
        self.add(self.one, self.two, self.second)

    def send(self):
        for copy in self.copies_3:
            copy.start()

    def close(self):
        for copy in self.copies_3:
            copy.wait()
        total = self.mine[self.one, self.two, self.at.z].astype(F32)
        for step in range(self.at.planes - 1):
            total = total + self.far[step].astype(F32)
        return total


def last_kernel(
    planes,
    micros,
    rows,
    vec_ref,
    keep_ref,
    sums_ref,
    square_ref,
    mr_ref,
    grp_ref,
    mv_ref,
    gv_ref,
    mk_ref,
    gk_ref,
    recept_w,
    value_w,
    key_w,
    x_ref,
    da_ref,
    gmid_ref,
    part1_ref,
    part2_ref,
    rest1_ref,
    rest2_ref,
    grad_out,
    sums_out,
    own_output,
    own_gate,
    own_recept,
    own_value,
    own_key,
    own_hidden,
    own_return,
    left_s,
    right_s,
    w_s,
    x_s,
    da_s,
    total_s,
    g_s,
    sums_s,
    parts,
    across,
    first,
    second,
    far,
    own_s,
    pay_a,
    halo_a,
    flat_s,
    flat_recv,
    load_sem,
    out_sem,
    rs_sem,
    s_sem,
    ff_far,
    ff_total,
    own1_s,
    own2_s,
    ff_sem,
    ready_s,
    core_sem,
):
    at = Place(planes)
    tokens = micros * rows
    outs = []

    def put(source, target):
        copy = pltpu.make_async_copy(source, target, out_sem.at[len(outs)])
        copy.start()
        outs.append(copy)

    loaded = []

    def load(source, target):
        copy = pltpu.make_async_copy(source, target, load_sem.at[len(loaded)])
        copy.start()
        loaded.append(copy)
        return copy

    sides = (
        (mr_ref, grp_ref),
        (mv_ref, gv_ref),
        (mk_ref, gk_ref),
    )
    right_loads, w_loads = ([], [])
    for index, source in enumerate((recept_w, value_w, key_w)):
        right_loads.append(load(sides[index][1], right_s.at[index]))
        w_loads.append(load(source, w_s.at[index]))
    greet(
        [at.other, at.side_x, at.side_y]
        + [at.plane(step) for step in range(1, planes)]
        + [at.ahead(1), at.ahead(-1)]
    )
    core = at.core
    lefts, rights = (slice(0, 512), slice(512, 1024))
    reduces = []
    for index in range(5):
        mine = ready_s.at[index] if index < 2 else parts.at[index - 2, core]
        halves = []
        for kind, cols in enumerate((lefts, rights)):
            halves.append(
                ReduceSquare(
                    at,
                    mine.at[:, :, :, :, cols],
                    first.at[index, :, :, :, cols],
                    second.at[index, :, :, cols],
                    far.at[index, :, :, cols],
                    rs_sem.at[index, kind],
                    kind == 0,
                    square_ref.at[index, :, :, :, :, cols] if index < 2 else None,
                )
            )
        reduces.append(halves)

    def begin(index):
        for half in reduces[index]:
            half.begin()

    def middle(index):
        for half in reduces[index]:
            half.middle()

    def last(index):
        for half in reduces[index]:
            half.last()
            half.send()

    def close(index, target):
        for half, cols in zip(reduces[index], (lefts, rights)):
            own_s[index, :, cols] = half.close()
        put(own_s.at[index], target)

    core_copies = [
        remote(
            parts.at[index, 1 - core],
            across.at[index],
            core_sem.at[index, 0],
            core_sem.at[index, 1],
            at.other,
        )
        for index in range(3)
    ]
    ff_loads = [load(part1_ref, ff_total.at[0]), load(part2_ref, ff_total.at[1])]
    ff_copies = [
        remote(rest, ff_far.at[index], ff_sem.at[index, 0], ff_sem.at[index, 1], at.plane(2))
        for index, rest in enumerate((rest1_ref, rest2_ref))
    ]
    begin(0)
    begin(1)
    ready_load = load(square_ref, ready_s)
    left_loads = [load(left, left_s.at[index]) for index, (left, _) in enumerate(sides)]
    row_loads = [load(x_ref, x_s), load(da_ref, da_s), load(gmid_ref, total_s)]
    mixes = (vec_ref[6:7, :], vec_ref[5:6, :], vec_ref[4:5, :])
    heads = jnp.zeros((16 * micros, 1024), F32)
    for index in range(3):
        right_loads[index].wait()
        w_loads[index].wait()
        picked = jnp.concatenate(
            [right_s[index, m * rows : m * rows + 16, :] for m in range(micros)], axis=0
        )
        heads = heads + dot(picked, w_s[index], NT) * (1.0 - mixes[index])
    for m in range(micros):
        pay_a[m : m + 1, :] = heads[16 * m : 16 * m + 1] * wide(
            keep_ref[m * rows : m * rows + 8, :], 1024
        )[0:1]
    pay_a[micros:, :] = jnp.zeros((8 - micros, 1024), F32)
    halo_copy = remote(pay_a, halo_a, s_sem.at[0, 0], s_sem.at[0, 1], at.ahead(-1))
    halo_copy.start()
    for copy in ff_copies:
        copy.start()
    sums_s[...] = jnp.zeros_like(sums_s)

    def fill(index):
        left_loads[index].wait()
        fill_square(parts.at[index], left_s.at[index], right_s.at[index], planes, 512)
        core_copies[index].start()

    def settle(index):
        core_copies[index].wait()
        add_square(parts.at[index, core], across.at[index], planes)

    def back(index):
        @pl.loop(0, 2)
        def _(i):
            span = tile(i, tokens // 2)
            g_s[index, span, :] = dot(right_s[index, span, :], w_s[index], NT)

    fill(0)
    ready_load.wait()
    middle(0)
    fill(1)
    settle(0)
    begin(2)
    fill(2)
    settle(1)
    middle(1)
    begin(3)
    settle(2)
    back(0)
    last(0)
    back(1)
    back(2)
    for copy in row_loads:
        copy.wait()
    block = 32
    gain = vec_ref[0:1, :]

    def combine(b):
        span = tile(b, block)
        grads = [g_s[index, span, :] for index in range(3)]
        shift = sum(grad * (1.0 - mix) for grad, mix in zip(grads, mixes))
        return (span, grads, shift * wide(keep_ref[span, :], 1024))

    at_last = lax.broadcasted_iota(jnp.int32, (block, 1024), 0) == block - 1
    halo_copy.wait()
    for m in range(micros):

        def back_a(i, after, m=m):
            span, grads, shift = combine((m + 1) * (rows // block) - 1 - i)
            delta = da_s[span, :]
            for index, grad in enumerate(grads):
                sum_rows(sums_s, 2 - index, grad * delta)
            moved = jnp.where(at_last, after, pltpu.roll(shift, block - 1, 0))
            grad = sum(part * mix for part, mix in zip(grads, mixes)) + moved
            unit, inverse = unit_of(x_s[span, :].astype(F32))
            sum_rows(sums_s, 3, grad * unit)
            sum_rows(sums_s, 4, grad)
            total_s[span, :] = total_s[span, :] + norm_back_rows(grad, unit, inverse, gain)
            return shift[0:1, :]

        lax.fori_loop(0, rows // block, back_a, halo_a[m : m + 1, :], unroll=2)
    put(total_s, grad_out)
    flat_s[0] = sums_ref[...]
    for index, row in enumerate((4, 5, 6, 0, 1)):
        flat_s[0, row : row + 1, :] = jnp.sum(sums_s[index], axis=0, keepdims=True)

    def flat_copy(level, slot, device):
        return remote(
            flat_s.at[level], flat_recv.at[slot], s_sem.at[1 + slot, 0], s_sem.at[1 + slot, 1], device
        )

    over_core = flat_copy(0, 0, at.other)
    over_core.start()
    over_core.wait()
    flat_s[1] = flat_s[0] + flat_recv[0]
    over_x = flat_copy(1, 1, at.side_x)
    middle(2)
    over_x.start()
    begin(4)
    last(1)
    middle(3)
    over_x.wait()
    flat_s[2] = flat_s[1] + flat_recv[1]
    over_y = flat_copy(2, 2, at.side_y)
    over_y.start()
    last(2)
    middle(4)
    last(3)
    over_y.wait()
    flat_s[3] = flat_s[2] + flat_recv[2]
    flat_copies = []
    for step in range(1, planes):
        to = lax.rem(at.z + step, planes)
        lanes = tile(at.dp * (planes // 2) + lax.div(to, 2), 128)
        slot = 2 + step
        flat_copies.append(
            remote(
                flat_s.at[3, :, lanes],
                flat_recv.at[slot, :, lanes],
                s_sem.at[1 + slot, 0],
                s_sem.at[1 + slot, 1],
                at.plane(step),
            )
        )
    for copy in flat_copies:
        copy.start()
    for copy in ff_loads + ff_copies:
        copy.wait()
    own1_s[...] = ff_total[0] + ff_far[0].astype(F32)
    own2_s[...] = (ff_total[1] + ff_far[1].astype(F32)).T
    put(own1_s, own_hidden)
    put(own2_s, own_return)
    last(4)
    close(0, own_output)
    close(1, own_gate)
    close(2, own_recept)
    for copy in flat_copies:
        copy.wait()
    lanes = tile(at.dp * (planes // 2) + lax.div(at.z, 2), 128)
    flat_s[0, :, lanes] = flat_s[3, :, lanes] + sum(
        flat_recv[2 + step, :, lanes] for step in range(1, planes)
    )
    put(flat_s.at[0], sums_out)
    close(3, own_value)
    close(4, own_key)
    for copy in outs:
        copy.wait()


def last_call(planes, micros, rows, operands):
    tokens = micros * rows

    def hold(count, kind):
        return pltpu.VMEM((count, tokens, 1024), kind)

    quarter = operands[-4].shape
    piece = (1024 // (8 * planes), 1024)
    sems = pltpu.SemaphoreType.DMA
    few = pltpu.VMEM((8, 1024), F32)
    return pl.pallas_call(
        functools.partial(last_kernel, planes, micros, rows),
        out_shape=[
            jax.ShapeDtypeStruct((tokens, 1024), F32),
            jax.ShapeDtypeStruct((16, 1024), F32),
        ]
        + [jax.ShapeDtypeStruct(piece, F32)] * 5
        + [jax.ShapeDtypeStruct(quarter, F32), jax.ShapeDtypeStruct(quarter[::-1], F32)],
        in_specs=[VM] * 3 + [ANY] * 17,
        out_specs=[ANY] * 9,
        scratch_shapes=[
            hold(3, BF),
            hold(3, BF),
            pltpu.VMEM((3, 1024, 1024), BF),
            pltpu.VMEM((tokens, 1024), BF),
            pltpu.VMEM((tokens, 1024), F32),
            pltpu.VMEM((tokens, 1024), F32),
            hold(3, F32),
            pltpu.VMEM((5, 8, 1024), F32),
            pltpu.VMEM((3, 2, 2, 2, planes) + piece, BF),
            pltpu.VMEM((3, 2, 2, planes) + piece, BF),
            pltpu.VMEM((5, 2, planes) + piece, BF),
            pltpu.VMEM((5, planes) + piece, BF),
            pltpu.VMEM((5, planes - 1) + piece, BF),
            pltpu.VMEM((5,) + piece, F32),
            few,
            few,
            pltpu.VMEM((4, 16, 1024), F32),
            pltpu.VMEM((2 + planes, 16, 1024), F32),
            sems((18,)),
            sems((9,)),
            sems((5, 2, 1 + planes, 2)),
            sems((3 + planes, 2)),
            pltpu.VMEM((2,) + quarter, BF),
            pltpu.VMEM((2,) + quarter, F32),
            pltpu.VMEM(quarter, F32),
            pltpu.VMEM(quarter[::-1], F32),
            sems((2, 2)),
            pltpu.VMEM((2, 2, 2, planes) + piece, BF),
            sems((3, 2)),
        ],
        compiler_params=pltpu.CompilerParams(
            collective_id=2, has_side_effects=True, vmem_limit_bytes=62 << 20
        ),
        cost_estimate=pl.CostEstimate(
            flops=16 * tokens * 1024 * 1024, bytes_accessed=30 << 20, transcendentals=0
        ),
        name="time_mix_weights",
    )(*operands)


def one_micro(block_in, seg_ids, grad_out, vectors, matrices, hidden_w, return_w):
    (
        gain_one,
        bias_one,
        decay_vec,
        extra_array,
        mix_key,
        mix_value,
        mix_recept,
        gain_two,
        bias_two,
        mix_hidden,
        mix_gate,
    ) = vectors
    key_w, value_w, recept_w, output_w, gate_w = matrices
    row_count = block_in.shape[0]
    model_width = block_in.shape[1]
    seg_float = seg_ids.astype(jnp.float32)
    normed_a, unit_a, inv_a = layer_norm(block_in, gain_one, bias_one)
    prev_row, prev_seg = from_behind((normed_a[-1:], seg_float[-1:]), "mp", 1)
    same_row = jnp.concatenate(
        [
            (seg_float[:1] == prev_seg).astype(jnp.float32),
            (seg_ids[1:] == seg_ids[:-1]).astype(jnp.float32),
        ]
    )
    same_col = same_row[:, None]
    shifted_a = jnp.concatenate([prev_row, normed_a[:-1]], axis=0) * same_col
    delta_a = normed_a - shifted_a
    low_key = reduced_precision(shifted_a + delta_a * mix_key)
    low_value = reduced_precision(shifted_a + delta_a * mix_value)
    low_recept = reduced_precision(shifted_a + delta_a * mix_recept)
    lookup_start = product(low_key, key_w)
    content_start = product(low_value, value_w)
    recept = jax.nn.sigmoid(product(low_recept, recept_w))
    feature_fading = jnp.exp(decay_vec)
    positions = jnp.arange(row_count, dtype=jnp.float32)[:, None]
    rising = jnp.exp(positions * feature_fading)
    falling = jnp.exp(-(positions - 1.0) * feature_fading)
    falling_zero = jnp.exp(-positions * feature_fading)
    raised_lookup = jnp.exp(lookup_start)
    weighted_average = raised_lookup * content_start
    order_rows = jnp.arange(row_count)
    lower_tri = jnp.logical_and(
        seg_ids[:, None] == seg_ids[None, :], order_rows[None, :] < order_rows[:, None]
    ).astype(jnp.float32)
    last_mask = (seg_ids == seg_ids[-1]).astype(jnp.float32)
    first_mask = (seg_ids == seg_ids[0]).astype(jnp.float32) * same_row[0]
    forward_mat = jnp.concatenate([lower_tri, last_mask[None]], axis=0)
    stacked = jnp.concatenate(
        [
            rising * weighted_average,
            rising * raised_lookup,
            positions * rising * weighted_average,
            positions * rising * raised_lookup,
        ],
        axis=1,
    )
    summed = jnp.dot(forward_mat, stacked, precision=HIGH)
    inner_sums = summed[:row_count]
    closing = summed[row_count]
    num_loc = falling * inner_sums[:, :model_width]
    den_loc = falling * inner_sums[:, model_width : 2 * model_width]
    num_der = (
        -(positions - 1.0) * num_loc + falling * inner_sums[:, 2 * model_width : 3 * model_width]
    )
    den_der = -(positions - 1.0) * den_loc + falling * inner_sums[:, 3 * model_width :]
    end_fall = jnp.exp(-(row_count - 1.0) * feature_fading)
    state_num = end_fall * closing[:model_width]
    state_den = end_fall * closing[model_width : 2 * model_width]
    state_num_der = (
        -(row_count - 1.0) * state_num + end_fall * closing[2 * model_width : 3 * model_width]
    )
    state_den_der = -(row_count - 1.0) * state_den + end_fall * closing[3 * model_width :]
    uniform_flag = (seg_ids[-1] == seg_ids[0]).astype(jnp.float32) * same_row[0]
    carry_pass = uniform_flag * jnp.exp(-row_count * feature_fading)
    carry_der = -row_count * carry_pass
    zero_vec = jnp.zeros_like(feature_fading)
    one_vec = jnp.ones_like(feature_fading)
    in_num, in_den, in_num_der, in_den_der, pass_total, pass_der = carried_in(
        (state_num, state_den, state_num_der, state_den_der, carry_pass, carry_der),
        "mp",
        state_join,
        (zero_vec, zero_vec, zero_vec, zero_vec, one_vec, zero_vec),
        False,
    )
    carried = first_mask[:, None] * falling_zero
    dividend = num_loc + carried * in_num
    divisor_portion = den_loc + carried * in_den
    numer_der = num_der + carried * (in_num_der - positions * in_num)
    denom_der = den_der + carried * (in_den_der - positions * in_den)
    extra_summand = jnp.exp(extra_array + lookup_start)
    divisor_complete = divisor_portion + extra_summand
    mixture_result = (dividend + extra_summand * content_start) / divisor_complete
    gated = reduced_precision(recept * mixture_result)
    block_mid = block_in + product(gated, output_w)
    normed_b, unit_b, inv_b = layer_norm(block_mid, gain_two, bias_two)
    prev_mid = from_behind(normed_b[-1:], "mp", 1)
    shifted_b = jnp.concatenate([prev_mid, normed_b[:-1]], axis=0) * same_col
    delta_b = normed_b - shifted_b
    low_hidden = reduced_precision(shifted_b + delta_b * mix_hidden)
    low_gate = reduced_precision(shifted_b + delta_b * mix_gate)
    gate_two = jax.nn.sigmoid(product(low_gate, gate_w))
    hidden_rows = lax.all_gather(low_hidden, "mp", axis=0, tiled=True)
    pre_act = product(hidden_rows, hidden_w)
    rectified = jnp.maximum(pre_act, 0.0)
    squared = reduced_precision(rectified * rectified)
    returned = lax.psum_scatter(
        product(squared, return_w).astype(jnp.bfloat16), "mp", scatter_dimension=0, tiled=True
    ).astype(jnp.float32)
    output = block_mid + gate_two * returned
    grad_ret = reduced_precision(grad_out * gate_two)
    grad_gate_pre = reduced_precision(grad_out * returned * gate_two * (1.0 - gate_two))
    d_gate_w = (low_gate, grad_gate_pre)
    grad_low_gate = product_nt(grad_gate_pre, gate_w)
    grad_rows = lax.all_gather(grad_ret, "mp", axis=0, tiled=True)
    grad_squared = product_nt(grad_rows, return_w)
    d_return = (squared, grad_rows)
    grad_pre = reduced_precision(grad_squared * 2.0 * rectified)
    d_hidden = (hidden_rows, grad_pre)
    grad_low_hidden = lax.psum_scatter(
        product_nt(grad_pre, hidden_w).astype(jnp.bfloat16), "mp", scatter_dimension=0, tiled=True
    ).astype(jnp.float32)
    d_mix_hidden = jnp.sum(grad_low_hidden * delta_b, axis=0)
    d_mix_gate = jnp.sum(grad_low_gate * delta_b, axis=0)
    grad_shift_b = (
        grad_low_hidden * (1.0 - mix_hidden) + grad_low_gate * (1.0 - mix_gate)
    ) * same_col
    from_next_b = from_behind(grad_shift_b[:1], "mp", -1)
    grad_norm_b = (
        grad_low_hidden * mix_hidden
        + grad_low_gate * mix_gate
        + jnp.concatenate([grad_shift_b[1:], from_next_b], axis=0)
    )
    grad_mid_norm, d_gain_two, d_bias_two = norm_back(grad_norm_b, unit_b, inv_b, gain_two)
    grad_mid = grad_out + grad_mid_norm
    grad_att = reduced_precision(grad_mid)
    d_output_w = (gated, grad_att)
    grad_gated = product_nt(grad_att, output_w)
    grad_recept_pre = reduced_precision(grad_gated * mixture_result * recept * (1.0 - recept))
    grad_mixed = grad_gated * recept
    d_recept_w = (low_recept, grad_recept_pre)
    grad_low_recept = product_nt(grad_recept_pre, recept_w)
    dividend_adjoint = grad_mixed / divisor_complete
    divisor_adjoint = -dividend_adjoint * mixture_result
    extra_derivative_part = dividend_adjoint * content_start + divisor_adjoint
    extra_derivative = jnp.sum(extra_derivative_part * extra_summand, axis=0)
    d_rate = jnp.sum(dividend_adjoint * numer_der + divisor_adjoint * denom_der, axis=0)
    backward_mat = jnp.concatenate([lower_tri.T, first_mask[None]], axis=0)
    back_sum = jnp.dot(
        backward_mat,
        jnp.concatenate([falling * dividend_adjoint, falling * divisor_adjoint], axis=1),
        precision=HIGH,
    )
    step_back = jnp.exp(-feature_fading)
    from_num = step_back * back_sum[row_count, :model_width]
    from_den = step_back * back_sum[row_count, model_width:]
    out_num, out_den, out_pass = carried_in(
        (from_num, from_den, carry_pass), "mp", suffix_join, (zero_vec, zero_vec, one_vec), True
    )
    tail_fall = last_mask[:, None] * jnp.exp(-(row_count - 1.0 - positions) * feature_fading)
    cumulative_dividend = rising * back_sum[:row_count, :model_width] + tail_fall * out_num
    running_denominator = rising * back_sum[:row_count, model_width:] + tail_fall * out_den
    value_gradient = reduced_precision(
        dividend_adjoint * extra_summand + cumulative_dividend * raised_lookup
    )
    key_gradient = reduced_precision(
        extra_derivative_part * extra_summand
        + cumulative_dividend * weighted_average
        + running_denominator * raised_lookup
    )
    d_key_w = (low_key, key_gradient)
    d_value_w = (low_value, value_gradient)
    grad_low_key = product_nt(key_gradient, key_w)
    grad_low_value = product_nt(value_gradient, value_w)
    d_mix_key = jnp.sum(grad_low_key * delta_a, axis=0)
    d_mix_value = jnp.sum(grad_low_value * delta_a, axis=0)
    d_mix_recept = jnp.sum(grad_low_recept * delta_a, axis=0)
    grad_shift_a = (
        grad_low_key * (1.0 - mix_key)
        + grad_low_value * (1.0 - mix_value)
        + grad_low_recept * (1.0 - mix_recept)
    ) * same_col
    from_next_a = from_behind(grad_shift_a[:1], "mp", -1)
    grad_norm_a = (
        grad_low_key * mix_key
        + grad_low_value * mix_value
        + grad_low_recept * mix_recept
        + jnp.concatenate([grad_shift_a[1:], from_next_a], axis=0)
    )
    grad_in_norm, d_gain_one, d_bias_one = norm_back(grad_norm_a, unit_a, inv_a, gain_one)
    input_grad = grad_mid + grad_in_norm
    grads = (
        d_gain_one,
        d_bias_one,
        d_rate * feature_fading,
        extra_derivative,
        d_mix_key,
        d_mix_value,
        d_mix_recept,
        d_key_w,
        d_value_w,
        d_recept_w,
        d_output_w,
        d_gain_two,
        d_bias_two,
        d_mix_hidden,
        d_mix_gate,
        d_hidden,
        d_return,
        d_gate_w,
    )
    return (output, input_grad, grads)


def generic_body(
    incoming_signal,
    series_number_table,
    upstream_adjoint,
    first_scaling_factor,
    first_scaling_offset,
    logarithmic_fading_speeds,
    present_step_extra,
    lookup_shift_mixture,
    content_shift_mixture,
    admit_lookup_shift_mixture,
    attention_lookup_matrix,
    attention_content_matrix,
    attention_admit_matrix,
    attention_result_matrix,
    second_scaling_factor,
    second_scaling_offset,
    inner_shift_mixture,
    admit_shift_mixture,
    feedforward_lookup_matrix,
    feedforward_content_matrix,
    feedforward_admit_matrix,
):
    hidden_full, return_full = (feedforward_lookup_matrix, feedforward_content_matrix)
    vectors = tuple(
        (
            start_item.astype(jnp.float32)
            for start_item in (
                first_scaling_factor,
                first_scaling_offset,
                logarithmic_fading_speeds,
                present_step_extra,
                lookup_shift_mixture,
                content_shift_mixture,
                admit_lookup_shift_mixture,
                second_scaling_factor,
                second_scaling_offset,
                inner_shift_mixture,
                admit_shift_mixture,
            )
        )
    )
    matrices = (
        attention_lookup_matrix,
        attention_content_matrix,
        attention_admit_matrix,
        attention_result_matrix,
        feedforward_admit_matrix,
    )
    output, input_grad, grads = jax.vmap(
        lambda rows, ids, adjoint: one_micro(
            rows, ids, adjoint, vectors, matrices, hidden_full, return_full
        )
    )(
        incoming_signal[:, 0].astype(jnp.float32),
        series_number_table[:, 0],
        upstream_adjoint[:, 0].astype(jnp.float32),
    )
    totals = tuple(
        product_tn(*(side.reshape(-1, side.shape[-1]) for side in grad))
        if isinstance(grad, tuple)
        else jnp.sum(grad, axis=0)
        for grad in grads
    )
    square = [index for index in range(18) if totals[index].shape == totals[7].shape]
    lines = [index for index in range(18) if totals[index].ndim == 1]
    wide = lax.psum_scatter(
        jnp.concatenate([reduced_precision(totals[index]) for index in square], axis=1),
        ("dp", "mp"),
        scatter_dimension=0,
        tiled=True,
    ).astype(jnp.float32)
    thin = lax.psum_scatter(
        jnp.stack([totals[index] for index in lines], axis=1),
        ("dp", "mp"),
        scatter_dimension=0,
        tiled=True,
    )
    held = dict(zip(square, jnp.split(wide, len(square), axis=1)))
    held.update({index: thin[:, place] for place, index in enumerate(lines)})
    output, input_grad = (output[:, None], input_grad[:, None])
    owned = tuple(held[index] for index in sorted(held))
    hidden_own, return_own = (
        lax.psum_scatter(
            totals[15].astype(jnp.bfloat16), "dp", scatter_dimension=0, tiled=True
        ).astype(jnp.float32),
        lax.psum_scatter(
            totals[16].astype(jnp.bfloat16), "dp", scatter_dimension=1, tiled=True
        ).astype(jnp.float32),
    )
    return (
        output,
        input_grad,
        owned[0],
        owned[1],
        owned[2],
        owned[3],
        owned[4],
        owned[5],
        owned[6],
        owned[7],
        owned[8],
        owned[9],
        owned[10],
        owned[11],
        owned[12],
        owned[13],
        owned[14],
        hidden_own,
        return_own,
        owned[15],
    )


def hand_over(count, *refs):
    sems = refs[3 * count]
    ins, outs = ([], [])
    for index in range(count):
        held = refs[2 * count + index]
        ins.append(pltpu.make_async_copy(refs[index], held, sems.at[0, index]))
        outs.append(pltpu.make_async_copy(held, refs[count + index], sems.at[1, index]))
        ins[-1].start()
    for index in range(count):
        ins[index].wait()
        outs[index].start()
    for copy in outs:
        copy.wait()


def hand_call(arrays):
    count = len(arrays)
    return pl.pallas_call(
        functools.partial(hand_over, count),
        out_shape=[jax.ShapeDtypeStruct(part.shape, part.dtype) for part in arrays],
        in_specs=[ANY] * count,
        out_specs=[ANY] * count,
        scratch_shapes=[pltpu.VMEM(part.shape, part.dtype) for part in arrays]
        + [pltpu.SemaphoreType.DMA((2, count))],
        compiler_params=pltpu.CompilerParams(vmem_limit_bytes=60 << 20),
        name="hand_over",
    )(*arrays)


def kernel_body(
    incoming_signal,
    series_number_table,
    upstream_adjoint,
    first_scaling_factor,
    first_scaling_offset,
    logarithmic_fading_speeds,
    present_step_extra,
    lookup_shift_mixture,
    content_shift_mixture,
    admit_lookup_shift_mixture,
    attention_lookup_matrix,
    attention_content_matrix,
    attention_admit_matrix,
    attention_result_matrix,
    second_scaling_factor,
    second_scaling_offset,
    inner_shift_mixture,
    admit_shift_mixture,
    feedforward_lookup_matrix,
    feedforward_content_matrix,
    feedforward_admit_matrix,
):
    hidden_full, return_full = (feedforward_lookup_matrix, feedforward_content_matrix)
    matrices = (
        attention_lookup_matrix,
        attention_content_matrix,
        attention_admit_matrix,
        attention_result_matrix,
        feedforward_admit_matrix,
    )
    micros, _, rows, depth = incoming_signal.shape
    planes = lax.axis_size("mp") // 2
    x = incoming_signal.reshape(micros * rows, depth)
    adjoint = upstream_adjoint.reshape(micros * rows, depth)
    operands = (
        x,
        series_number_table.reshape(micros, rows),
        adjoint,
        first_scaling_factor,
        first_scaling_offset,
        logarithmic_fading_speeds,
        present_step_extra,
        lookup_shift_mixture,
        content_shift_mixture,
        admit_lookup_shift_mixture,
        second_scaling_factor,
        second_scaling_offset,
        inner_shift_mixture,
        admit_shift_mixture,
        *matrices,
        hidden_full,
        return_full,
    )
    (
        keys, values, recept, num, den, mid, gate, mk, mv, mr, gated, mg, delta_a, delta_b,
        keep, segs, table, segcol, segrow, mh_all, ret_all, w1_all, w2_all, ret_acc, gmh_acc,
        parts1, parts2,
    ) = forward_call(planes, micros, rows, operands)
    key_w, value_w, recept_w, output_w, gate_w = matrices
    (
        output, grad_mid, grad_gate, grad_att, grad_recept, grad_key, grad_value, sums,
        part1, part2, rest1, rest2, squares,
    ) = middle_call(
        planes,
        micros,
        rows,
        (
            table, keep, segs, segcol, segrow, w1_all, w2_all, mh_all, ret_all, ret_acc, gmh_acc,
            parts1, parts2, mid, gate, adjoint, delta_b, keys, values, recept, num, den,
            gate_w, output_w, gated, mg,
        ),
    )
    (
        input_grad, sums, own_output, own_gate, own_recept, own_value, own_key, own_hidden,
        own_return,
    ) = last_call(
        planes,
        micros,
        rows,
        (
            table, keep, sums, squares, mr, grad_recept, mv, grad_value,
            mk, grad_key, recept_w, value_w, key_w, x, delta_a, grad_mid,
            part1, part2, rest1, rest2,
        ),
    )
    (
        output, input_grad, own_key, own_value, own_recept, own_output, own_hidden, own_return,
        own_gate,
    ) = hand_call(
        (
            output, input_grad, own_key, own_value, own_recept, own_output, own_hidden,
            own_return, own_gate,
        )
    )
    span = depth // (lax.axis_size("dp") * lax.axis_size("mp"))
    mine = lax.dynamic_slice_in_dim(
        sums, lax.axis_index(("dp", "mp")) * span, span, axis=1
    )
    line = [mine[index] for index in range(11)]
    shape = incoming_signal.shape
    return (
        output.reshape(shape),
        input_grad.reshape(shape),
        *line[:7],
        own_key,
        own_value,
        own_recept,
        own_output,
        *line[7:],
        own_hidden,
        own_return,
        own_gate,
    )


def solution(mesh):
    placed = (
        P(None, "dp", "mp", None),
        P(None, "dp", "mp"),
        P(None, "dp", "mp", None),
        P(),
        P(),
        P(),
        P(),
        P(),
        P(),
        P(),
        P(),
        P(),
        P(),
        P(),
        P(),
        P(),
        P(),
        P(),
        P(None, "mp"),
        P("mp", None),
        P(),
    )
    fits = mesh.shape["dp"] == 4 and mesh.shape["mp"] == 8
    return jax.shard_map(
        kernel_body if fits else generic_body,
        mesh=mesh,
        in_specs=placed,
        out_specs=(
            P(None, "dp", "mp", None),
            P(None, "dp", "mp", None),
            P(("dp", "mp")),
            P(("dp", "mp")),
            P(("dp", "mp")),
            P(("dp", "mp")),
            P(("dp", "mp")),
            P(("dp", "mp")),
            P(("dp", "mp")),
            P(("dp", "mp"), None),
            P(("dp", "mp"), None),
            P(("dp", "mp"), None),
            P(("dp", "mp"), None),
            P(("dp", "mp")),
            P(("dp", "mp")),
            P(("dp", "mp")),
            P(("dp", "mp")),
            P("dp", "mp"),
            P("mp", "dp"),
            P(("dp", "mp"), None),
        ),
        check_vma=False,
    )
```

```python
import functools

import jax
import jax.numpy as jnp
from jax import lax
from jax.experimental import pallas as pl
from jax.experimental.pallas import tpu as pltpu
from jax.sharding import PartitionSpec as P

EPS = 1e-05
HIGH = lax.Precision.HIGHEST


def from_behind(block, axis, distance):
    devices = range(lax.axis_size(axis))
    route = [(i - distance, i) for i in devices if i - distance in devices]
    return lax.ppermute(block, axis, route)


def carried_in(shard, axis, combine, identity, reverse):
    length, mine = (lax.axis_size(axis), lax.axis_index(axis))
    everything = jax.tree.map(lambda part: lax.all_gather(part, axis), shard)
    start = jax.tree.map(
        lambda part, zero: jnp.broadcast_to(jnp.asarray(zero, part.dtype), part.shape),
        shard,
        identity,
    )

    def step(k, before):
        at = length - 1 - k if reverse else k
        reached = at > mine if reverse else at < mine
        new = combine(before, jax.tree.map(lambda part: part[at], everything))
        return jax.tree.map(lambda a, b: jnp.where(reached, a, b), new, before)

    return lax.fori_loop(0, length, step, start)


def reduced_precision(values):
    return values.astype(jnp.bfloat16)


def product(left, right):
    return jnp.dot(left, right, preferred_element_type=jnp.float32)


def product_tn(left, right):
    return lax.dot_general(
        left, right, (((0,), (0,)), ((), ())), preferred_element_type=jnp.float32
    )


def product_nt(left, right):
    return lax.dot_general(
        left, right, (((1,), (1,)), ((), ())), preferred_element_type=jnp.float32
    )


def layer_norm(values, gain, bias):
    average = jnp.mean(values, axis=-1, keepdims=True)
    centre = values - average
    inverse = lax.rsqrt(jnp.mean(centre * centre, axis=-1, keepdims=True) + EPS)
    unit = centre * inverse
    return (unit * gain + bias, unit, inverse)


def norm_back(grad_in, unit, inverse, gain):
    scaled = grad_in * gain
    grad_values = inverse * (
        scaled
        - jnp.mean(scaled, axis=-1, keepdims=True)
        - unit * jnp.mean(scaled * unit, axis=-1, keepdims=True)
    )
    return (grad_values, jnp.sum(grad_in * unit, axis=0), jnp.sum(grad_in, axis=0))


def state_join(earlier, latter):
    return (
        latter[4] * earlier[0] + latter[0],
        latter[4] * earlier[1] + latter[1],
        latter[4] * earlier[2] + latter[5] * earlier[0] + latter[2],
        latter[4] * earlier[3] + latter[5] * earlier[1] + latter[3],
        earlier[4] * latter[4],
        earlier[5] * latter[4] + earlier[4] * latter[5],
    )


def suffix_join(earlier, latter):
    return (
        latter[0] + latter[2] * earlier[0],
        latter[1] + latter[2] * earlier[1],
        latter[2] * earlier[2],
    )


BF = jnp.bfloat16
F32 = jnp.float32
MESH = pl.DeviceIdType.MESH
NN = (((1,), (0,)), ((), ()))
NT = (((1,), (1,)), ((), ()))
TN = (((0,), (0,)), ((), ()))


def dot(left, right, form=NN):
    return lax.dot_general(left, right, form, preferred_element_type=F32)


def dot_exact_left(left, right):
    high = right.astype(BF)
    rest = (right - high.astype(F32)).astype(BF)
    return dot(left, high) + dot(left, rest)


def wide(lanes, width):
    return jnp.concatenate([lanes] * (width // 128), axis=1)


def tile(index, size):
    return pl.ds(pl.multiple_of(index * size, size), size)


def unit_of(values):
    average = jnp.mean(values, axis=-1, keepdims=True)
    centre = values - average
    inverse = lax.rsqrt(jnp.mean(centre * centre, axis=-1, keepdims=True) + EPS)
    return (centre * inverse, inverse)


def remote(source, target, send, receive, device):
    return pltpu.make_async_remote_copy(
        src_ref=source,
        dst_ref=target,
        send_sem=send,
        recv_sem=receive,
        device_id=device,
        device_id_type=MESH,
    )


class Place:
    def __init__(self, planes):
        self.planes = planes
        self.dp, self.mp = (lax.axis_index("dp"), lax.axis_index("mp"))
        self.z = lax.div(self.mp, 2)
        self.core = lax.rem(self.mp, 2)
        self.count = 2 * planes
        self.other = (self.dp, self.mp + 1 - 2 * self.core)
        self.side_x = (self.dp + 1 - 2 * lax.rem(self.dp, 2), self.mp)
        self.side_y = (lax.rem(self.dp + 2, 4), self.mp)

    def ahead(self, steps):
        return (self.dp, lax.rem(self.mp + steps + self.count, self.count))

    def plane(self, steps):
        return (self.dp, lax.rem(self.z + steps + self.planes, self.planes) * 2 + self.core)


def greet(devices):
    barrier = pltpu.get_barrier_semaphore()
    for device in devices:
        pl.semaphore_signal(barrier, inc=1, device_id=device, device_id_type=MESH)
    pl.semaphore_wait(barrier, len(devices))


def feed_rows(w1, w2, mh2, gr2, sq_s, gp_s, ret_acc, gmh_acc, fresh):
    def rows_of(i):
        span = tile(i, 256)
        pre = dot(mh2[span, :], w1[...])
        rectified = jnp.maximum(pre, 0.0)
        squared = (rectified * rectified).astype(BF)
        sq_s[span, :] = squared
        grad_squared = dot(gr2[span, :], w2[...], NT)
        grad_pre = (grad_squared * 2.0 * rectified).astype(BF)
        gp_s[span, :] = grad_pre
        if fresh:
            ret_acc[span, :] = dot(squared, w2[...])
            gmh_acc[span, :] = dot(grad_pre, w1[...], NT)
        else:
            ret_acc[span, :] += dot(squared, w2[...])
            gmh_acc[span, :] += dot(grad_pre, w1[...], NT)

    return rows_of


def feed_grads(mh2, gr2, sq_s, gp_s, parts1, parts2):
    @pl.loop(0, 4)
    def _(q):
        line, side = (lax.div(q, 2), lax.rem(q, 2))
        cols = tile(q, 256)
        parts1[side, line] = dot(mh2[:, cols], gp_s[...], TN).astype(BF)
        parts2[line, side] = dot(gr2[:, cols], sq_s[...], TN).astype(BF)


def forward_kernel(
    planes,
    micros,
    rows,
    x_ref,
    table_ref,
    adj_ref,
    *refs,
):
    (
    lines, refs) = (refs[:11], refs[11:])
    (
    key_w,
    value_w,
    recept_w,
    output_w,
    gate_w,
    w1_ref,
    w2_ref,
    k_out,
    v_out,
    r_out,
    num_out,
    den_out,
    mid_out,
    gate_out,
    mk_out,
    mv_out,
    mr_out,
    gated_out,
    mg_out,
    da_out,
    db_out,
    keep_out,
    segs_out,
    vec_out,
    segcol_out,
    segrow_out,
    mh_all,
    ret_all,
    w1_all,
    w2_all,
    ret_acc_out,
    gmh_acc_out,
    parts1_out,
    parts2_out,
    wk,
    wv,
    wr,
    wo,
    wg,
    k_s,
    v_s,
    r_s,
    num_s,
    den_s,
    mid_s,
    gate_s,
    xb_s,
    da_s,
    mk_s,
    mv_s,
    mr_s,
    gated_s,
    mg_s,
    keep_s,
    segcol_ref,
    segrow_ref,
    segpay_ref,
    last_ref,
    mask_s,
    halo_a,
    near_a,
    pay_b,
    halo_b,
    segs_s,
    state_own,
    state_other,
    state_chip,
    state_in,
    carry_s,
    w_sem,
    out_sem,
    small_sem,
    z_sem,
    s_sem,
    vec_ref,
    mh2,
    gr2,
    sq_s,
    gp_s,
    ret_acc,
    gmh_acc,
    parts1,
    parts2,
    ff_sem,
    ) = refs
    at = Place(planes)
    dp, mp, z, core = (at.dp, at.mp, at.z, at.core)
    tokens = micros * rows
    peers = [at.ahead(step) for step in range(1, at.count)]
    greet(peers + [at.side_x, at.side_y])

    for index, line in enumerate(lines):
        vec_ref[index : index + 1, :] = line[...].astype(F32).reshape(1, 1024)
    vec_ref[11:16, :] = jnp.zeros((5, 1024), F32)

    numbers = table_ref[...].astype(F32)
    rest = jnp.zeros((8 - micros, rows), F32)
    segrow_ref[...] = jnp.concatenate([numbers, rest], axis=0)
    columns = segrow_ref[...].T
    ends = [jnp.broadcast_to(numbers[:, at_end], (micros, 128)) for at_end in (slice(rows - 1, rows), slice(0, 1))]
    segpay_ref[...] = jnp.concatenate([ends[0], ends[0], ends[1], ends[1]], axis=0)
    last_ref[...] = jnp.zeros((8, 1024), F32)
    for m in range(micros):
        segcol_ref[m * rows : (m + 1) * rows, :] = jnp.broadcast_to(columns[:, m : m + 1], (rows, 128))
        last_ref[m : m + 1, :] = x_ref[(m + 1) * rows - 16 : (m + 1) * rows, :].astype(F32)[15:16]

    quarter1, quarter2 = (w1_ref.shape[0] // 4, w2_ref.shape[0] // 4)
    q1, q2 = (tile(dp, quarter1), tile(dp, quarter2))
    z_copies = {}
    for step in (1, planes - 1):
        to = at.plane(-step)
        z_copies[step - 1] = (
            remote(w1_ref.at[q1], w1_all.at[step - 1, q1], z_sem.at[step - 1, 0, 0], z_sem.at[step - 1, 0, 1], to),
            remote(w2_ref.at[q2], w2_all.at[step - 1, q2], z_sem.at[step - 1, 1, 0], z_sem.at[step - 1, 1, 1], to),
        )
    half1 = tile(lax.div(dp, 2), 2 * quarter1)
    far2 = tile(lax.rem(dp + 2, 4), quarter2)
    back = at.plane(-1)
    onward_1 = remote(w1_all.at[0, half1], w1_all.at[1, half1], z_sem.at[1, 0, 0], z_sem.at[1, 0, 1], back)
    onward_2 = (
        remote(w2_all.at[0, q2], w2_all.at[1, q2], z_sem.at[1, 1, 0], z_sem.at[1, 1, 1], back),
        remote(w2_all.at[0, far2], w2_all.at[1, far2], z_sem.at[1, 2, 0], z_sem.at[1, 2, 1], back),
    )

    halo_copy = remote(last_ref, halo_a, small_sem.at[0, 0], small_sem.at[0, 1], at.ahead(1))
    halo_copy.start()
    seg_copies = [
        remote(segpay_ref, segs_s.at[mp], small_sem.at[1 + step, 0], small_sem.at[1 + step, 1], device)
        for step, device in enumerate(peers)
    ]
    for copy in seg_copies:
        copy.start()
    segs_s[mp] = segpay_ref[...]
    loads = []
    for index, (source, target) in enumerate(
        ((key_w, wk), (value_w, wv), (recept_w, wr), (output_w, wo), (gate_w, wg))
    ):
        loads.append(pltpu.make_async_copy(source, target, w_sem.at[index]))
        loads[-1].start()
    for copy in z_copies[0]:
        copy.start()
    halo_copy.wait()
    for copy in seg_copies:
        copy.wait()

    side1 = tile(dp + 1 - 2 * lax.rem(dp, 2), quarter1)

    def hop(array, span, step, index, device):
        part = array.at[step, span]
        return remote(part, part, z_sem.at[step, index, 0], z_sem.at[step, index, 1], device)

    def early(step):
        return (
            hop(w1_all, q1, step, 2, at.side_x),
            hop(w2_all, q2, step, 3, at.side_y),
            hop(w2_all, q2, step, 5, at.side_x),
            hop(w1_all, q1, step, 4, at.side_y),
        )

    def late(step):
        return (
            hop(w1_all, side1, step, 7, at.side_y),
            hop(w2_all, far2, step, 6, at.side_x),
        )

    def across(step):
        return (
            hop(w1_all, half1, step, 4, at.side_y),
            hop(w2_all, q2, step, 5, at.side_x),
            hop(w2_all, far2, step, 6, at.side_x),
        )

    def start(group):
        for copy in group:
            copy.start()

    def finish(group):
        for copy in group:
            copy.wait()

    early_0, early_2 = (early(0), early(2))
    late_0, across_1, late_2 = (late(0), across(1), late(2))

    before = lax.rem(mp + at.count - 1, at.count)
    has_before = mp > 0
    first_row = lax.broadcasted_iota(jnp.int32, (rows, 128), 0) == 0
    row_at = lax.broadcasted_iota(jnp.int32, (rows, rows), 0)
    col_at = lax.broadcasted_iota(jnp.int32, (rows, rows), 1)
    for m in range(micros):
        here = segcol_ref[m * rows : (m + 1) * rows, :]
        behind = jnp.where(
            first_row, segs_s[before, m : m + 1, :], pltpu.roll(here, 1, 0)
        )
        same = jnp.logical_and(
            here == behind, jnp.logical_or(jnp.logical_not(first_row), has_before)
        )
        keep_s[m * rows : (m + 1) * rows, :] = same.astype(F32)
        mask_s[m] = jnp.logical_and(
            here == segrow_ref[m : m + 1, :], col_at < row_at
        ).astype(F32).astype(BF)

    block = 32
    at_first = lax.broadcasted_iota(jnp.int32, (block, 1024), 0) == 0
    gain, bias = (vec_ref[0:1, :], vec_ref[1:2, :])
    near_a[...] = unit_of(halo_a[...])[0] * gain + bias
    for m in range(micros):

        def mix_a(b, prev, m=m):
            span = tile(m * (rows // block) + b, block)
            normed = unit_of(x_ref[span, :].astype(F32))[0] * gain + bias
            shifted = jnp.where(at_first, prev, pltpu.roll(normed, 1, 0)) * wide(
                keep_s[span, :], 1024
            )
            delta = normed - shifted
            da_s[span, :] = delta
            mk_s[span, :] = (shifted + delta * vec_ref[4:5, :]).astype(BF)
            mv_s[span, :] = (shifted + delta * vec_ref[5:6, :]).astype(BF)
            mr_s[span, :] = (shifted + delta * vec_ref[6:7, :]).astype(BF)
            return normed[block - 1 : block, :]

        lax.fori_loop(0, rows // block, mix_a, near_a[m : m + 1, :], unroll=2)

    outs = []

    def put(source, target):
        copy = pltpu.make_async_copy(source, target, out_sem.at[len(outs)])
        copy.start()
        outs.append(copy)

    put(da_s, da_out)
    put(keep_s, keep_out)
    put(segs_s, segs_out)
    put(segcol_ref, segcol_out)
    put(vec_ref, vec_out)
    put(segrow_ref, segrow_out)
    put(mk_s, mk_out)
    put(mv_s, mv_out)
    put(mr_s, mr_out)

    loads[0].wait()
    loads[1].wait()
    width = 256
    place = lax.broadcasted_iota(jnp.int32, (rows, width), 0).astype(F32)

    @pl.loop(0, 1024 // width)
    def _(i):
        cols = tile(i, width)
        rate = jnp.exp(vec_ref[2:3, cols])
        rising = jnp.exp(place * rate)
        falling = jnp.exp((1.0 - place) * rate)
        step_back = jnp.exp(-rate)
        keys = dot(mk_s[...], wk[:, cols])
        values = dot(mv_s[...], wv[:, cols])
        for m in range(micros):
            span = slice(m * rows, (m + 1) * rows)
            key, value = (keys[span], values[span])
            raised = jnp.exp(key)
            weighted = raised * value
            num = falling * dot_exact_left(mask_s[m], rising * weighted)
            den = falling * dot_exact_left(mask_s[m], rising * raised)
            k_s[span, cols] = key
            v_s[span, cols] = value
            num_s[span, cols] = num
            den_s[span, cols] = den
            state_own[m : m + 1, cols] = step_back * num[rows - 1 :] + weighted[rows - 1 :]
            state_own[micros + m : micros + m + 1, cols] = (
                step_back * den[rows - 1 :] + raised[rows - 1 :]
            )

    put(k_s, k_out)
    put(v_s, v_out)
    core_copy = remote(state_own, state_other, s_sem.at[0, 0], s_sem.at[0, 1], at.other)
    core_copy.start()
    z_copies[2][0].start()
    finish(z_copies[0])
    start(early_0)

    loads[2].wait()

    @pl.loop(0, 2)
    def _(i):
        span = tile(i, tokens // 2)
        r_s[span, :] = jax.nn.sigmoid(dot(mr_s[span, :], wr[...]))

    put(r_s, r_out)

    pair = lax.div(mp, 2) * 2
    decay_all = jnp.exp(-float(rows) * jnp.exp(vec_ref[2:3, :]))
    core_copy.wait()

    def last_of(device):
        return wide(segs_s[lax.rem(device + at.count, at.count), 0 : 2 * micros, :], 1024)

    even = jnp.where(core == 0, state_own[...], state_other[...])
    odd = jnp.where(core == 0, state_other[...], state_own[...])
    state_chip[...] = odd + jnp.where(last_of(pair) == last_of(pair + 1), decay_all * even, 0.0)
    chip_copies = [
        remote(state_chip, state_in.at[step - 1], s_sem.at[step, 0], s_sem.at[step, 1], at.plane(step))
        for step in range(1, planes)
    ]
    start(chip_copies)
    finish(early_0[0:2])
    start(late_0)
    finish(chip_copies)
    z_copies[2][1].start()
    total = jnp.zeros_like(state_chip[...])
    power = jnp.ones_like(decay_all)
    for step in range(1, planes):
        fits = jnp.logical_and(
            last_of(pair - 2 * step + 1) == last_of(pair - 1), z >= step
        )
        total = total + jnp.where(fits, power * state_in[step - 1], 0.0)
        power = power * decay_all * decay_all
    joined = state_other[...] + jnp.where(last_of(pair) == last_of(pair - 1), decay_all * total, 0.0)
    carry_s[...] = jnp.where(core == 0, total, joined)

    @pl.loop(0, 1024 // width)
    def _(i):
        cols = tile(i, width)
        rate = jnp.exp(vec_ref[2:3, cols])
        falling = jnp.exp(-place * rate)
        extra = vec_ref[3:4, cols]
        for m in range(micros):
            span = slice(m * rows, (m + 1) * rows)
            fits = jnp.logical_and(
                segcol_ref[span, :] == segs_s[before, m : m + 1, :], has_before
            ).astype(F32)
            carried = wide(fits, width) * falling
            num = num_s[span, cols] + carried * carry_s[m : m + 1, cols]
            den = den_s[span, cols] + carried * carry_s[micros + m : micros + m + 1, cols]
            bonus = jnp.exp(extra + k_s[span, cols])
            mixed = (num + bonus * v_s[span, cols]) / (den + bonus)
            num_s[span, cols] = num
            den_s[span, cols] = den
            gated_s[span, cols] = (r_s[span, cols] * mixed).astype(BF)

    put(num_s, num_out)
    put(den_s, den_out)
    put(gated_s, gated_out)
    loads[3].wait()

    @pl.loop(0, 2)
    def _(i):
        span = tile(i, tokens // 2)
        mid_s[span, :] = x_ref[span, :].astype(F32) + dot(gated_s[span, :], wo[...])

    put(mid_s, mid_out)
    gain_b, bias_b = (vec_ref[7:8, :], vec_ref[8:9, :])

    def norm_b(b):
        span = tile(b, block)
        xb_s[span, :] = unit_of(mid_s[span, :])[0] * gain_b + bias_b

    for m in range(micros):
        norm_b((m + 1) * (rows // block) - 1)
        pay_b[m : m + 1, :] = xb_s[(m + 1) * rows - 1 : (m + 1) * rows, :]
    pay_b[micros:, :] = jnp.zeros((8 - micros, 1024), F32)
    halo_b_copy = remote(pay_b, halo_b, s_sem.at[planes, 0], s_sem.at[planes, 1], at.ahead(1))
    halo_b_copy.start()
    for m in range(micros):

        @pl.loop(m * (rows // block), (m + 1) * (rows // block) - 1)
        def _(b):
            norm_b(b)

    halo_b_copy.wait()
    onward_1.start()
    start(onward_2)
    finish(z_copies[2])
    start(early_2)
    for m in range(micros):

        def mix_b(b, prev, m=m):
            span = tile(m * (rows // block) + b, block)
            normed = xb_s[span, :]
            shifted = jnp.where(at_first, prev, pltpu.roll(normed, 1, 0)) * wide(
                keep_s[span, :], 1024
            )
            delta = normed - shifted
            xb_s[span, :] = delta
            mh2[span, :] = (shifted + delta * vec_ref[9:10, :]).astype(BF)
            mg_s[span, :] = (shifted + delta * vec_ref[10:11, :]).astype(BF)
            return normed[block - 1 : block, :]

        lax.fori_loop(0, rows // block, mix_b, halo_b[m : m + 1, :], unroll=2)

    own, far = (slice(0, tokens), slice(tokens, 2 * tokens))
    mh_copy = remote(
        mh2.at[own], mh2.at[far], s_sem.at[planes + 1, 0], s_sem.at[planes + 1, 1], at.other
    )
    mh_copy.start()
    put(mg_s, mg_out)
    put(xb_s, db_out)
    loads[4].wait()

    @pl.loop(0, 2)
    def _(i):
        span = tile(i, tokens // 2)
        gate = jax.nn.sigmoid(dot(mg_s[span, :], wg[...]))
        gate_s[span, :] = gate
        gr2[span, :] = (adj_ref[span, :].astype(F32) * gate).astype(BF)

    ret_copy = remote(
        gr2.at[own], gr2.at[far], s_sem.at[planes + 2, 0], s_sem.at[planes + 2, 1], at.other
    )
    ret_copy.start()
    put(gate_s, gate_out)
    hidden = w1_ref.shape[1]
    w1_own, w2_own = (wk.at[:, 0:hidden], wv.at[0:hidden])
    w1_next, w2_next = (wk.at[:, hidden : 2 * hidden], wv.at[hidden : 2 * hidden])
    ff_loads = [
        pltpu.make_async_copy(source, target, ff_sem.at[index])
        for index, (source, target) in enumerate(
            ((w1_ref, w1_own), (w2_ref, w2_own), (w1_all.at[0], w1_next), (w2_all.at[0], w2_next))
        )
    ]
    ff_loads[0].start()
    ff_loads[1].start()
    ff_loads[0].wait()
    ff_loads[1].wait()
    half = tokens // 256
    step = feed_rows(w1_own, w2_own, mh2, gr2, sq_s, gp_s, ret_acc, gmh_acc, True)
    pl.loop(0, half)(step)
    mh_copy.wait()
    ret_copy.wait()
    finish(early_2[0:2])
    start(late_2)
    put(mh2, mh_all)
    put(gr2, ret_all)
    finish(early_0[2:4] + late_0)
    ff_loads[2].start()
    ff_loads[3].start()
    pl.loop(half, 2 * half)(step)
    feed_grads(mh2, gr2, sq_s, gp_s, parts1.at[0], parts2.at[0])
    onward_1.wait()
    across_1[0].start()
    put(parts1.at[0], parts1_out.at[0])
    put(parts2.at[0], parts2_out.at[0])
    ff_loads[2].wait()
    ff_loads[3].wait()
    step = feed_rows(w1_next, w2_next, mh2, gr2, sq_s, gp_s, ret_acc, gmh_acc, False)
    pl.loop(0, half)(step)
    onward_2[0].wait()
    across_1[1].start()
    pl.loop(half, 2 * half)(step)
    onward_2[1].wait()
    across_1[2].start()
    put(ret_acc, ret_acc_out)
    put(gmh_acc, gmh_acc_out)
    feed_grads(mh2, gr2, sq_s, gp_s, parts1.at[1], parts2.at[1])
    put(parts1.at[1], parts1_out.at[1])
    put(parts2.at[1], parts2_out.at[1])
    finish(early_2[2:4] + late_2)
    finish(across_1)
    for copy in outs:
        copy.wait()


ANY = pl.BlockSpec(memory_space=pl.ANY)
VM = pl.BlockSpec(memory_space=pltpu.VMEM)


def forward_call(planes, micros, rows, operands):
    tokens = micros * rows
    hidden = operands[-1].shape[0]

    def big(kind):
        return jax.ShapeDtypeStruct((tokens, 1024), kind)

    def hold(kind):
        return pltpu.VMEM((tokens, 1024), kind)

    square = pltpu.VMEM((1024, 1024), BF)
    few = pltpu.VMEM((8, 1024), F32)
    pair = pltpu.SemaphoreType.DMA
    return pl.pallas_call(
        functools.partial(forward_kernel, planes, micros, rows),
        out_shape=[big(F32)] * 7
        + [big(BF)] * 5
        + [big(F32)] * 2
        + [
            jax.ShapeDtypeStruct((tokens, 128), F32),
            jax.ShapeDtypeStruct((2 * planes, 16, 128), F32),
            jax.ShapeDtypeStruct((16, 1024), F32),
            jax.ShapeDtypeStruct((tokens, 128), F32),
            jax.ShapeDtypeStruct((8, rows), F32),
        ]
        + [jax.ShapeDtypeStruct((2 * tokens, 1024), BF)] * 2
        + [
            jax.ShapeDtypeStruct((planes - 1, 1024, hidden), BF),
            jax.ShapeDtypeStruct((planes - 1, hidden, 1024), BF),
        ]
        + [jax.ShapeDtypeStruct((2 * tokens, 1024), F32)] * 2
        + [jax.ShapeDtypeStruct((2, 2, 2, 256, hidden), BF)] * 2,
        in_specs=[VM] * 14 + [ANY] * 7,
        out_specs=[ANY] * 27,
        scratch_shapes=[square] * 5
        + [hold(F32)] * 9
        + [hold(BF)] * 5
        + [
            pltpu.VMEM((tokens, 128), F32),
            pltpu.VMEM((tokens, 128), F32),
            pltpu.VMEM((8, rows), F32),
            pltpu.VMEM((4 * micros, 128), F32),
            few,
            pltpu.VMEM((micros, rows, rows), BF),
            few,
            few,
            few,
            few,
            pltpu.VMEM((2 * planes, 16, 128), F32),
            few,
            few,
            few,
            pltpu.VMEM((planes - 1, 8, 1024), F32),
            few,
            pair((5,)),
            pair((29,)),
            pair((2 * planes + 1, 2)),
            pair((planes - 1, 8, 2)),
            pair((planes + 3, 2)),
            pltpu.VMEM((16, 1024), F32),
            pltpu.VMEM((2 * tokens, 1024), BF),
            pltpu.VMEM((2 * tokens, 1024), BF),
            pltpu.VMEM((2 * tokens, hidden), BF),
            pltpu.VMEM((2 * tokens, hidden), BF),
            pltpu.VMEM((2 * tokens, 1024), F32),
            pltpu.VMEM((2 * tokens, 1024), F32),
            pltpu.VMEM((2, 2, 2, 256, hidden), BF),
            pltpu.VMEM((2, 2, 2, 256, hidden), BF),
            pair((4,)),
        ],
        compiler_params=pltpu.CompilerParams(
            collective_id=0, has_side_effects=True, vmem_limit_bytes=62 << 20
        ),
        cost_estimate=pl.CostEstimate(
            flops=36 * tokens * 1024 * 1024, bytes_accessed=40 << 20, transcendentals=6 * tokens * 1024
        ),
        name="time_mix_forward",
    )(*operands)


class Reduce:
    def __init__(self, at, parts, first, second, far, sems, slot, x_first, source=None):
        self.at, self.parts, self.slot = (at, parts, slot if far is not None else 0)
        side = lax.rem(at.dp, 2)
        line = lax.div(at.dp, 2)
        self.one, self.two = (side, line) if x_first else (line, side)
        near, next_to = (at.side_x, at.side_y) if x_first else (at.side_y, at.side_x)
        self.first, self.second, self.far = (first, second, far)
        self.copy_1 = remote(
            (parts if source is None else source).at[1 - self.one],
            first,
            sems.at[0, 0],
            sems.at[0, 1],
            near,
        )
        self.copy_2 = remote(
            parts.at[self.one, 1 - self.two], second, sems.at[1, 0], sems.at[1, 1], next_to
        )
        if self.slot:
            self.copy_3 = remote(
                parts.at[self.one, self.two], far, sems.at[2, 0], sems.at[2, 1], at.plane(slot)
            )

    def start(self):
        self.copy_1.start()

    def add(self, half, other):
        mine = self.parts.at[self.one, half]

        @pl.loop(0, mine.shape[0] // 64)
        def _(i):
            span = tile(i, 64)
            mine[span, :] = (mine[span, :].astype(F32) + other[span, :].astype(F32)).astype(BF)

    def middle(self):
        self.copy_1.wait()
        self.add(1 - self.two, self.first.at[1 - self.two])
        self.copy_2.start()
        self.add(self.two, self.first.at[self.two])

    def last(self):
        self.copy_2.wait()
        self.add(self.two, self.second)
        if self.slot:
            self.copy_3.start()

    def close(self):
        if self.slot:
            self.copy_3.wait()


def sum_rows(into, index, values):
    total = values[0:8]
    for start in range(8, values.shape[0], 8):
        total = total + values[start : start + 8]
    into[index] = into[index] + total


def norm_back_rows(grad, unit, inverse, gain):
    scaled = grad * gain
    return inverse * (
        scaled
        - jnp.mean(scaled, axis=-1, keepdims=True)
        - unit * jnp.mean(scaled * unit, axis=-1, keepdims=True)
    )


def fill_square(parts, left, right, planes, split):
    @pl.loop(0, 4)
    def _(q):
        line, side = (lax.div(q, 2), lax.rem(q, 2))
        made = dot(left[:, tile(q, 256)], right[...], TN).astype(BF)
        pieces = made.reshape(planes, 2, 256 // (2 * planes), 1024)
        for core in range(2):
            if split > 0:
                parts[core, side, line, :, :, 0:split] = pieces[:, core, :, 0:split]
            if split < 1024:
                parts[core, line, side, :, :, split:1024] = pieces[:, core, :, split:1024]


def add_square(mine, other, planes):
    for one in range(2):
        for two in range(2):

            @pl.loop(0, planes)
            def _(i):
                mine[one, two, i] = (
                    mine[one, two, i].astype(F32) + other[one, two, i].astype(F32)
                ).astype(BF)


def middle_kernel(
    planes,
    micros,
    rows,
    vec_ref,
    keep_ref,
    segs_ref,
    segcol_ref,
    segrow_ref,
    w1_all,
    w2_all,
    mh_all,
    ret_all,
    ret_acc_ref,
    gmh_acc_ref,
    parts1_ref,
    parts2_ref,
    mid_ref,
    gate_ref,
    adj_ref,
    db_ref,
    k_ref,
    v_ref,
    r_ref,
    num_ref,
    den_ref,
    gate_w,
    output_w,
    gated_ref,
    mg_ref,
    out_ref,
    gmid_out,
    ggp_out,
    gatt_out,
    grp_out,
    gk_out,
    gv_out,
    sums_out,
    own1_out,
    own2_out,
    rest1_out,
    rest2_out,
    square_out,
    parts1,
    parts2,
    first1,
    first2,
    second1,
    second2,
    far1,
    far2,
    ret_acc,
    gmh_acc,
    ret_send,
    gmh_send,
    ret_recv,
    gmh_recv,
    mid_s,
    gate_s,
    adj_s,
    db_s,
    sums_s,
    sums_flat,
    mask_s,
    pay_b,
    halo_b,
    state_own,
    state_other,
    state_chip,
    state_in,
    carry_s,
    load_sem,
    out_sem,
    rs_sem,
    s_sem,
    square_parts,
    square_across,
    square_sem,
    ahead_s,
    ahead_sem,
):
    at = Place(planes)
    dp, mp, z, core = (at.dp, at.mp, at.z, at.core)
    tokens = micros * rows
    hidden = w1_all.shape[2]
    outs = []

    def put(source, target):
        copy = pltpu.make_async_copy(source, target, out_sem.at[len(outs)])
        copy.start()
        outs.append(copy)

    loaded = []

    def load(source, target):
        copy = pltpu.make_async_copy(source, target, load_sem.at[len(loaded)])
        copy.start()
        loaded.append(copy)
        return copy

    greet(
        [at.other, at.side_x, at.side_y]
        + [at.plane(step) for step in range(1, planes)]
        + [at.ahead(1), at.ahead(-1)]
    )
    half_cols = hidden // 2
    early, late_half = (slice(0, half_cols), slice(half_cols, hidden))

    def group(slot, cols, sem, source):
        made = []
        for kind, (parts, first, second, far, parts_ref) in enumerate(
            (
                (parts1, first1, second1, far1, parts1_ref),
                (parts2, first2, second2, far2, parts2_ref),
            )
        ):
            made.append(
                Reduce(
                    at,
                    parts.at[slot, :, :, :, cols],
                    first.at[slot, :, :, cols],
                    second.at[slot, :, cols],
                    far.at[slot // 2, :, cols] if slot % 2 else None,
                    rs_sem.at[sem, kind],
                    slot,
                    kind == 0,
                    parts_ref.at[slot, :, :, :, cols] if source else None,
                )
            )
        return made

    everything = slice(0, hidden)
    reduces = {
        "near": group(1, late_half, 0, True),
        "own": group(0, late_half, 1, True),
        "joined": group(0, early, 2, False),
        3: group(3, everything, 3, False),
        2: group(2, everything, 4, False),
    }
    ahead_copies = [
        remote(
            parts_ref.at[1, :, :, :, early],
            ahead_s.at[kind],
            ahead_sem.at[kind, 0],
            ahead_sem.at[kind, 1],
            at.plane(1),
        )
        for kind, parts_ref in enumerate((parts1_ref, parts2_ref))
    ]
    ret_copy = remote(ret_send, ret_recv, s_sem.at[0, 0], s_sem.at[0, 1], at.other)
    gmh_copy = remote(gmh_send, gmh_recv, s_sem.at[1, 0], s_sem.at[1, 1], at.other)

    def begin(name):
        for reduce in reduces[name]:
            reduce.start()

    def middle(name):
        for reduce in reduces[name]:
            reduce.middle()

    def last(name):
        for reduce in reduces[name]:
            reduce.last()

    begin("near")
    begin("own")
    for copy in ahead_copies:
        copy.start()

    def feed_forward(w1, w2, mh2, gr2, sq_s, gp_s):
        mh_load = [load(mh_all, mh2), load(ret_all, gr2)]
        order = (planes - 1, planes - 2)
        slots = []
        part_loads = []
        for index, slot in enumerate(order):
            slots.append(
                (load(w1_all.at[slot - 1], w1.at[index]), load(w2_all.at[slot - 1], w2.at[index]))
            )
            if index == 0:
                mh_load += [load(ret_acc_ref, ret_acc), load(gmh_acc_ref, gmh_acc)]
                for part in (1, 0):
                    part_loads.append(load(parts1_ref.at[part], parts1.at[part]))
                    part_loads.append(load(parts2_ref.at[part], parts2.at[part]))
        late = [load(mid_ref, mid_s), load(gate_ref, gate_s), load(adj_ref, adj_s), load(db_ref, db_s)]
        for copy in mh_load:
            copy.wait()
        half = tokens // 256
        for index, slot in enumerate(order):
            for copy in slots[index]:
                copy.wait()
            step = feed_rows(
                w1.at[index], w2.at[index], mh2, gr2, sq_s, gp_s, ret_acc, gmh_acc, False
            )
            pl.loop(half, 2 * half)(step)
            if index == 0:
                for copy in part_loads:
                    copy.wait()
                middle("near")
            else:

                @pl.loop(0, tokens // 64)
                def _(i):
                    span = tile(i, 64)
                    far_span = tile(tokens // 64 + i, 64)
                    ret_send[span, :] = ret_acc[far_span, :].astype(BF)
                    gmh_send[span, :] = gmh_acc[far_span, :].astype(BF)

                ret_copy.start()
                gmh_copy.start()
            pl.loop(0, half)(step)
            if index == 0:
                middle("own")
            feed_grads(mh2, gr2, sq_s, gp_s, parts1.at[slot], parts2.at[slot])
            if index == 0:
                begin(slot)
        for copy in late:
            copy.wait()

    pl.run_scoped(
        feed_forward,
        pltpu.VMEM((2, 1024, hidden), BF),
        pltpu.VMEM((2, hidden, 1024), BF),
        pltpu.VMEM((2 * tokens, 1024), BF),
        pltpu.VMEM((2 * tokens, 1024), BF),
        pltpu.VMEM((2 * tokens, hidden), BF),
        pltpu.VMEM((2 * tokens, hidden), BF),
    )
    own = slice(0, tokens)
    far = slice(tokens, 2 * tokens)
    block = 32

    def attention(k_s, v_s, r_s, num_s, den_s, wg, wo, ggp_s, gatt_s, grp_s, gk_s, gv_s):
        need_wg = load(gate_w, wg)
        need_wo = load(output_w, wo)
        need = [
            load(k_ref, k_s),
            load(v_ref, v_s),
            load(r_ref, r_s),
            load(num_ref, num_s),
            load(den_ref, den_s),
        ]
        sums_s[...] = jnp.zeros_like(sums_s)
        row_at = lax.broadcasted_iota(jnp.int32, (rows, rows), 0)
        col_at = lax.broadcasted_iota(jnp.int32, (rows, rows), 1)
        for m in range(micros):
            mask_s[m] = jnp.logical_and(
                segcol_ref[m * rows : (m + 1) * rows, :] == segrow_ref[m : m + 1, :],
                col_at > row_at,
            ).astype(F32).astype(BF)
        ret_copy.wait()
        need_gated = load(gated_ref, ret_send)

        @pl.loop(0, tokens // block)
        def _(b):
            span = tile(b, block)
            returned = ret_acc[span, :] + ret_recv[span, :].astype(F32)
            gate = gate_s[span, :]
            product_in = gate * returned
            ret_acc[span, :] = mid_s[span, :] + product_in
            ggp_s[span, :] = (adj_s[span, :].astype(F32) * product_in * (1.0 - gate)).astype(BF)

        put(ret_acc.at[own], out_ref)
        put(ggp_s, ggp_out)
        need_wg.wait()

        @pl.loop(0, 2)
        def _(i):
            span = tile(i, tokens // 2)
            ret_acc[tile(2 + i, tokens // 2), :] = dot(ggp_s[span, :], wg[...], NT)

        for kind, parts in enumerate((parts1, parts2)):
            ahead_copies[kind].wait()
            for one in range(2):
                for two in range(2):

                    @pl.loop(0, 4)
                    def _(i, kind=kind, parts=parts, one=one, two=two):
                        span = tile(i, 64)
                        parts[0, one, two, span, early] = (
                            parts[0, one, two, span, early].astype(F32)
                            + ahead_s[kind, one, two, span, :].astype(F32)
                        ).astype(BF)

        begin("joined")
        gmg = ret_acc.at[far]
        gmh_copy.wait()
        need_mg = load(mg_ref, gmh_send)
        mix_h, mix_g = (vec_ref[9:10, :], vec_ref[10:11, :])
        gain = vec_ref[7:8, :]

        def combine(b):
            span = tile(b, block)
            grad_h = gmh_acc[span, :] + gmh_recv[span, :].astype(F32)
            grad_g = gmg[span, :]
            shift = (grad_h * (1.0 - mix_h) + grad_g * (1.0 - mix_g)) * wide(keep_ref[span, :], 1024)
            return (span, grad_h, grad_g, shift)

        for m in range(micros):
            pay_b[m : m + 1, :] = combine(m * (rows // block))[3][0:1, :]
        pay_b[micros:, :] = jnp.zeros((8 - micros, 1024), F32)
        halo_copy = remote(pay_b, halo_b, s_sem.at[2, 0], s_sem.at[2, 1], at.ahead(-1))
        halo_copy.start()
        at_last = lax.broadcasted_iota(jnp.int32, (block, 1024), 0) == block - 1
        halo_copy.wait()
        last("near")
        last("own")
        middle(3)
        begin(2)
        for m in range(micros):

            def back_b(i, after, m=m):
                span, grad_h, grad_g, shift = combine((m + 1) * (rows // block) - 1 - i)
                delta = db_s[span, :]
                sum_rows(sums_s, 9, grad_h * delta)
                sum_rows(sums_s, 10, grad_g * delta)
                moved = jnp.where(at_last, after, pltpu.roll(shift, block - 1, 0))
                grad = grad_h * mix_h + grad_g * mix_g + moved
                unit, inverse = unit_of(mid_s[span, :])
                sum_rows(sums_s, 7, grad * unit)
                sum_rows(sums_s, 8, grad)
                total = adj_s[span, :].astype(F32) + norm_back_rows(grad, unit, inverse, gain)
                gmh_acc[span, :] = total
                gatt_s[span, :] = total.astype(BF)
                return shift[0:1, :]

            lax.fori_loop(0, rows // block, back_b, halo_b[m : m + 1, :], unroll=2)

        put(gmh_acc.at[own], gmid_out)
        put(gatt_s, gatt_out)
        need_wo.wait()

        @pl.loop(0, 2)
        def _(i):
            span = tile(i, tokens // 2)
            gmh_acc[tile(2 + i, tokens // 2), :] = dot(gatt_s[span, :], wo[...], NT)

        middle("joined")
        for copy in need:
            copy.wait()
        width = 256
        place = lax.broadcasted_iota(jnp.int32, (rows, width), 0).astype(F32)

        @pl.loop(0, 1024 // width)
        def _(i):
            cols = tile(i, width)
            rate = jnp.exp(vec_ref[2:3, cols])
            rising = jnp.exp(place * rate)
            falling = jnp.exp((1.0 - place) * rate)
            step_back = jnp.exp(-rate)
            extra = vec_ref[3:4, cols]
            for m in range(micros):
                span = slice(m * rows, (m + 1) * rows)
                far_span = slice(tokens + m * rows, tokens + (m + 1) * rows)
                bonus = jnp.exp(extra + k_s[span, cols])
                recept = r_s[span, cols]
                inverse = 1.0 / (den_s[span, cols] + bonus)
                mixed = (num_s[span, cols] + bonus * v_s[span, cols]) * inverse
                grad_gated = gmh_acc[far_span, cols]
                grad_mixed = grad_gated * recept
                grp_s[span, cols] = (grad_mixed * mixed * (1.0 - recept)).astype(BF)
                up = grad_mixed * inverse
                down = -up * mixed
                up_sum = rising * dot_exact_left(mask_s[m], falling * up)
                down_sum = rising * dot_exact_left(mask_s[m], falling * down)
                gmh_acc[far_span, cols] = up
                db_s[span, cols] = down
                mid_s[span, cols] = up_sum
                gate_s[span, cols] = down_sum
                state_own[m : m + 1, cols] = up[0:1] + step_back * up_sum[0:1]
                state_own[micros + m : micros + m + 1, cols] = down[0:1] + step_back * down_sum[0:1]

        put(grp_s, grp_out)
        core_copy = remote(state_own, state_other, s_sem.at[3, 0], s_sem.at[3, 1], at.other)
        core_copy.start()
        pair = lax.div(mp, 2) * 2
        decay_all = jnp.exp(-float(rows) * jnp.exp(vec_ref[2:3, :]))

        def seen(device, last):
            index = lax.rem(device + at.count, at.count)
            start = 0 if last else 2 * micros
            return wide(segs_ref[index, start : start + 2 * micros, :], 1024)

        core_copy.wait()
        even = jnp.where(core == 0, state_own[...], state_other[...])
        odd = jnp.where(core == 0, state_other[...], state_own[...])
        state_chip[...] = even + jnp.where(
            seen(pair, False) == seen(pair + 1, False), decay_all * odd, 0.0
        )
        chip_copies = [
            remote(state_chip, state_in.at[step - 1], s_sem.at[3 + step, 0], s_sem.at[3 + step, 1], at.plane(-step))
            for step in range(1, planes)
        ]
        for copy in chip_copies:
            copy.start()
        for copy in chip_copies:
            copy.wait()
        total = jnp.zeros_like(state_chip[...])
        power = jnp.ones_like(decay_all)
        for step in range(1, planes):
            fits = jnp.logical_and(
                seen(pair + 2 * step, False) == seen(mp, True), z + step < planes
            )
            total = total + jnp.where(fits, power * state_in[step - 1], 0.0)
            power = power * decay_all * decay_all
        joined = decay_all * total + jnp.where(
            seen(pair + 1, False) == seen(pair, True), state_other[...], 0.0
        )
        carry_s[...] = jnp.where(core == 0, joined, total)
        last(3)

        @pl.loop(0, 1024 // width)
        def _(i):
            cols = tile(i, width)
            rate = jnp.exp(vec_ref[2:3, cols])
            tail = jnp.exp((place - (rows - 1.0)) * rate)
            extra = vec_ref[3:4, cols]
            step_back = jnp.exp(-rate)
            for m in range(micros):
                span = slice(m * rows, (m + 1) * rows)
                far_span = slice(tokens + m * rows, tokens + (m + 1) * rows)
                fits = (segcol_ref[span, :] == segs_ref[mp, m : m + 1, :]).astype(F32)
                carried = wide(fits, width) * tail
                up_sum = mid_s[span, cols] + carried * carry_s[m : m + 1, cols]
                down_sum = gate_s[span, cols] + carried * carry_s[micros + m : micros + m + 1, cols]
                up, down = (gmh_acc[far_span, cols], db_s[span, cols])
                key, value = (k_s[span, cols], v_s[span, cols])
                bonus = jnp.exp(extra + key)
                raised = jnp.exp(key)
                direct = (up * value + down) * bonus
                gk_s[span, cols] = (direct + raised * (value * up_sum + down_sum)).astype(BF)
                gv_s[span, cols] = (up * bonus + raised * up_sum).astype(BF)
                rate_part = -rate * step_back * (up_sum * num_s[span, cols] + down_sum * den_s[span, cols])
                for index, part in ((2, rate_part), (3, direct)):
                    summed = part[0:8]
                    for start in range(8, rows, 8):
                        summed = summed + part[start : start + 8]
                    sums_s[index, :, cols] = sums_s[index, :, cols] + summed

        put(gk_s, gk_out)
        put(gv_s, gv_out)
        for index in range(16):
            sums_flat[index : index + 1, :] = jnp.sum(sums_s[index], axis=0, keepdims=True)
        put(sums_flat, sums_out)
        need_gated.wait()
        need_mg.wait()
        square_copies = []
        for index, (left, right) in enumerate(((ret_send, gatt_s), (gmh_send, ggp_s))):
            fill_square(square_parts.at[index], left, right, planes, 512)
            square_copies.append(
                remote(
                    square_parts.at[index, 1 - core],
                    square_across.at[index],
                    square_sem.at[index, 0],
                    square_sem.at[index, 1],
                    at.other,
                )
            )
            square_copies[index].start()
        middle(2)
        for index in range(2):
            square_copies[index].wait()
            add_square(square_parts.at[index, core], square_across.at[index], planes)
            put(square_parts.at[index, core], square_out.at[index])
        last("joined")
        for name in ("near", 3):
            for reduce in reduces[name]:
                reduce.close()
        for parts, far_parts, own_s, own_out, one, two in (
            (parts1, far1, mid_s, own1_out, lax.rem(dp, 2), lax.div(dp, 2)),
            (parts2, far2, gate_s, own2_out, lax.div(dp, 2), lax.rem(dp, 2)),
        ):
            total = parts[0, one, two].astype(F32) + far_parts[1].astype(F32)
            own_s[0:256, early] = total[:, early]
            own_s[0:256, late_half] = total[:, late_half] + far_parts[0, :, late_half].astype(F32)
            put(own_s.at[0:256, 0:hidden], own_out)
        last(2)
        put(parts1.at[2, lax.rem(dp, 2), lax.div(dp, 2)], rest1_out)
        put(parts2.at[2, lax.div(dp, 2), lax.rem(dp, 2)], rest2_out)
        for copy in outs:
            copy.wait()

    def hold(kind):
        return pltpu.VMEM((tokens, 1024), kind)

    square = pltpu.VMEM((1024, 1024), BF)
    pl.run_scoped(attention, *([hold(F32)] * 5), square, square, *([hold(BF)] * 5))


def middle_call(planes, micros, rows, operands):
    tokens = micros * rows
    hidden = operands[5].shape[2]

    def big(kind):
        return jax.ShapeDtypeStruct((tokens, 1024), kind)

    def hold(count, kind):
        return pltpu.VMEM((count, 1024), kind)

    few = hold(8, F32)
    quarter = (256, hidden)
    piece = (planes, 256 // (2 * planes), 1024)
    sems = pltpu.SemaphoreType.DMA
    return pl.pallas_call(
        functools.partial(middle_kernel, planes, micros, rows),
        out_shape=[big(F32)] * 2
        + [big(BF)] * 5
        + [jax.ShapeDtypeStruct((16, 1024), F32)]
        + [jax.ShapeDtypeStruct(quarter, F32)] * 2
        + [jax.ShapeDtypeStruct(quarter, BF)] * 2
        + [jax.ShapeDtypeStruct((2, 2, 2) + piece, BF)],
        in_specs=[VM] * 5 + [ANY] * 21,
        out_specs=[ANY] * 13,
        scratch_shapes=[pltpu.VMEM((planes, 2, 2) + quarter, BF)] * 2
        + [pltpu.VMEM((planes, 2) + quarter, BF)] * 2
        + [pltpu.VMEM((planes,) + quarter, BF)] * 2
        + [pltpu.VMEM((2,) + quarter, BF)] * 2
        + [hold(2 * tokens, F32)] * 2
        + [hold(tokens, BF)] * 4
        + [hold(tokens, F32), hold(tokens, F32), hold(tokens, BF), hold(tokens, F32)]
        + [
            pltpu.VMEM((16, 8, 1024), F32),
            pltpu.VMEM((16, 1024), F32),
            pltpu.VMEM((micros, rows, rows), BF),
            few,
            few,
            few,
            few,
            few,
            pltpu.VMEM((planes - 1, 8, 1024), F32),
            few,
            sems((25,)),
            sems((14,)),
            sems((planes + 1, 2, 3, 2)),
            sems((3 + planes, 2)),
            pltpu.VMEM((2, 2, 2, 2) + piece, BF),
            pltpu.VMEM((2, 2, 2) + piece, BF),
            sems((2, 2)),
            pltpu.VMEM((2, 2, 2, 256, hidden // 2), BF),
            sems((2, 2)),
        ],
        compiler_params=pltpu.CompilerParams(
            collective_id=1, has_side_effects=True, vmem_limit_bytes=63 << 20
        ),
        cost_estimate=pl.CostEstimate(
            flops=52 * tokens * 1024 * 1024, bytes_accessed=60 << 20, transcendentals=6 * tokens * 1024
        ),
        name="channel_mix_and_adjoint",
    )(*operands)


class ReduceSquare:
    def __init__(self, at, mine, first, second, far, sems, x_first, source=None):
        self.at, self.mine, self.first, self.second, self.far = (at, mine, first, second, far)
        side = lax.rem(at.dp, 2)
        line = lax.div(at.dp, 2)
        self.one, self.two = (side, line) if x_first else (line, side)
        near, next_to = (at.side_x, at.side_y) if x_first else (at.side_y, at.side_x)
        self.copy_1 = remote(
            (mine if source is None else source).at[1 - self.one],
            first,
            sems.at[0, 0],
            sems.at[0, 1],
            near,
        )
        self.copy_2 = remote(
            mine.at[self.one, 1 - self.two], second, sems.at[1, 0], sems.at[1, 1], next_to
        )
        self.copies_3 = [
            remote(
                mine.at[self.one, self.two, lax.rem(at.z + step, at.planes)],
                far.at[step - 1],
                sems.at[1 + step, 0],
                sems.at[1 + step, 1],
                at.plane(step),
            )
            for step in range(1, at.planes)
        ]

    def add(self, one, two, other):
        @pl.loop(0, self.at.planes)
        def _(i):
            self.mine[one, two, i] = (
                self.mine[one, two, i].astype(F32) + other[i].astype(F32)
            ).astype(BF)

    def begin(self):
        self.copy_1.start()

    def middle(self):
        self.copy_1.wait()
        self.add(self.one, 1 - self.two, self.first.at[1 - self.two])
        self.copy_2.start()
        self.add(self.one, self.two, self.first.at[self.two])

    def last(self):
        self.copy_2.wait()
        self.add(self.one, self.two, self.second)

    def send(self):
        for copy in self.copies_3:
            copy.start()

    def close(self):
        for copy in self.copies_3:
            copy.wait()
        total = self.mine[self.one, self.two, self.at.z].astype(F32)
        for step in range(self.at.planes - 1):
            total = total + self.far[step].astype(F32)
        return total


def last_kernel(
    planes,
    micros,
    rows,
    vec_ref,
    keep_ref,
    sums_ref,
    square_ref,
    mr_ref,
    grp_ref,
    mv_ref,
    gv_ref,
    mk_ref,
    gk_ref,
    recept_w,
    value_w,
    key_w,
    x_ref,
    da_ref,
    gmid_ref,
    part1_ref,
    part2_ref,
    rest1_ref,
    rest2_ref,
    grad_out,
    sums_out,
    own_output,
    own_gate,
    own_recept,
    own_value,
    own_key,
    own_hidden,
    own_return,
    left_s,
    right_s,
    w_s,
    x_s,
    da_s,
    total_s,
    g_s,
    sums_s,
    parts,
    across,
    first,
    second,
    far,
    own_s,
    pay_a,
    halo_a,
    flat_s,
    flat_recv,
    load_sem,
    out_sem,
    rs_sem,
    s_sem,
    ff_far,
    ff_total,
    own1_s,
    own2_s,
    ff_sem,
    ready_s,
    core_sem,
):
    at = Place(planes)
    tokens = micros * rows
    outs = []

    def put(source, target):
        copy = pltpu.make_async_copy(source, target, out_sem.at[len(outs)])
        copy.start()
        outs.append(copy)

    loaded = []

    def load(source, target):
        copy = pltpu.make_async_copy(source, target, load_sem.at[len(loaded)])
        copy.start()
        loaded.append(copy)
        return copy

    sides = (
        (mr_ref, grp_ref),
        (mv_ref, gv_ref),
        (mk_ref, gk_ref),
    )
    right_loads, w_loads = ([], [])
    for index, source in enumerate((recept_w, value_w, key_w)):
        right_loads.append(load(sides[index][1], right_s.at[index]))
        w_loads.append(load(source, w_s.at[index]))
    greet(
        [at.other, at.side_x, at.side_y]
        + [at.plane(step) for step in range(1, planes)]
        + [at.ahead(1), at.ahead(-1)]
    )
    core = at.core
    lefts, rights = (slice(0, 512), slice(512, 1024))
    reduces = []
    for index in range(5):
        mine = ready_s.at[index] if index < 2 else parts.at[index - 2, core]
        halves = []
        for kind, cols in enumerate((lefts, rights)):
            halves.append(
                ReduceSquare(
                    at,
                    mine.at[:, :, :, :, cols],
                    first.at[index, :, :, :, cols],
                    second.at[index, :, :, cols],
                    far.at[index, :, :, cols],
                    rs_sem.at[index, kind],
                    kind == 0,
                    square_ref.at[index, :, :, :, :, cols] if index < 2 else None,
                )
            )
        reduces.append(halves)

    def begin(index):
        for half in reduces[index]:
            half.begin()

    def middle(index):
        for half in reduces[index]:
            half.middle()

    def last(index):
        for half in reduces[index]:
            half.last()
            half.send()

    def close(index, target):
        for half, cols in zip(reduces[index], (lefts, rights)):
            own_s[index, :, cols] = half.close()
        put(own_s.at[index], target)

    core_copies = [
        remote(
            parts.at[index, 1 - core],
            across.at[index],
            core_sem.at[index, 0],
            core_sem.at[index, 1],
            at.other,
        )
        for index in range(3)
    ]
    ff_loads = [load(part1_ref, ff_total.at[0]), load(part2_ref, ff_total.at[1])]
    ff_copies = [
        remote(rest, ff_far.at[index], ff_sem.at[index, 0], ff_sem.at[index, 1], at.plane(2))
        for index, rest in enumerate((rest1_ref, rest2_ref))
    ]
    begin(0)
    begin(1)
    ready_load = load(square_ref, ready_s)
    left_loads = [load(left, left_s.at[index]) for index, (left, _) in enumerate(sides)]
    row_loads = [load(x_ref, x_s), load(da_ref, da_s), load(gmid_ref, total_s)]
    mixes = (vec_ref[6:7, :], vec_ref[5:6, :], vec_ref[4:5, :])
    heads = jnp.zeros((16 * micros, 1024), F32)
    for index in range(3):
        right_loads[index].wait()
        w_loads[index].wait()
        picked = jnp.concatenate(
            [right_s[index, m * rows : m * rows + 16, :] for m in range(micros)], axis=0
        )
        heads = heads + dot(picked, w_s[index], NT) * (1.0 - mixes[index])
    for m in range(micros):
        pay_a[m : m + 1, :] = heads[16 * m : 16 * m + 1] * wide(
            keep_ref[m * rows : m * rows + 8, :], 1024
        )[0:1]
    pay_a[micros:, :] = jnp.zeros((8 - micros, 1024), F32)
    halo_copy = remote(pay_a, halo_a, s_sem.at[0, 0], s_sem.at[0, 1], at.ahead(-1))
    halo_copy.start()
    for copy in ff_copies:
        copy.start()
    sums_s[...] = jnp.zeros_like(sums_s)

    def fill(index):
        left_loads[index].wait()
        fill_square(parts.at[index], left_s.at[index], right_s.at[index], planes, 512)
        core_copies[index].start()

    def settle(index):
        core_copies[index].wait()
        add_square(parts.at[index, core], across.at[index], planes)

    def back(index):
        @pl.loop(0, 2)
        def _(i):
            span = tile(i, tokens // 2)
            g_s[index, span, :] = dot(right_s[index, span, :], w_s[index], NT)

    fill(0)
    ready_load.wait()
    middle(0)
    fill(1)
    settle(0)
    begin(2)
    fill(2)
    settle(1)
    middle(1)
    begin(3)
    settle(2)
    back(0)
    last(0)
    back(1)
    back(2)
    for copy in row_loads:
        copy.wait()
    block = 32
    gain = vec_ref[0:1, :]

    def combine(b):
        span = tile(b, block)
        grads = [g_s[index, span, :] for index in range(3)]
        shift = sum(grad * (1.0 - mix) for grad, mix in zip(grads, mixes))
        return (span, grads, shift * wide(keep_ref[span, :], 1024))

    at_last = lax.broadcasted_iota(jnp.int32, (block, 1024), 0) == block - 1
    halo_copy.wait()
    for m in range(micros):

        def back_a(i, after, m=m):
            span, grads, shift = combine((m + 1) * (rows // block) - 1 - i)
            delta = da_s[span, :]
            for index, grad in enumerate(grads):
                sum_rows(sums_s, 2 - index, grad * delta)
            moved = jnp.where(at_last, after, pltpu.roll(shift, block - 1, 0))
            grad = sum(part * mix for part, mix in zip(grads, mixes)) + moved
            unit, inverse = unit_of(x_s[span, :].astype(F32))
            sum_rows(sums_s, 3, grad * unit)
            sum_rows(sums_s, 4, grad)
            total_s[span, :] = total_s[span, :] + norm_back_rows(grad, unit, inverse, gain)
            return shift[0:1, :]

        lax.fori_loop(0, rows // block, back_a, halo_a[m : m + 1, :], unroll=2)
    put(total_s, grad_out)
    flat_s[0] = sums_ref[...]
    for index, row in enumerate((4, 5, 6, 0, 1)):
        flat_s[0, row : row + 1, :] = jnp.sum(sums_s[index], axis=0, keepdims=True)

    def flat_copy(level, slot, device):
        return remote(
            flat_s.at[level], flat_recv.at[slot], s_sem.at[1 + slot, 0], s_sem.at[1 + slot, 1], device
        )

    over_core = flat_copy(0, 0, at.other)
    over_core.start()
    over_core.wait()
    flat_s[1] = flat_s[0] + flat_recv[0]
    over_x = flat_copy(1, 1, at.side_x)
    middle(2)
    over_x.start()
    begin(4)
    last(1)
    middle(3)
    over_x.wait()
    flat_s[2] = flat_s[1] + flat_recv[1]
    over_y = flat_copy(2, 2, at.side_y)
    over_y.start()
    last(2)
    middle(4)
    last(3)
    over_y.wait()
    flat_s[3] = flat_s[2] + flat_recv[2]
    flat_copies = []
    for step in range(1, planes):
        to = lax.rem(at.z + step, planes)
        lanes = tile(at.dp * (planes // 2) + lax.div(to, 2), 128)
        slot = 2 + step
        flat_copies.append(
            remote(
                flat_s.at[3, :, lanes],
                flat_recv.at[slot, :, lanes],
                s_sem.at[1 + slot, 0],
                s_sem.at[1 + slot, 1],
                at.plane(step),
            )
        )
    for copy in flat_copies:
        copy.start()
    for copy in ff_loads + ff_copies:
        copy.wait()
    own1_s[...] = ff_total[0] + ff_far[0].astype(F32)
    own2_s[...] = (ff_total[1] + ff_far[1].astype(F32)).T
    put(own1_s, own_hidden)
    put(own2_s, own_return)
    last(4)
    close(0, own_output)
    close(1, own_gate)
    close(2, own_recept)
    for copy in flat_copies:
        copy.wait()
    lanes = tile(at.dp * (planes // 2) + lax.div(at.z, 2), 128)
    flat_s[0, :, lanes] = flat_s[3, :, lanes] + sum(
        flat_recv[2 + step, :, lanes] for step in range(1, planes)
    )
    put(flat_s.at[0], sums_out)
    close(3, own_value)
    close(4, own_key)
    for copy in outs:
        copy.wait()


def last_call(planes, micros, rows, operands):
    tokens = micros * rows

    def hold(count, kind):
        return pltpu.VMEM((count, tokens, 1024), kind)

    quarter = operands[-4].shape
    piece = (1024 // (8 * planes), 1024)
    sems = pltpu.SemaphoreType.DMA
    few = pltpu.VMEM((8, 1024), F32)
    return pl.pallas_call(
        functools.partial(last_kernel, planes, micros, rows),
        out_shape=[
            jax.ShapeDtypeStruct((tokens, 1024), F32),
            jax.ShapeDtypeStruct((16, 1024), F32),
        ]
        + [jax.ShapeDtypeStruct(piece, F32)] * 5
        + [jax.ShapeDtypeStruct(quarter, F32), jax.ShapeDtypeStruct(quarter[::-1], F32)],
        in_specs=[VM] * 3 + [ANY] * 17,
        out_specs=[ANY] * 9,
        scratch_shapes=[
            hold(3, BF),
            hold(3, BF),
            pltpu.VMEM((3, 1024, 1024), BF),
            pltpu.VMEM((tokens, 1024), BF),
            pltpu.VMEM((tokens, 1024), F32),
            pltpu.VMEM((tokens, 1024), F32),
            hold(3, F32),
            pltpu.VMEM((5, 8, 1024), F32),
            pltpu.VMEM((3, 2, 2, 2, planes) + piece, BF),
            pltpu.VMEM((3, 2, 2, planes) + piece, BF),
            pltpu.VMEM((5, 2, planes) + piece, BF),
            pltpu.VMEM((5, planes) + piece, BF),
            pltpu.VMEM((5, planes - 1) + piece, BF),
            pltpu.VMEM((5,) + piece, F32),
            few,
            few,
            pltpu.VMEM((4, 16, 1024), F32),
            pltpu.VMEM((2 + planes, 16, 1024), F32),
            sems((18,)),
            sems((9,)),
            sems((5, 2, 1 + planes, 2)),
            sems((3 + planes, 2)),
            pltpu.VMEM((2,) + quarter, BF),
            pltpu.VMEM((2,) + quarter, F32),
            pltpu.VMEM(quarter, F32),
            pltpu.VMEM(quarter[::-1], F32),
            sems((2, 2)),
            pltpu.VMEM((2, 2, 2, planes) + piece, BF),
            sems((3, 2)),
        ],
        compiler_params=pltpu.CompilerParams(
            collective_id=2, has_side_effects=True, vmem_limit_bytes=62 << 20
        ),
        cost_estimate=pl.CostEstimate(
            flops=16 * tokens * 1024 * 1024, bytes_accessed=30 << 20, transcendentals=0
        ),
        name="time_mix_weights",
    )(*operands)


def one_micro(block_in, seg_ids, grad_out, vectors, matrices, hidden_w, return_w):
    (
        gain_one,
        bias_one,
        decay_vec,
        extra_array,
        mix_key,
        mix_value,
        mix_recept,
        gain_two,
        bias_two,
        mix_hidden,
        mix_gate,
    ) = vectors
    key_w, value_w, recept_w, output_w, gate_w = matrices
    row_count = block_in.shape[0]
    model_width = block_in.shape[1]
    seg_float = seg_ids.astype(jnp.float32)
    normed_a, unit_a, inv_a = layer_norm(block_in, gain_one, bias_one)
    prev_row, prev_seg = from_behind((normed_a[-1:], seg_float[-1:]), "mp", 1)
    same_row = jnp.concatenate(
        [
            (seg_float[:1] == prev_seg).astype(jnp.float32),
            (seg_ids[1:] == seg_ids[:-1]).astype(jnp.float32),
        ]
    )
    same_col = same_row[:, None]
    shifted_a = jnp.concatenate([prev_row, normed_a[:-1]], axis=0) * same_col
    delta_a = normed_a - shifted_a
    low_key = reduced_precision(shifted_a + delta_a * mix_key)
    low_value = reduced_precision(shifted_a + delta_a * mix_value)
    low_recept = reduced_precision(shifted_a + delta_a * mix_recept)
    lookup_start = product(low_key, key_w)
    content_start = product(low_value, value_w)
    recept = jax.nn.sigmoid(product(low_recept, recept_w))
    feature_fading = jnp.exp(decay_vec)
    positions = jnp.arange(row_count, dtype=jnp.float32)[:, None]
    rising = jnp.exp(positions * feature_fading)
    falling = jnp.exp(-(positions - 1.0) * feature_fading)
    falling_zero = jnp.exp(-positions * feature_fading)
    raised_lookup = jnp.exp(lookup_start)
    weighted_average = raised_lookup * content_start
    order_rows = jnp.arange(row_count)
    lower_tri = jnp.logical_and(
        seg_ids[:, None] == seg_ids[None, :], order_rows[None, :] < order_rows[:, None]
    ).astype(jnp.float32)
    last_mask = (seg_ids == seg_ids[-1]).astype(jnp.float32)
    first_mask = (seg_ids == seg_ids[0]).astype(jnp.float32) * same_row[0]
    forward_mat = jnp.concatenate([lower_tri, last_mask[None]], axis=0)
    stacked = jnp.concatenate(
        [
            rising * weighted_average,
            rising * raised_lookup,
            positions * rising * weighted_average,
            positions * rising * raised_lookup,
        ],
        axis=1,
    )
    summed = jnp.dot(forward_mat, stacked, precision=HIGH)
    inner_sums = summed[:row_count]
    closing = summed[row_count]
    num_loc = falling * inner_sums[:, :model_width]
    den_loc = falling * inner_sums[:, model_width : 2 * model_width]
    num_der = (
        -(positions - 1.0) * num_loc + falling * inner_sums[:, 2 * model_width : 3 * model_width]
    )
    den_der = -(positions - 1.0) * den_loc + falling * inner_sums[:, 3 * model_width :]
    end_fall = jnp.exp(-(row_count - 1.0) * feature_fading)
    state_num = end_fall * closing[:model_width]
    state_den = end_fall * closing[model_width : 2 * model_width]
    state_num_der = (
        -(row_count - 1.0) * state_num + end_fall * closing[2 * model_width : 3 * model_width]
    )
    state_den_der = -(row_count - 1.0) * state_den + end_fall * closing[3 * model_width :]
    uniform_flag = (seg_ids[-1] == seg_ids[0]).astype(jnp.float32) * same_row[0]
    carry_pass = uniform_flag * jnp.exp(-row_count * feature_fading)
    carry_der = -row_count * carry_pass
    zero_vec = jnp.zeros_like(feature_fading)
    one_vec = jnp.ones_like(feature_fading)
    in_num, in_den, in_num_der, in_den_der, pass_total, pass_der = carried_in(
        (state_num, state_den, state_num_der, state_den_der, carry_pass, carry_der),
        "mp",
        state_join,
        (zero_vec, zero_vec, zero_vec, zero_vec, one_vec, zero_vec),
        False,
    )
    carried = first_mask[:, None] * falling_zero
    dividend = num_loc + carried * in_num
    divisor_portion = den_loc + carried * in_den
    numer_der = num_der + carried * (in_num_der - positions * in_num)
    denom_der = den_der + carried * (in_den_der - positions * in_den)
    extra_summand = jnp.exp(extra_array + lookup_start)
    divisor_complete = divisor_portion + extra_summand
    mixture_result = (dividend + extra_summand * content_start) / divisor_complete
    gated = reduced_precision(recept * mixture_result)
    block_mid = block_in + product(gated, output_w)
    normed_b, unit_b, inv_b = layer_norm(block_mid, gain_two, bias_two)
    prev_mid = from_behind(normed_b[-1:], "mp", 1)
    shifted_b = jnp.concatenate([prev_mid, normed_b[:-1]], axis=0) * same_col
    delta_b = normed_b - shifted_b
    low_hidden = reduced_precision(shifted_b + delta_b * mix_hidden)
    low_gate = reduced_precision(shifted_b + delta_b * mix_gate)
    gate_two = jax.nn.sigmoid(product(low_gate, gate_w))
    hidden_rows = lax.all_gather(low_hidden, "mp", axis=0, tiled=True)
    pre_act = product(hidden_rows, hidden_w)
    rectified = jnp.maximum(pre_act, 0.0)
    squared = reduced_precision(rectified * rectified)
    returned = lax.psum_scatter(
        product(squared, return_w).astype(jnp.bfloat16), "mp", scatter_dimension=0, tiled=True
    ).astype(jnp.float32)
    output = block_mid + gate_two * returned
    grad_ret = reduced_precision(grad_out * gate_two)
    grad_gate_pre = reduced_precision(grad_out * returned * gate_two * (1.0 - gate_two))
    d_gate_w = (low_gate, grad_gate_pre)
    grad_low_gate = product_nt(grad_gate_pre, gate_w)
    grad_rows = lax.all_gather(grad_ret, "mp", axis=0, tiled=True)
    grad_squared = product_nt(grad_rows, return_w)
    d_return = (squared, grad_rows)
    grad_pre = reduced_precision(grad_squared * 2.0 * rectified)
    d_hidden = (hidden_rows, grad_pre)
    grad_low_hidden = lax.psum_scatter(
        product_nt(grad_pre, hidden_w).astype(jnp.bfloat16), "mp", scatter_dimension=0, tiled=True
    ).astype(jnp.float32)
    d_mix_hidden = jnp.sum(grad_low_hidden * delta_b, axis=0)
    d_mix_gate = jnp.sum(grad_low_gate * delta_b, axis=0)
    grad_shift_b = (
        grad_low_hidden * (1.0 - mix_hidden) + grad_low_gate * (1.0 - mix_gate)
    ) * same_col
    from_next_b = from_behind(grad_shift_b[:1], "mp", -1)
    grad_norm_b = (
        grad_low_hidden * mix_hidden
        + grad_low_gate * mix_gate
        + jnp.concatenate([grad_shift_b[1:], from_next_b], axis=0)
    )
    grad_mid_norm, d_gain_two, d_bias_two = norm_back(grad_norm_b, unit_b, inv_b, gain_two)
    grad_mid = grad_out + grad_mid_norm
    grad_att = reduced_precision(grad_mid)
    d_output_w = (gated, grad_att)
    grad_gated = product_nt(grad_att, output_w)
    grad_recept_pre = reduced_precision(grad_gated * mixture_result * recept * (1.0 - recept))
    grad_mixed = grad_gated * recept
    d_recept_w = (low_recept, grad_recept_pre)
    grad_low_recept = product_nt(grad_recept_pre, recept_w)
    dividend_adjoint = grad_mixed / divisor_complete
    divisor_adjoint = -dividend_adjoint * mixture_result
    extra_derivative_part = dividend_adjoint * content_start + divisor_adjoint
    extra_derivative = jnp.sum(extra_derivative_part * extra_summand, axis=0)
    d_rate = jnp.sum(dividend_adjoint * numer_der + divisor_adjoint * denom_der, axis=0)
    backward_mat = jnp.concatenate([lower_tri.T, first_mask[None]], axis=0)
    back_sum = jnp.dot(
        backward_mat,
        jnp.concatenate([falling * dividend_adjoint, falling * divisor_adjoint], axis=1),
        precision=HIGH,
    )
    step_back = jnp.exp(-feature_fading)
    from_num = step_back * back_sum[row_count, :model_width]
    from_den = step_back * back_sum[row_count, model_width:]
    out_num, out_den, out_pass = carried_in(
        (from_num, from_den, carry_pass), "mp", suffix_join, (zero_vec, zero_vec, one_vec), True
    )
    tail_fall = last_mask[:, None] * jnp.exp(-(row_count - 1.0 - positions) * feature_fading)
    cumulative_dividend = rising * back_sum[:row_count, :model_width] + tail_fall * out_num
    running_denominator = rising * back_sum[:row_count, model_width:] + tail_fall * out_den
    value_gradient = reduced_precision(
        dividend_adjoint * extra_summand + cumulative_dividend * raised_lookup
    )
    key_gradient = reduced_precision(
        extra_derivative_part * extra_summand
        + cumulative_dividend * weighted_average
        + running_denominator * raised_lookup
    )
    d_key_w = (low_key, key_gradient)
    d_value_w = (low_value, value_gradient)
    grad_low_key = product_nt(key_gradient, key_w)
    grad_low_value = product_nt(value_gradient, value_w)
    d_mix_key = jnp.sum(grad_low_key * delta_a, axis=0)
    d_mix_value = jnp.sum(grad_low_value * delta_a, axis=0)
    d_mix_recept = jnp.sum(grad_low_recept * delta_a, axis=0)
    grad_shift_a = (
        grad_low_key * (1.0 - mix_key)
        + grad_low_value * (1.0 - mix_value)
        + grad_low_recept * (1.0 - mix_recept)
    ) * same_col
    from_next_a = from_behind(grad_shift_a[:1], "mp", -1)
    grad_norm_a = (
        grad_low_key * mix_key
        + grad_low_value * mix_value
        + grad_low_recept * mix_recept
        + jnp.concatenate([grad_shift_a[1:], from_next_a], axis=0)
    )
    grad_in_norm, d_gain_one, d_bias_one = norm_back(grad_norm_a, unit_a, inv_a, gain_one)
    input_grad = grad_mid + grad_in_norm
    grads = (
        d_gain_one,
        d_bias_one,
        d_rate * feature_fading,
        extra_derivative,
        d_mix_key,
        d_mix_value,
        d_mix_recept,
        d_key_w,
        d_value_w,
        d_recept_w,
        d_output_w,
        d_gain_two,
        d_bias_two,
        d_mix_hidden,
        d_mix_gate,
        d_hidden,
        d_return,
        d_gate_w,
    )
    return (output, input_grad, grads)


def generic_body(
    incoming_signal,
    series_number_table,
    upstream_adjoint,
    first_scaling_factor,
    first_scaling_offset,
    logarithmic_fading_speeds,
    present_step_extra,
    lookup_shift_mixture,
    content_shift_mixture,
    admit_lookup_shift_mixture,
    attention_lookup_matrix,
    attention_content_matrix,
    attention_admit_matrix,
    attention_result_matrix,
    second_scaling_factor,
    second_scaling_offset,
    inner_shift_mixture,
    admit_shift_mixture,
    feedforward_lookup_matrix,
    feedforward_content_matrix,
    feedforward_admit_matrix,
):
    hidden_full, return_full = (feedforward_lookup_matrix, feedforward_content_matrix)
    vectors = tuple(
        (
            start_item.astype(jnp.float32)
            for start_item in (
                first_scaling_factor,
                first_scaling_offset,
                logarithmic_fading_speeds,
                present_step_extra,
                lookup_shift_mixture,
                content_shift_mixture,
                admit_lookup_shift_mixture,
                second_scaling_factor,
                second_scaling_offset,
                inner_shift_mixture,
                admit_shift_mixture,
            )
        )
    )
    matrices = (
        attention_lookup_matrix,
        attention_content_matrix,
        attention_admit_matrix,
        attention_result_matrix,
        feedforward_admit_matrix,
    )
    output, input_grad, grads = jax.vmap(
        lambda rows, ids, adjoint: one_micro(
            rows, ids, adjoint, vectors, matrices, hidden_full, return_full
        )
    )(
        incoming_signal[:, 0].astype(jnp.float32),
        series_number_table[:, 0],
        upstream_adjoint[:, 0].astype(jnp.float32),
    )
    totals = tuple(
        product_tn(*(side.reshape(-1, side.shape[-1]) for side in grad))
        if isinstance(grad, tuple)
        else jnp.sum(grad, axis=0)
        for grad in grads
    )
    square = [index for index in range(18) if totals[index].shape == totals[7].shape]
    lines = [index for index in range(18) if totals[index].ndim == 1]
    wide = lax.psum_scatter(
        jnp.concatenate([reduced_precision(totals[index]) for index in square], axis=1),
        ("dp", "mp"),
        scatter_dimension=0,
        tiled=True,
    ).astype(jnp.float32)
    thin = lax.psum_scatter(
        jnp.stack([totals[index] for index in lines], axis=1),
        ("dp", "mp"),
        scatter_dimension=0,
        tiled=True,
    )
    held = dict(zip(square, jnp.split(wide, len(square), axis=1)))
    held.update({index: thin[:, place] for place, index in enumerate(lines)})
    output, input_grad = (output[:, None], input_grad[:, None])
    owned = tuple(held[index] for index in sorted(held))
    hidden_own, return_own = (
        lax.psum_scatter(
            totals[15].astype(jnp.bfloat16), "dp", scatter_dimension=0, tiled=True
        ).astype(jnp.float32),
        lax.psum_scatter(
            totals[16].astype(jnp.bfloat16), "dp", scatter_dimension=1, tiled=True
        ).astype(jnp.float32),
    )
    return (
        output,
        input_grad,
        owned[0],
        owned[1],
        owned[2],
        owned[3],
        owned[4],
        owned[5],
        owned[6],
        owned[7],
        owned[8],
        owned[9],
        owned[10],
        owned[11],
        owned[12],
        owned[13],
        owned[14],
        hidden_own,
        return_own,
        owned[15],
    )


def hand_over(count, *refs):
    sems = refs[3 * count]
    ins, outs = ([], [])
    for index in range(count):
        held = refs[2 * count + index]
        ins.append(pltpu.make_async_copy(refs[index], held, sems.at[0, index]))
        outs.append(pltpu.make_async_copy(held, refs[count + index], sems.at[1, index]))
        ins[-1].start()
    for index in range(count):
        ins[index].wait()
        outs[index].start()
    for copy in outs:
        copy.wait()


def hand_call(arrays):
    count = len(arrays)
    return pl.pallas_call(
        functools.partial(hand_over, count),
        out_shape=[jax.ShapeDtypeStruct(part.shape, part.dtype) for part in arrays],
        in_specs=[ANY] * count,
        out_specs=[ANY] * count,
        scratch_shapes=[pltpu.VMEM(part.shape, part.dtype) for part in arrays]
        + [pltpu.SemaphoreType.DMA((2, count))],
        compiler_params=pltpu.CompilerParams(vmem_limit_bytes=60 << 20),
        name="hand_over",
    )(*arrays)


def kernel_body(
    incoming_signal,
    series_number_table,
    upstream_adjoint,
    first_scaling_factor,
    first_scaling_offset,
    logarithmic_fading_speeds,
    present_step_extra,
    lookup_shift_mixture,
    content_shift_mixture,
    admit_lookup_shift_mixture,
    attention_lookup_matrix,
    attention_content_matrix,
    attention_admit_matrix,
    attention_result_matrix,
    second_scaling_factor,
    second_scaling_offset,
    inner_shift_mixture,
    admit_shift_mixture,
    feedforward_lookup_matrix,
    feedforward_content_matrix,
    feedforward_admit_matrix,
):
    hidden_full, return_full = (feedforward_lookup_matrix, feedforward_content_matrix)
    matrices = (
        attention_lookup_matrix,
        attention_content_matrix,
        attention_admit_matrix,
        attention_result_matrix,
        feedforward_admit_matrix,
    )
    micros, _, rows, depth = incoming_signal.shape
    planes = lax.axis_size("mp") // 2
    x = incoming_signal.reshape(micros * rows, depth)
    adjoint = upstream_adjoint.reshape(micros * rows, depth)
    operands = (
        x,
        series_number_table.reshape(micros, rows),
        adjoint,
        first_scaling_factor,
        first_scaling_offset,
        logarithmic_fading_speeds,
        present_step_extra,
        lookup_shift_mixture,
        content_shift_mixture,
        admit_lookup_shift_mixture,
        second_scaling_factor,
        second_scaling_offset,
        inner_shift_mixture,
        admit_shift_mixture,
        *matrices,
        hidden_full,
        return_full,
    )
    (
        keys, values, recept, num, den, mid, gate, mk, mv, mr, gated, mg, delta_a, delta_b,
        keep, segs, table, segcol, segrow, mh_all, ret_all, w1_all, w2_all, ret_acc, gmh_acc,
        parts1, parts2,
    ) = forward_call(planes, micros, rows, operands)
    key_w, value_w, recept_w, output_w, gate_w = matrices
    (
        output, grad_mid, grad_gate, grad_att, grad_recept, grad_key, grad_value, sums,
        part1, part2, rest1, rest2, squares,
    ) = middle_call(
        planes,
        micros,
        rows,
        (
            table, keep, segs, segcol, segrow, w1_all, w2_all, mh_all, ret_all, ret_acc, gmh_acc,
            parts1, parts2, mid, gate, adjoint, delta_b, keys, values, recept, num, den,
            gate_w, output_w, gated, mg,
        ),
    )
    (
        input_grad, sums, own_output, own_gate, own_recept, own_value, own_key, own_hidden,
        own_return,
    ) = last_call(
        planes,
        micros,
        rows,
        (
            table, keep, sums, squares, mr, grad_recept, mv, grad_value,
            mk, grad_key, recept_w, value_w, key_w, x, delta_a, grad_mid,
            part1, part2, rest1, rest2,
        ),
    )
    (
        output, input_grad, own_key, own_value, own_recept, own_output, own_hidden, own_return,
        own_gate,
    ) = hand_call(
        (
            output, input_grad, own_key, own_value, own_recept, own_output, own_hidden,
            own_return, own_gate,
        )
    )
    span = depth // (lax.axis_size("dp") * lax.axis_size("mp"))
    mine = lax.dynamic_slice_in_dim(
        sums, lax.axis_index(("dp", "mp")) * span, span, axis=1
    )
    line = [mine[index] for index in range(11)]
    shape = incoming_signal.shape
    return (
        output.reshape(shape),
        input_grad.reshape(shape),
        *line[:7],
        own_key,
        own_value,
        own_recept,
        own_output,
        *line[7:],
        own_hidden,
        own_return,
        own_gate,
    )


def solution(mesh):
    placed = (
        P(None, "dp", "mp", None),
        P(None, "dp", "mp"),
        P(None, "dp", "mp", None),
        P(),
        P(),
        P(),
        P(),
        P(),
        P(),
        P(),
        P(),
        P(),
        P(),
        P(),
        P(),
        P(),
        P(),
        P(),
        P(None, "mp"),
        P("mp", None),
        P(),
    )
    fits = mesh.shape["dp"] == 4 and mesh.shape["mp"] == 8
    return jax.shard_map(
        kernel_body if fits else generic_body,
        mesh=mesh,
        in_specs=placed,
        out_specs=(
            P(None, "dp", "mp", None),
            P(None, "dp", "mp", None),
            P(("dp", "mp")),
            P(("dp", "mp")),
            P(("dp", "mp")),
            P(("dp", "mp")),
            P(("dp", "mp")),
            P(("dp", "mp")),
            P(("dp", "mp")),
            P(("dp", "mp"), None),
            P(("dp", "mp"), None),
            P(("dp", "mp"), None),
            P(("dp", "mp"), None),
            P(("dp", "mp")),
            P(("dp", "mp")),
            P(("dp", "mp")),
            P(("dp", "mp")),
            P("dp", "mp"),
            P("mp", "dp"),
            P(("dp", "mp"), None),
        ),
        check_vma=False,
    )
```
